32 devices in a mesh: rep: 2 (over y), seq: 4 (over z), tp: 2 (over x), pp: 2 (over core).
Axes of the slice: x: 2, y: 2, z: 4, core: 2. Of those that a mesh axis runs over, the one named last changes fastest.
Arguments:
- queries: bfloat16 [128, 32, 8192], P(('rep', 'seq'), None, ('tp', 'pp')), parts along dimension 0, may hold values from -26 to 26
- resp_kv: bfloat16 [128, 32, 8, 256], P(('rep', 'seq'), None, 'tp'), parts along dimension 0, may hold values from -4.5 to 4.5
- prompt_kv: bfloat16 [8, 2048, 8, 256], P(('rep', 'seq'), None, 'tp'), parts along dimension 0, may hold values from -4.5 to 4.5
- lengths: int32 [128], P(('rep', 'seq')), parts along dimension 0, may hold values from 8 to 32
- group_of: int32 [128], P(('rep', 'seq')), parts along dimension 0, may hold values from 0 to 3, as said below
Outputs:
- mixed: bfloat16 [128, 32, 8192], P(('rep', 'seq'), None, ('tp', 'pp')), parts along dimension 0
The draws below stay inside these ranges and needn't reach their ends.
There are 2 independent parts, one for each index of `rep`. The reference program is written for one: setup_inputs(seed, part) draws one part's arguments, and reference() takes and returns one part's arrays. A program takes and returns all parts, laid end to end along the dimension named above; each array names one. Nothing has to cross between parts.
Inputs may be any that keep to these rules, and one draw needn't show every extreme that they name: `group_of`: each device of seq holds 16 responses; every prompt is answered by exactly 16 responses; at most 8 of the responses of one device answer the same prompt, and every device has a prompt with exactly 8 of its responses.
All inputs are finite; a program needn't handle non-finite values.
Results may differ from the reference program's by a relative error of at most 0.0049.
Values may be sent and summed in bfloat16 or wider, within the bound.
No kernel may reach another device: no remote copies, remote signals or barrier semaphores. Data moves between devices by JAX's collectives and lax.ppermute only.
A program may use at most 128 MiB of HBM per device.

```python
import jax
import jax.numpy as jnp
from jax import lax

HD = 128
QHEADS = 64
KVH = 8
GROUP = 16
PLEN = 2048
RLEN = 32
CAP = 8
PROMPTS = 4
RESPONSES = 64
N_SEQ = 4


def draw_queries(key, part):
    key = jax.random.fold_in(key, 1)
    key_base = jax.random.fold_in(key, 0)
    shape_full = (RESPONSES, RLEN, QHEADS, HD)
    values = jnp.clip(jax.random.normal(key_base, shape_full, jnp.float32), -4.5, 4.5)
    return values.reshape(RESPONSES, RLEN, QHEADS * HD).astype(jnp.bfloat16)


def draw_prompt_kv(key, part):
    key = jax.random.fold_in(key, 2)
    key_base = jax.random.fold_in(key, 0)
    shape_full = (PROMPTS, PLEN, KVH, 2 * HD)
    values = jnp.clip(jax.random.normal(key_base, shape_full, jnp.float32), -4.5, 4.5)
    return values.astype(jnp.bfloat16)


def draw_lengths(key, part):
    key = jax.random.fold_in(key, 3)
    key_lens, key_pick = jax.random.split(key, 2)
    drawn = jax.random.randint(key_lens, (RESPONSES,), RLEN // 4, RLEN + 1)
    picked = jax.random.randint(key_pick, (), 0, RESPONSES)
    return drawn.at[picked].set(RLEN).astype(jnp.int32)


def draw_group_of(key, part):
    key = jax.random.fold_in(key, 4)
    key_pairs, key_cols, key_rows, key_order = jax.random.split(key, 4)
    half_cap = CAP // 2
    offsets = jax.random.randint(key_pairs, (N_SEQ // 2,), -half_cap, half_cap + 1)
    offsets = offsets.at[0].set(half_cap)
    pattern = jnp.stack([half_cap + offsets, half_cap - offsets], axis=1).reshape(N_SEQ)
    column_perm = jax.random.permutation(key_cols, N_SEQ)
    row_perm = jax.random.permutation(key_rows, N_SEQ)
    counts = pattern[(column_perm[None, :] - row_perm[:, None]) % N_SEQ]
    running = jnp.cumsum(counts, axis=1)
    slot_ids = jnp.arange(GROUP)
    groups = jnp.sum((running[:, None, :] <= slot_ids[None, :, None]).astype(jnp.int32), axis=2)
    order_keys = jax.random.split(key_order, N_SEQ)
    orders = jax.vmap(lambda order_key: jax.random.permutation(order_key, GROUP))(order_keys)
    groups = jnp.take_along_axis(groups, orders, axis=1)
    return groups.reshape(RESPONSES).astype(jnp.int32)


def shard_levels(rng, shape, cuts, least, top_value):
    loudness, own = 1.0, jax.random.fold_in(rng, 6)
    for axis_at, parts in cuts:
        steps = jnp.exp(jax.random.uniform(jax.random.fold_in(own, axis_at), (parts,), jnp.float32, least / len(cuts), top_value / len(cuts)))
        loudness = loudness * jnp.repeat(steps, shape[axis_at] // parts).reshape([-1 if axis == axis_at else 1 for axis in range(len(shape))])
    return loudness


def normal_values(own_key, extent, scale, bound, pieces=(), held_as=jnp.bfloat16):
    values = jax.random.normal(own_key, extent, jnp.float32) * scale
    if len(pieces) > 0:
        values = shard_levels(own_key, extent, pieces, -0.22, 0.18) * values
    return jnp.clip(values, min=-bound, max=bound).astype(held_as)


def setup_inputs(seed: int = 0, part: int = 0) -> dict:
    streams_of = jax.random.split(jax.random.key(seed), 6)
    part_keys = jax.random.split(jax.random.fold_in(streams_of[5], part), 6)
    return {
        "queries": draw_queries(jax.random.fold_in(jax.random.fold_in(streams_of[5], part), 71), part),
        "resp_kv": normal_values(part_keys[1], (RESPONSES, RLEN, KVH, 2 * HD), 1.0, 4.5, ((0, 4), (2, 2))),
        "prompt_kv": draw_prompt_kv(jax.random.fold_in(jax.random.fold_in(streams_of[5], part), 71), part),
        "lengths": draw_lengths(jax.random.fold_in(jax.random.fold_in(streams_of[5], part), 71), part),
        "group_of": draw_group_of(jax.random.fold_in(jax.random.fold_in(streams_of[5], part), 71), part),
    }


def attend(q_rows, resp_pairs, prompt_pairs, length):
    head_size = resp_pairs.shape[2] // 2
    kv_count = resp_pairs.shape[1]
    row_count = q_rows.shape[0]
    per_kv = q_rows.shape[1] // (kv_count * head_size)
    score_scale = head_size ** -0.5
    query = q_rows.reshape(row_count, kv_count, per_kv, head_size).astype(jnp.float32)
    prompt_keys = prompt_pairs[:, :, :head_size].astype(jnp.float32)
    prompt_vals = prompt_pairs[:, :, head_size:].astype(jnp.float32)
    own_keys = resp_pairs[:, :, :head_size].astype(jnp.float32)
    own_vals = resp_pairs[:, :, head_size:].astype(jnp.float32)
    prompt_scores = jnp.einsum("tkgd,skd->kgts", query, prompt_keys) * score_scale
    own_scores = jnp.einsum("tkgd,skd->kgts", query, own_keys) * score_scale
    causal = jnp.arange(row_count)[:, None] >= jnp.arange(row_count)[None, :]
    own_scores = jnp.where(causal, own_scores, -1e30)
    peak_score = jnp.maximum(jnp.max(prompt_scores, axis=-1), jnp.max(own_scores, axis=-1))
    prompt_exp = jnp.exp(prompt_scores - peak_score[..., None])
    own_exp = jnp.exp(own_scores - peak_score[..., None])
    denominator = jnp.sum(prompt_exp, axis=-1) + jnp.sum(own_exp, axis=-1)
    prompt_weights = (prompt_exp / denominator[..., None]).astype(jnp.bfloat16).astype(jnp.float32)
    own_weights = (own_exp / denominator[..., None]).astype(jnp.bfloat16).astype(jnp.float32)
    output = jnp.einsum("kgts,skd->tkgd", prompt_weights, prompt_vals) + jnp.einsum("kgts,skd->tkgd", own_weights, own_vals)
    output = output.reshape(row_count, kv_count * per_kv * head_size)
    alive_rows = jnp.arange(row_count) < length
    return jnp.where(alive_rows[:, None], output, 0.0).astype(jnp.bfloat16)


def reference(queries, resp_kv, prompt_kv, lengths, group_of):
    def single(record):
        q_rows, resp_pairs, prompt_index, length = record
        prompt_pairs = lax.dynamic_index_in_dim(prompt_kv, prompt_index, 0, keepdims=False)
        return attend(q_rows, resp_pairs, prompt_pairs, length)

    return lax.map(single, (queries, resp_kv, group_of, lengths))
```

```python
import functools
import math

import jax
import jax.numpy as jnp
from jax import lax
from jax.experimental import pallas as pl
from jax.experimental.pallas import tpu as pltpu
from jax.sharding import PartitionSpec as P

QHEADS = 64
KVH = 8
HD = 128
LOG2E = math.log2(math.e)


def one_head(q_tile, own_tile, kv_buf, vt_buf, length, per_kv, plen, s_buf):
    rlen = q_tile.shape[0]
    cols = per_kv * rlen
    block = 256
    scale = HD ** -0.5 * LOG2E
    q_rows = jnp.concatenate([q_tile[:, g * HD:(g + 1) * HD] for g in range(per_kv)], axis=0)
    nt = (((1,), (1,)), ((), ()))
    own = lax.dot_general(own_tile[:, :HD], q_rows, nt, preferred_element_type=jnp.float32)
    own_at = lax.broadcasted_iota(jnp.int32, (rlen, cols), 0)
    token_at = lax.broadcasted_iota(jnp.int32, (rlen, cols), 1) % rlen
    own = jnp.where(own_at <= token_at, own, -1e30)
    peak = jnp.max(own, axis=0, keepdims=True)
    for at in range(0, plen, block):
        part = lax.dot_general(kv_buf[at:at + block, :HD], q_rows, nt, preferred_element_type=jnp.float32)
        s_buf[at:at + block, :] = part
        peak = jnp.maximum(peak, jnp.max(part, axis=0, keepdims=True))
    own_exp = jnp.exp2((own - peak) * scale)
    total = jnp.sum(own_exp, axis=0, keepdims=True)
    tn = (((0,), (0,)), ((), ()))
    acc = lax.dot_general(own_tile[:, HD:], own_exp.astype(jnp.bfloat16), tn, preferred_element_type=jnp.float32)
    for at in range(0, plen, block):
        part = jnp.exp2((s_buf[at:at + block, :] - peak) * scale)
        total = total + jnp.sum(part, axis=0, keepdims=True)
        acc = acc + jnp.dot(vt_buf[:, at:at + block], part.astype(jnp.bfloat16), preferred_element_type=jnp.float32)
    out = (acc / total).T
    alive = lax.broadcasted_iota(jnp.int32, (rlen, HD), 0) < length
    return [jnp.where(alive, out[g * rlen:(g + 1) * rlen, :], 0.0).astype(jnp.bfloat16) for g in range(per_kv)]


def attend_kernel(load_kv, n_cand, per_kv, head, cap, meta, q_ref, own_ref, *rest):
    cands = rest[:n_cand]
    out_ref = rest[n_cand + 1]
    q_buf, own_buf, kv_buf, vt_buf, s_buf, o_buf, q_sem, own_sem, kv_sem, o_sem = rest[n_cand + 2:]
    plen = kv_buf.shape[0]
    width = per_kv * HD
    lanes = pl.ds(head * width, width)
    count = meta[0]

    def q_copy(i, slot):
        return pltpu.make_async_copy(q_ref.at[meta[1 + i], :, lanes], q_buf.at[slot], q_sem.at[slot])

    def own_copy(i, slot):
        return pltpu.make_async_copy(own_ref.at[meta[1 + i]], own_buf.at[slot], own_sem.at[slot])

    def o_copy(i, slot):
        return pltpu.make_async_copy(o_buf.at[slot], out_ref.at[meta[1 + i], :, lanes], o_sem.at[slot])

    @pl.when(count > 0)
    def _():
        q_copy(0, 0).start()
        own_copy(0, 0).start()

        def step(i, before):
            slot = lax.rem(i, 2)
            source = meta[1 + cap + i]

            @pl.when(i + 1 < count)
            def _():
                q_copy(i + 1, 1 - slot).start()
                own_copy(i + 1, 1 - slot).start()

            @pl.when(source != before)
            def _():
                load_kv(cands, source, kv_buf, kv_sem)
                vt_buf[...] = kv_buf[:, HD:].T

            q_copy(i, slot).wait()
            own_copy(i, slot).wait()

            @pl.when(i >= 2)
            def _():
                o_copy(i, slot).wait()

            parts = one_head(q_buf[slot], own_buf[slot], kv_buf, vt_buf, meta[1 + 2 * cap + i], per_kv, plen, s_buf)
            for g in range(per_kv):
                o_buf[slot, :, g * HD:(g + 1) * HD] = parts[g]
            o_copy(i, slot).start()
            return source

        lax.fori_loop(0, count, step, jnp.int32(-1))
        o_copy(0, 0).wait()

        @pl.when(count > 1)
        def _():
            o_copy(0, 1).wait()


def load_stacked(cands, source, kv_buf, kv_sem):
    copy = pltpu.make_async_copy(cands[0].at[source], kv_buf, kv_sem)
    copy.start()
    copy.wait()


def attend(meta, cap, queries, own, cands, out, head, per_kv, plen, load_kv):
    rlen = queries.shape[1]
    width = per_kv * HD
    cols = per_kv * rlen
    hbm = pl.BlockSpec(memory_space=pl.ANY)
    n_cand = len(cands)
    return pl.pallas_call(
        functools.partial(attend_kernel, load_kv, n_cand, per_kv, head, cap),
        out_shape=jax.ShapeDtypeStruct(out.shape, out.dtype),
        in_specs=[pl.BlockSpec(memory_space=pltpu.SMEM)] + [hbm] * (3 + n_cand),
        out_specs=hbm,
        input_output_aliases={3 + n_cand: 0},
        scratch_shapes=[
            pltpu.VMEM((2, rlen, width), jnp.bfloat16),
            pltpu.VMEM((2, rlen, 2 * HD), jnp.bfloat16),
            pltpu.VMEM((plen, 2 * HD), jnp.bfloat16),
            pltpu.VMEM((HD, plen), jnp.bfloat16),
            pltpu.VMEM((plen, cols), jnp.float32),
            pltpu.VMEM((2, rlen, width), jnp.bfloat16),
            pltpu.SemaphoreType.DMA((2,)),
            pltpu.SemaphoreType.DMA((2,)),
            pltpu.SemaphoreType.DMA,
            pltpu.SemaphoreType.DMA((2,)),
        ],
        compiler_params=pltpu.CompilerParams(vmem_limit_bytes=32 * 1024 * 1024),
        cost_estimate=pl.CostEstimate(flops=1 << 31, bytes_accessed=1 << 23, transcendentals=1 << 23),
    )(meta, queries, own, *cands, out)


def ranked(valid, key, source, lengths):
    n = valid.shape[0]
    at = jnp.arange(n)
    key = jnp.where(valid, key, 1 << 20) * n + at
    rank = jnp.sum((key[None, :] < key[:, None]).astype(jnp.int32), axis=1)
    place = rank[None, :] == at[:, None]

    def put(values):
        return jnp.sum(jnp.where(place, values[None, :], 0), axis=1)

    return jnp.concatenate([jnp.sum(valid.astype(jnp.int32))[None], put(at), put(source), put(lengths)]).astype(jnp.int32)


def shards(queries, resp_kv, prompt_kv, lengths, group_of):
    local_heads = queries.shape[2] // HD
    group = QHEADS // KVH
    kv_needed = max(local_heads // group, 1)
    per_kv = local_heads // kv_needed
    first_head = lax.axis_index("pp") * local_heads // group
    plen = prompt_kv.shape[1]
    cap = group_of.shape[0]
    meta = ranked(jnp.ones((cap,), bool), group_of, group_of, lengths)
    out = jnp.zeros(queries.shape, jnp.bfloat16)
    for head in range(kv_needed):
        mine = lax.dynamic_index_in_dim(prompt_kv, first_head + head, 2, keepdims=False)
        own = lax.dynamic_index_in_dim(resp_kv, first_head + head, 2, keepdims=False)
        whole = lax.all_gather(mine, "seq", axis=0, tiled=True)
        out = attend(meta, cap, queries, own, [whole], out, head, per_kv, plen, load_stacked)
    return out


def solution(mesh):
    placed = (
        P(("rep", "seq"), None, ("tp", "pp")),
        P(("rep", "seq"), None, "tp", None),
        P(("rep", "seq"), None, "tp", None),
        P(("rep", "seq")),
        P(("rep", "seq")),
    )
    return jax.shard_map(
        shards,
        mesh=mesh,
        in_specs=placed,
        out_specs=P(("rep", "seq"), None, ("tp", "pp")),
        check_vma=False,
    )
```

```python
import functools
import math

import jax
import jax.numpy as jnp
from jax import lax
from jax.experimental import pallas as pl
from jax.experimental.pallas import tpu as pltpu
from jax.sharding import PartitionSpec as P

QHEADS = 64
KVH = 8
HD = 128
LOG2E = math.log2(math.e)
VMEM_BYTES = 56 * 1024 * 1024
SLOTS = 8


def one_head(q_tile, own_tile, kv_buf, vt_buf, length, per_kv, plen, s_buf):
    rlen = q_tile.shape[0]
    cols = per_kv * rlen
    block = 256
    scale = HD ** -0.5 * LOG2E
    q_rows = jnp.concatenate([q_tile[:, g * HD:(g + 1) * HD] for g in range(per_kv)], axis=0)
    nt = (((1,), (1,)), ((), ()))
    own = lax.dot_general(own_tile[:, :HD], q_rows, nt, preferred_element_type=jnp.float32)
    own_at = lax.broadcasted_iota(jnp.int32, (rlen, cols), 0)
    token_at = lax.broadcasted_iota(jnp.int32, (rlen, cols), 1) % rlen
    own = jnp.where(own_at <= token_at, own, -1e30)
    peak = jnp.max(own, axis=0, keepdims=True)
    for at in range(0, plen, block):
        part = lax.dot_general(kv_buf[at:at + block, :HD], q_rows, nt, preferred_element_type=jnp.float32)
        s_buf[at:at + block, :] = part
        peak = jnp.maximum(peak, jnp.max(part, axis=0, keepdims=True))
    own_exp = jnp.exp2((own - peak) * scale)
    total = jnp.sum(own_exp, axis=0, keepdims=True)
    tn = (((0,), (0,)), ((), ()))
    acc = lax.dot_general(own_tile[:, HD:], own_exp.astype(jnp.bfloat16), tn, preferred_element_type=jnp.float32)
    for at in range(0, plen, block):
        part = jnp.exp2((s_buf[at:at + block, :] - peak) * scale)
        total = total + jnp.sum(part, axis=0, keepdims=True)
        acc = acc + jnp.dot(vt_buf[:, at:at + block], part.astype(jnp.bfloat16), preferred_element_type=jnp.float32)
    out = (acc / total).T
    alive = lax.broadcasted_iota(jnp.int32, (rlen, HD), 0) < length
    return [jnp.where(alive, out[g * rlen:(g + 1) * rlen, :], 0.0).astype(jnp.bfloat16) for g in range(per_kv)]


def attend_kernel(n_cand, parts, per_kv, head, cap, split, two, fresh, meta, *refs):
    refs = list(refs)
    q_refs, own_refs = [refs.pop(0)], [refs.pop(0)]
    if two:
        q_refs.append(refs.pop(0))
        own_refs.append(refs.pop(0))
    cands = [refs.pop(0) for _ in range(n_cand * parts)]
    if not fresh:
        refs = refs[2 if two else 1:]
    out_refs = [refs.pop(0)]
    if two:
        out_refs.append(refs.pop(0))
    q_buf, own_buf, kv_buf, vt_buf, s_buf, o_buf, q_sem, own_sem, kv_sem, o_sem = refs
    plen = kv_buf.shape[0]
    width = per_kv * HD
    count = meta[0]

    def each_array(i, act):
        at = meta[1 + i]
        if not two:
            act(0, at, pl.ds(head * width, width))
            return

        @pl.when(at < split)
        def _():
            act(0, at, pl.ds(head * width, width))

        @pl.when(at >= split)
        def _():
            act(1, at - split, pl.ds(0, width))

    def fetch(i, slot):
        def act(which, at, lanes):
            pltpu.make_async_copy(q_refs[which].at[at, :, lanes], q_buf.at[slot], q_sem.at[slot]).start()
            pltpu.make_async_copy(own_refs[which].at[at], own_buf.at[slot], own_sem.at[slot]).start()

        each_array(i, act)

    def fetched(slot):
        pltpu.make_async_copy(q_refs[0].at[0, :, pl.ds(0, width)], q_buf.at[slot], q_sem.at[slot]).wait()
        pltpu.make_async_copy(own_refs[0].at[0], own_buf.at[slot], own_sem.at[slot]).wait()

    def store(i, slot):
        def act(which, at, lanes):
            pltpu.make_async_copy(o_buf.at[slot], out_refs[which].at[at, :, lanes], o_sem.at[slot]).start()

        each_array(i, act)

    def stored(slot):
        pltpu.make_async_copy(o_buf.at[slot], out_refs[0].at[0, :, pl.ds(0, width)], o_sem.at[slot]).wait()

    def load(source):
        if parts == 0:
            raise ValueError
        if n_cand == 1 and len(cands[0].shape) == 3:
            copy = pltpu.make_async_copy(cands[0].at[source], kv_buf, kv_sem)
            copy.start()
            copy.wait()
            return
        rows = plen // parts
        for which in range(n_cand):
            @pl.when(source == which)
            def _():
                for part in range(parts):
                    pltpu.make_async_copy(cands[which * parts + part], kv_buf.at[pl.ds(part * rows, rows)], kv_sem).start()

        pltpu.make_async_copy(kv_buf, kv_buf, kv_sem).wait()

    @pl.when(count > 0)
    def _():
        fetch(0, 0)

        def step(i, before):
            slot = lax.rem(i, 2)
            source = meta[1 + cap + i]

            @pl.when(i + 1 < count)
            def _():
                fetch(i + 1, 1 - slot)

            @pl.when(source != before)
            def _():
                load(source)
                vt_buf[...] = kv_buf[:, HD:].T

            fetched(slot)

            @pl.when(i >= 2)
            def _():
                stored(slot)

            tiles = one_head(q_buf[slot], own_buf[slot], kv_buf, vt_buf, meta[1 + 2 * cap + i], per_kv, plen, s_buf)
            for g in range(per_kv):
                o_buf[slot, :, g * HD:(g + 1) * HD] = tiles[g]
            store(i, slot)
            return source

        lax.fori_loop(0, count, step, jnp.int32(-1))
        stored(0)

        @pl.when(count > 1)
        def _():
            stored(1)


def attend(meta, cap, queries, own, cands, parts, outs, head, per_kv, plen, items, fresh=False):
    rlen = queries[0].shape[1]
    width = per_kv * HD
    cols = per_kv * rlen
    two = len(queries) == 2
    hbm = pl.BlockSpec(memory_space=pl.ANY)
    n_cand = len(cands) // parts
    operands = [meta]
    for q_array, own_array in zip(queries, own):
        operands += [q_array, own_array]
    operands += cands
    aliases = {}
    if not fresh:
        aliases = {len(operands) + i: i for i in range(len(outs))}
        operands += outs
    result = pl.pallas_call(
        functools.partial(attend_kernel, n_cand, parts, per_kv, head, cap, queries[0].shape[0], two, fresh),
        out_shape=[jax.ShapeDtypeStruct(o.shape, o.dtype) for o in outs],
        in_specs=[pl.BlockSpec(memory_space=pltpu.SMEM)] + [hbm] * (len(operands) - 1),
        out_specs=[hbm] * len(outs),
        input_output_aliases=aliases,
        scratch_shapes=[
            pltpu.VMEM((2, rlen, width), jnp.bfloat16),
            pltpu.VMEM((2, rlen, 2 * HD), jnp.bfloat16),
            pltpu.VMEM((plen, 2 * HD), jnp.bfloat16),
            pltpu.VMEM((HD, plen), jnp.bfloat16),
            pltpu.VMEM((plen, cols), jnp.float32),
            pltpu.VMEM((2, rlen, width), jnp.bfloat16),
            pltpu.SemaphoreType.DMA((2,)),
            pltpu.SemaphoreType.DMA((2,)),
            pltpu.SemaphoreType.DMA,
            pltpu.SemaphoreType.DMA((2,)),
        ],
        compiler_params=pltpu.CompilerParams(vmem_limit_bytes=VMEM_BYTES),
        cost_estimate=pl.CostEstimate(flops=int(items * 1.2e9), bytes_accessed=1 << 21, transcendentals=0),
    )(*operands)
    return result


def merge_kernel(slots, width, meta, *refs):
    received, out_ref, sem = refs[:2], refs[3], refs[4]
    count = meta[0]

    def copy(j, head):
        lanes = pl.ds(head * width, width)
        return pltpu.make_async_copy(received[head].at[j], out_ref.at[meta[1 + j], :, lanes], sem)

    def start(j, _):
        copy(j, 0).start()
        copy(j, 1).start()
        return 0

    def wait(j, _):
        copy(j, 0).wait()
        copy(j, 1).wait()
        return 0

    lax.fori_loop(0, count, start, 0)
    lax.fori_loop(0, count, wait, 0)


def merge(meta, received, out, width):
    hbm = pl.BlockSpec(memory_space=pl.ANY)
    return pl.pallas_call(
        functools.partial(merge_kernel, received[0].shape[0], width),
        out_shape=jax.ShapeDtypeStruct(out.shape, out.dtype),
        in_specs=[pl.BlockSpec(memory_space=pltpu.SMEM)] + [hbm] * 3,
        out_specs=hbm,
        input_output_aliases={3: 0},
        scratch_shapes=[pltpu.SemaphoreType.DMA],
        compiler_params=pltpu.CompilerParams(vmem_limit_bytes=VMEM_BYTES),
    )(meta, *received, out)


def ranked(valid, key, source, lengths):
    n = valid.shape[0]
    at = jnp.arange(n)
    key = jnp.where(valid, key, 1 << 20) * n + at
    rank = jnp.sum((key[None, :] < key[:, None]).astype(jnp.int32), axis=1)
    place = rank[None, :] == at[:, None]

    def put(values):
        return jnp.sum(jnp.where(place, values[None, :], 0), axis=1)

    return jnp.concatenate([jnp.sum(valid.astype(jnp.int32))[None], put(at), put(source), put(lengths)]).astype(jnp.int32)


def after(value, *others):
    return lax.optimization_barrier((value,) + others)[0]


def gathered(queries, resp_kv, prompt_kv, lengths, group_of, first_head, kv_needed, per_kv):
    plen = prompt_kv.shape[1]
    cap = group_of.shape[0]
    meta = ranked(jnp.ones((cap,), bool), group_of, group_of, lengths)
    out = jnp.zeros(queries.shape, jnp.bfloat16)
    for head in range(kv_needed):
        mine = lax.dynamic_index_in_dim(prompt_kv, first_head + head, 2, keepdims=False)
        own = lax.dynamic_index_in_dim(resp_kv, first_head + head, 2, keepdims=False)
        whole = lax.all_gather(mine, "seq", axis=0, tiled=True)
        [out] = attend(meta, cap, [queries], [own], [whole], 1, [out], head, per_kv, plen, 16)
    return out


def counted(groups, prompt):
    return jnp.sum((groups == prompt).astype(jnp.int32))


def relayed(queries, resp_kv, prompt_kv, lengths, group_of, first_head, per_kv):
    me = lax.axis_index("seq")
    plen = prompt_kv.shape[1]
    half = plen // 2
    cap, rlen = queries.shape[0], queries.shape[1]
    width = per_kv * HD
    middle, inward, outward = [(1, 2), (2, 1)], [(0, 1), (3, 2)], [(1, 0), (2, 3)]

    mine = []
    source = prompt_kv
    for head in range(2):
        for part in range(2):
            piece = lax.dynamic_slice(source, (0, part * half, first_head + head, 0), (1, half, 1, 2 * HD))
            piece = piece.reshape(half, 2 * HD)
            source, piece = lax.optimization_barrier((source, piece))
            mine.append(piece)

    def send(pairs, value):
        return lax.ppermute(value, "seq", pairs)

    mid, inn, out_got = [None] * 8, [None] * 6, [None] * 4
    for k in range(2):
        mid[k] = send(middle, mine[k])
        inn[k] = send(inward, mine[k])

    facts = lax.all_gather(jnp.stack([group_of, lengths]), "seq", axis=0)
    facts = after(facts, mine[1])
    is_inner = (me == 1) | (me == 2)
    low = me < 2
    outer, inner = jnp.where(low, 0, 3), jnp.where(low, 1, 2)
    far_inner, far_outer = jnp.where(low, 2, 1), jnp.where(low, 3, 0)
    their_groups = jnp.where(low, facts[0, 0], facts[3, 0])
    their_lengths = jnp.where(low, facts[0, 1], facts[3, 1])
    far_groups = jnp.where(low, facts[3, 0], facts[0, 0])
    straight = counted(their_groups, far_inner) >= counted(their_groups, far_outer)
    far_straight = counted(far_groups, inner) >= counted(far_groups, outer)
    early = jnp.where(straight, far_inner, far_outer)
    late = jnp.where(straight, far_outer, far_inner)
    takes_inner = counted(their_groups, inner) >= counted(their_groups, early)
    taken = jnp.where(takes_inner, inner, early)
    handed = (their_groups != outer) & (their_groups != taken)
    handed_list = ranked(handed, jnp.zeros((cap,), jnp.int32), their_groups, their_lengths)
    handed_at = handed_list[1:1 + SLOTS]
    handed_group = handed_list[1 + cap:1 + cap + SLOTS]
    handed_length = handed_list[1 + 2 * cap:1 + 2 * cap + SLOTS]
    handed_valid = (jnp.arange(SLOTS) < handed_list[0]) & is_inner

    group24 = jnp.concatenate([group_of, handed_group])
    length24 = jnp.concatenate([lengths, handed_length])
    is_local = jnp.arange(cap + SLOTS) < cap
    valid24 = jnp.concatenate([jnp.ones((cap,), bool), handed_valid])
    zero24 = jnp.zeros((cap + SLOTS,), jnp.int32)
    zero16 = jnp.zeros((cap,), jnp.int32)
    meta_own = ranked(group_of == me, zero16, zero16, lengths)
    meta_near = ranked((group_of == outer) & is_inner, zero16, zero16, lengths)
    meta_taken = ranked((group_of == taken) & ~is_inner, zero16, zero16, lengths)
    source24 = jnp.where(group24 == early, jnp.where(straight, 1, 2), 0)
    meta_early = ranked(
        valid24 & is_inner & ((group24 == early) | ((group24 == inner) & ~is_local)), source24, source24, length24)
    late_source = jnp.where(straight, zero24, 1)
    is_late = valid24 & is_inner & (group24 == late)
    meta_late = ranked(is_late, is_local.astype(jnp.int32), late_source, length24)
    meta_late_handed = ranked(is_late & ~is_local, zero24, late_source, length24)
    meta_late_local = ranked((is_late & is_local)[:cap], zero16, late_source[:cap], lengths)
    meta_merge = jnp.where(is_inner, 0, handed_list)

    own = [lax.dynamic_index_in_dim(resp_kv, first_head + head, 2, keepdims=False) for head in range(2)]
    out = jax.ShapeDtypeStruct(queries.shape, jnp.bfloat16)
    handed_shape = jax.ShapeDtypeStruct((SLOTS, rlen, width), jnp.bfloat16)

    def run(meta, items, head, cands, outs, extra=None, fresh=False):
        if extra is None:
            return attend(meta, cap, [queries], [own[head]], cands, 2, outs, head, per_kv, plen, items, fresh)
        return attend(meta, cap + SLOTS, [queries, extra[0]], [own[head], extra[1]], cands, 2, outs, head, per_kv, plen, items, fresh)

    def forwarded(k):
        return jnp.where(takes_inner, mine[k], jnp.where(straight, mid[k], mid[2 + k]))

    def given(head):
        q_part = queries[:, :, head * width:(head + 1) * width]
        return jnp.take(q_part, handed_at, axis=0, mode="clip"), jnp.take(own[head], handed_at, axis=0, mode="clip")

    [out] = run(meta_own, 4, 0, mine[0:2], [out], fresh=True)
    inn[2] = send(inward, after(mine[2], inn[0]))
    mid[2] = send(middle, after(jnp.where(far_straight, mine[2], inn[0]), mid[0]))
    [out] = run(meta_own, 4, 1, mine[2:4], [out])
    inn[3] = send(inward, after(mine[3], inn[1]))
    mid[3] = send(middle, after(jnp.where(far_straight, mine[3], inn[1]), mid[1]))
    [out] = run(meta_near, 4, 0, inn[0:2], [out])
    gave = [None, None]
    q0, k0 = given(0)
    gave[0] = (send(inward, after(q0, inn[2])), send(inward, after(k0, inn[2])))
    mid[4] = send(middle, after(jnp.where(far_straight, inn[0], inn[2]), mid[2]))
    out_got[0] = send(outward, after(forwarded(0), mid[2]))
    [out] = run(meta_near, 4, 1, inn[2:4], [out])
    q1, k1 = given(1)
    gave[1] = (send(inward, after(q1, inn[3])), send(inward, after(k1, inn[3])))
    mid[5] = send(middle, after(jnp.where(far_straight, inn[1], inn[3]), mid[3]))
    out_got[1] = send(outward, after(forwarded(1), mid[3]))
    done = [handed_shape, handed_shape]
    early_cands = lambda h: mine[2 * h:2 * h + 2] + mid[2 * h:2 * h + 2] + mid[2 + 2 * h:4 + 2 * h]
    got0 = jnp.zeros(handed_shape.shape, handed_shape.dtype)
    got1 = jnp.zeros(handed_shape.shape, handed_shape.dtype)
    out, got0 = run(meta_early, 6, 0, early_cands(0), [out, got0], gave[0])
    mid[6] = send(middle, after(jnp.where(far_straight, inn[2], mine[2]), mid[4]))
    out_got[2] = send(outward, after(forwarded(2), mid[4]))
    out, got1 = run(meta_early, 6, 1, early_cands(1), [out, got1], gave[1])
    mid[7] = send(middle, after(jnp.where(far_straight, inn[3], mine[3]), mid[5]))
    out_got[3] = send(outward, after(forwarded(3), mid[5]))
    out, got0 = run(meta_late, 4, 0, mid[4:6] + mid[0:2], [out, got0], gave[0])
    back0 = send(outward, got0)
    [out] = run(meta_taken, 4, 0, out_got[0:2], [out])
    out, got1 = run(meta_late_handed, 2, 1, mid[6:8] + mid[6:8], [out, got1], gave[1])
    back1 = send(outward, got1)
    [out] = run(meta_late_local, 4, 1, mid[6:8] + mid[6:8], [out])
    [out] = run(meta_taken, 4, 1, out_got[2:4], [out])
    return merge(meta_merge, [back0, back1], out, width)


def shards(queries, resp_kv, prompt_kv, lengths, group_of):
    local_heads = queries.shape[2] // HD
    group = QHEADS // KVH
    kv_needed = max(local_heads // group, 1)
    per_kv = local_heads // kv_needed
    first_head = lax.axis_index("pp") * local_heads // group
    args = (queries, resp_kv, prompt_kv, lengths, group_of, first_head)
    if lax.axis_size("seq") == 4 and kv_needed == 2 and prompt_kv.shape[0] == 1:
        return relayed(*args, per_kv)
    return gathered(*args, kv_needed, per_kv)


def solution(mesh):
    placed = (
        P(("rep", "seq"), None, ("tp", "pp")),
        P(("rep", "seq"), None, "tp", None),
        P(("rep", "seq"), None, "tp", None),
        P(("rep", "seq")),
        P(("rep", "seq")),
    )
    return jax.shard_map(
        shards,
        mesh=mesh,
        in_specs=placed,
        out_specs=P(("rep", "seq"), None, ("tp", "pp")),
        check_vma=False,
    )
```

```python
import functools
import math

import jax
import jax.numpy as jnp
from jax import lax
from jax.experimental import pallas as pl
from jax.experimental.pallas import tpu as pltpu
from jax.sharding import PartitionSpec as P

QHEADS = 64
KVH = 8
HD = 128
LOG2E = math.log2(math.e)
VMEM_BYTES = 56 * 1024 * 1024
SLOTS = 8
HBM = pl.BlockSpec(memory_space=pl.ANY)
SMEM = pl.BlockSpec(memory_space=pltpu.SMEM)


def one_head(q_tile, own_tile, kv_buf, vt_buf, length, per_kv, plen, s_buf):
    rlen = q_tile.shape[0]
    cols = per_kv * rlen
    block = 256
    scale = HD ** -0.5 * LOG2E
    q_rows = jnp.concatenate([q_tile[:, g * HD:(g + 1) * HD] for g in range(per_kv)], axis=0)
    nt = (((1,), (1,)), ((), ()))
    own = lax.dot_general(own_tile[:, :HD], q_rows, nt, preferred_element_type=jnp.float32)
    own_at = lax.broadcasted_iota(jnp.int32, (rlen, cols), 0)
    token_at = lax.broadcasted_iota(jnp.int32, (rlen, cols), 1) % rlen
    own = jnp.where(own_at <= token_at, own, -1e30)
    peak = jnp.max(own, axis=0, keepdims=True)
    for at in range(0, plen, block):
        part = lax.dot_general(kv_buf[at:at + block, :HD], q_rows, nt, preferred_element_type=jnp.float32)
        s_buf[at:at + block, :] = part
        peak = jnp.maximum(peak, jnp.max(part, axis=0, keepdims=True))
    own_exp = jnp.exp2((own - peak) * scale)
    total = jnp.sum(own_exp, axis=0, keepdims=True)
    tn = (((0,), (0,)), ((), ()))
    acc = lax.dot_general(own_tile[:, HD:], own_exp.astype(jnp.bfloat16), tn, preferred_element_type=jnp.float32)
    for at in range(0, plen, block):
        part = jnp.exp2((s_buf[at:at + block, :] - peak) * scale)
        total = total + jnp.sum(part, axis=0, keepdims=True)
        acc = acc + jnp.dot(vt_buf[:, at:at + block], part.astype(jnp.bfloat16), preferred_element_type=jnp.float32)
    out = (acc / total).T
    alive = lax.broadcasted_iota(jnp.int32, (rlen, HD), 0) < length
    return [jnp.where(alive, out[g * rlen:(g + 1) * rlen, :], 0.0).astype(jnp.bfloat16) for g in range(per_kv)]


def listed(items, cap, count, groups, lengths, target, source, first, slots):
    def look(at, state):
        n, slot = state
        hit = groups[at] == target

        @pl.when(hit)
        def _():
            items[n] = first + (slot if slots else at)
            items[cap + n] = source
            items[2 * cap + n] = lengths[at]

        step = hit.astype(jnp.int32)
        return n + step, slot + step

    return lax.fori_loop(0, groups.shape[0], look, (count, jnp.int32(0)))[0]


def attend_kernel(passes, n_cand, per_kv, head, two, fresh, *refs):
    refs = list(refs)
    facts, groups, lengths = refs[:3]
    refs = refs[3:]
    if two:
        far_groups, far_lengths, x_ref = refs[:3]
        refs = refs[3:]
    q_ref, own_ref = refs[:2]
    cands, refs = refs[2:2 + n_cand], refs[2 + n_cand:]
    n_out = 2 if two else 1
    if not fresh:
        refs = refs[n_out:]
    outs, refs = refs[:n_out], refs[n_out:]
    items, q_buf, own_buf, kv_buf, vt_buf, s_buf, o_buf, q_sem, own_sem, kv_sem, o_sem = refs
    local = groups.shape[0]
    cap = items.shape[0] // 3
    width = per_kv * HD
    stacked = passes is None

    count = jnp.int32(0)
    if stacked:
        def one_prompt(prompt, n):
            return listed(items, cap, n, groups, lengths, prompt, prompt, 0, False)

        count = lax.fori_loop(0, cands[0].shape[0], one_prompt, count)
    else:
        for far, target, source in passes:
            if far:
                count = listed(items, cap, count, far_groups, far_lengths, facts[target], facts[source], local, True)
            else:
                count = listed(items, cap, count, groups, lengths, facts[target], facts[source], 0, False)

    def each_array(i, act_local, act_far):
        at = items[i]
        if not two:
            act_local(at)
            return

        @pl.when(at < local)
        def _():
            act_local(at)

        @pl.when(at >= local)
        def _():
            act_far(at - local)

    mine = pl.ds(head * width, width)
    first, last = pl.ds(0, width), pl.ds(width, 2 * HD)

    def fetch(i, slot):
        def here(at):
            pltpu.make_async_copy(q_ref.at[at, :, mine], q_buf.at[slot], q_sem.at[slot]).start()
            pltpu.make_async_copy(own_ref.at[at], own_buf.at[slot], own_sem.at[slot]).start()

        def far(at):
            pltpu.make_async_copy(x_ref.at[at, :, first], q_buf.at[slot], q_sem.at[slot]).start()
            pltpu.make_async_copy(x_ref.at[at, :, last], own_buf.at[slot], own_sem.at[slot]).start()

        each_array(i, here, far)

    def fetched(slot):
        pltpu.make_async_copy(q_ref.at[0, :, first], q_buf.at[slot], q_sem.at[slot]).wait()
        pltpu.make_async_copy(own_ref.at[0], own_buf.at[slot], own_sem.at[slot]).wait()

    def store(i, slot):
        def here(at):
            pltpu.make_async_copy(o_buf.at[slot], outs[0].at[at, :, mine], o_sem.at[slot]).start()

        def far(at):
            pltpu.make_async_copy(o_buf.at[slot], outs[1].at[at], o_sem.at[slot]).start()

        each_array(i, here, far)

    def stored(slot):
        pltpu.make_async_copy(o_buf.at[slot], outs[0].at[0, :, first], o_sem.at[slot]).wait()

    def load(source):
        if stacked:
            pltpu.make_async_copy(cands[0].at[source], kv_buf, kv_sem).start()
        else:
            for which in range(n_cand):
                @pl.when(source == which)
                def _():
                    pltpu.make_async_copy(cands[which], kv_buf, kv_sem).start()

        pltpu.make_async_copy(kv_buf, kv_buf, kv_sem).wait()

    @pl.when(count > 0)
    def _():
        fetch(0, 0)

        def step(i, before):
            slot = lax.rem(i, 2)
            source = items[cap + i]

            @pl.when(i + 1 < count)
            def _():
                fetch(i + 1, 1 - slot)

            @pl.when(source != before)
            def _():
                load(source)
                vt_buf[...] = kv_buf[:, HD:].T

            fetched(slot)

            @pl.when(i >= 2)
            def _():
                stored(slot)

            tiles = one_head(q_buf[slot], own_buf[slot], kv_buf, vt_buf, items[2 * cap + i], per_kv, kv_buf.shape[0], s_buf)
            for g in range(per_kv):
                o_buf[slot, :, g * HD:(g + 1) * HD] = tiles[g]
            store(i, slot)
            return source

        lax.fori_loop(0, count, step, jnp.int32(-1))
        stored(0)

        @pl.when(count > 1)
        def _():
            stored(1)


def attend(facts, groups, lengths, queries, own, cands, outs, head, per_kv, passes, items, far=None, fresh=False):
    rlen = queries.shape[1]
    plen = cands[0].shape[-2]
    width = per_kv * HD
    small = [facts, groups, lengths] + (list(far[:2]) if far else [])
    large = ([far[2]] if far else []) + [queries, own] + cands
    operands = small + large
    aliases = {}
    if not fresh:
        aliases = {len(operands) + i: i for i in range(len(outs))}
        operands += outs
    cap = groups.shape[0] + (SLOTS if far else 0)
    return pl.pallas_call(
        functools.partial(attend_kernel, passes, len(cands), per_kv, head, far is not None, fresh),
        out_shape=[jax.ShapeDtypeStruct(o.shape, o.dtype) for o in outs],
        in_specs=[SMEM] * len(small) + [HBM] * (len(operands) - len(small)),
        out_specs=[HBM] * len(outs),
        input_output_aliases=aliases,
        scratch_shapes=[
            pltpu.SMEM((3 * cap,), jnp.int32),
            pltpu.VMEM((2, rlen, width), jnp.bfloat16),
            pltpu.VMEM((2, rlen, 2 * HD), jnp.bfloat16),
            pltpu.VMEM((plen, 2 * HD), jnp.bfloat16),
            pltpu.VMEM((HD, plen), jnp.bfloat16),
            pltpu.VMEM((plen, per_kv * rlen), jnp.float32),
            pltpu.VMEM((2, rlen, width), jnp.bfloat16),
            pltpu.SemaphoreType.DMA((2,)),
            pltpu.SemaphoreType.DMA((2,)),
            pltpu.SemaphoreType.DMA,
            pltpu.SemaphoreType.DMA((2,)),
        ],
        compiler_params=pltpu.CompilerParams(vmem_limit_bytes=VMEM_BYTES),
        cost_estimate=pl.CostEstimate(flops=int(items * 1.2e9), bytes_accessed=1 << 21, transcendentals=0),
    )(*operands)


def pack_kernel(target, width, facts, groups, q_ref, own0, own1, out0, out1, sem):
    owns, outs = (own0, own1), (out0, out1)

    def copies(at, slot):
        made = []
        for head in range(2):
            made.append(pltpu.make_async_copy(
                q_ref.at[at, :, pl.ds(head * width, width)], outs[head].at[slot, :, pl.ds(0, width)], sem))
            made.append(pltpu.make_async_copy(owns[head].at[at], outs[head].at[slot, :, pl.ds(width, 2 * HD)], sem))
        return made

    def each(act):
        def look(at, slot):
            hit = groups[at] == facts[target]

            @pl.when(hit)
            def _():
                for copy in copies(at, slot):
                    act(copy)

            return slot + hit.astype(jnp.int32)

        lax.fori_loop(0, groups.shape[0], look, jnp.int32(0))

    each(lambda copy: copy.start())
    each(lambda copy: copy.wait())


def pack(facts, target, groups, queries, own, width):
    shape = jax.ShapeDtypeStruct((SLOTS, queries.shape[1], width + 2 * HD), queries.dtype)
    return pl.pallas_call(
        functools.partial(pack_kernel, target, width),
        out_shape=[shape, shape],
        in_specs=[SMEM, SMEM, HBM, HBM, HBM],
        out_specs=[HBM, HBM],
        scratch_shapes=[pltpu.SemaphoreType.DMA],
        compiler_params=pltpu.CompilerParams(vmem_limit_bytes=VMEM_BYTES),
    )(facts, groups, queries, *own)


def merge_kernel(target, width, facts, groups, got0, got1, old, out, sem):
    got = (got0, got1)

    def each(act):
        def look(at, slot):
            hit = groups[at] == facts[target]

            @pl.when(hit)
            def _():
                for head in range(2):
                    act(pltpu.make_async_copy(got[head].at[slot], out.at[at, :, pl.ds(head * width, width)], sem))

            return slot + hit.astype(jnp.int32)

        lax.fori_loop(0, groups.shape[0], look, jnp.int32(0))

    each(lambda copy: copy.start())
    each(lambda copy: copy.wait())


def merge(facts, target, groups, got, out, width):
    return pl.pallas_call(
        functools.partial(merge_kernel, target, width),
        out_shape=jax.ShapeDtypeStruct(out.shape, out.dtype),
        in_specs=[SMEM, SMEM, HBM, HBM, HBM],
        out_specs=HBM,
        input_output_aliases={4: 0},
        scratch_shapes=[pltpu.SemaphoreType.DMA],
        compiler_params=pltpu.CompilerParams(vmem_limit_bytes=VMEM_BYTES),
    )(facts, groups, *got, out)


def after(value, *others):
    return lax.optimization_barrier((value,) + others)[0]


def gathered(queries, resp_kv, prompt_kv, lengths, group_of, first_head, kv_needed, per_kv):
    out = jax.ShapeDtypeStruct(queries.shape, jnp.bfloat16)
    facts = jnp.zeros((8,), jnp.int32)
    for head in range(kv_needed):
        mine = lax.dynamic_index_in_dim(prompt_kv, first_head + head, 2, keepdims=False)
        own = lax.dynamic_index_in_dim(resp_kv, first_head + head, 2, keepdims=False)
        whole = lax.all_gather(mine, "seq", axis=0, tiled=True)
        [out] = attend(facts, group_of, lengths, queries, own, [whole], [out], head, per_kv, None, 16, fresh=head == 0)
    return out


def relayed(queries, resp_kv, prompt_kv, lengths, group_of, first_head, per_kv):
    me = lax.axis_index("seq")
    width = per_kv * HD
    middle, inward, outward = [(1, 2), (2, 1)], [(0, 1), (3, 2)], [(1, 0), (2, 3)]

    def send(pairs, value):
        return lax.ppermute(value, "seq", pairs)

    by_head = after(jnp.transpose(prompt_kv[0], (1, 0, 2)))
    mine, mid, inn, out_got = [], [], [], []
    for head in range(2):
        mine.append(lax.dynamic_index_in_dim(by_head, first_head + head, 0, keepdims=False))
        inn.append(send(inward, mine[head]))
        mid.append(send(middle, mine[head]))
        out_got.append(send(outward, mine[head]))
    far_groups, far_lengths = send(inward, group_of), send(inward, lengths)

    low = me < 2
    is_inner = (me == 1) | (me == 2)
    outer, inner = jnp.where(low, 0, 3), jnp.where(low, 1, 2)
    far_inner, far_outer = jnp.where(low, 2, 1), jnp.where(low, 3, 0)
    facts = jnp.stack([
        me,
        jnp.zeros_like(me),
        jnp.where(is_inner, outer, inner),
        jnp.where(is_inner, 0, 2),
        jnp.where(is_inner, far_inner, -1),
        jnp.ones_like(me),
        jnp.where(is_inner, far_outer, -1),
        jnp.where(is_inner, far_outer, far_inner),
        jnp.where(is_inner, 0, 1),
        jnp.where(is_inner, -1, far_outer),
    ]).astype(jnp.int32)

    own_by_head = after(jnp.transpose(resp_kv, (2, 0, 1, 3)))
    own = [lax.dynamic_index_in_dim(own_by_head, first_head + head, 0, keepdims=False) for head in range(2)]
    packed = pack(facts, 9, group_of, queries, own, width)
    out = jax.ShapeDtypeStruct(queries.shape, jnp.bfloat16)
    back_shape = jax.ShapeDtypeStruct((SLOTS, queries.shape[1], width), jnp.bfloat16)

    def run(head, cands, outs, passes, items, far=None, fresh=False):
        return attend(facts, group_of, lengths, queries, own[head], cands, outs, head, per_kv, passes, items, far, fresh)

    for head in range(2):
        [out] = run(head, [mine[head]], [out], [(False, 0, 1)], 4, fresh=head == 0)
    mid.append(send(middle, inn[0]))
    mid.append(send(middle, inn[1]))
    out_got.append(send(outward, mid[0]))
    out_got.append(send(outward, mid[1]))
    far = [send(inward, after(packed[head], inn[1])) for head in range(2)]
    for head in range(2):
        [out] = run(head, [inn[head], mid[head], out_got[head]], [out], [(False, 2, 3), (False, 4, 5)], 8)
    back = [None, None]
    far_all = [(far_groups, far_lengths, far[head]) for head in range(2)]
    zeros = jnp.zeros(back_shape.shape, back_shape.dtype)
    out, back[0] = run(0, [mid[2], out_got[2]], [out, zeros], [(True, 6, 1), (False, 7, 8)], 8, far_all[0])
    back[0] = send(outward, back[0])
    out, back[1] = run(1, [mid[3]], [out, zeros], [(True, 6, 1)], 4, far_all[1])
    back[1] = send(outward, back[1])
    [out] = run(1, [mid[3], out_got[3]], [out], [(False, 7, 8)], 4)
    return merge(facts, 9, group_of, back, out, width)


def shards(queries, resp_kv, prompt_kv, lengths, group_of):
    local_heads = queries.shape[2] // HD
    group = QHEADS // KVH
    kv_needed = max(local_heads // group, 1)
    per_kv = local_heads // kv_needed
    first_head = lax.axis_index("pp") * local_heads // group
    args = (queries, resp_kv, prompt_kv, lengths, group_of, first_head)
    if lax.axis_size("seq") == 4 and kv_needed == 2 and prompt_kv.shape[0] == 1:
        return relayed(*args, per_kv)
    return gathered(*args, kv_needed, per_kv)


def solution(mesh):
    placed = (
        P(("rep", "seq"), None, ("tp", "pp")),
        P(("rep", "seq"), None, "tp", None),
        P(("rep", "seq"), None, "tp", None),
        P(("rep", "seq")),
        P(("rep", "seq")),
    )
    return jax.shard_map(
        shards,
        mesh=mesh,
        in_specs=placed,
        out_specs=P(("rep", "seq"), None, ("tp", "pp")),
        check_vma=False,
    )
```

```python
import functools
import math

import jax
import jax.numpy as jnp
from jax import lax
from jax.experimental import pallas as pl
from jax.experimental.pallas import tpu as pltpu
from jax.sharding import PartitionSpec as P

QHEADS = 64
KVH = 8
HD = 128
LOG2E = math.log2(math.e)
VMEM_BYTES = 56 * 1024 * 1024
SLOTS = 8
HBM = pl.BlockSpec(memory_space=pl.ANY)
SMEM = pl.BlockSpec(memory_space=pltpu.SMEM)
VMEM = pl.BlockSpec(memory_space=pltpu.VMEM)


def one_head(q_tile, own_tile, kv_buf, vt_buf, length, per_kv, plen, s_buf):
    rlen = q_tile.shape[0]
    cols = per_kv * rlen
    block = 256
    scale = HD ** -0.5 * LOG2E
    q_rows = jnp.concatenate([q_tile[:, g * HD:(g + 1) * HD] for g in range(per_kv)], axis=0)
    nt = (((1,), (1,)), ((), ()))
    own = lax.dot_general(own_tile[:, :HD], q_rows, nt, preferred_element_type=jnp.float32)
    own_at = lax.broadcasted_iota(jnp.int32, (rlen, cols), 0)
    token_at = lax.broadcasted_iota(jnp.int32, (rlen, cols), 1) % rlen
    own = jnp.where(own_at <= token_at, own, -1e30)
    peak = jnp.max(own, axis=0, keepdims=True)
    for at in range(0, plen, block):
        part = lax.dot_general(kv_buf[at:at + block, :HD], q_rows, nt, preferred_element_type=jnp.float32)
        s_buf[at:at + block, :] = part
        peak = jnp.maximum(peak, jnp.max(part, axis=0, keepdims=True))
    own_exp = jnp.exp2((own - peak) * scale)
    total = jnp.sum(own_exp, axis=0, keepdims=True)
    tn = (((0,), (0,)), ((), ()))
    acc = lax.dot_general(own_tile[:, HD:], own_exp.astype(jnp.bfloat16), tn, preferred_element_type=jnp.float32)
    for at in range(0, plen, block):
        part = jnp.exp2((s_buf[at:at + block, :] - peak) * scale)
        total = total + jnp.sum(part, axis=0, keepdims=True)
        acc = acc + jnp.dot(vt_buf[:, at:at + block], part.astype(jnp.bfloat16), preferred_element_type=jnp.float32)
    out = (acc / total).T
    alive = lax.broadcasted_iota(jnp.int32, (rlen, HD), 0) < length
    return [jnp.where(alive, out[g * rlen:(g + 1) * rlen, :], 0.0).astype(jnp.bfloat16) for g in range(per_kv)]


def listed(items, cap, count, groups, lengths, target, source, first, slots):
    def look(at, state):
        n, slot = state
        hit = groups[at] == target

        @pl.when(hit)
        def _():
            items[n] = first + (slot if slots else at)
            items[cap + n] = source
            items[2 * cap + n] = lengths[at]

        step = hit.astype(jnp.int32)
        return n + step, slot + step

    return lax.fori_loop(0, groups.shape[0], look, (count, jnp.int32(0)))[0]


def attend_kernel(passes, n_cand, per_kv, head, two, fresh, *refs):
    refs = list(refs)
    facts, groups, lengths = refs[:3]
    refs = refs[3:]
    if two:
        far_facts, x_ref = refs[:2]
        refs = refs[2:]
    q_ref, own_ref = refs[:2]
    cands, refs = refs[2:2 + n_cand], refs[2 + n_cand:]
    n_out = 2 if two else 1
    if not fresh:
        refs = refs[1:]
    outs, refs = refs[:n_out], refs[n_out:]
    items, q_buf, own_buf, kv_buf, vt_buf, s_buf, o_buf, q_sem, own_sem, kv_sem, o_sem = refs
    local = groups.shape[0]
    cap = items.shape[0] // 3
    width = per_kv * HD
    stacked = passes is None

    count = jnp.int32(0)
    if stacked:
        def one_prompt(prompt, n):
            return listed(items, cap, n, groups, lengths, prompt, prompt, 0, False)

        count = lax.fori_loop(0, cands[0].shape[0], one_prompt, count)
    else:
        for far, target, source in passes:
            if far:
                count = listed(items, cap, count, far_facts.at[0], far_facts.at[1], facts[target], facts[source], local, True)
            else:
                count = listed(items, cap, count, groups, lengths, facts[target], facts[source], 0, False)

    def each_array(i, act_local, act_far):
        at = items[i]
        if not two:
            act_local(at)
            return

        @pl.when(at < local)
        def _():
            act_local(at)

        @pl.when(at >= local)
        def _():
            act_far(at - local)

    mine = pl.ds(head * width, width)
    first, last = pl.ds(0, width), pl.ds(width, 2 * HD)

    def fetch(i, slot):
        def here(at):
            pltpu.make_async_copy(q_ref.at[at, :, mine], q_buf.at[slot], q_sem.at[slot]).start()
            pltpu.make_async_copy(own_ref.at[at], own_buf.at[slot], own_sem.at[slot]).start()

        def far(at):
            pltpu.make_async_copy(x_ref.at[at, :, first], q_buf.at[slot], q_sem.at[slot]).start()
            pltpu.make_async_copy(x_ref.at[at, :, last], own_buf.at[slot], own_sem.at[slot]).start()

        each_array(i, here, far)

    def fetched(slot):
        pltpu.make_async_copy(q_ref.at[0, :, first], q_buf.at[slot], q_sem.at[slot]).wait()
        pltpu.make_async_copy(own_ref.at[0], own_buf.at[slot], own_sem.at[slot]).wait()

    def store(i, slot):
        def here(at):
            pltpu.make_async_copy(o_buf.at[slot], outs[0].at[at, :, mine], o_sem.at[slot]).start()

        def far(at):
            pltpu.make_async_copy(o_buf.at[slot], outs[1].at[at], o_sem.at[slot]).start()

        each_array(i, here, far)

    def stored(slot):
        pltpu.make_async_copy(o_buf.at[slot], outs[0].at[0, :, first], o_sem.at[slot]).wait()

    def load(source):
        if stacked:
            pltpu.make_async_copy(cands[0].at[source], kv_buf, kv_sem).start()
        else:
            for which in range(n_cand):
                @pl.when(source == which)
                def _():
                    pltpu.make_async_copy(cands[which], kv_buf, kv_sem).start()

        pltpu.make_async_copy(kv_buf, kv_buf, kv_sem).wait()

    @pl.when(count > 0)
    def _():
        fetch(0, 0)

        def step(i, before):
            slot = lax.rem(i, 2)
            source = items[cap + i]

            @pl.when(i + 1 < count)
            def _():
                fetch(i + 1, 1 - slot)

            @pl.when(source != before)
            def _():
                load(source)
                vt_buf[...] = kv_buf[:, HD:].T

            fetched(slot)

            @pl.when(i >= 2)
            def _():
                stored(slot)

            tiles = one_head(q_buf[slot], own_buf[slot], kv_buf, vt_buf, items[2 * cap + i], per_kv, kv_buf.shape[0], s_buf)
            for g in range(per_kv):
                o_buf[slot, :, g * HD:(g + 1) * HD] = tiles[g]
            store(i, slot)
            return source

        lax.fori_loop(0, count, step, jnp.int32(-1))
        stored(0)

        @pl.when(count > 1)
        def _():
            stored(1)


def attend(facts, groups, lengths, queries, own, cands, outs, head, per_kv, passes, items, far=None, fresh=False):
    rlen = queries.shape[1]
    plen = cands[0].shape[-2]
    width = per_kv * HD
    small = [facts, groups, lengths] + ([far[0]] if far else [])
    large = ([far[1]] if far else []) + [queries, own] + cands
    operands = small + large
    aliases = {}
    if not fresh:
        aliases = {len(operands): 0}
        operands = operands + [outs[0]]
    cap = groups.shape[0] + (SLOTS if far else 0)
    return pl.pallas_call(
        functools.partial(attend_kernel, passes, len(cands), per_kv, head, far is not None, fresh),
        out_shape=[jax.ShapeDtypeStruct(o.shape, o.dtype) for o in outs],
        in_specs=[SMEM] * len(small) + [HBM] * (len(operands) - len(small)),
        out_specs=[HBM] * len(outs),
        input_output_aliases=aliases,
        scratch_shapes=[
            pltpu.SMEM((3 * cap,), jnp.int32),
            pltpu.VMEM((2, rlen, width), jnp.bfloat16),
            pltpu.VMEM((2, rlen, 2 * HD), jnp.bfloat16),
            pltpu.VMEM((plen, 2 * HD), jnp.bfloat16),
            pltpu.VMEM((HD, plen), jnp.bfloat16),
            pltpu.VMEM((plen, per_kv * rlen), jnp.float32),
            pltpu.VMEM((2, rlen, width), jnp.bfloat16),
            pltpu.SemaphoreType.DMA((2,)),
            pltpu.SemaphoreType.DMA((2,)),
            pltpu.SemaphoreType.DMA,
            pltpu.SemaphoreType.DMA((2,)),
        ],
        compiler_params=pltpu.CompilerParams(vmem_limit_bytes=VMEM_BYTES),
        cost_estimate=pl.CostEstimate(flops=int(items * 1.2e9), bytes_accessed=1 << 21, transcendentals=0),
    )(*operands)


def pack_kernel(target, width, facts, groups, q_ref, own0, own1, out0, out1, sem):
    owns, outs = (own0, own1), (out0, out1)

    def each(act):
        def look(at, slot):
            hit = groups[at] == facts[target]

            @pl.when(hit)
            def _():
                for head in range(2):
                    part = pl.ds(head * width, width)
                    act(pltpu.make_async_copy(q_ref.at[at, :, part], outs[head].at[slot, :, pl.ds(0, width)], sem))
                    act(pltpu.make_async_copy(owns[head].at[at], outs[head].at[slot, :, pl.ds(width, 2 * HD)], sem))

            return slot + hit.astype(jnp.int32)

        lax.fori_loop(0, groups.shape[0], look, jnp.int32(0))

    each(lambda copy: copy.start())
    each(lambda copy: copy.wait())


def pack(facts, target, groups, queries, own, width):
    shape = jax.ShapeDtypeStruct((SLOTS, queries.shape[1], width + 2 * HD), queries.dtype)
    return pl.pallas_call(
        functools.partial(pack_kernel, target, width),
        out_shape=[shape, shape],
        in_specs=[SMEM, SMEM, HBM, HBM, HBM],
        out_specs=[VMEM, VMEM],
        scratch_shapes=[pltpu.SemaphoreType.DMA],
        compiler_params=pltpu.CompilerParams(vmem_limit_bytes=VMEM_BYTES),
    )(facts, groups, queries, *own)


def merge_kernel(target, width, facts, groups, got0, got1, old, out, sem):
    got = (got0, got1)

    def each(act):
        def look(at, slot):
            hit = groups[at] == facts[target]

            @pl.when(hit)
            def _():
                for head in range(2):
                    act(pltpu.make_async_copy(got[head].at[slot], out.at[at, :, pl.ds(head * width, width)], sem))

            return slot + hit.astype(jnp.int32)

        lax.fori_loop(0, groups.shape[0], look, jnp.int32(0))

    each(lambda copy: copy.start())
    each(lambda copy: copy.wait())


def merge(facts, target, groups, got, out, width):
    return pl.pallas_call(
        functools.partial(merge_kernel, target, width),
        out_shape=jax.ShapeDtypeStruct(out.shape, out.dtype),
        in_specs=[SMEM, SMEM, VMEM, VMEM, HBM],
        out_specs=HBM,
        input_output_aliases={4: 0},
        scratch_shapes=[pltpu.SemaphoreType.DMA],
        compiler_params=pltpu.CompilerParams(vmem_limit_bytes=VMEM_BYTES),
    )(facts, groups, *got, out)


def after(value, *others):
    return lax.optimization_barrier((value,) + others)[0]


def gathered(queries, resp_kv, prompt_kv, lengths, group_of, first_head, kv_needed, per_kv):
    out = jax.ShapeDtypeStruct(queries.shape, jnp.bfloat16)
    facts = jnp.zeros((8,), jnp.int32)
    for head in range(kv_needed):
        mine = lax.dynamic_index_in_dim(prompt_kv, first_head + head, 2, keepdims=False)
        own = lax.dynamic_index_in_dim(resp_kv, first_head + head, 2, keepdims=False)
        whole = lax.all_gather(mine, "seq", axis=0, tiled=True)
        [out] = attend(facts, group_of, lengths, queries, own, [whole], [out], head, per_kv, None, 16, fresh=head == 0)
    return out


def relayed(queries, resp_kv, prompt_kv, lengths, group_of, first_head, per_kv):
    me = lax.axis_index("seq")
    width = per_kv * HD
    middle, inward, outward = [(1, 2), (2, 1)], [(0, 1), (3, 2)], [(1, 0), (2, 3)]

    def send(pairs, value):
        return lax.ppermute(value, "seq", pairs)

    by_head = after(jnp.transpose(prompt_kv[0], (1, 0, 2)))
    far_facts = send(inward, jnp.stack([group_of, lengths]))
    mine, mid, inn, out_got = [], [], [], []
    for head in range(2):
        mine.append(lax.dynamic_index_in_dim(by_head, first_head + head, 0, keepdims=False))
        inn.append(send(inward, after(mine[head], far_facts) if head else mine[head]))
        mid.append(send(middle, mine[head]))
        out_got.append(send(outward, mine[head]))

    low = me < 2
    is_inner = (me == 1) | (me == 2)
    outer, inner = jnp.where(low, 0, 3), jnp.where(low, 1, 2)
    far_inner, far_outer = jnp.where(low, 2, 1), jnp.where(low, 3, 0)
    facts = jnp.stack([
        me,
        jnp.zeros_like(me),
        jnp.where(is_inner, outer, inner),
        jnp.where(is_inner, 0, 2),
        jnp.where(is_inner, far_inner, -1),
        jnp.ones_like(me),
        jnp.where(is_inner, far_outer, -1),
        jnp.where(is_inner, far_outer, far_inner),
        jnp.where(is_inner, 0, 1),
        jnp.where(is_inner, -1, far_outer),
    ]).astype(jnp.int32)

    own_by_head = after(jnp.transpose(resp_kv, (2, 0, 1, 3)))
    own = [lax.dynamic_index_in_dim(own_by_head, first_head + head, 0, keepdims=False) for head in range(2)]
    packed = pack(facts, 9, group_of, queries, own, width)
    out = jax.ShapeDtypeStruct(queries.shape, jnp.bfloat16)
    back_shape = jax.ShapeDtypeStruct((SLOTS, queries.shape[1], width), jnp.bfloat16)

    def run(head, cands, outs, passes, items, far=None, fresh=False):
        return attend(facts, group_of, lengths, queries, own[head], cands, outs, head, per_kv, passes, items, far, fresh)

    for head in range(2):
        [out] = run(head, [mine[head]], [out], [(False, 0, 1)], 4, fresh=head == 0)
    mid.append(send(middle, inn[0]))
    mid.append(send(middle, inn[1]))
    out_got.append(send(outward, mid[0]))
    out_got.append(send(outward, mid[1]))
    far = [send(inward, after(packed[head], inn[1])) for head in range(2)]
    for head in range(2):
        [out] = run(head, [inn[head], mid[head], out_got[head]], [out], [(False, 2, 3), (False, 4, 5)], 8)
    back = [None, None]
    far_all = [(far_facts, far[head]) for head in range(2)]
    out, back[0] = run(0, [mid[2], out_got[2]], [out, back_shape], [(True, 6, 1), (False, 7, 8)], 8, far_all[0])
    back[0] = send(outward, back[0])
    out, back[1] = run(1, [mid[3]], [out, back_shape], [(True, 6, 1)], 4, far_all[1])
    back[1] = send(outward, back[1])
    [out] = run(1, [mid[3], out_got[3]], [out], [(False, 7, 8)], 4)
    return merge(facts, 9, group_of, back, out, width)


def shards(queries, resp_kv, prompt_kv, lengths, group_of):
    local_heads = queries.shape[2] // HD
    group = QHEADS // KVH
    kv_needed = max(local_heads // group, 1)
    per_kv = local_heads // kv_needed
    first_head = lax.axis_index("pp") * local_heads // group
    args = (queries, resp_kv, prompt_kv, lengths, group_of, first_head)
    if lax.axis_size("seq") == 4 and kv_needed == 2 and prompt_kv.shape[0] == 1:
        return relayed(*args, per_kv)
    return gathered(*args, kv_needed, per_kv)


def solution(mesh):
    placed = (
        P(("rep", "seq"), None, ("tp", "pp")),
        P(("rep", "seq"), None, "tp", None),
        P(("rep", "seq"), None, "tp", None),
        P(("rep", "seq")),
        P(("rep", "seq")),
    )
    return jax.shard_map(
        shards,
        mesh=mesh,
        in_specs=placed,
        out_specs=P(("rep", "seq"), None, ("tp", "pp")),
        check_vma=False,
    )
```

```python
import functools
import math

import jax
import jax.numpy as jnp
from jax import lax
from jax.experimental import pallas as pl
from jax.experimental.pallas import tpu as pltpu
from jax.sharding import PartitionSpec as P

QHEADS = 64
KVH = 8
HD = 128
LOG2E = math.log2(math.e)
VMEM_BYTES = 56 * 1024 * 1024
SLOTS = 8
HBM = pl.BlockSpec(memory_space=pl.ANY)
SMEM = pl.BlockSpec(memory_space=pltpu.SMEM)
VMEM = pl.BlockSpec(memory_space=pltpu.VMEM)


NT = (((1,), (1,)), ((), ()))
TN = (((0,), (0,)), ((), ()))
BLOCK = 256


def stacked_heads(q_tile, per_kv):
    return jnp.concatenate([q_tile[:, g * HD:(g + 1) * HD] for g in range(per_kv)], axis=0)


def own_scores(own_tile, q_rows, rlen):
    own = lax.dot_general(own_tile[:, :HD], q_rows, NT, preferred_element_type=jnp.float32)
    own_at = lax.broadcasted_iota(jnp.int32, own.shape, 0)
    token_at = lax.broadcasted_iota(jnp.int32, own.shape, 1) % rlen
    return jnp.where(own_at <= token_at, own, -1e30)


def two_stages(after_q, after_own, after_kv, after_s, after_u, after_peak, now):
    rlen = after_own.shape[0]
    per_kv = after_q.shape[1] // HD
    plen = after_kv.shape[0]
    scale = HD ** -0.5 * LOG2E
    q_rows = stacked_heads(after_q, per_kv)
    own = own_scores(after_own, q_rows, rlen)
    after_u[...] = own
    after_top = jnp.max(own, axis=0, keepdims=True)
    if now is not None:
        s_ref, u_ref, peak_ref, own_tile, vt_ref, length = now
        peak = peak_ref[0:1, :]
        part = jnp.exp2((u_ref[...] - peak) * scale)
        total = jnp.sum(part, axis=0, keepdims=True)
        acc = lax.dot_general(own_tile[:, HD:], part.astype(jnp.bfloat16), TN, preferred_element_type=jnp.float32)
    for at in range(0, plen, BLOCK):
        rows = pl.ds(at, BLOCK)
        fresh = lax.dot_general(after_kv[rows, :HD], q_rows, NT, preferred_element_type=jnp.float32)
        after_s[rows, :] = fresh
        after_top = jnp.maximum(after_top, jnp.max(fresh, axis=0, keepdims=True))
        if now is not None:
            part = jnp.exp2((s_ref[rows, :] - peak) * scale)
            total = total + jnp.sum(part, axis=0, keepdims=True)
            acc = acc + jnp.dot(vt_ref[:, rows], part.astype(jnp.bfloat16), preferred_element_type=jnp.float32)
    after_peak[...] = jnp.broadcast_to(after_top, after_peak.shape)
    if now is None:
        return None
    out = (acc * (1.0 / total)).T
    alive = lax.broadcasted_iota(jnp.int32, (rlen, HD), 0) < length
    return [jnp.where(alive, out[g * rlen:(g + 1) * rlen, :], 0.0).astype(jnp.bfloat16) for g in range(per_kv)]


def listed(items, cap, count, groups, lengths, target, source, first, slots):
    def look(at, state):
        n, slot = state
        hit = groups[at] == target

        @pl.when(hit)
        def _():
            items[n] = first + (slot if slots else at)
            items[cap + n] = source
            items[2 * cap + n] = lengths[at]

        step = hit.astype(jnp.int32)
        return n + step, slot + step

    return lax.fori_loop(0, groups.shape[0], look, (count, jnp.int32(0)))[0]


def attend_kernel(passes, n_cand, per_kv, head, two, fresh, *refs):
    refs = list(refs)
    facts, groups, lengths = refs[:3]
    refs = refs[3:]
    if two:
        far_facts, x_ref = refs[:2]
        refs = refs[2:]
    q_ref, own_ref = refs[:2]
    cands, refs = refs[2:2 + n_cand], refs[2 + n_cand:]
    n_out = 2 if two else 1
    if not fresh:
        refs = refs[1:]
    outs, refs = refs[:n_out], refs[n_out:]
    items, q_buf, own_buf, kv_buf, vt_buf, s_buf, u_buf, peak_buf, o_buf, q_sem, own_sem, kv_sem, o_sem = refs
    local = groups.shape[0]
    cap = items.shape[0] // 3
    width = per_kv * HD
    stacked = passes is None

    count = jnp.int32(0)
    if stacked:
        def one_prompt(prompt, n):
            return listed(items, cap, n, groups, lengths, prompt, prompt, 0, False)

        count = lax.fori_loop(0, cands[0].shape[0], one_prompt, count)
    else:
        for far, target, source in passes:
            if far:
                count = listed(items, cap, count, far_facts.at[0], far_facts.at[1], facts[target], facts[source], local, True)
            else:
                count = listed(items, cap, count, groups, lengths, facts[target], facts[source], 0, False)

    def each_array(i, act_local, act_far):
        at = items[i]
        if not two:
            act_local(at)
            return

        @pl.when(at < local)
        def _():
            act_local(at)

        @pl.when(at >= local)
        def _():
            act_far(at - local)

    mine = pl.ds(head * width, width)
    first, last = pl.ds(0, width), pl.ds(width, 2 * HD)

    def fetch(i):
        slot, third = lax.rem(i, 2), lax.rem(i, 3)

        def here(at):
            pltpu.make_async_copy(q_ref.at[at, :, mine], q_buf.at[slot], q_sem.at[slot]).start()
            pltpu.make_async_copy(own_ref.at[at], own_buf.at[third], own_sem.at[third]).start()

        def far(at):
            pltpu.make_async_copy(x_ref.at[at, :, first], q_buf.at[slot], q_sem.at[slot]).start()
            pltpu.make_async_copy(x_ref.at[at, :, last], own_buf.at[third], own_sem.at[third]).start()

        each_array(i, here, far)

    def fetched(i):
        slot, third = lax.rem(i, 2), lax.rem(i, 3)
        pltpu.make_async_copy(q_ref.at[0, :, first], q_buf.at[slot], q_sem.at[slot]).wait()
        pltpu.make_async_copy(own_ref.at[0], own_buf.at[third], own_sem.at[third]).wait()

    def store(i, slot):
        def here(at):
            pltpu.make_async_copy(o_buf.at[slot], outs[0].at[at, :, mine], o_sem.at[slot]).start()

        def far(at):
            pltpu.make_async_copy(o_buf.at[slot], outs[1].at[at], o_sem.at[slot]).start()

        each_array(i, here, far)

    def stored(slot):
        pltpu.make_async_copy(o_buf.at[slot], outs[0].at[0, :, first], o_sem.at[slot]).wait()

    def load(source, into):
        if stacked:
            pltpu.make_async_copy(cands[0].at[source], kv_buf.at[into], kv_sem).start()
        else:
            for which in range(n_cand):
                @pl.when(source == which)
                def _():
                    pltpu.make_async_copy(cands[which], kv_buf.at[into], kv_sem).start()

        pltpu.make_async_copy(kv_buf.at[into], kv_buf.at[into], kv_sem).wait()
        vt_buf[into] = kv_buf[into, :, HD:].T

    @pl.when(count > 0)
    def _():
        fetch(jnp.int32(0))

        @pl.when(count > 1)
        def _():
            fetch(jnp.int32(1))

        load(items[cap], 0)
        fetched(jnp.int32(0))
        two_stages(q_buf[0], own_buf[0], kv_buf.at[0], s_buf.at[0], u_buf.at[0], peak_buf.at[0], None)

        def step(i, held):
            slot = lax.rem(i, 2)
            more = i + 1 < count
            moved = more & (items[cap + jnp.minimum(i + 1, count - 1)] != items[cap + i])
            holds = jnp.where(moved, 1 - held, held)

            @pl.when(more)
            def _():
                fetched(i + 1)

            @pl.when(i + 2 < count)
            def _():
                fetch(i + 2)

            @pl.when(moved)
            def _():
                load(items[cap + i + 1], holds)

            @pl.when(i >= 2)
            def _():
                stored(slot)

            now = (s_buf.at[slot], u_buf.at[slot], peak_buf.at[slot], own_buf[lax.rem(i, 3)], vt_buf.at[held], items[2 * cap + i])
            tiles = two_stages(
                q_buf[1 - slot], own_buf[lax.rem(i + 1, 3)], kv_buf.at[holds],
                s_buf.at[1 - slot], u_buf.at[1 - slot], peak_buf.at[1 - slot], now)
            for g in range(per_kv):
                o_buf[slot, :, g * HD:(g + 1) * HD] = tiles[g]
            store(i, slot)
            return holds

        lax.fori_loop(0, count, step, jnp.int32(0))
        stored(0)

        @pl.when(count > 1)
        def _():
            stored(1)


def attend(facts, groups, lengths, queries, own, cands, outs, head, per_kv, passes, items, far=None, fresh=False):
    rlen = queries.shape[1]
    plen = cands[0].shape[-2]
    width = per_kv * HD
    small = [facts, groups, lengths] + ([far[0]] if far else [])
    large = ([far[1]] if far else []) + [queries, own] + cands
    operands = small + large
    aliases = {}
    if not fresh:
        aliases = {len(operands): 0}
        operands = operands + [outs[0]]
    cap = groups.shape[0] + (SLOTS if far else 0)
    return pl.pallas_call(
        functools.partial(attend_kernel, passes, len(cands), per_kv, head, far is not None, fresh),
        out_shape=[jax.ShapeDtypeStruct(o.shape, o.dtype) for o in outs],
        in_specs=[SMEM] * len(small) + [HBM] * (len(operands) - len(small)),
        out_specs=[HBM] * len(outs),
        input_output_aliases=aliases,
        scratch_shapes=[
            pltpu.SMEM((3 * cap,), jnp.int32),
            pltpu.VMEM((2, rlen, width), jnp.bfloat16),
            pltpu.VMEM((3, rlen, 2 * HD), jnp.bfloat16),
            pltpu.VMEM((2, plen, 2 * HD), jnp.bfloat16),
            pltpu.VMEM((2, HD, plen), jnp.bfloat16),
            pltpu.VMEM((2, plen, per_kv * rlen), jnp.float32),
            pltpu.VMEM((2, rlen, per_kv * rlen), jnp.float32),
            pltpu.VMEM((2, 8, per_kv * rlen), jnp.float32),
            pltpu.VMEM((2, rlen, width), jnp.bfloat16),
            pltpu.SemaphoreType.DMA((2,)),
            pltpu.SemaphoreType.DMA((3,)),
            pltpu.SemaphoreType.DMA,
            pltpu.SemaphoreType.DMA((2,)),
        ],
        compiler_params=pltpu.CompilerParams(vmem_limit_bytes=VMEM_BYTES),
        cost_estimate=pl.CostEstimate(flops=int(items * 1.2e9), bytes_accessed=1 << 21, transcendentals=0),
    )(*operands)


def pack_kernel(target, width, facts, groups, q_ref, own0, own1, out0, out1, sem):
    owns, outs = (own0, own1), (out0, out1)

    def each(act):
        def look(at, slot):
            hit = groups[at] == facts[target]

            @pl.when(hit)
            def _():
                for head in range(2):
                    part = pl.ds(head * width, width)
                    act(pltpu.make_async_copy(q_ref.at[at, :, part], outs[head].at[slot, :, pl.ds(0, width)], sem))
                    act(pltpu.make_async_copy(owns[head].at[at], outs[head].at[slot, :, pl.ds(width, 2 * HD)], sem))

            return slot + hit.astype(jnp.int32)

        lax.fori_loop(0, groups.shape[0], look, jnp.int32(0))

    each(lambda copy: copy.start())
    each(lambda copy: copy.wait())


def pack(facts, target, groups, queries, own, width):
    shape = jax.ShapeDtypeStruct((SLOTS, queries.shape[1], width + 2 * HD), queries.dtype)
    return pl.pallas_call(
        functools.partial(pack_kernel, target, width),
        out_shape=[shape, shape],
        in_specs=[SMEM, SMEM, HBM, HBM, HBM],
        out_specs=[VMEM, VMEM],
        scratch_shapes=[pltpu.SemaphoreType.DMA],
        compiler_params=pltpu.CompilerParams(vmem_limit_bytes=VMEM_BYTES),
    )(facts, groups, queries, *own)


def merge_kernel(target, width, facts, groups, got0, got1, old, out, sem):
    got = (got0, got1)

    def each(act):
        def look(at, slot):
            hit = groups[at] == facts[target]

            @pl.when(hit)
            def _():
                for head in range(2):
                    act(pltpu.make_async_copy(got[head].at[slot], out.at[at, :, pl.ds(head * width, width)], sem))

            return slot + hit.astype(jnp.int32)

        lax.fori_loop(0, groups.shape[0], look, jnp.int32(0))

    each(lambda copy: copy.start())
    each(lambda copy: copy.wait())


def merge(facts, target, groups, got, out, width):
    return pl.pallas_call(
        functools.partial(merge_kernel, target, width),
        out_shape=jax.ShapeDtypeStruct(out.shape, out.dtype),
        in_specs=[SMEM, SMEM, VMEM, VMEM, HBM],
        out_specs=HBM,
        input_output_aliases={4: 0},
        scratch_shapes=[pltpu.SemaphoreType.DMA],
        compiler_params=pltpu.CompilerParams(vmem_limit_bytes=VMEM_BYTES),
    )(facts, groups, *got, out)


def after(value, *others):
    return lax.optimization_barrier((value,) + others)[0]


def gathered(queries, resp_kv, prompt_kv, lengths, group_of, first_head, kv_needed, per_kv):
    out = jax.ShapeDtypeStruct(queries.shape, jnp.bfloat16)
    facts = jnp.zeros((8,), jnp.int32)
    for head in range(kv_needed):
        mine = lax.dynamic_index_in_dim(prompt_kv, first_head + head, 2, keepdims=False)
        own = lax.dynamic_index_in_dim(resp_kv, first_head + head, 2, keepdims=False)
        whole = lax.all_gather(mine, "seq", axis=0, tiled=True)
        [out] = attend(facts, group_of, lengths, queries, own, [whole], [out], head, per_kv, None, 16, fresh=head == 0)
    return out


def relayed(queries, resp_kv, prompt_kv, lengths, group_of, first_head, per_kv):
    me = lax.axis_index("seq")
    width = per_kv * HD
    middle, inward, outward = [(1, 2), (2, 1)], [(0, 1), (3, 2)], [(1, 0), (2, 3)]

    def send(pairs, value):
        return lax.ppermute(value, "seq", pairs)

    far_facts = send(inward, jnp.stack([group_of, lengths]))
    by_head = after(jnp.transpose(prompt_kv[0], (1, 0, 2)))
    mine = [lax.dynamic_index_in_dim(by_head, first_head + head, 0, keepdims=False) for head in range(2)]
    mine[0] = after(mine[0], far_facts)
    inn, mid, out_got = [], [], []
    for head in range(2):
        inn.append(send(inward, mine[head]))
        mid.append(send(middle, mine[head]))
    for head in range(2):
        out_got.append(send(outward, mine[head]))

    low = me < 2
    is_inner = (me == 1) | (me == 2)
    outer, inner = jnp.where(low, 0, 3), jnp.where(low, 1, 2)
    far_inner, far_outer = jnp.where(low, 2, 1), jnp.where(low, 3, 0)
    facts = jnp.stack([
        me,
        jnp.zeros_like(me),
        jnp.where(is_inner, outer, inner),
        jnp.where(is_inner, 0, 2),
        jnp.where(is_inner, far_inner, -1),
        jnp.ones_like(me),
        jnp.where(is_inner, far_outer, -1),
        jnp.where(is_inner, far_outer, far_inner),
        jnp.where(is_inner, 0, 1),
        jnp.where(is_inner, -1, far_outer),
    ]).astype(jnp.int32)

    own_by_head = after(jnp.transpose(resp_kv, (2, 0, 1, 3)))
    own = [lax.dynamic_index_in_dim(own_by_head, first_head + head, 0, keepdims=False) for head in range(2)]
    packed = pack(facts, 9, group_of, queries, own, width)
    out = jax.ShapeDtypeStruct(queries.shape, jnp.bfloat16)
    back_shape = jax.ShapeDtypeStruct((SLOTS, queries.shape[1], width), jnp.bfloat16)

    def run(head, cands, outs, passes, items, far=None, fresh=False):
        return attend(facts, group_of, lengths, queries, own[head], cands, outs, head, per_kv, passes, items, far, fresh)

    for head in range(2):
        [out] = run(head, [mine[head]], [out], [(False, 0, 1)], 4, fresh=head == 0)
    mid.append(send(middle, inn[0]))
    mid.append(send(middle, inn[1]))
    out_got.append(send(outward, mid[0]))
    out_got.append(send(outward, mid[1]))
    far = [send(inward, after(packed[head], inn[1])) for head in range(2)]
    facts = after(facts, *inn, *mid[:2], *out_got[:2])
    for head in range(2):
        [out] = run(head, [inn[head], mid[head], out_got[head]], [out], [(False, 2, 3), (False, 4, 5)], 8)
    back = [None, None]
    far_all = [(far_facts, far[head]) for head in range(2)]
    out, back[0] = run(0, [mid[2], out_got[2]], [out, back_shape], [(True, 6, 1), (False, 7, 8)], 8, far_all[0])
    back[0] = send(outward, back[0])
    out, back[1] = run(1, [mid[3]], [out, back_shape], [(True, 6, 1)], 4, far_all[1])
    back[1] = send(outward, back[1])
    [out] = run(1, [mid[3], out_got[3]], [out], [(False, 7, 8)], 4)
    return merge(facts, 9, group_of, back, out, width)


def shards(queries, resp_kv, prompt_kv, lengths, group_of):
    local_heads = queries.shape[2] // HD
    group = QHEADS // KVH
    kv_needed = max(local_heads // group, 1)
    per_kv = local_heads // kv_needed
    first_head = lax.axis_index("pp") * local_heads // group
    args = (queries, resp_kv, prompt_kv, lengths, group_of, first_head)
    if lax.axis_size("seq") == 4 and kv_needed == 2 and prompt_kv.shape[0] == 1:
        return relayed(*args, per_kv)
    return gathered(*args, kv_needed, per_kv)


def solution(mesh):
    placed = (
        P(("rep", "seq"), None, ("tp", "pp")),
        P(("rep", "seq"), None, "tp", None),
        P(("rep", "seq"), None, "tp", None),
        P(("rep", "seq")),
        P(("rep", "seq")),
    )
    return jax.shard_map(
        shards,
        mesh=mesh,
        in_specs=placed,
        out_specs=P(("rep", "seq"), None, ("tp", "pp")),
        check_vma=False,
    )
```

```python
import functools
import math

import jax
import jax.numpy as jnp
from jax import lax
from jax.experimental import pallas as pl
from jax.experimental.pallas import tpu as pltpu
from jax.sharding import PartitionSpec as P

QHEADS = 64
KVH = 8
HD = 128
LOG2E = math.log2(math.e)
VMEM_BYTES = 56 * 1024 * 1024
SLOTS = 8
HBM = pl.BlockSpec(memory_space=pl.ANY)
SMEM = pl.BlockSpec(memory_space=pltpu.SMEM)
VMEM = pl.BlockSpec(memory_space=pltpu.VMEM)


TN = (((0,), (0,)), ((), ()))
BLOCK = 256


def stacked_heads(q_tile, per_kv):
    return jnp.concatenate([q_tile[:, g * HD:(g + 1) * HD] for g in range(per_kv)], axis=0)


def own_scores(own_tile, q_cols, rlen):
    own = jnp.dot(own_tile[:, :HD], q_cols, preferred_element_type=jnp.float32)
    own_at = lax.broadcasted_iota(jnp.int32, own.shape, 0)
    token_at = lax.broadcasted_iota(jnp.int32, own.shape, 1) % rlen
    return jnp.where(own_at <= token_at, own, -1e30)


def two_stages(after_q, after_own, after_kv, after_s, after_u, after_peak, now):
    rlen = after_own.shape[0]
    per_kv = after_q.shape[1] // HD
    plen = after_kv.shape[0]
    scale = HD ** -0.5 * LOG2E
    q_cols = stacked_heads(after_q, per_kv).T
    own = own_scores(after_own, q_cols, rlen)
    after_u[...] = own
    after_top = jnp.max(own, axis=0, keepdims=True)
    if now is not None:
        s_ref, u_ref, peak_ref, own_tile, vt_ref, length = now
        peak = peak_ref[0:1, :]
        part = jnp.exp2((u_ref[...] - peak) * scale)
        total = jnp.sum(part, axis=0, keepdims=True)
        acc = lax.dot_general(own_tile[:, HD:], part.astype(jnp.bfloat16), TN, preferred_element_type=jnp.float32)
    for at in range(0, plen, BLOCK):
        rows = pl.ds(at, BLOCK)
        fresh = jnp.dot(after_kv[rows, :HD], q_cols, preferred_element_type=jnp.float32)
        after_s[rows, :] = fresh
        after_top = jnp.maximum(after_top, jnp.max(fresh, axis=0, keepdims=True))
        if now is not None:
            part = jnp.exp2((s_ref[rows, :] - peak) * scale)
            total = total + jnp.sum(part, axis=0, keepdims=True)
            acc = acc + jnp.dot(vt_ref[:, rows], part.astype(jnp.bfloat16), preferred_element_type=jnp.float32)
    after_peak[...] = jnp.broadcast_to(after_top, after_peak.shape)
    if now is None:
        return None
    out = (acc * (1.0 / total)).T
    alive = lax.broadcasted_iota(jnp.int32, (rlen, HD), 0) < length
    return [jnp.where(alive, out[g * rlen:(g + 1) * rlen, :], 0.0).astype(jnp.bfloat16) for g in range(per_kv)]


def listed(items, cap, count, groups, lengths, target, source):
    def look(at, n):
        hit = groups[at] == target

        @pl.when(hit)
        def _():
            items[n] = at
            items[cap + n] = source
            items[2 * cap + n] = lengths[at]

        return n + hit.astype(jnp.int32)

    return lax.fori_loop(0, groups.shape[0], look, count)


def attend_kernel(passes, n_cand, per_kv, head, two, fresh, *refs):
    refs = list(refs)
    facts, groups, lengths = refs[:3]
    refs = refs[3:]
    if two:
        x_ref, refs = refs[0], refs[1:]
    q_ref, own_ref = refs[:2]
    cands, refs = refs[2:2 + n_cand], refs[2 + n_cand:]
    n_out = 2 if two else 1
    if not fresh:
        refs = refs[1:]
    outs, refs = refs[:n_out], refs[n_out:]
    items, at_slot, q_buf, own_buf, kv_buf, vt_buf, s0, s1, u0, u1, peak0, peak1, o_buf, info, q_sem, own_sem, kv_sem, o_sem = refs
    s_buf, u_buf, peak_buf = (s0, s1), (u0, u1), (peak0, peak1)
    local = groups.shape[0]
    cap = items.shape[0] // 3
    width = per_kv * HD
    stacked = passes is None

    count = jnp.int32(0)
    if stacked:
        def one_prompt(prompt, n):
            return listed(items, cap, n, groups, lengths, prompt, prompt)

        count = lax.fori_loop(0, cands[0].shape[0], one_prompt, count)
    else:
        for far, target, source in passes:
            if not far:
                count = listed(items, cap, count, groups, lengths, facts[target], facts[source])
                continue
            notes = pltpu.make_async_copy(x_ref.at[:, :, pl.ds(2 * (width + 2 * HD), HD)], info, kv_sem)
            notes.start()
            notes.wait()
            for slot in range(SLOTS):
                length = jnp.max(info[slot, 0:16, :].astype(jnp.float32)).astype(jnp.int32)
                hit = (length > 0) & (facts[target] >= 0)

                @pl.when(hit)
                def _():
                    items[count] = local + slot
                    items[cap + count] = facts[source]
                    items[2 * cap + count] = length

                count = count + hit.astype(jnp.int32)

    def each_array(i, act_local, act_far):
        at = items[i]
        if not two:
            act_local(at)
            return

        @pl.when(at < local)
        def _():
            act_local(at)

        @pl.when(at >= local)
        def _():
            act_far(at - local)

    mine = pl.ds(head * width, width)
    first = pl.ds(0, width)
    handed_q = pl.ds(head * (width + 2 * HD), width)
    handed_own = pl.ds(head * (width + 2 * HD) + width, 2 * HD)

    def fetch(i):
        slot, third = lax.rem(i, 2), lax.rem(i, 3)

        def here(at):
            pltpu.make_async_copy(q_ref.at[at, :, mine], q_buf.at[slot], q_sem.at[slot]).start()
            pltpu.make_async_copy(own_ref.at[at], own_buf.at[third], own_sem.at[third]).start()

        def far(at):
            pltpu.make_async_copy(x_ref.at[at, :, handed_q], q_buf.at[slot], q_sem.at[slot]).start()
            pltpu.make_async_copy(x_ref.at[at, :, handed_own], own_buf.at[third], own_sem.at[third]).start()

        each_array(i, here, far)

    def fetched(i):
        slot, third = lax.rem(i, 2), lax.rem(i, 3)
        pltpu.make_async_copy(q_ref.at[0, :, first], q_buf.at[slot], q_sem.at[slot]).wait()
        pltpu.make_async_copy(own_ref.at[0], own_buf.at[third], own_sem.at[third]).wait()

    def store(i, slot):
        def here(at):
            pltpu.make_async_copy(o_buf.at[slot], outs[0].at[at, :, mine], o_sem.at[slot]).start()

        def far(at):
            pltpu.make_async_copy(o_buf.at[slot], outs[1].at[at], o_sem.at[slot]).start()

        each_array(i, here, far)

    def stored(slot):
        pltpu.make_async_copy(o_buf.at[slot], outs[0].at[0, :, first], o_sem.at[slot]).wait()

    def load(source, into):
        if stacked:
            pltpu.make_async_copy(cands[0].at[source], kv_buf.at[into], kv_sem).start()
        else:
            for which in range(n_cand):
                @pl.when(source == which)
                def _():
                    source_ref = cands[which].at[head] if len(cands[which].shape) == 3 else cands[which]
                    pltpu.make_async_copy(source_ref, kv_buf.at[into], kv_sem).start()

        pltpu.make_async_copy(kv_buf.at[into], kv_buf.at[into], kv_sem).wait()
        vt_buf[into] = kv_buf[into, :, HD:].T

    @pl.when(count > 0)
    def _():
        fetch(jnp.int32(0))

        @pl.when(count > 1)
        def _():
            fetch(jnp.int32(1))

        load(items[cap], 0)
        at_slot[0] = 0
        fetched(jnp.int32(0))
        two_stages(q_buf[0], own_buf[0], kv_buf.at[0], s_buf[0], u_buf[0], peak_buf[0], None)

        def one(i, slot):
            held = at_slot[0]
            more = i + 1 < count
            moved = more & (items[cap + jnp.minimum(i + 1, count - 1)] != items[cap + i])
            holds = jnp.where(moved, 1 - held, held)
            at_slot[0] = holds

            @pl.when(more)
            def _():
                fetched(i + 1)

            @pl.when(i + 2 < count)
            def _():
                fetch(i + 2)

            @pl.when(moved)
            def _():
                load(items[cap + i + 1], holds)

            @pl.when(i >= 2)
            def _():
                stored(slot)

            now = (s_buf[slot], u_buf[slot], peak_buf[slot], own_buf[lax.rem(i, 3)], vt_buf.at[held], items[2 * cap + i])
            tiles = two_stages(
                q_buf[1 - slot], own_buf[lax.rem(i + 1, 3)], kv_buf.at[holds],
                s_buf[1 - slot], u_buf[1 - slot], peak_buf[1 - slot], now)
            for g in range(per_kv):
                o_buf[slot, :, g * HD:(g + 1) * HD] = tiles[g]
            store(i, slot)

        def pair(j, _):
            one(2 * j, 0)

            @pl.when(2 * j + 1 < count)
            def _():
                one(2 * j + 1, 1)

            return 0

        lax.fori_loop(0, lax.div(count + 1, 2), pair, 0)
        stored(0)

        @pl.when(count > 1)
        def _():
            stored(1)


def attend(facts, groups, lengths, queries, own, cands, outs, head, per_kv, passes, items, far=None, fresh=False):
    rlen = queries.shape[1]
    plen = cands[0].shape[-2]
    width = per_kv * HD
    small = [facts, groups, lengths]
    large = ([far] if far is not None else []) + [queries, own] + cands
    operands = small + large
    aliases = {}
    if not fresh:
        aliases = {len(operands): 0}
        operands = operands + [outs[0]]
    cap = groups.shape[0] + (SLOTS if far is not None else 0)
    return pl.pallas_call(
        functools.partial(attend_kernel, passes, len(cands), per_kv, head, far is not None, fresh),
        out_shape=[jax.ShapeDtypeStruct(o.shape, o.dtype) for o in outs],
        in_specs=[SMEM] * len(small) + [HBM] * (len(operands) - len(small)),
        out_specs=[HBM] * len(outs),
        input_output_aliases=aliases,
        scratch_shapes=[
            pltpu.SMEM((3 * cap,), jnp.int32),
            pltpu.SMEM((1,), jnp.int32),
            pltpu.VMEM((2, rlen, width), jnp.bfloat16),
            pltpu.VMEM((3, rlen, 2 * HD), jnp.bfloat16),
            pltpu.VMEM((2, plen, 2 * HD), jnp.bfloat16),
            pltpu.VMEM((2, HD, plen), jnp.bfloat16),
            pltpu.VMEM((plen, per_kv * rlen), jnp.float32),
            pltpu.VMEM((plen, per_kv * rlen), jnp.float32),
            pltpu.VMEM((rlen, per_kv * rlen), jnp.float32),
            pltpu.VMEM((rlen, per_kv * rlen), jnp.float32),
            pltpu.VMEM((8, per_kv * rlen), jnp.float32),
            pltpu.VMEM((8, per_kv * rlen), jnp.float32),
            pltpu.VMEM((2, rlen, width), jnp.bfloat16),
            pltpu.VMEM((SLOTS, rlen, HD), jnp.bfloat16),
            pltpu.SemaphoreType.DMA((2,)),
            pltpu.SemaphoreType.DMA((3,)),
            pltpu.SemaphoreType.DMA,
            pltpu.SemaphoreType.DMA((2,)),
        ],
        compiler_params=pltpu.CompilerParams(vmem_limit_bytes=VMEM_BYTES),
        cost_estimate=pl.CostEstimate(flops=int(items * 1.2e9), bytes_accessed=1 << 21, transcendentals=0),
    )(*operands)


def pack_kernel(target, width, facts, groups, lengths, q_ref, own0, own1, out, sem):
    owns = (own0, own1)
    step = width + 2 * HD
    notes = pl.ds(2 * step, HD)
    out[:, :, notes] = jnp.zeros((SLOTS, out.shape[1], HD), out.dtype)

    def each(act, note):
        def look(at, slot):
            hit = groups[at] == facts[target]

            @pl.when(hit)
            def _():
                for head in range(2):
                    part = pl.ds(head * width, width)
                    act(pltpu.make_async_copy(q_ref.at[at, :, part], out.at[slot, :, pl.ds(head * step, width)], sem))
                    act(pltpu.make_async_copy(owns[head].at[at], out.at[slot, :, pl.ds(head * step + width, 2 * HD)], sem))
                if note:
                    length = jnp.full((out.shape[1], HD), lengths[at], jnp.int32)
                    out[slot, :, notes] = length.astype(jnp.float32).astype(out.dtype)

            return slot + hit.astype(jnp.int32)

        lax.fori_loop(0, groups.shape[0], look, jnp.int32(0))

    each(lambda copy: copy.start(), True)
    each(lambda copy: copy.wait(), False)


def pack(facts, target, groups, lengths, queries, own, width):
    shape = jax.ShapeDtypeStruct((SLOTS, queries.shape[1], 2 * (width + 2 * HD) + HD), queries.dtype)
    return pl.pallas_call(
        functools.partial(pack_kernel, target, width),
        out_shape=shape,
        in_specs=[SMEM, SMEM, SMEM, HBM, HBM, HBM],
        out_specs=VMEM,
        scratch_shapes=[pltpu.SemaphoreType.DMA],
        compiler_params=pltpu.CompilerParams(vmem_limit_bytes=1 << 23),
    )(facts, groups, lengths, queries, *own)


def gate_kernel(value, other, out):
    pass


def gate(value, other):
    return pl.pallas_call(
        gate_kernel,
        out_shape=jax.ShapeDtypeStruct(value.shape, value.dtype),
        in_specs=[HBM, HBM],
        out_specs=HBM,
        input_output_aliases={0: 0},
    )(value, other)


def merge_kernel(target, width, facts, groups, got0, got1, old, out, sem):
    got = (got0, got1)

    def each(act):
        def look(at, slot):
            hit = groups[at] == facts[target]

            @pl.when(hit)
            def _():
                for head in range(2):
                    act(pltpu.make_async_copy(got[head].at[slot], out.at[at, :, pl.ds(head * width, width)], sem))

            return slot + hit.astype(jnp.int32)

        lax.fori_loop(0, groups.shape[0], look, jnp.int32(0))

    each(lambda copy: copy.start())
    each(lambda copy: copy.wait())


def merge(facts, target, groups, got, out, width):
    return pl.pallas_call(
        functools.partial(merge_kernel, target, width),
        out_shape=jax.ShapeDtypeStruct(out.shape, out.dtype),
        in_specs=[SMEM, SMEM, VMEM, VMEM, HBM],
        out_specs=HBM,
        input_output_aliases={4: 0},
        scratch_shapes=[pltpu.SemaphoreType.DMA],
        compiler_params=pltpu.CompilerParams(vmem_limit_bytes=1 << 23),
    )(facts, groups, *got, out)


def after(value, *others):
    return lax.optimization_barrier((value,) + others)[0]


def gathered(queries, resp_kv, prompt_kv, lengths, group_of, first_head, kv_needed, per_kv):
    out = jax.ShapeDtypeStruct(queries.shape, jnp.bfloat16)
    facts = jnp.zeros((8,), jnp.int32)
    for head in range(kv_needed):
        mine = lax.dynamic_index_in_dim(prompt_kv, first_head + head, 2, keepdims=False)
        own = lax.dynamic_index_in_dim(resp_kv, first_head + head, 2, keepdims=False)
        whole = lax.all_gather(mine, "seq", axis=0, tiled=True)
        [out] = attend(facts, group_of, lengths, queries, own, [whole], [out], head, per_kv, None, 16, fresh=head == 0)
    return out


def relayed(queries, resp_kv, prompt_kv, lengths, group_of, first_head, per_kv):
    me = lax.axis_index("seq")
    width = per_kv * HD
    middle, inward, outward = [(1, 2), (2, 1)], [(0, 1), (3, 2)], [(1, 0), (2, 3)]

    def send(pairs, value):
        return lax.ppermute(value, "seq", pairs)

    by_head = after(jnp.transpose(prompt_kv[0], (1, 0, 2)))
    mine = after(lax.dynamic_slice_in_dim(by_head, first_head, 2, 0))
    near = [send(inward, lax.index_in_dim(mine, head, 0, keepdims=False)) for head in range(2)]
    across = send(middle, mine)
    inner_prompt = send(outward, mine)

    low = me < 2
    is_inner = (me == 1) | (me == 2)
    outer, inner = jnp.where(low, 0, 3), jnp.where(low, 1, 2)
    far_inner, far_outer = jnp.where(low, 2, 1), jnp.where(low, 3, 0)
    facts = jnp.stack([
        me,
        jnp.zeros_like(me),
        jnp.where(is_inner, outer, inner),
        jnp.where(is_inner, 0, 2),
        jnp.where(is_inner, far_inner, -1),
        jnp.ones_like(me),
        jnp.where(is_inner, far_outer, -1),
        jnp.where(is_inner, far_outer, far_inner),
        jnp.where(is_inner, 0, 1),
        jnp.where(is_inner, -1, far_outer),
    ]).astype(jnp.int32)

    own_by_head = after(jnp.transpose(resp_kv, (2, 0, 1, 3)))
    own = [lax.dynamic_index_in_dim(own_by_head, first_head + head, 0, keepdims=False) for head in range(2)]
    packed = pack(facts, 9, group_of, lengths, queries, own, width)
    out = jax.ShapeDtypeStruct(queries.shape, jnp.bfloat16)
    back_shape = jax.ShapeDtypeStruct((SLOTS, queries.shape[1], width), jnp.bfloat16)

    def run(head, cands, outs, passes, items, far=None, fresh=False):
        return attend(facts, group_of, lengths, queries, own[head], cands, outs, head, per_kv, passes, items, far, fresh)

    for head in range(2):
        [out] = run(head, [mine], [out], [(False, 0, 1)], 4, fresh=head == 0)
    last = [send(middle, near[0]), send(middle, gate(near[1], near[0]))]
    far_inner_prompt = send(outward, across)
    handed = send(inward, gate(packed, near[1]))
    for head in range(2):
        [out] = run(head, [near[head], across, inner_prompt], [out], [(False, 2, 3), (False, 4, 5)], 8)
    back = [None, None]
    for head in range(2):
        out, back[head] = run(head, [last[head]], [out, back_shape], [(True, 6, 1)], 4, handed)
        back[head] = send(outward, back[head])
        [out] = run(head, [last[head], far_inner_prompt], [out], [(False, 7, 8)], 4)
    return merge(facts, 9, group_of, back, out, width)


def shards(queries, resp_kv, prompt_kv, lengths, group_of):
    local_heads = queries.shape[2] // HD
    group = QHEADS // KVH
    kv_needed = max(local_heads // group, 1)
    per_kv = local_heads // kv_needed
    first_head = lax.axis_index("pp") * local_heads // group
    args = (queries, resp_kv, prompt_kv, lengths, group_of, first_head)
    if lax.axis_size("seq") == 4 and kv_needed == 2 and prompt_kv.shape[0] == 1:
        return relayed(*args, per_kv)
    return gathered(*args, kv_needed, per_kv)


def solution(mesh):
    placed = (
        P(("rep", "seq"), None, ("tp", "pp")),
        P(("rep", "seq"), None, "tp", None),
        P(("rep", "seq"), None, "tp", None),
        P(("rep", "seq")),
        P(("rep", "seq")),
    )
    return jax.shard_map(
        shards,
        mesh=mesh,
        in_specs=placed,
        out_specs=P(("rep", "seq"), None, ("tp", "pp")),
        check_vma=False,
    )
```

```python
import functools
import math

import jax
import jax.numpy as jnp
from jax import lax
from jax.experimental import pallas as pl
from jax.experimental.pallas import tpu as pltpu
from jax.sharding import PartitionSpec as P

QHEADS = 64
KVH = 8
HD = 128
LOG2E = math.log2(math.e)
VMEM_BYTES = 56 * 1024 * 1024
SLOTS = 8
HBM = pl.BlockSpec(memory_space=pl.ANY)
SMEM = pl.BlockSpec(memory_space=pltpu.SMEM)
VMEM = pl.BlockSpec(memory_space=pltpu.VMEM)


TN = (((0,), (0,)), ((), ()))
BLOCK = 256


def stacked_heads(q_tile, per_kv):
    return jnp.concatenate([q_tile[:, g * HD:(g + 1) * HD] for g in range(per_kv)], axis=0)


def own_scores(own_tile, q_cols, rlen):
    own = jnp.dot(own_tile[:, :HD], q_cols, preferred_element_type=jnp.float32)
    own_at = lax.broadcasted_iota(jnp.int32, own.shape, 0)
    token_at = lax.broadcasted_iota(jnp.int32, own.shape, 1) % rlen
    return jnp.where(own_at <= token_at, own, -1e30)


def two_stages(after_q, after_own, after_kv, after_s, after_u, after_peak, now):
    rlen = after_own.shape[0]
    per_kv = after_q.shape[1] // HD
    plen = after_kv.shape[0]
    scale = HD ** -0.5 * LOG2E
    q_cols = stacked_heads(after_q, per_kv).T
    own = own_scores(after_own, q_cols, rlen)
    after_u[...] = own
    after_top = jnp.max(own, axis=0, keepdims=True)
    if now is not None:
        s_ref, u_ref, peak_ref, own_tile, vt_ref, length = now
        peak = peak_ref[0:1, :]
        part = jnp.exp2((u_ref[...] - peak) * scale)
        total = jnp.sum(part, axis=0, keepdims=True)
        acc = lax.dot_general(own_tile[:, HD:], part.astype(jnp.bfloat16), TN, preferred_element_type=jnp.float32)
    for at in range(0, plen, BLOCK):
        rows = pl.ds(at, BLOCK)
        fresh = jnp.dot(after_kv[rows, :HD], q_cols, preferred_element_type=jnp.float32)
        after_s[rows, :] = fresh
        after_top = jnp.maximum(after_top, jnp.max(fresh, axis=0, keepdims=True))
        if now is not None:
            part = jnp.exp2((s_ref[rows, :] - peak) * scale)
            total = total + jnp.sum(part, axis=0, keepdims=True)
            acc = acc + jnp.dot(vt_ref[:, rows], part.astype(jnp.bfloat16), preferred_element_type=jnp.float32)
    after_peak[...] = jnp.broadcast_to(after_top, after_peak.shape)
    if now is None:
        return None
    out = (acc * (1.0 / total)).T
    alive = lax.broadcasted_iota(jnp.int32, (rlen, HD), 0) < length
    return [jnp.where(alive, out[g * rlen:(g + 1) * rlen, :], 0.0).astype(jnp.bfloat16) for g in range(per_kv)]


def listed(items, cap, count, groups, lengths, target, source):
    def look(at, n):
        hit = groups[at] == target

        @pl.when(hit)
        def _():
            items[n] = at
            items[cap + n] = source
            items[2 * cap + n] = lengths[at]

        return n + hit.astype(jnp.int32)

    return lax.fori_loop(0, groups.shape[0], look, count)


def attend_kernel(passes, n_cand, per_kv, head, two, fresh, waits, *refs):
    refs = list(refs)
    facts, groups, lengths = refs[:3]
    refs = refs[3:]
    if two:
        x_ref, refs = refs[0], refs[1:]
    q_ref, own_ref = refs[:2]
    cands, refs = refs[2:2 + n_cand], refs[2 + n_cand + waits:]
    n_out = 2 if two else 1
    if not fresh:
        refs = refs[1:]
    outs, refs = refs[:n_out], refs[n_out:]
    items, at_slot, q_buf, own_buf, kv_buf, vt_buf, s0, s1, u0, u1, peak0, peak1, o_buf, info, q_sem, own_sem, kv_sem, o_sem = refs
    s_buf, u_buf, peak_buf = (s0, s1), (u0, u1), (peak0, peak1)
    local = groups.shape[0]
    cap = items.shape[0] // 3
    width = per_kv * HD
    stacked = passes is None

    count = jnp.int32(0)
    if stacked:
        def one_prompt(prompt, n):
            return listed(items, cap, n, groups, lengths, prompt, prompt)

        count = lax.fori_loop(0, cands[0].shape[0], one_prompt, count)
    else:
        for far, target, source in passes:
            if not far:
                count = listed(items, cap, count, groups, lengths, facts[target], facts[source])
                continue
            notes = pltpu.make_async_copy(x_ref.at[:, :, pl.ds(2 * (width + 2 * HD), HD)], info, kv_sem)
            notes.start()
            notes.wait()
            for slot in range(SLOTS):
                length = jnp.max(info[slot, 0:16, :].astype(jnp.float32)).astype(jnp.int32)
                hit = (length > 0) & (facts[target] >= 0)

                @pl.when(hit)
                def _():
                    items[count] = local + slot
                    items[cap + count] = facts[source]
                    items[2 * cap + count] = length

                count = count + hit.astype(jnp.int32)

    def each_array(i, act_local, act_far):
        at = items[i]
        if not two:
            act_local(at)
            return

        @pl.when(at < local)
        def _():
            act_local(at)

        @pl.when(at >= local)
        def _():
            act_far(at - local)

    mine = pl.ds(head * width, width)
    first = pl.ds(0, width)
    handed_q = pl.ds(head * (width + 2 * HD), width)
    handed_own = pl.ds(head * (width + 2 * HD) + width, 2 * HD)

    def fetch(i):
        slot, third = lax.rem(i, 2), lax.rem(i, 3)

        def here(at):
            pltpu.make_async_copy(q_ref.at[at, :, mine], q_buf.at[slot], q_sem.at[slot]).start()
            pltpu.make_async_copy(own_ref.at[at], own_buf.at[third], own_sem.at[third]).start()

        def far(at):
            pltpu.make_async_copy(x_ref.at[at, :, handed_q], q_buf.at[slot], q_sem.at[slot]).start()
            pltpu.make_async_copy(x_ref.at[at, :, handed_own], own_buf.at[third], own_sem.at[third]).start()

        each_array(i, here, far)

    def fetched(i):
        slot, third = lax.rem(i, 2), lax.rem(i, 3)
        pltpu.make_async_copy(q_ref.at[0, :, first], q_buf.at[slot], q_sem.at[slot]).wait()
        pltpu.make_async_copy(own_ref.at[0], own_buf.at[third], own_sem.at[third]).wait()

    def store(i, slot):
        def here(at):
            pltpu.make_async_copy(o_buf.at[slot], outs[0].at[at, :, mine], o_sem.at[slot]).start()

        def far(at):
            pltpu.make_async_copy(o_buf.at[slot], outs[1].at[at], o_sem.at[slot]).start()

        each_array(i, here, far)

    def stored(slot):
        pltpu.make_async_copy(o_buf.at[slot], outs[0].at[0, :, first], o_sem.at[slot]).wait()

    def load(source, into):
        if stacked:
            pltpu.make_async_copy(cands[0].at[source], kv_buf.at[into], kv_sem).start()
        else:
            for which in range(n_cand):
                @pl.when(source == which)
                def _():
                    source_ref = cands[which].at[head] if len(cands[which].shape) == 3 else cands[which]
                    pltpu.make_async_copy(source_ref, kv_buf.at[into], kv_sem).start()

        pltpu.make_async_copy(kv_buf.at[into], kv_buf.at[into], kv_sem).wait()
        vt_buf[into] = kv_buf[into, :, HD:].T

    @pl.when(count > 0)
    def _():
        fetch(jnp.int32(0))

        @pl.when(count > 1)
        def _():
            fetch(jnp.int32(1))

        load(items[cap], 0)
        at_slot[0] = 0
        fetched(jnp.int32(0))
        two_stages(q_buf[0], own_buf[0], kv_buf.at[0], s_buf[0], u_buf[0], peak_buf[0], None)

        def one(i, slot):
            held = at_slot[0]
            more = i + 1 < count
            moved = more & (items[cap + jnp.minimum(i + 1, count - 1)] != items[cap + i])
            holds = jnp.where(moved, 1 - held, held)
            at_slot[0] = holds

            @pl.when(more)
            def _():
                fetched(i + 1)

            @pl.when(i + 2 < count)
            def _():
                fetch(i + 2)

            @pl.when(moved)
            def _():
                load(items[cap + i + 1], holds)

            @pl.when(i >= 2)
            def _():
                stored(slot)

            now = (s_buf[slot], u_buf[slot], peak_buf[slot], own_buf[lax.rem(i, 3)], vt_buf.at[held], items[2 * cap + i])
            tiles = two_stages(
                q_buf[1 - slot], own_buf[lax.rem(i + 1, 3)], kv_buf.at[holds],
                s_buf[1 - slot], u_buf[1 - slot], peak_buf[1 - slot], now)
            for g in range(per_kv):
                o_buf[slot, :, g * HD:(g + 1) * HD] = tiles[g]
            store(i, slot)

        def pair(j, _):
            one(2 * j, 0)

            @pl.when(2 * j + 1 < count)
            def _():
                one(2 * j + 1, 1)

            return 0

        lax.fori_loop(0, lax.div(count + 1, 2), pair, 0)
        stored(0)

        @pl.when(count > 1)
        def _():
            stored(1)


def attend(facts, groups, lengths, queries, own, cands, outs, head, per_kv, passes, items, far=None, fresh=False, wait_for=None):
    rlen = queries.shape[1]
    plen = cands[0].shape[-2]
    width = per_kv * HD
    small = [facts, groups, lengths]
    large = ([far] if far is not None else []) + [queries, own] + cands
    operands = small + large + ([] if wait_for is None else [wait_for])
    aliases = {}
    if not fresh:
        aliases = {len(operands): 0}
        operands = operands + [outs[0]]
    cap = groups.shape[0] + (SLOTS if far is not None else 0)
    return pl.pallas_call(
        functools.partial(attend_kernel, passes, len(cands), per_kv, head, far is not None, fresh, wait_for is not None),
        out_shape=[jax.ShapeDtypeStruct(o.shape, o.dtype) for o in outs],
        in_specs=[SMEM] * len(small) + [HBM] * (len(operands) - len(small)),
        out_specs=[HBM] * len(outs),
        input_output_aliases=aliases,
        scratch_shapes=[
            pltpu.SMEM((3 * cap,), jnp.int32),
            pltpu.SMEM((1,), jnp.int32),
            pltpu.VMEM((2, rlen, width), jnp.bfloat16),
            pltpu.VMEM((3, rlen, 2 * HD), jnp.bfloat16),
            pltpu.VMEM((2, plen, 2 * HD), jnp.bfloat16),
            pltpu.VMEM((2, HD, plen), jnp.bfloat16),
            pltpu.VMEM((plen, per_kv * rlen), jnp.float32),
            pltpu.VMEM((plen, per_kv * rlen), jnp.float32),
            pltpu.VMEM((rlen, per_kv * rlen), jnp.float32),
            pltpu.VMEM((rlen, per_kv * rlen), jnp.float32),
            pltpu.VMEM((8, per_kv * rlen), jnp.float32),
            pltpu.VMEM((8, per_kv * rlen), jnp.float32),
            pltpu.VMEM((2, rlen, width), jnp.bfloat16),
            pltpu.VMEM((SLOTS, rlen, HD), jnp.bfloat16),
            pltpu.SemaphoreType.DMA((2,)),
            pltpu.SemaphoreType.DMA((3,)),
            pltpu.SemaphoreType.DMA,
            pltpu.SemaphoreType.DMA((2,)),
        ],
        compiler_params=pltpu.CompilerParams(vmem_limit_bytes=VMEM_BYTES),
        cost_estimate=pl.CostEstimate(flops=items << 20, bytes_accessed=1 << 16, transcendentals=0),
    )(*operands)


def pack_kernel(target, width, facts, groups, lengths, q_ref, own0, own1, out, sem):
    owns = (own0, own1)
    step = width + 2 * HD
    notes = pl.ds(2 * step, HD)
    out[:, :, notes] = jnp.zeros((SLOTS, out.shape[1], HD), out.dtype)

    def each(act, note):
        def look(at, slot):
            hit = groups[at] == facts[target]

            @pl.when(hit)
            def _():
                for head in range(2):
                    part = pl.ds(head * width, width)
                    act(pltpu.make_async_copy(q_ref.at[at, :, part], out.at[slot, :, pl.ds(head * step, width)], sem))
                    act(pltpu.make_async_copy(owns[head].at[at], out.at[slot, :, pl.ds(head * step + width, 2 * HD)], sem))
                if note:
                    length = jnp.full((out.shape[1], HD), lengths[at], jnp.int32)
                    out[slot, :, notes] = length.astype(jnp.float32).astype(out.dtype)

            return slot + hit.astype(jnp.int32)

        lax.fori_loop(0, groups.shape[0], look, jnp.int32(0))

    each(lambda copy: copy.start(), True)
    each(lambda copy: copy.wait(), False)


def pack(facts, target, groups, lengths, queries, own, width):
    shape = jax.ShapeDtypeStruct((SLOTS, queries.shape[1], 2 * (width + 2 * HD) + HD), queries.dtype)
    return pl.pallas_call(
        functools.partial(pack_kernel, target, width),
        out_shape=shape,
        in_specs=[SMEM, SMEM, SMEM, HBM, HBM, HBM],
        out_specs=VMEM,
        scratch_shapes=[pltpu.SemaphoreType.DMA],
        compiler_params=pltpu.CompilerParams(vmem_limit_bytes=1 << 23),
    )(facts, groups, lengths, queries, *own)


def gate_kernel(value, other, out):
    pass


def gate(value, other):
    return pl.pallas_call(
        gate_kernel,
        out_shape=jax.ShapeDtypeStruct(value.shape, value.dtype),
        in_specs=[HBM, HBM],
        out_specs=HBM,
        input_output_aliases={0: 0},
    )(value, other)


def merge_kernel(target, width, facts, groups, got0, got1, old, out, sem):
    got = (got0, got1)

    def each(act):
        def look(at, slot):
            hit = groups[at] == facts[target]

            @pl.when(hit)
            def _():
                for head in range(2):
                    act(pltpu.make_async_copy(got[head].at[slot], out.at[at, :, pl.ds(head * width, width)], sem))

            return slot + hit.astype(jnp.int32)

        lax.fori_loop(0, groups.shape[0], look, jnp.int32(0))

    each(lambda copy: copy.start())
    each(lambda copy: copy.wait())


def merge(facts, target, groups, got, out, width):
    return pl.pallas_call(
        functools.partial(merge_kernel, target, width),
        out_shape=jax.ShapeDtypeStruct(out.shape, out.dtype),
        in_specs=[SMEM, SMEM, VMEM, VMEM, HBM],
        out_specs=HBM,
        input_output_aliases={4: 0},
        scratch_shapes=[pltpu.SemaphoreType.DMA],
        compiler_params=pltpu.CompilerParams(vmem_limit_bytes=1 << 23),
    )(facts, groups, *got, out)


def after(value, *others):
    return lax.optimization_barrier((value,) + others)[0]


def gathered(queries, resp_kv, prompt_kv, lengths, group_of, first_head, kv_needed, per_kv):
    out = jax.ShapeDtypeStruct(queries.shape, jnp.bfloat16)
    facts = jnp.zeros((8,), jnp.int32)
    for head in range(kv_needed):
        mine = lax.dynamic_index_in_dim(prompt_kv, first_head + head, 2, keepdims=False)
        own = lax.dynamic_index_in_dim(resp_kv, first_head + head, 2, keepdims=False)
        whole = lax.all_gather(mine, "seq", axis=0, tiled=True)
        [out] = attend(facts, group_of, lengths, queries, own, [whole], [out], head, per_kv, None, 16, fresh=head == 0)
    return out


def relayed(queries, resp_kv, prompt_kv, lengths, group_of, first_head, per_kv):
    me = lax.axis_index("seq")
    width = per_kv * HD
    middle, inward, outward = [(1, 2), (2, 1)], [(0, 1), (3, 2)], [(1, 0), (2, 3)]

    def send(pairs, value):
        return lax.ppermute(value, "seq", pairs)

    def two_heads(start):
        def cut(pairs):
            return jnp.transpose(pairs[:, start:start + 2], (1, 0, 2))

        return cut

    splits = prompt_kv.shape[2] // 2
    mine = lax.switch(first_head // 2, [two_heads(2 * at) for at in range(splits)], prompt_kv[0])
    across = send(middle, mine)
    near = [send(inward, lax.index_in_dim(mine, head, 0, keepdims=False)) for head in range(2)]
    inner_prompt = send(outward, mine)

    low = me < 2
    is_inner = (me == 1) | (me == 2)
    outer, inner = jnp.where(low, 0, 3), jnp.where(low, 1, 2)
    far_inner, far_outer = jnp.where(low, 2, 1), jnp.where(low, 3, 0)
    facts = jnp.stack([
        me,
        jnp.zeros_like(me),
        jnp.where(is_inner, outer, inner),
        jnp.where(is_inner, 0, 2),
        jnp.where(is_inner, far_inner, -1),
        jnp.ones_like(me),
        jnp.where(is_inner, far_outer, -1),
        jnp.where(is_inner, far_outer, far_inner),
        jnp.where(is_inner, 0, 1),
        jnp.where(is_inner, -1, far_outer),
    ]).astype(jnp.int32)

    own_by_head = after(jnp.transpose(resp_kv, (2, 0, 1, 3)))
    own = [lax.dynamic_index_in_dim(own_by_head, first_head + head, 0, keepdims=False) for head in range(2)]
    packed = pack(facts, 9, group_of, lengths, queries, own, width)
    out = jax.ShapeDtypeStruct(queries.shape, jnp.bfloat16)
    back_shape = jax.ShapeDtypeStruct((SLOTS, queries.shape[1], width), jnp.bfloat16)

    def run(head, cands, outs, passes, items, far=None, fresh=False, wait_for=None):
        return attend(
            facts, group_of, lengths, queries, own[head], cands, outs, head, per_kv, passes, items, far, fresh, wait_for)

    [out] = run(0, [mine], [out], [(False, 0, 1)], 4, fresh=True)
    [out] = run(1, [mine], [out], [(False, 0, 1)], 4, wait_for=near[0])
    last = [send(middle, near[0])]
    near[1] = gate(near[1], out)
    last.append(send(middle, near[1]))
    across = gate(across, near[1])
    far_inner_prompt = send(outward, across)
    handed = send(inward, gate(packed, near[1]))
    for head in range(2):
        [out] = run(head, [near[head], across, inner_prompt], [out], [(False, 2, 3), (False, 4, 5)], 8, wait_for=near[1])
    back = [None, None]
    for head in range(2):
        out, back[head] = run(head, [last[head]], [out, back_shape], [(True, 6, 1)], 4, handed)
        back[head] = send(outward, back[head])
        [out] = run(head, [last[head], far_inner_prompt], [out], [(False, 7, 8)], 4)
    return merge(facts, 9, group_of, back, out, width)


def shards(queries, resp_kv, prompt_kv, lengths, group_of):
    local_heads = queries.shape[2] // HD
    group = QHEADS // KVH
    kv_needed = max(local_heads // group, 1)
    per_kv = local_heads // kv_needed
    first_head = lax.axis_index("pp") * local_heads // group
    args = (queries, resp_kv, prompt_kv, lengths, group_of, first_head)
    if lax.axis_size("seq") == 4 and kv_needed == 2 and prompt_kv.shape[0] == 1:
        return relayed(*args, per_kv)
    return gathered(*args, kv_needed, per_kv)


def solution(mesh):
    placed = (
        P(("rep", "seq"), None, ("tp", "pp")),
        P(("rep", "seq"), None, "tp", None),
        P(("rep", "seq"), None, "tp", None),
        P(("rep", "seq")),
        P(("rep", "seq")),
    )
    return jax.shard_map(
        shards,
        mesh=mesh,
        in_specs=placed,
        out_specs=P(("rep", "seq"), None, ("tp", "pp")),
        check_vma=False,
    )
```

```python
import functools
import math

import jax
import jax.numpy as jnp
from jax import lax
from jax.experimental import pallas as pl
from jax.experimental.pallas import tpu as pltpu
from jax.sharding import PartitionSpec as P

QHEADS = 64
KVH = 8
HD = 128
LOG2E = math.log2(math.e)
VMEM_BYTES = 56 * 1024 * 1024
SLOTS = 8
HBM = pl.BlockSpec(memory_space=pl.ANY)
SMEM = pl.BlockSpec(memory_space=pltpu.SMEM)
VMEM = pl.BlockSpec(memory_space=pltpu.VMEM)


TN = (((0,), (0,)), ((), ()))
BLOCK = 256


def stacked_heads(q_tile, per_kv):
    return jnp.concatenate([q_tile[:, g * HD:(g + 1) * HD] for g in range(per_kv)], axis=0)


def own_scores(own_tile, q_cols, rlen):
    own = jnp.dot(own_tile[:, :HD], q_cols, preferred_element_type=jnp.float32)
    own_at = lax.broadcasted_iota(jnp.int32, own.shape, 0)
    token_at = lax.broadcasted_iota(jnp.int32, own.shape, 1) % rlen
    return jnp.where(own_at <= token_at, own, -1e30)


def two_stages(after_q, after_own, after_kv, after_s, after_u, after_peak, now):
    rlen = after_own.shape[0]
    per_kv = after_q.shape[1] // HD
    plen = after_kv.shape[0]
    scale = HD ** -0.5 * LOG2E
    q_cols = stacked_heads(after_q, per_kv).T
    own = own_scores(after_own, q_cols, rlen)
    after_u[...] = own
    after_top = jnp.max(own, axis=0, keepdims=True)
    if now is not None:
        s_ref, u_ref, peak_ref, own_tile, vt_ref, length = now
        peak = peak_ref[0:1, :]
        part = jnp.exp2((u_ref[...] - peak) * scale)
        total = jnp.sum(part, axis=0, keepdims=True)
        acc = lax.dot_general(own_tile[:, HD:], part.astype(jnp.bfloat16), TN, preferred_element_type=jnp.float32)
    for at in range(0, plen, BLOCK):
        rows = pl.ds(at, BLOCK)
        fresh = jnp.dot(after_kv[rows, :HD], q_cols, preferred_element_type=jnp.float32)
        after_s[rows, :] = fresh
        after_top = jnp.maximum(after_top, jnp.max(fresh, axis=0, keepdims=True))
        if now is not None:
            part = jnp.exp2((s_ref[rows, :] - peak) * scale)
            total = total + jnp.sum(part, axis=0, keepdims=True)
            acc = acc + jnp.dot(vt_ref[:, rows], part.astype(jnp.bfloat16), preferred_element_type=jnp.float32)
    after_peak[...] = jnp.broadcast_to(after_top, after_peak.shape)
    if now is None:
        return None
    out = (acc * (1.0 / total)).T
    alive = lax.broadcasted_iota(jnp.int32, (rlen, HD), 0) < length
    return [jnp.where(alive, out[g * rlen:(g + 1) * rlen, :], 0.0).astype(jnp.bfloat16) for g in range(per_kv)]


def listed(items, cap, count, groups, lengths, target, source):
    def look(at, n):
        hit = groups[at] == target

        @pl.when(hit)
        def _():
            items[n] = at
            items[cap + n] = source
            items[2 * cap + n] = lengths[at]

        return n + hit.astype(jnp.int32)

    return lax.fori_loop(0, groups.shape[0], look, count)


def attend_kernel(passes, n_cand, per_kv, head, two, fresh, waits, *refs):
    refs = list(refs)
    facts, groups, lengths = refs[:3]
    refs = refs[3:]
    if two:
        x_ref, refs = refs[0], refs[1:]
    q_ref, own_ref = refs[:2]
    cands, refs = refs[2:2 + n_cand], refs[2 + n_cand + waits:]
    n_out = 2 if two else 1
    if not fresh:
        refs = refs[1:]
    outs, refs = refs[:n_out], refs[n_out:]
    items, at_slot, q_buf, own_buf, kv_buf, vt_buf, s0, s1, u0, u1, peak0, peak1, o_buf, info, q_sem, own_sem, kv_sem, o_sem = refs
    s_buf, u_buf, peak_buf = (s0, s1), (u0, u1), (peak0, peak1)
    local = groups.shape[0]
    cap = items.shape[0] // 3
    width = per_kv * HD
    stacked = passes is None

    count = jnp.int32(0)
    if stacked:
        def one_prompt(prompt, n):
            return listed(items, cap, n, groups, lengths, prompt, prompt)

        count = lax.fori_loop(0, cands[0].shape[0], one_prompt, count)
    else:
        for far, target, source in passes:
            if not far:
                count = listed(items, cap, count, groups, lengths, facts[target], facts[source])
                continue
            notes = pltpu.make_async_copy(x_ref.at[:, :, pl.ds(2 * (width + 2 * HD), HD)], info, kv_sem)
            notes.start()
            notes.wait()
            for slot in range(SLOTS):
                length = jnp.max(info[slot, 0:16, :].astype(jnp.float32)).astype(jnp.int32)
                hit = (length > 0) & (facts[target] >= 0)

                @pl.when(hit)
                def _():
                    items[count] = local + slot
                    items[cap + count] = facts[source]
                    items[2 * cap + count] = length

                count = count + hit.astype(jnp.int32)

    def each_array(i, act_local, act_far):
        at = items[i]
        if not two:
            act_local(at)
            return

        @pl.when(at < local)
        def _():
            act_local(at)

        @pl.when(at >= local)
        def _():
            act_far(at - local)

    mine = pl.ds(head * width, width)
    first = pl.ds(0, width)
    handed_q = pl.ds(head * (width + 2 * HD), width)
    handed_own = pl.ds(head * (width + 2 * HD) + width, 2 * HD)

    def fetch(i):
        slot, third = lax.rem(i, 2), lax.rem(i, 3)

        def here(at):
            pltpu.make_async_copy(q_ref.at[at, :, mine], q_buf.at[slot], q_sem.at[slot]).start()
            pltpu.make_async_copy(own_ref.at[at], own_buf.at[third], own_sem.at[third]).start()

        def far(at):
            pltpu.make_async_copy(x_ref.at[at, :, handed_q], q_buf.at[slot], q_sem.at[slot]).start()
            pltpu.make_async_copy(x_ref.at[at, :, handed_own], own_buf.at[third], own_sem.at[third]).start()

        each_array(i, here, far)

    def fetched(i):
        slot, third = lax.rem(i, 2), lax.rem(i, 3)
        pltpu.make_async_copy(q_ref.at[0, :, first], q_buf.at[slot], q_sem.at[slot]).wait()
        pltpu.make_async_copy(own_ref.at[0], own_buf.at[third], own_sem.at[third]).wait()

    def store(i, slot):
        def here(at):
            pltpu.make_async_copy(o_buf.at[slot], outs[0].at[at, :, mine], o_sem.at[slot]).start()

        def far(at):
            pltpu.make_async_copy(o_buf.at[slot], outs[1].at[at], o_sem.at[slot]).start()

        each_array(i, here, far)

    def stored(slot):
        pltpu.make_async_copy(o_buf.at[slot], outs[0].at[0, :, first], o_sem.at[slot]).wait()

    def load(source, into):
        if stacked:
            pltpu.make_async_copy(cands[0].at[source], kv_buf.at[into], kv_sem).start()
        else:
            for which in range(n_cand):
                @pl.when(source == which)
                def _():
                    source_ref = cands[which].at[head] if len(cands[which].shape) == 3 else cands[which]
                    pltpu.make_async_copy(source_ref, kv_buf.at[into], kv_sem).start()

        pltpu.make_async_copy(kv_buf.at[into], kv_buf.at[into], kv_sem).wait()
        vt_buf[into] = kv_buf[into, :, HD:].T

    @pl.when(count > 0)
    def _():
        fetch(jnp.int32(0))

        @pl.when(count > 1)
        def _():
            fetch(jnp.int32(1))

        load(items[cap], 0)
        at_slot[0] = 0
        fetched(jnp.int32(0))
        two_stages(q_buf[0], own_buf[0], kv_buf.at[0], s_buf[0], u_buf[0], peak_buf[0], None)

        def one(i, slot):
            held = at_slot[0]
            more = i + 1 < count
            moved = more & (items[cap + jnp.minimum(i + 1, count - 1)] != items[cap + i])
            holds = jnp.where(moved, 1 - held, held)
            at_slot[0] = holds

            @pl.when(more)
            def _():
                fetched(i + 1)

            @pl.when(i + 2 < count)
            def _():
                fetch(i + 2)

            @pl.when(moved)
            def _():
                load(items[cap + i + 1], holds)

            @pl.when(i >= 2)
            def _():
                stored(slot)

            now = (s_buf[slot], u_buf[slot], peak_buf[slot], own_buf[lax.rem(i, 3)], vt_buf.at[held], items[2 * cap + i])
            tiles = two_stages(
                q_buf[1 - slot], own_buf[lax.rem(i + 1, 3)], kv_buf.at[holds],
                s_buf[1 - slot], u_buf[1 - slot], peak_buf[1 - slot], now)
            for g in range(per_kv):
                o_buf[slot, :, g * HD:(g + 1) * HD] = tiles[g]
            store(i, slot)

        def pair(j, _):
            one(2 * j, 0)

            @pl.when(2 * j + 1 < count)
            def _():
                one(2 * j + 1, 1)

            return 0

        lax.fori_loop(0, lax.div(count + 1, 2), pair, 0)
        stored(0)

        @pl.when(count > 1)
        def _():
            stored(1)


def attend(facts, groups, lengths, queries, own, cands, outs, head, per_kv, passes, items, far=None, fresh=False, wait_for=None):
    rlen = queries.shape[1]
    plen = cands[0].shape[-2]
    width = per_kv * HD
    small = [facts, groups, lengths]
    large = ([far] if far is not None else []) + [queries, own] + cands
    operands = small + large + ([] if wait_for is None else [wait_for])
    aliases = {}
    if not fresh:
        aliases = {len(operands): 0}
        operands = operands + [outs[0]]
    cap = groups.shape[0] + (SLOTS if far is not None else 0)
    return pl.pallas_call(
        functools.partial(attend_kernel, passes, len(cands), per_kv, head, far is not None, fresh, wait_for is not None),
        out_shape=[jax.ShapeDtypeStruct(o.shape, o.dtype) for o in outs],
        in_specs=[SMEM] * len(small) + [HBM] * (len(operands) - len(small)),
        out_specs=[HBM] * len(outs),
        input_output_aliases=aliases,
        scratch_shapes=[
            pltpu.SMEM((3 * cap,), jnp.int32),
            pltpu.SMEM((1,), jnp.int32),
            pltpu.VMEM((2, rlen, width), jnp.bfloat16),
            pltpu.VMEM((3, rlen, 2 * HD), jnp.bfloat16),
            pltpu.VMEM((2, plen, 2 * HD), jnp.bfloat16),
            pltpu.VMEM((2, HD, plen), jnp.bfloat16),
            pltpu.VMEM((plen, per_kv * rlen), jnp.float32),
            pltpu.VMEM((plen, per_kv * rlen), jnp.float32),
            pltpu.VMEM((rlen, per_kv * rlen), jnp.float32),
            pltpu.VMEM((rlen, per_kv * rlen), jnp.float32),
            pltpu.VMEM((8, per_kv * rlen), jnp.float32),
            pltpu.VMEM((8, per_kv * rlen), jnp.float32),
            pltpu.VMEM((2, rlen, width), jnp.bfloat16),
            pltpu.VMEM((SLOTS, rlen, HD), jnp.bfloat16),
            pltpu.SemaphoreType.DMA((2,)),
            pltpu.SemaphoreType.DMA((3,)),
            pltpu.SemaphoreType.DMA,
            pltpu.SemaphoreType.DMA((2,)),
        ],
        compiler_params=pltpu.CompilerParams(vmem_limit_bytes=VMEM_BYTES),
        cost_estimate=pl.CostEstimate(flops=items << 20, bytes_accessed=1 << 16, transcendentals=0),
    )(*operands)


def pack_kernel(target, width, facts, groups, lengths, q_ref, own0, own1, out, sem):
    owns = (own0, own1)
    step = width + 2 * HD
    notes = pl.ds(2 * step, HD)
    out[:, :, notes] = jnp.zeros((SLOTS, out.shape[1], HD), out.dtype)

    def each(act, note):
        def look(at, slot):
            hit = groups[at] == facts[target]

            @pl.when(hit)
            def _():
                for head in range(2):
                    part = pl.ds(head * width, width)
                    act(pltpu.make_async_copy(q_ref.at[at, :, part], out.at[slot, :, pl.ds(head * step, width)], sem))
                    act(pltpu.make_async_copy(owns[head].at[at], out.at[slot, :, pl.ds(head * step + width, 2 * HD)], sem))
                if note:
                    length = jnp.full((out.shape[1], HD), lengths[at], jnp.int32)
                    out[slot, :, notes] = length.astype(jnp.float32).astype(out.dtype)

            return slot + hit.astype(jnp.int32)

        lax.fori_loop(0, groups.shape[0], look, jnp.int32(0))

    each(lambda copy: copy.start(), True)
    each(lambda copy: copy.wait(), False)


def pack(facts, target, groups, lengths, queries, own, width):
    shape = jax.ShapeDtypeStruct((SLOTS, queries.shape[1], 2 * (width + 2 * HD) + HD), queries.dtype)
    return pl.pallas_call(
        functools.partial(pack_kernel, target, width),
        out_shape=shape,
        in_specs=[SMEM, SMEM, SMEM, HBM, HBM, HBM],
        out_specs=VMEM,
        scratch_shapes=[pltpu.SemaphoreType.DMA],
        compiler_params=pltpu.CompilerParams(vmem_limit_bytes=1 << 23),
    )(facts, groups, lengths, queries, *own)


def gate_kernel(*refs):
    pass


def gate(value, *others):
    return pl.pallas_call(
        gate_kernel,
        out_shape=jax.ShapeDtypeStruct(value.shape, value.dtype),
        in_specs=[HBM] * (1 + len(others)),
        out_specs=HBM,
        input_output_aliases={0: 0},
    )(value, *others)


def merge_kernel(target, width, facts, groups, got0, got1, old, out, sem):
    got = (got0, got1)

    def each(act):
        def look(at, slot):
            hit = groups[at] == facts[target]

            @pl.when(hit)
            def _():
                for head in range(2):
                    act(pltpu.make_async_copy(got[head].at[slot], out.at[at, :, pl.ds(head * width, width)], sem))

            return slot + hit.astype(jnp.int32)

        lax.fori_loop(0, groups.shape[0], look, jnp.int32(0))

    each(lambda copy: copy.start())
    each(lambda copy: copy.wait())


def merge(facts, target, groups, got, out, width):
    return pl.pallas_call(
        functools.partial(merge_kernel, target, width),
        out_shape=jax.ShapeDtypeStruct(out.shape, out.dtype),
        in_specs=[SMEM, SMEM, VMEM, VMEM, HBM],
        out_specs=HBM,
        input_output_aliases={4: 0},
        scratch_shapes=[pltpu.SemaphoreType.DMA],
        compiler_params=pltpu.CompilerParams(vmem_limit_bytes=1 << 23),
    )(facts, groups, *got, out)


def after(value, *others):
    return lax.optimization_barrier((value,) + others)[0]


def gathered(queries, resp_kv, prompt_kv, lengths, group_of, first_head, kv_needed, per_kv):
    out = jax.ShapeDtypeStruct(queries.shape, jnp.bfloat16)
    facts = jnp.zeros((8,), jnp.int32)
    for head in range(kv_needed):
        mine = lax.dynamic_index_in_dim(prompt_kv, first_head + head, 2, keepdims=False)
        own = lax.dynamic_index_in_dim(resp_kv, first_head + head, 2, keepdims=False)
        whole = lax.all_gather(mine, "seq", axis=0, tiled=True)
        [out] = attend(facts, group_of, lengths, queries, own, [whole], [out], head, per_kv, None, 16, fresh=head == 0)
    return out


def relayed(queries, resp_kv, prompt_kv, lengths, group_of, first_head, per_kv):
    me = lax.axis_index("seq")
    width = per_kv * HD
    middle, inward, outward = [(1, 2), (2, 1)], [(0, 1), (3, 2)], [(1, 0), (2, 3)]

    def send(pairs, value):
        return lax.ppermute(value, "seq", pairs)

    def two_heads(start):
        return lambda pairs: pairs[:, start:start + 2]

    splits = prompt_kv.shape[2] // 2
    pairs = lax.switch(first_head // 2, [two_heads(2 * at) for at in range(splits)], prompt_kv[0])
    mine = [pairs[:, head] for head in range(2)]
    across, near = [], []
    for head in range(2):
        across.append(send(middle, mine[head]))
        near.append(send(inward, mine[head]))
    inner_prompt = send(outward, jnp.transpose(pairs, (1, 0, 2)))

    low = me < 2
    is_inner = (me == 1) | (me == 2)
    outer, inner = jnp.where(low, 0, 3), jnp.where(low, 1, 2)
    far_inner, far_outer = jnp.where(low, 2, 1), jnp.where(low, 3, 0)
    facts = jnp.stack([
        me,
        jnp.zeros_like(me),
        jnp.where(is_inner, outer, inner),
        jnp.where(is_inner, 0, 2),
        jnp.where(is_inner, far_inner, -1),
        jnp.ones_like(me),
        jnp.where(is_inner, far_outer, -1),
        jnp.where(is_inner, far_outer, far_inner),
        jnp.where(is_inner, 0, 1),
        jnp.where(is_inner, -1, far_outer),
    ]).astype(jnp.int32)

    own_by_head = after(jnp.transpose(resp_kv, (2, 0, 1, 3)))
    own = [lax.dynamic_index_in_dim(own_by_head, first_head + head, 0, keepdims=False) for head in range(2)]
    packed = pack(facts, 9, group_of, lengths, queries, own, width)
    out = jax.ShapeDtypeStruct(queries.shape, jnp.bfloat16)
    back_shape = jax.ShapeDtypeStruct((SLOTS, queries.shape[1], width), jnp.bfloat16)

    def run(head, cands, outs, passes, items, far=None, fresh=False, wait_for=None):
        return attend(
            facts, group_of, lengths, queries, own[head], cands, outs, head, per_kv, passes, items, far, fresh, wait_for)

    [out] = run(0, [mine[0]], [out], [(False, 0, 1)], 4, fresh=True, wait_for=packed)
    near[0] = gate(near[0], out)
    last = [send(middle, near[0])]
    [out] = run(1, [mine[1]], [out], [(False, 0, 1)], 4)
    near[1] = gate(near[1], out)
    last.append(send(middle, near[1]))
    across = [gate(across[head], out) for head in range(2)]
    far_inner_prompt = [send(outward, across[head]) for head in range(2)]
    handed = send(inward, gate(packed, near[0]))
    for head in range(2):
        [out] = run(head, [near[head], across[head], inner_prompt], [out], [(False, 2, 3), (False, 4, 5)], 8, wait_for=near[1])
    back = [None, None]
    for head in range(2):
        out, back[head] = run(head, [last[head]], [out, back_shape], [(True, 6, 1)], 4, handed)
        back[head] = send(outward, back[head])
        [out] = run(head, [last[head], far_inner_prompt[head]], [out], [(False, 7, 8)], 4)
    return merge(facts, 9, group_of, back, out, width)


def shards(queries, resp_kv, prompt_kv, lengths, group_of):
    local_heads = queries.shape[2] // HD
    group = QHEADS // KVH
    kv_needed = max(local_heads // group, 1)
    per_kv = local_heads // kv_needed
    first_head = lax.axis_index("pp") * local_heads // group
    args = (queries, resp_kv, prompt_kv, lengths, group_of, first_head)
    if lax.axis_size("seq") == 4 and kv_needed == 2 and prompt_kv.shape[0] == 1:
        return relayed(*args, per_kv)
    return gathered(*args, kv_needed, per_kv)


def solution(mesh):
    placed = (
        P(("rep", "seq"), None, ("tp", "pp")),
        P(("rep", "seq"), None, "tp", None),
        P(("rep", "seq"), None, "tp", None),
        P(("rep", "seq")),
        P(("rep", "seq")),
    )
    return jax.shard_map(
        shards,
        mesh=mesh,
        in_specs=placed,
        out_specs=P(("rep", "seq"), None, ("tp", "pp")),
        check_vma=False,
    )
```

```python
import functools
import math

import jax
import jax.numpy as jnp
from jax import lax
from jax.experimental import pallas as pl
from jax.experimental.pallas import tpu as pltpu
from jax.sharding import PartitionSpec as P

QHEADS = 64
KVH = 8
HD = 128
LOG2E = math.log2(math.e)
VMEM_BYTES = 56 * 1024 * 1024
SLOTS = 8
HBM = pl.BlockSpec(memory_space=pl.ANY)
SMEM = pl.BlockSpec(memory_space=pltpu.SMEM)
VMEM = pl.BlockSpec(memory_space=pltpu.VMEM)


TN = (((0,), (0,)), ((), ()))
BLOCK = 256


def stacked_heads(q_tile, per_kv):
    return jnp.concatenate([q_tile[:, g * HD:(g + 1) * HD] for g in range(per_kv)], axis=0)


def own_scores(own_tile, q_cols, rlen):
    own = jnp.dot(own_tile[:, :HD], q_cols, preferred_element_type=jnp.float32)
    own_at = lax.broadcasted_iota(jnp.int32, own.shape, 0)
    token_at = lax.broadcasted_iota(jnp.int32, own.shape, 1) % rlen
    return jnp.where(own_at <= token_at, own, -1e30)


def two_stages(after_q, after_own, after_kv, after_s, after_u, after_peak, now):
    rlen = after_own.shape[0]
    per_kv = after_q.shape[1] // HD
    plen = after_kv.shape[0]
    scale = HD ** -0.5 * LOG2E
    q_cols = stacked_heads(after_q, per_kv).T
    own = own_scores(after_own, q_cols, rlen)
    after_u[...] = own
    after_top = jnp.max(own, axis=0, keepdims=True)
    if now is not None:
        s_ref, u_ref, peak_ref, own_tile, vt_ref, length = now
        peak = peak_ref[0:1, :]
        part = jnp.exp2((u_ref[...] - peak) * scale)
        total = jnp.sum(part, axis=0, keepdims=True)
        acc = lax.dot_general(own_tile[:, HD:], part.astype(jnp.bfloat16), TN, preferred_element_type=jnp.float32)
    for at in range(0, plen, BLOCK):
        rows = pl.ds(at, BLOCK)
        fresh = jnp.dot(after_kv[rows, :HD], q_cols, preferred_element_type=jnp.float32)
        after_s[rows, :] = fresh
        after_top = jnp.maximum(after_top, jnp.max(fresh, axis=0, keepdims=True))
        if now is not None:
            part = jnp.exp2((s_ref[rows, :] - peak) * scale)
            total = total + jnp.sum(part, axis=0, keepdims=True)
            acc = acc + jnp.dot(vt_ref[:, rows], part.astype(jnp.bfloat16), preferred_element_type=jnp.float32)
    after_peak[...] = jnp.broadcast_to(after_top, after_peak.shape)
    if now is None:
        return None
    out = (acc * (1.0 / total)).T
    alive = lax.broadcasted_iota(jnp.int32, (rlen, HD), 0) < length
    return [jnp.where(alive, out[g * rlen:(g + 1) * rlen, :], 0.0).astype(jnp.bfloat16) for g in range(per_kv)]


def listed(items, cap, count, groups, lengths, target, source):
    def look(at, n):
        hit = groups[at] == target

        @pl.when(hit)
        def _():
            items[n] = at
            items[cap + n] = source
            items[2 * cap + n] = lengths[at]

        return n + hit.astype(jnp.int32)

    return lax.fori_loop(0, groups.shape[0], look, count)


def attend_kernel(passes, n_cand, per_kv, head, two, fresh, waits, *refs):
    refs = list(refs)
    facts, groups, lengths = refs[:3]
    refs = refs[3:]
    if two:
        x_ref, refs = refs[0], refs[1:]
    q_ref, own_ref = refs[:2]
    cands, refs = refs[2:2 + n_cand], refs[2 + n_cand + waits:]
    n_out = 2 if two else 1
    if not fresh:
        refs = refs[1:]
    outs, refs = refs[:n_out], refs[n_out:]
    items, at_slot, q_buf, own_buf, kv_buf, vt_buf, s0, s1, u0, u1, peak0, peak1, o_buf, info, q_sem, own_sem, kv_sem, o_sem = refs
    s_buf, u_buf, peak_buf = (s0, s1), (u0, u1), (peak0, peak1)
    local = groups.shape[0]
    cap = items.shape[0] // 3
    width = per_kv * HD
    stacked = passes is None

    count = jnp.int32(0)
    if stacked:
        def one_prompt(prompt, n):
            return listed(items, cap, n, groups, lengths, prompt, prompt)

        count = lax.fori_loop(0, cands[0].shape[0], one_prompt, count)
    else:
        for far, target, source in passes:
            if not far:
                count = listed(items, cap, count, groups, lengths, facts[target], facts[source])
                continue
            notes = pltpu.make_async_copy(x_ref.at[:, :, pl.ds(2 * (width + 2 * HD), HD)], info, kv_sem)
            notes.start()
            notes.wait()
            for slot in range(SLOTS):
                length = jnp.max(info[slot, 0:16, :].astype(jnp.float32)).astype(jnp.int32)
                hit = (length > 0) & (facts[target] >= 0)

                @pl.when(hit)
                def _():
                    items[count] = local + slot
                    items[cap + count] = facts[source]
                    items[2 * cap + count] = length

                count = count + hit.astype(jnp.int32)

    def each_array(i, act_local, act_far):
        at = items[i]
        if not two:
            act_local(at)
            return

        @pl.when(at < local)
        def _():
            act_local(at)

        @pl.when(at >= local)
        def _():
            act_far(at - local)

    mine = pl.ds(head * width, width)
    first = pl.ds(0, width)
    handed_q = pl.ds(head * (width + 2 * HD), width)
    handed_own = pl.ds(head * (width + 2 * HD) + width, 2 * HD)

    def fetch(i):
        slot, third = lax.rem(i, 2), lax.rem(i, 3)

        def here(at):
            pltpu.make_async_copy(q_ref.at[at, :, mine], q_buf.at[slot], q_sem.at[slot]).start()
            pltpu.make_async_copy(own_ref.at[at], own_buf.at[third], own_sem.at[third]).start()

        def far(at):
            pltpu.make_async_copy(x_ref.at[at, :, handed_q], q_buf.at[slot], q_sem.at[slot]).start()
            pltpu.make_async_copy(x_ref.at[at, :, handed_own], own_buf.at[third], own_sem.at[third]).start()

        each_array(i, here, far)

    def fetched(i):
        slot, third = lax.rem(i, 2), lax.rem(i, 3)
        pltpu.make_async_copy(q_ref.at[0, :, first], q_buf.at[slot], q_sem.at[slot]).wait()
        pltpu.make_async_copy(own_ref.at[0], own_buf.at[third], own_sem.at[third]).wait()

    def store(i, slot):
        def here(at):
            pltpu.make_async_copy(o_buf.at[slot], outs[0].at[at, :, mine], o_sem.at[slot]).start()

        def far(at):
            pltpu.make_async_copy(o_buf.at[slot], outs[1].at[at], o_sem.at[slot]).start()

        each_array(i, here, far)

    def stored(slot):
        pltpu.make_async_copy(o_buf.at[slot], outs[0].at[0, :, first], o_sem.at[slot]).wait()

    def load(source, into):
        if stacked:
            pltpu.make_async_copy(cands[0].at[source], kv_buf.at[into], kv_sem).start()
        else:
            for which in range(n_cand):
                @pl.when(source == which)
                def _():
                    source_ref = cands[which].at[head] if len(cands[which].shape) == 3 else cands[which]
                    pltpu.make_async_copy(source_ref, kv_buf.at[into], kv_sem).start()

        pltpu.make_async_copy(kv_buf.at[into], kv_buf.at[into], kv_sem).wait()
        vt_buf[into] = kv_buf[into, :, HD:].T

    @pl.when(count > 0)
    def _():
        fetch(jnp.int32(0))

        @pl.when(count > 1)
        def _():
            fetch(jnp.int32(1))

        load(items[cap], 0)
        at_slot[0] = 0
        fetched(jnp.int32(0))
        two_stages(q_buf[0], own_buf[0], kv_buf.at[0], s_buf[0], u_buf[0], peak_buf[0], None)

        def one(i, slot):
            held = at_slot[0]
            more = i + 1 < count
            moved = more & (items[cap + jnp.minimum(i + 1, count - 1)] != items[cap + i])
            holds = jnp.where(moved, 1 - held, held)
            at_slot[0] = holds

            @pl.when(more)
            def _():
                fetched(i + 1)

            @pl.when(i + 2 < count)
            def _():
                fetch(i + 2)

            @pl.when(moved)
            def _():
                load(items[cap + i + 1], holds)

            @pl.when(i >= 2)
            def _():
                stored(slot)

            now = (s_buf[slot], u_buf[slot], peak_buf[slot], own_buf[lax.rem(i, 3)], vt_buf.at[held], items[2 * cap + i])
            tiles = two_stages(
                q_buf[1 - slot], own_buf[lax.rem(i + 1, 3)], kv_buf.at[holds],
                s_buf[1 - slot], u_buf[1 - slot], peak_buf[1 - slot], now)
            for g in range(per_kv):
                o_buf[slot, :, g * HD:(g + 1) * HD] = tiles[g]
            store(i, slot)

        def pair(j, _):
            one(2 * j, 0)

            @pl.when(2 * j + 1 < count)
            def _():
                one(2 * j + 1, 1)

            return 0

        lax.fori_loop(0, lax.div(count + 1, 2), pair, 0)
        stored(0)

        @pl.when(count > 1)
        def _():
            stored(1)


def attend(facts, groups, lengths, queries, own, cands, outs, head, per_kv, passes, items, far=None, fresh=False, wait_for=None):
    rlen = queries.shape[1]
    plen = cands[0].shape[-2]
    width = per_kv * HD
    small = [facts, groups, lengths]
    large = ([far] if far is not None else []) + [queries, own] + cands
    operands = small + large + ([] if wait_for is None else [wait_for])
    aliases = {}
    if not fresh:
        aliases = {len(operands): 0}
        operands = operands + [outs[0]]
    cap = groups.shape[0] + (SLOTS if far is not None else 0)
    return pl.pallas_call(
        functools.partial(attend_kernel, passes, len(cands), per_kv, head, far is not None, fresh, wait_for is not None),
        out_shape=[jax.ShapeDtypeStruct(o.shape, o.dtype) for o in outs],
        in_specs=[SMEM] * len(small) + [HBM] * (len(operands) - len(small)),
        out_specs=[HBM] * len(outs),
        input_output_aliases=aliases,
        scratch_shapes=[
            pltpu.SMEM((3 * cap,), jnp.int32),
            pltpu.SMEM((1,), jnp.int32),
            pltpu.VMEM((2, rlen, width), jnp.bfloat16),
            pltpu.VMEM((3, rlen, 2 * HD), jnp.bfloat16),
            pltpu.VMEM((2, plen, 2 * HD), jnp.bfloat16),
            pltpu.VMEM((2, HD, plen), jnp.bfloat16),
            pltpu.VMEM((plen, per_kv * rlen), jnp.float32),
            pltpu.VMEM((plen, per_kv * rlen), jnp.float32),
            pltpu.VMEM((rlen, per_kv * rlen), jnp.float32),
            pltpu.VMEM((rlen, per_kv * rlen), jnp.float32),
            pltpu.VMEM((8, per_kv * rlen), jnp.float32),
            pltpu.VMEM((8, per_kv * rlen), jnp.float32),
            pltpu.VMEM((2, rlen, width), jnp.bfloat16),
            pltpu.VMEM((SLOTS, rlen, HD), jnp.bfloat16),
            pltpu.SemaphoreType.DMA((2,)),
            pltpu.SemaphoreType.DMA((3,)),
            pltpu.SemaphoreType.DMA,
            pltpu.SemaphoreType.DMA((2,)),
        ],
        compiler_params=pltpu.CompilerParams(vmem_limit_bytes=VMEM_BYTES),
        cost_estimate=pl.CostEstimate(flops=items << 20, bytes_accessed=1 << 16, transcendentals=0),
    )(*operands)


def pack_kernel(target, width, facts, groups, lengths, q_ref, own0, own1, out, sem):
    owns = (own0, own1)
    step = width + 2 * HD
    notes = pl.ds(2 * step, HD)
    out[:, :, notes] = jnp.zeros((SLOTS, out.shape[1], HD), out.dtype)

    def each(act, note):
        def look(at, slot):
            hit = groups[at] == facts[target]

            @pl.when(hit)
            def _():
                for head in range(2):
                    part = pl.ds(head * width, width)
                    act(pltpu.make_async_copy(q_ref.at[at, :, part], out.at[slot, :, pl.ds(head * step, width)], sem))
                    act(pltpu.make_async_copy(owns[head].at[at], out.at[slot, :, pl.ds(head * step + width, 2 * HD)], sem))
                if note:
                    length = jnp.full((out.shape[1], HD), lengths[at], jnp.int32)
                    out[slot, :, notes] = length.astype(jnp.float32).astype(out.dtype)

            return slot + hit.astype(jnp.int32)

        lax.fori_loop(0, groups.shape[0], look, jnp.int32(0))

    each(lambda copy: copy.start(), True)
    each(lambda copy: copy.wait(), False)


def pack(facts, target, groups, lengths, queries, own, width):
    shape = jax.ShapeDtypeStruct((SLOTS, queries.shape[1], 2 * (width + 2 * HD) + HD), queries.dtype)
    return pl.pallas_call(
        functools.partial(pack_kernel, target, width),
        out_shape=shape,
        in_specs=[SMEM, SMEM, SMEM, HBM, HBM, HBM],
        out_specs=VMEM,
        scratch_shapes=[pltpu.SemaphoreType.DMA],
        compiler_params=pltpu.CompilerParams(vmem_limit_bytes=1 << 23),
    )(facts, groups, lengths, queries, *own)


def gate_kernel(*refs):
    pass


def gate(value, *others):
    return pl.pallas_call(
        gate_kernel,
        out_shape=jax.ShapeDtypeStruct(value.shape, value.dtype),
        in_specs=[HBM] * (1 + len(others)),
        out_specs=HBM,
        input_output_aliases={0: 0},
    )(value, *others)


def merge_kernel(target, head, facts, groups, got, old, out, sem):
    width = got.shape[2]

    def each(act):
        def look(at, slot):
            hit = groups[at] == facts[target]

            @pl.when(hit)
            def _():
                act(pltpu.make_async_copy(got.at[slot], out.at[at, :, pl.ds(head * width, width)], sem))

            return slot + hit.astype(jnp.int32)

        lax.fori_loop(0, groups.shape[0], look, jnp.int32(0))

    each(lambda copy: copy.start())
    each(lambda copy: copy.wait())


def merge(facts, target, groups, got, out, head):
    return pl.pallas_call(
        functools.partial(merge_kernel, target, head),
        out_shape=jax.ShapeDtypeStruct(out.shape, out.dtype),
        in_specs=[SMEM, SMEM, VMEM, HBM],
        out_specs=HBM,
        input_output_aliases={3: 0},
        scratch_shapes=[pltpu.SemaphoreType.DMA],
        compiler_params=pltpu.CompilerParams(vmem_limit_bytes=1 << 23),
    )(facts, groups, got, out)


def after(value, *others):
    return lax.optimization_barrier((value,) + others)[0]


def gathered(queries, resp_kv, prompt_kv, lengths, group_of, first_head, kv_needed, per_kv):
    out = jax.ShapeDtypeStruct(queries.shape, jnp.bfloat16)
    facts = jnp.zeros((8,), jnp.int32)
    for head in range(kv_needed):
        mine = lax.dynamic_index_in_dim(prompt_kv, first_head + head, 2, keepdims=False)
        own = lax.dynamic_index_in_dim(resp_kv, first_head + head, 2, keepdims=False)
        whole = lax.all_gather(mine, "seq", axis=0, tiled=True)
        [out] = attend(facts, group_of, lengths, queries, own, [whole], [out], head, per_kv, None, 16, fresh=head == 0)
    return out


def relayed(queries, resp_kv, prompt_kv, lengths, group_of, first_head, per_kv):
    me = lax.axis_index("seq")
    width = per_kv * HD
    middle, inward, outward = [(1, 2), (2, 1)], [(0, 1), (3, 2)], [(1, 0), (2, 3)]

    def send(pairs, value):
        return lax.ppermute(value, "seq", pairs)

    def two_heads(start):
        return lambda pairs: jnp.transpose(pairs[:, start:start + 2], (1, 0, 2))

    splits = prompt_kv.shape[2] // 2
    mine = lax.switch(first_head // 2, [two_heads(2 * at) for at in range(splits)], prompt_kv[0])
    across = send(middle, mine)
    near = [send(inward, lax.index_in_dim(mine, head, 0, keepdims=False)) for head in range(2)]
    inner_prompt = send(outward, mine)

    low = me < 2
    is_inner = (me == 1) | (me == 2)
    outer, inner = jnp.where(low, 0, 3), jnp.where(low, 1, 2)
    far_inner, far_outer = jnp.where(low, 2, 1), jnp.where(low, 3, 0)
    facts = jnp.stack([
        me,
        jnp.zeros_like(me),
        jnp.where(is_inner, outer, inner),
        jnp.where(is_inner, 0, 2),
        jnp.where(is_inner, far_inner, -1),
        jnp.ones_like(me),
        jnp.where(is_inner, far_outer, -1),
        jnp.where(is_inner, far_outer, far_inner),
        jnp.where(is_inner, 0, 1),
        jnp.where(is_inner, -1, far_outer),
    ]).astype(jnp.int32)

    own_by_head = after(jnp.transpose(resp_kv, (2, 0, 1, 3)))
    own = [lax.dynamic_index_in_dim(own_by_head, first_head + head, 0, keepdims=False) for head in range(2)]
    packed = pack(facts, 9, group_of, lengths, queries, own, width)
    out = jax.ShapeDtypeStruct(queries.shape, jnp.bfloat16)
    back_shape = jax.ShapeDtypeStruct((SLOTS, queries.shape[1], width), jnp.bfloat16)

    def run(head, cands, outs, passes, items, far=None, fresh=False, wait_for=None):
        return attend(
            facts, group_of, lengths, queries, own[head], cands, outs, head, per_kv, passes, items, far, fresh, wait_for)

    [out] = run(0, [mine], [out], [(False, 0, 1)], 4, fresh=True, wait_for=packed)
    near[0] = gate(near[0], out)
    last = [send(middle, near[0])]
    handed = send(inward, gate(packed, near[0]))
    [out] = run(1, [mine], [out], [(False, 0, 1)], 4)
    near[1] = gate(near[1], out)
    last.append(send(middle, near[1]))
    across = gate(across, out)
    far_inner_prompt = [send(outward, lax.index_in_dim(across, head, 0, keepdims=False)) for head in range(2)]
    for head in range(2):
        [out] = run(head, [near[head], across, inner_prompt], [out], [(False, 2, 3), (False, 4, 5)], 8, wait_for=near[1])
    back = [None, None]
    for head in range(2):
        out, back[head] = run(head, [last[head]], [out, back_shape], [(True, 6, 1)], 4, handed)
        back[head] = send(outward, back[head])
        if head == 1:
            out = merge(facts, 9, group_of, back[0], out, 0)
        [out] = run(head, [last[head], far_inner_prompt[head]], [out], [(False, 7, 8)], 4)
    return merge(facts, 9, group_of, back[1], out, 1)


def shards(queries, resp_kv, prompt_kv, lengths, group_of):
    local_heads = queries.shape[2] // HD
    group = QHEADS // KVH
    kv_needed = max(local_heads // group, 1)
    per_kv = local_heads // kv_needed
    first_head = lax.axis_index("pp") * local_heads // group
    args = (queries, resp_kv, prompt_kv, lengths, group_of, first_head)
    if lax.axis_size("seq") == 4 and kv_needed == 2 and prompt_kv.shape[0] == 1:
        return relayed(*args, per_kv)
    return gathered(*args, kv_needed, per_kv)


def solution(mesh):
    placed = (
        P(("rep", "seq"), None, ("tp", "pp")),
        P(("rep", "seq"), None, "tp", None),
        P(("rep", "seq"), None, "tp", None),
        P(("rep", "seq")),
        P(("rep", "seq")),
    )
    return jax.shard_map(
        shards,
        mesh=mesh,
        in_specs=placed,
        out_specs=P(("rep", "seq"), None, ("tp", "pp")),
        check_vma=False,
    )
```

```python
import functools
import math

import jax
import jax.numpy as jnp
from jax import lax
from jax.experimental import pallas as pl
from jax.experimental.pallas import tpu as pltpu
from jax.sharding import PartitionSpec as P

QHEADS = 64
KVH = 8
HD = 128
LOG2E = math.log2(math.e)
VMEM_BYTES = 56 * 1024 * 1024
SLOTS = 8
HBM = pl.BlockSpec(memory_space=pl.ANY)
SMEM = pl.BlockSpec(memory_space=pltpu.SMEM)
VMEM = pl.BlockSpec(memory_space=pltpu.VMEM)


TN = (((0,), (0,)), ((), ()))
BLOCK = 256


def stacked_heads(q_tile, per_kv):
    return jnp.concatenate([q_tile[:, g * HD:(g + 1) * HD] for g in range(per_kv)], axis=0)


def own_scores(own_tile, q_cols, rlen):
    own = jnp.dot(own_tile[:, :HD], q_cols, preferred_element_type=jnp.float32)
    own_at = lax.broadcasted_iota(jnp.int32, own.shape, 0)
    token_at = lax.broadcasted_iota(jnp.int32, own.shape, 1) % rlen
    return jnp.where(own_at <= token_at, own, -1e30)


def two_stages(after_q, after_own, after_kv, after_s, after_u, after_peak, now):
    rlen = after_own.shape[0]
    per_kv = after_q.shape[1] // HD
    plen = after_kv.shape[0]
    scale = HD ** -0.5 * LOG2E
    q_cols = stacked_heads(after_q, per_kv).T
    own = own_scores(after_own, q_cols, rlen)
    after_u[...] = own
    after_top = jnp.max(own, axis=0, keepdims=True)
    if now is not None:
        s_ref, u_ref, peak_ref, own_tile, vt_ref, length = now
        peak = peak_ref[0:1, :]
        part = jnp.exp2((u_ref[...] - peak) * scale)
        total = jnp.sum(part, axis=0, keepdims=True)
        acc = lax.dot_general(own_tile[:, HD:], part.astype(jnp.bfloat16), TN, preferred_element_type=jnp.float32)
    for at in range(0, plen, BLOCK):
        rows = pl.ds(at, BLOCK)
        fresh = jnp.dot(after_kv[rows, :HD], q_cols, preferred_element_type=jnp.float32)
        after_s[rows, :] = fresh
        after_top = jnp.maximum(after_top, jnp.max(fresh, axis=0, keepdims=True))
        if now is not None:
            part = jnp.exp2((s_ref[rows, :] - peak) * scale)
            total = total + jnp.sum(part, axis=0, keepdims=True)
            acc = acc + jnp.dot(vt_ref[:, rows], part.astype(jnp.bfloat16), preferred_element_type=jnp.float32)
    after_peak[...] = jnp.broadcast_to(after_top, after_peak.shape)
    if now is None:
        return None
    out = (acc * (1.0 / total)).T
    alive = lax.broadcasted_iota(jnp.int32, (rlen, HD), 0) < length
    return [jnp.where(alive, out[g * rlen:(g + 1) * rlen, :], 0.0).astype(jnp.bfloat16) for g in range(per_kv)]


def listed(items, cap, count, groups, lengths, target, source):
    def look(at, n):
        hit = groups[at] == target

        @pl.when(hit)
        def _():
            items[n] = at
            items[cap + n] = source
            items[2 * cap + n] = lengths[at]

        return n + hit.astype(jnp.int32)

    return lax.fori_loop(0, groups.shape[0], look, count)


def attend_kernel(passes, n_cand, per_kv, head, two, fresh, waits, *refs):
    refs = list(refs)
    facts, groups, lengths = refs[:3]
    refs = refs[3:]
    if two:
        x_ref, refs = refs[0], refs[1:]
    q_ref, own_ref = refs[:2]
    cands, refs = refs[2:2 + n_cand], refs[2 + n_cand + waits:]
    n_out = 2 if two else 1
    if not fresh:
        refs = refs[1:]
    outs, token, refs = refs[:n_out], refs[n_out], refs[n_out + 1:]
    items, at_slot, q_buf, own_buf, kv_buf, vt_buf, s0, s1, u0, u1, peak0, peak1, o_buf, info, q_sem, own_sem, kv_sem, o_sem = refs
    s_buf, u_buf, peak_buf = (s0, s1), (u0, u1), (peak0, peak1)
    local = groups.shape[0]
    cap = items.shape[0] // 3
    width = per_kv * HD
    stacked = passes is None

    count = jnp.int32(0)
    if stacked:
        def one_prompt(prompt, n):
            return listed(items, cap, n, groups, lengths, prompt, prompt)

        count = lax.fori_loop(0, cands[0].shape[0], one_prompt, count)
    else:
        for far, target, source in passes:
            if not far:
                count = listed(items, cap, count, groups, lengths, facts[target], facts[source])
                continue
            notes = pltpu.make_async_copy(x_ref.at[:, :, pl.ds(2 * (width + 2 * HD), HD)], info, kv_sem)
            notes.start()
            notes.wait()
            for slot in range(SLOTS):
                length = jnp.max(info[slot, 0:16, :].astype(jnp.float32)).astype(jnp.int32)
                hit = (length > 0) & (facts[target] >= 0)

                @pl.when(hit)
                def _():
                    items[count] = local + slot
                    items[cap + count] = facts[source]
                    items[2 * cap + count] = length

                count = count + hit.astype(jnp.int32)

    token[0] = count

    def each_array(i, act_local, act_far):
        at = items[i]
        if not two:
            act_local(at)
            return

        @pl.when(at < local)
        def _():
            act_local(at)

        @pl.when(at >= local)
        def _():
            act_far(at - local)

    mine = pl.ds(head * width, width)
    first = pl.ds(0, width)
    handed_q = pl.ds(head * (width + 2 * HD), width)
    handed_own = pl.ds(head * (width + 2 * HD) + width, 2 * HD)

    def fetch(i):
        slot, third = lax.rem(i, 2), lax.rem(i, 3)

        def here(at):
            pltpu.make_async_copy(q_ref.at[at, :, mine], q_buf.at[slot], q_sem.at[slot]).start()
            pltpu.make_async_copy(own_ref.at[at], own_buf.at[third], own_sem.at[third]).start()

        def far(at):
            pltpu.make_async_copy(x_ref.at[at, :, handed_q], q_buf.at[slot], q_sem.at[slot]).start()
            pltpu.make_async_copy(x_ref.at[at, :, handed_own], own_buf.at[third], own_sem.at[third]).start()

        each_array(i, here, far)

    def fetched(i):
        slot, third = lax.rem(i, 2), lax.rem(i, 3)
        pltpu.make_async_copy(q_ref.at[0, :, first], q_buf.at[slot], q_sem.at[slot]).wait()
        pltpu.make_async_copy(own_ref.at[0], own_buf.at[third], own_sem.at[third]).wait()

    def store(i, slot):
        def here(at):
            pltpu.make_async_copy(o_buf.at[slot], outs[0].at[at, :, mine], o_sem.at[slot]).start()

        def far(at):
            pltpu.make_async_copy(o_buf.at[slot], outs[1].at[at], o_sem.at[slot]).start()

        each_array(i, here, far)

    def stored(slot):
        pltpu.make_async_copy(o_buf.at[slot], outs[0].at[0, :, first], o_sem.at[slot]).wait()

    def load(source, into):
        if stacked:
            pltpu.make_async_copy(cands[0].at[source], kv_buf.at[into], kv_sem).start()
        else:
            for which in range(n_cand):
                @pl.when(source == which)
                def _():
                    source_ref = cands[which].at[head] if len(cands[which].shape) == 3 else cands[which]
                    pltpu.make_async_copy(source_ref, kv_buf.at[into], kv_sem).start()

        pltpu.make_async_copy(kv_buf.at[into], kv_buf.at[into], kv_sem).wait()
        vt_buf[into] = kv_buf[into, :, HD:].T

    @pl.when(count > 0)
    def _():
        fetch(jnp.int32(0))

        @pl.when(count > 1)
        def _():
            fetch(jnp.int32(1))

        load(items[cap], 0)
        at_slot[0] = 0
        fetched(jnp.int32(0))
        two_stages(q_buf[0], own_buf[0], kv_buf.at[0], s_buf[0], u_buf[0], peak_buf[0], None)

        def one(i, slot):
            held = at_slot[0]
            more = i + 1 < count
            moved = more & (items[cap + jnp.minimum(i + 1, count - 1)] != items[cap + i])
            holds = jnp.where(moved, 1 - held, held)
            at_slot[0] = holds

            @pl.when(more)
            def _():
                fetched(i + 1)

            @pl.when(i + 2 < count)
            def _():
                fetch(i + 2)

            @pl.when(moved)
            def _():
                load(items[cap + i + 1], holds)

            @pl.when(i >= 2)
            def _():
                stored(slot)

            now = (s_buf[slot], u_buf[slot], peak_buf[slot], own_buf[lax.rem(i, 3)], vt_buf.at[held], items[2 * cap + i])
            tiles = two_stages(
                q_buf[1 - slot], own_buf[lax.rem(i + 1, 3)], kv_buf.at[holds],
                s_buf[1 - slot], u_buf[1 - slot], peak_buf[1 - slot], now)
            for g in range(per_kv):
                o_buf[slot, :, g * HD:(g + 1) * HD] = tiles[g]
            store(i, slot)

        def pair(j, _):
            one(2 * j, 0)

            @pl.when(2 * j + 1 < count)
            def _():
                one(2 * j + 1, 1)

            return 0

        lax.fori_loop(0, lax.div(count + 1, 2), pair, 0)
        stored(0)

        @pl.when(count > 1)
        def _():
            stored(1)


def attend(facts, groups, lengths, queries, own, cands, outs, head, per_kv, passes, items, far=None, fresh=False, wait_for=None):
    rlen = queries.shape[1]
    plen = cands[0].shape[-2]
    width = per_kv * HD
    small = [facts, groups, lengths]
    large = ([far] if far is not None else []) + [queries, own] + cands
    operands = small + large + ([] if wait_for is None else [wait_for])
    aliases = {}
    if not fresh:
        aliases = {len(operands): 0}
        operands = operands + [outs[0]]
    cap = groups.shape[0] + (SLOTS if far is not None else 0)
    return pl.pallas_call(
        functools.partial(attend_kernel, passes, len(cands), per_kv, head, far is not None, fresh, wait_for is not None),
        out_shape=[jax.ShapeDtypeStruct(o.shape, o.dtype) for o in outs] + [jax.ShapeDtypeStruct((1,), jnp.int32)],
        in_specs=[SMEM] * len(small) + [HBM] * (len(operands) - len(small)),
        out_specs=[HBM] * len(outs) + [SMEM],
        input_output_aliases=aliases,
        scratch_shapes=[
            pltpu.SMEM((3 * cap,), jnp.int32),
            pltpu.SMEM((1,), jnp.int32),
            pltpu.VMEM((2, rlen, width), jnp.bfloat16),
            pltpu.VMEM((3, rlen, 2 * HD), jnp.bfloat16),
            pltpu.VMEM((2, plen, 2 * HD), jnp.bfloat16),
            pltpu.VMEM((2, HD, plen), jnp.bfloat16),
            pltpu.VMEM((plen, per_kv * rlen), jnp.float32),
            pltpu.VMEM((plen, per_kv * rlen), jnp.float32),
            pltpu.VMEM((rlen, per_kv * rlen), jnp.float32),
            pltpu.VMEM((rlen, per_kv * rlen), jnp.float32),
            pltpu.VMEM((8, per_kv * rlen), jnp.float32),
            pltpu.VMEM((8, per_kv * rlen), jnp.float32),
            pltpu.VMEM((2, rlen, width), jnp.bfloat16),
            pltpu.VMEM((SLOTS, rlen, HD), jnp.bfloat16),
            pltpu.SemaphoreType.DMA((2,)),
            pltpu.SemaphoreType.DMA((3,)),
            pltpu.SemaphoreType.DMA,
            pltpu.SemaphoreType.DMA((2,)),
        ],
        compiler_params=pltpu.CompilerParams(vmem_limit_bytes=VMEM_BYTES),
        cost_estimate=pl.CostEstimate(flops=items << 20, bytes_accessed=1 << 16, transcendentals=0),
    )(*operands)


def pack_kernel(target, width, facts, groups, lengths, q_ref, own0, own1, out, sem):
    owns = (own0, own1)
    step = width + 2 * HD
    notes = pl.ds(2 * step, HD)
    out[:, :, notes] = jnp.zeros((SLOTS, out.shape[1], HD), out.dtype)

    def each(act, note):
        def look(at, slot):
            hit = groups[at] == facts[target]

            @pl.when(hit)
            def _():
                for head in range(2):
                    part = pl.ds(head * width, width)
                    act(pltpu.make_async_copy(q_ref.at[at, :, part], out.at[slot, :, pl.ds(head * step, width)], sem))
                    act(pltpu.make_async_copy(owns[head].at[at], out.at[slot, :, pl.ds(head * step + width, 2 * HD)], sem))
                if note:
                    length = jnp.full((out.shape[1], HD), lengths[at], jnp.int32)
                    out[slot, :, notes] = length.astype(jnp.float32).astype(out.dtype)

            return slot + hit.astype(jnp.int32)

        lax.fori_loop(0, groups.shape[0], look, jnp.int32(0))

    each(lambda copy: copy.start(), True)
    each(lambda copy: copy.wait(), False)


def pack(facts, target, groups, lengths, queries, own, width):
    shape = jax.ShapeDtypeStruct((SLOTS, queries.shape[1], 2 * (width + 2 * HD) + HD), queries.dtype)
    return pl.pallas_call(
        functools.partial(pack_kernel, target, width),
        out_shape=shape,
        in_specs=[SMEM, SMEM, SMEM, HBM, HBM, HBM],
        out_specs=VMEM,
        scratch_shapes=[pltpu.SemaphoreType.DMA],
        compiler_params=pltpu.CompilerParams(vmem_limit_bytes=1 << 23),
    )(facts, groups, lengths, queries, *own)


def gate_kernel(*refs):
    pass


def gate(value, *others):
    return pl.pallas_call(
        gate_kernel,
        out_shape=jax.ShapeDtypeStruct(value.shape, value.dtype),
        in_specs=[HBM] + [SMEM if other.ndim == 1 else HBM for other in others],
        out_specs=HBM,
        input_output_aliases={0: 0},
    )(value, *others)


def cut_kernel(pair, out0, out1, sem):
    copies = [pltpu.make_async_copy(pair.at[head], out, sem.at[head]) for head, out in enumerate((out0, out1))]
    for copy in copies:
        copy.start()
    for copy in copies:
        copy.wait()


def cut(pair):
    shape = jax.ShapeDtypeStruct(pair.shape[1:], pair.dtype)
    return pl.pallas_call(
        cut_kernel,
        out_shape=[shape, shape],
        in_specs=[HBM],
        out_specs=[VMEM, VMEM],
        scratch_shapes=[pltpu.SemaphoreType.DMA((2,))],
        compiler_params=pltpu.CompilerParams(vmem_limit_bytes=1 << 23),
    )(pair)


def merge_kernel(target, head, facts, groups, got, old, out, sem):
    width = got.shape[2]

    def each(act):
        def look(at, slot):
            hit = groups[at] == facts[target]

            @pl.when(hit)
            def _():
                act(pltpu.make_async_copy(got.at[slot], out.at[at, :, pl.ds(head * width, width)], sem))

            return slot + hit.astype(jnp.int32)

        lax.fori_loop(0, groups.shape[0], look, jnp.int32(0))

    each(lambda copy: copy.start())
    each(lambda copy: copy.wait())


def merge(facts, target, groups, got, out, head):
    return pl.pallas_call(
        functools.partial(merge_kernel, target, head),
        out_shape=jax.ShapeDtypeStruct(out.shape, out.dtype),
        in_specs=[SMEM, SMEM, VMEM, HBM],
        out_specs=HBM,
        input_output_aliases={3: 0},
        scratch_shapes=[pltpu.SemaphoreType.DMA],
        compiler_params=pltpu.CompilerParams(vmem_limit_bytes=1 << 23),
    )(facts, groups, got, out)


def after(value, *others):
    return lax.optimization_barrier((value,) + others)[0]


def gathered(queries, resp_kv, prompt_kv, lengths, group_of, first_head, kv_needed, per_kv):
    out = jax.ShapeDtypeStruct(queries.shape, jnp.bfloat16)
    facts = jnp.zeros((8,), jnp.int32)
    for head in range(kv_needed):
        mine = lax.dynamic_index_in_dim(prompt_kv, first_head + head, 2, keepdims=False)
        own = lax.dynamic_index_in_dim(resp_kv, first_head + head, 2, keepdims=False)
        whole = lax.all_gather(mine, "seq", axis=0, tiled=True)
        out, _ = attend(facts, group_of, lengths, queries, own, [whole], [out], head, per_kv, None, 16, fresh=head == 0)
    return out


def relayed(queries, resp_kv, prompt_kv, lengths, group_of, first_head, per_kv):
    me = lax.axis_index("seq")
    width = per_kv * HD
    middle, inward, outward = [(1, 2), (2, 1)], [(0, 1), (3, 2)], [(1, 0), (2, 3)]

    def send(pairs, value):
        return lax.ppermute(value, "seq", pairs)

    def two_heads(start):
        return lambda pairs: jnp.transpose(pairs[:, start:start + 2], (1, 0, 2))

    splits = prompt_kv.shape[2] // 2
    mine = lax.switch(first_head // 2, [two_heads(2 * at) for at in range(splits)], prompt_kv[0])
    across = send(middle, mine)
    inner_prompt = send(outward, mine)
    near = [send(inward, part) for part in cut(mine)]

    low = me < 2
    is_inner = (me == 1) | (me == 2)
    outer, inner = jnp.where(low, 0, 3), jnp.where(low, 1, 2)
    far_inner, far_outer = jnp.where(low, 2, 1), jnp.where(low, 3, 0)
    facts = jnp.stack([
        me,
        jnp.zeros_like(me),
        jnp.where(is_inner, outer, inner),
        jnp.where(is_inner, 0, 2),
        jnp.where(is_inner, far_inner, -1),
        jnp.ones_like(me),
        jnp.where(is_inner, far_outer, -1),
        jnp.where(is_inner, far_outer, far_inner),
        jnp.where(is_inner, 0, 1),
        jnp.where(is_inner, -1, far_outer),
    ]).astype(jnp.int32)

    own_by_head = after(jnp.transpose(resp_kv, (2, 0, 1, 3)))
    own = [lax.dynamic_index_in_dim(own_by_head, first_head + head, 0, keepdims=False) for head in range(2)]
    packed = pack(facts, 9, group_of, lengths, queries, own, width)
    out = jax.ShapeDtypeStruct(queries.shape, jnp.bfloat16)
    back_shape = jax.ShapeDtypeStruct((SLOTS, queries.shape[1], width), jnp.bfloat16)

    def run(head, cands, outs, passes, items, far=None, fresh=False, wait_for=None):
        return attend(
            facts, group_of, lengths, queries, own[head], cands, outs, head, per_kv, passes, items, far, fresh, wait_for)

    out, token = run(0, [mine], [out], [(False, 0, 1)], 4, fresh=True, wait_for=packed)
    near[0] = gate(near[0], token)
    last = [send(middle, near[0])]
    handed = send(inward, gate(packed, near[0]))
    out, token = run(1, [mine], [out], [(False, 0, 1)], 4)
    near[1] = gate(near[1], token)
    last.append(send(middle, near[1]))
    across = gate(across, token, inner_prompt)
    far_inner_prompt = [send(outward, part) for part in cut(across)]
    for head in range(2):
        out, _ = run(head, [near[head], across, inner_prompt], [out], [(False, 2, 3), (False, 4, 5)], 8, wait_for=near[1])
    back = [None, None]
    for head in range(2):
        out, back[head], _ = run(head, [last[head]], [out, back_shape], [(True, 6, 1)], 4, handed)
        back[head] = send(outward, back[head])
        out, _ = run(head, [last[head], far_inner_prompt[head]], [out], [(False, 7, 8)], 4)
    for head in range(2):
        out = merge(facts, 9, group_of, back[head], out, head)
    return out


def shards(queries, resp_kv, prompt_kv, lengths, group_of):
    local_heads = queries.shape[2] // HD
    group = QHEADS // KVH
    kv_needed = max(local_heads // group, 1)
    per_kv = local_heads // kv_needed
    first_head = lax.axis_index("pp") * local_heads // group
    args = (queries, resp_kv, prompt_kv, lengths, group_of, first_head)
    if lax.axis_size("seq") == 4 and kv_needed == 2 and prompt_kv.shape[0] == 1:
        return relayed(*args, per_kv)
    return gathered(*args, kv_needed, per_kv)


def solution(mesh):
    placed = (
        P(("rep", "seq"), None, ("tp", "pp")),
        P(("rep", "seq"), None, "tp", None),
        P(("rep", "seq"), None, "tp", None),
        P(("rep", "seq")),
        P(("rep", "seq")),
    )
    return jax.shard_map(
        shards,
        mesh=mesh,
        in_specs=placed,
        out_specs=P(("rep", "seq"), None, ("tp", "pp")),
        check_vma=False,
    )
```

```python
import functools
import math

import jax
import jax.numpy as jnp
from jax import lax
from jax.experimental import pallas as pl
from jax.experimental.pallas import tpu as pltpu
from jax.sharding import PartitionSpec as P

QHEADS = 64
KVH = 8
HD = 128
LOG2E = math.log2(math.e)
VMEM_BYTES = 56 * 1024 * 1024
SLOTS = 8
HBM = pl.BlockSpec(memory_space=pl.ANY)
SMEM = pl.BlockSpec(memory_space=pltpu.SMEM)
VMEM = pl.BlockSpec(memory_space=pltpu.VMEM)


TN = (((0,), (0,)), ((), ()))
BLOCK = 512
CHUNK = 32


def stacked_heads(q_tile, per_kv):
    return jnp.concatenate([q_tile[:, g * HD:(g + 1) * HD] for g in range(per_kv)], axis=0)


def own_scores(own_tile, q_cols, rlen):
    own = jnp.dot(own_tile[:, :HD], q_cols, preferred_element_type=jnp.float32)
    own_at = lax.broadcasted_iota(jnp.int32, own.shape, 0)
    token_at = lax.broadcasted_iota(jnp.int32, own.shape, 1) % rlen
    return jnp.where(own_at <= token_at, own, -1e30)


def folded(values, op):
    return op(values.reshape(values.shape[0] // 8, 8, values.shape[1]), axis=0)


def two_stages(after_q, after_own, after_kv, after_s, after_u, after_peak, now):
    rlen = after_own.shape[0]
    per_kv = after_q.shape[1] // HD
    plen = after_kv.shape[0]
    scale = HD ** -0.5 * LOG2E
    q_cols = stacked_heads(after_q, per_kv).T
    own = own_scores(after_own, q_cols, rlen)
    after_u[...] = own
    after_top = folded(own, jnp.max)
    if now is not None:
        s_ref, u_ref, peak_ref, own_tile, vt_ref, p_ref, length = now
        peak = peak_ref[...]
        part = jnp.exp2((u_ref[...] - peak[0:1, :]) * scale)
        total = folded(part, jnp.sum)
        acc = lax.dot_general(own_tile[:, HD:], part.astype(jnp.bfloat16), TN, preferred_element_type=jnp.float32)
        spread = jnp.concatenate([peak] * (CHUNK // 8), axis=0)
    for at in range(0, plen, BLOCK):
        rows = pl.ds(at, BLOCK)
        fresh = jnp.dot(after_kv[rows, :HD], q_cols, preferred_element_type=jnp.float32)
        after_s[rows, :] = fresh
        after_top = jnp.maximum(after_top, folded(fresh, jnp.max))
        if now is not None:
            for chunk in range(at, at + BLOCK, CHUNK):
                part = jnp.exp2((s_ref[chunk:chunk + CHUNK, :] - spread) * scale)
                total = total + folded(part, jnp.sum)
                p_ref[chunk:chunk + CHUNK, :] = part.astype(jnp.bfloat16)
            acc = acc + jnp.dot(vt_ref[:, rows], p_ref[rows, :], preferred_element_type=jnp.float32)
    after_peak[...] = jnp.broadcast_to(jnp.max(after_top, axis=0, keepdims=True), after_peak.shape)
    if now is None:
        return None
    out = (acc * (1.0 / jnp.sum(total, axis=0, keepdims=True))).T
    alive = lax.broadcasted_iota(jnp.int32, (rlen, HD), 0) < length
    return [jnp.where(alive, out[g * rlen:(g + 1) * rlen, :], 0.0).astype(jnp.bfloat16) for g in range(per_kv)]


def listed(items, cap, count, groups, lengths, target, source):
    def look(at, n):
        hit = groups[at] == target

        @pl.when(hit)
        def _():
            items[n] = at
            items[cap + n] = source
            items[2 * cap + n] = lengths[at]

        return n + hit.astype(jnp.int32)

    return lax.fori_loop(0, groups.shape[0], look, count)


def attend_kernel(passes, n_cand, per_kv, head, two, fresh, waits, *refs):
    refs = list(refs)
    facts, groups, lengths = refs[:3]
    refs = refs[3:]
    if two:
        x_ref, refs = refs[0], refs[1:]
    q_ref, own_ref = refs[:2]
    cands, refs = refs[2:2 + n_cand], refs[2 + n_cand + waits:]
    n_out = 2 if two else 1
    if not fresh:
        refs = refs[1:]
    outs, token, refs = refs[:n_out], refs[n_out], refs[n_out + 1:]
    items, at_slot, q_buf, own_buf, kv_buf, vt_buf, s0, s1, u0, u1, peak0, peak1, p_buf, o_buf, info, q_sem, own_sem, kv_sem, o_sem = refs
    s_buf, u_buf, peak_buf = (s0, s1), (u0, u1), (peak0, peak1)
    local = groups.shape[0]
    cap = items.shape[0] // 3
    width = per_kv * HD
    stacked = passes is None

    count = jnp.int32(0)
    if stacked:
        def one_prompt(prompt, n):
            return listed(items, cap, n, groups, lengths, prompt, prompt)

        count = lax.fori_loop(0, cands[0].shape[0], one_prompt, count)
    else:
        for far, target, source in passes:
            if not far:
                count = listed(items, cap, count, groups, lengths, facts[target], facts[source])
                continue
            notes = pltpu.make_async_copy(x_ref.at[:, :, pl.ds(width + 2 * HD, HD)], info, kv_sem)
            notes.start()
            notes.wait()
            for slot in range(SLOTS):
                length = jnp.max(info[slot, 0:16, :].astype(jnp.float32)).astype(jnp.int32)
                hit = (length > 0) & (facts[target] >= 0)

                @pl.when(hit)
                def _():
                    items[count] = local + slot
                    items[cap + count] = facts[source]
                    items[2 * cap + count] = length

                count = count + hit.astype(jnp.int32)

    token[0] = count

    def each_array(i, act_local, act_far):
        at = items[i]
        if not two:
            act_local(at)
            return

        @pl.when(at < local)
        def _():
            act_local(at)

        @pl.when(at >= local)
        def _():
            act_far(at - local)

    mine = pl.ds(head * width, width)
    first = pl.ds(0, width)
    handed_own = pl.ds(width, 2 * HD)

    def fetch(i):
        slot, third = lax.rem(i, 2), lax.rem(i, 3)

        def here(at):
            pltpu.make_async_copy(q_ref.at[at, :, mine], q_buf.at[slot], q_sem.at[slot]).start()
            pltpu.make_async_copy(own_ref.at[at], own_buf.at[third], own_sem.at[third]).start()

        def far(at):
            pltpu.make_async_copy(x_ref.at[at, :, first], q_buf.at[slot], q_sem.at[slot]).start()
            pltpu.make_async_copy(x_ref.at[at, :, handed_own], own_buf.at[third], own_sem.at[third]).start()

        each_array(i, here, far)

    def fetched(i):
        slot, third = lax.rem(i, 2), lax.rem(i, 3)
        pltpu.make_async_copy(q_ref.at[0, :, first], q_buf.at[slot], q_sem.at[slot]).wait()
        pltpu.make_async_copy(own_ref.at[0], own_buf.at[third], own_sem.at[third]).wait()

    def store(i, slot):
        def here(at):
            pltpu.make_async_copy(o_buf.at[slot], outs[0].at[at, :, mine], o_sem.at[slot]).start()

        def far(at):
            pltpu.make_async_copy(o_buf.at[slot], outs[1].at[at], o_sem.at[slot]).start()

        each_array(i, here, far)

    def stored(slot):
        pltpu.make_async_copy(o_buf.at[slot], outs[0].at[0, :, first], o_sem.at[slot]).wait()

    def load(source, into):
        if stacked:
            pltpu.make_async_copy(cands[0].at[source], kv_buf.at[into], kv_sem).start()
        else:
            for which in range(n_cand):
                @pl.when(source == which)
                def _():
                    source_ref = cands[which].at[head] if len(cands[which].shape) == 3 else cands[which]
                    pltpu.make_async_copy(source_ref, kv_buf.at[into], kv_sem).start()

        pltpu.make_async_copy(kv_buf.at[into], kv_buf.at[into], kv_sem).wait()
        vt_buf[into] = kv_buf[into, :, HD:].T

    @pl.when(count > 0)
    def _():
        fetch(jnp.int32(0))

        @pl.when(count > 1)
        def _():
            fetch(jnp.int32(1))

        load(items[cap], 0)
        at_slot[0] = 0
        fetched(jnp.int32(0))
        two_stages(q_buf[0], own_buf[0], kv_buf.at[0], s_buf[0], u_buf[0], peak_buf[0], None)

        def one(i, slot):
            held = at_slot[0]
            more = i + 1 < count
            moved = more & (items[cap + jnp.minimum(i + 1, count - 1)] != items[cap + i])
            holds = jnp.where(moved, 1 - held, held)
            at_slot[0] = holds

            @pl.when(more)
            def _():
                fetched(i + 1)

            @pl.when(i + 2 < count)
            def _():
                fetch(i + 2)

            @pl.when(moved)
            def _():
                load(items[cap + i + 1], holds)

            @pl.when(i >= 2)
            def _():
                stored(slot)

            now = (s_buf[slot], u_buf[slot], peak_buf[slot], own_buf[lax.rem(i, 3)], vt_buf.at[held], p_buf, items[2 * cap + i])
            tiles = two_stages(
                q_buf[1 - slot], own_buf[lax.rem(i + 1, 3)], kv_buf.at[holds],
                s_buf[1 - slot], u_buf[1 - slot], peak_buf[1 - slot], now)
            for g in range(per_kv):
                o_buf[slot, :, g * HD:(g + 1) * HD] = tiles[g]
            store(i, slot)

        def pair(j, _):
            one(2 * j, 0)

            @pl.when(2 * j + 1 < count)
            def _():
                one(2 * j + 1, 1)

            return 0

        lax.fori_loop(0, lax.div(count + 1, 2), pair, 0)
        stored(0)

        @pl.when(count > 1)
        def _():
            stored(1)


def attend(facts, groups, lengths, queries, own, cands, outs, head, per_kv, passes, items, far=None, fresh=False, wait_for=None):
    rlen = queries.shape[1]
    plen = cands[0].shape[-2]
    width = per_kv * HD
    small = [facts, groups, lengths]
    large = ([far] if far is not None else []) + [queries, own] + cands
    operands = small + large + ([] if wait_for is None else [wait_for])
    aliases = {}
    if not fresh:
        aliases = {len(operands): 0}
        operands = operands + [outs[0]]
    cap = groups.shape[0] + (SLOTS if far is not None else 0)
    return pl.pallas_call(
        functools.partial(attend_kernel, passes, len(cands), per_kv, head, far is not None, fresh, wait_for is not None),
        out_shape=[jax.ShapeDtypeStruct(o.shape, o.dtype) for o in outs] + [jax.ShapeDtypeStruct((1,), jnp.int32)],
        in_specs=[SMEM] * len(small) + [HBM] * (len(operands) - len(small)),
        out_specs=[HBM] * len(outs) + [SMEM],
        input_output_aliases=aliases,
        scratch_shapes=[
            pltpu.SMEM((3 * cap,), jnp.int32),
            pltpu.SMEM((1,), jnp.int32),
            pltpu.VMEM((2, rlen, width), jnp.bfloat16),
            pltpu.VMEM((3, rlen, 2 * HD), jnp.bfloat16),
            pltpu.VMEM((2, plen, 2 * HD), jnp.bfloat16),
            pltpu.VMEM((2, HD, plen), jnp.bfloat16),
            pltpu.VMEM((plen, per_kv * rlen), jnp.float32),
            pltpu.VMEM((plen, per_kv * rlen), jnp.float32),
            pltpu.VMEM((rlen, per_kv * rlen), jnp.float32),
            pltpu.VMEM((rlen, per_kv * rlen), jnp.float32),
            pltpu.VMEM((8, per_kv * rlen), jnp.float32),
            pltpu.VMEM((8, per_kv * rlen), jnp.float32),
            pltpu.VMEM((plen, per_kv * rlen), jnp.bfloat16),
            pltpu.VMEM((2, rlen, width), jnp.bfloat16),
            pltpu.VMEM((SLOTS, rlen, HD), jnp.bfloat16),
            pltpu.SemaphoreType.DMA((2,)),
            pltpu.SemaphoreType.DMA((3,)),
            pltpu.SemaphoreType.DMA,
            pltpu.SemaphoreType.DMA((2,)),
        ],
        compiler_params=pltpu.CompilerParams(vmem_limit_bytes=VMEM_BYTES),
        cost_estimate=pl.CostEstimate(flops=items << 20, bytes_accessed=1 << 16, transcendentals=0),
    )(*operands)


def pack_kernel(target, width, facts, groups, lengths, q_ref, own0, own1, out0, out1, sem):
    owns, outs = (own0, own1), (out0, out1)
    notes = pl.ds(width + 2 * HD, HD)
    rlen = out0.shape[1]
    for out in outs:
        out[:, :, notes] = jnp.zeros((SLOTS, rlen, HD), out.dtype)

    def each(act, note):
        def look(at, slot):
            hit = groups[at] == facts[target]

            @pl.when(hit)
            def _():
                for head, out in enumerate(outs):
                    part = pl.ds(head * width, width)
                    act(pltpu.make_async_copy(q_ref.at[at, :, part], out.at[slot, :, pl.ds(0, width)], sem))
                    act(pltpu.make_async_copy(owns[head].at[at], out.at[slot, :, pl.ds(width, 2 * HD)], sem))
                    if note:
                        length = jnp.full((rlen, HD), lengths[at], jnp.int32)
                        out[slot, :, notes] = length.astype(jnp.float32).astype(out.dtype)

            return slot + hit.astype(jnp.int32)

        lax.fori_loop(0, groups.shape[0], look, jnp.int32(0))

    each(lambda copy: copy.start(), True)
    each(lambda copy: copy.wait(), False)


def pack(facts, target, groups, lengths, queries, own, width):
    shape = jax.ShapeDtypeStruct((SLOTS, queries.shape[1], width + 3 * HD), queries.dtype)
    return pl.pallas_call(
        functools.partial(pack_kernel, target, width),
        out_shape=[shape, shape],
        in_specs=[SMEM, SMEM, SMEM, HBM, HBM, HBM],
        out_specs=[VMEM, VMEM],
        scratch_shapes=[pltpu.SemaphoreType.DMA],
        compiler_params=pltpu.CompilerParams(vmem_limit_bytes=1 << 23),
    )(facts, groups, lengths, queries, *own)


def gate_kernel(*refs):
    pass


def gate(value, *others):
    return pl.pallas_call(
        gate_kernel,
        out_shape=jax.ShapeDtypeStruct(value.shape, value.dtype),
        in_specs=[HBM] + [SMEM if other.ndim == 1 else HBM for other in others],
        out_specs=HBM,
        input_output_aliases={0: 0},
    )(value, *others)


def cut_kernel(pair, out0, out1, sem):
    copies = [pltpu.make_async_copy(pair.at[head], out, sem.at[head]) for head, out in enumerate((out0, out1))]
    for copy in copies:
        copy.start()
    for copy in copies:
        copy.wait()


def cut(pair):
    shape = jax.ShapeDtypeStruct(pair.shape[1:], pair.dtype)
    return pl.pallas_call(
        cut_kernel,
        out_shape=[shape, shape],
        in_specs=[HBM],
        out_specs=[VMEM, VMEM],
        scratch_shapes=[pltpu.SemaphoreType.DMA((2,))],
        compiler_params=pltpu.CompilerParams(vmem_limit_bytes=1 << 23),
    )(pair)


def merge_kernel(target, head, facts, groups, got, old, out, sem):
    width = got.shape[2]

    def each(act):
        def look(at, slot):
            hit = groups[at] == facts[target]

            @pl.when(hit)
            def _():
                act(pltpu.make_async_copy(got.at[slot], out.at[at, :, pl.ds(head * width, width)], sem))

            return slot + hit.astype(jnp.int32)

        lax.fori_loop(0, groups.shape[0], look, jnp.int32(0))

    each(lambda copy: copy.start())
    each(lambda copy: copy.wait())


def merge(facts, target, groups, got, out, head):
    return pl.pallas_call(
        functools.partial(merge_kernel, target, head),
        out_shape=jax.ShapeDtypeStruct(out.shape, out.dtype),
        in_specs=[SMEM, SMEM, VMEM, HBM],
        out_specs=HBM,
        input_output_aliases={3: 0},
        scratch_shapes=[pltpu.SemaphoreType.DMA],
        compiler_params=pltpu.CompilerParams(vmem_limit_bytes=1 << 23),
    )(facts, groups, got, out)


def after(value, *others):
    return lax.optimization_barrier((value,) + others)[0]


def gathered(queries, resp_kv, prompt_kv, lengths, group_of, first_head, kv_needed, per_kv):
    out = jax.ShapeDtypeStruct(queries.shape, jnp.bfloat16)
    facts = jnp.zeros((8,), jnp.int32)
    for head in range(kv_needed):
        mine = lax.dynamic_index_in_dim(prompt_kv, first_head + head, 2, keepdims=False)
        own = lax.dynamic_index_in_dim(resp_kv, first_head + head, 2, keepdims=False)
        whole = lax.all_gather(mine, "seq", axis=0, tiled=True)
        out, _ = attend(facts, group_of, lengths, queries, own, [whole], [out], head, per_kv, None, 16, fresh=head == 0)
    return out


def relayed(queries, resp_kv, prompt_kv, lengths, group_of, first_head, per_kv):
    me = lax.axis_index("seq")
    width = per_kv * HD
    middle, inward, outward = [(1, 2), (2, 1)], [(0, 1), (3, 2)], [(1, 0), (2, 3)]

    def send(pairs, value):
        return lax.ppermute(value, "seq", pairs)

    def two_heads(start):
        return lambda pairs: jnp.transpose(pairs[:, start:start + 2], (1, 0, 2))

    splits = prompt_kv.shape[2] // 2
    mine = lax.switch(first_head // 2, [two_heads(2 * at) for at in range(splits)], prompt_kv[0])
    across = send(middle, mine)
    inner_prompt = send(outward, mine)
    near = [send(inward, part) for part in cut(mine)]

    low = me < 2
    is_inner = (me == 1) | (me == 2)
    outer, inner = jnp.where(low, 0, 3), jnp.where(low, 1, 2)
    far_inner, far_outer = jnp.where(low, 2, 1), jnp.where(low, 3, 0)
    facts = jnp.stack([
        me,
        jnp.zeros_like(me),
        jnp.where(is_inner, outer, inner),
        jnp.where(is_inner, 0, 2),
        jnp.where(is_inner, far_inner, -1),
        jnp.ones_like(me),
        jnp.where(is_inner, far_outer, -1),
        jnp.where(is_inner, far_outer, far_inner),
        jnp.where(is_inner, 0, 1),
        jnp.where(is_inner, -1, far_outer),
    ]).astype(jnp.int32)

    own_by_head = after(jnp.transpose(resp_kv, (2, 0, 1, 3)))
    own = [lax.dynamic_index_in_dim(own_by_head, first_head + head, 0, keepdims=False) for head in range(2)]
    packed = pack(facts, 9, group_of, lengths, queries, own, width)
    out = jax.ShapeDtypeStruct(queries.shape, jnp.bfloat16)
    back_shape = jax.ShapeDtypeStruct((SLOTS, queries.shape[1], width), jnp.bfloat16)

    def run(head, cands, outs, passes, items, far=None, fresh=False, wait_for=None):
        return attend(
            facts, group_of, lengths, queries, own[head], cands, outs, head, per_kv, passes, items, far, fresh, wait_for)

    out, token = run(0, [mine], [out], [(False, 0, 1)], 4, fresh=True, wait_for=packed[0])
    near[0] = gate(near[0], token)
    last = [send(middle, near[0])]
    handed = [send(inward, gate(part, near[0])) for part in packed]
    out, token = run(1, [mine], [out], [(False, 0, 1)], 4)
    near[1] = gate(near[1], token)
    last.append(send(middle, near[1]))
    across = gate(across, token, inner_prompt)
    parts = cut(across)
    far_inner_prompt = [send(outward, parts[0])]
    for head in range(2):
        out, token = run(head, [near[head], across, inner_prompt], [out], [(False, 2, 3), (False, 4, 5)], 8, wait_for=near[1])
        if head == 0:
            far_inner_prompt.append(send(outward, gate(parts[1], token)))
    back = [None, None]
    for head in range(2):
        out, back[head], _ = run(head, [last[head]], [out, back_shape], [(True, 6, 1)], 4, handed[head])
        back[head] = send(outward, back[head])
        out, _ = run(head, [last[head], far_inner_prompt[head]], [out], [(False, 7, 8)], 4)
    for head in range(2):
        out = merge(facts, 9, group_of, back[head], out, head)
    return out


def shards(queries, resp_kv, prompt_kv, lengths, group_of):
    local_heads = queries.shape[2] // HD
    group = QHEADS // KVH
    kv_needed = max(local_heads // group, 1)
    per_kv = local_heads // kv_needed
    first_head = lax.axis_index("pp") * local_heads // group
    args = (queries, resp_kv, prompt_kv, lengths, group_of, first_head)
    if lax.axis_size("seq") == 4 and kv_needed == 2 and prompt_kv.shape[0] == 1:
        return relayed(*args, per_kv)
    return gathered(*args, kv_needed, per_kv)


def solution(mesh):
    placed = (
        P(("rep", "seq"), None, ("tp", "pp")),
        P(("rep", "seq"), None, "tp", None),
        P(("rep", "seq"), None, "tp", None),
        P(("rep", "seq")),
        P(("rep", "seq")),
    )
    return jax.shard_map(
        shards,
        mesh=mesh,
        in_specs=placed,
        out_specs=P(("rep", "seq"), None, ("tp", "pp")),
        check_vma=False,
    )
```

```python
import functools
import math

import jax
import jax.numpy as jnp
from jax import lax
from jax.experimental import pallas as pl
from jax.experimental.pallas import tpu as pltpu
from jax.sharding import PartitionSpec as P

QHEADS = 64
KVH = 8
HD = 128
LOG2E = math.log2(math.e)
VMEM_BYTES = 56 * 1024 * 1024
SLOTS = 8
HBM = pl.BlockSpec(memory_space=pl.ANY)
SMEM = pl.BlockSpec(memory_space=pltpu.SMEM)
VMEM = pl.BlockSpec(memory_space=pltpu.VMEM)


TN = (((0,), (0,)), ((), ()))
BLOCK = 512
CHUNK = 32


def stacked_heads(q_tile, per_kv):
    return jnp.concatenate([q_tile[:, g * HD:(g + 1) * HD] for g in range(per_kv)], axis=0)


def own_scores(own_tile, q_cols, rlen):
    own = jnp.dot(own_tile[:, :HD], q_cols, preferred_element_type=jnp.float32)
    own_at = lax.broadcasted_iota(jnp.int32, own.shape, 0)
    token_at = lax.broadcasted_iota(jnp.int32, own.shape, 1) % rlen
    return jnp.where(own_at <= token_at, own, -1e30)


def folded(values, op):
    return op(values.reshape(values.shape[0] // 8, 8, values.shape[1]), axis=0)


def turn(q_tile, per_kv, out_ref):
    out_ref[...] = stacked_heads(q_tile, per_kv).T


def finish(acc_ref, total_ref, length, per_kv, out_ref):
    out = (acc_ref[...] * (1.0 / total_ref[0:1, :])).T
    rlen = out_ref.shape[0]
    alive = lax.broadcasted_iota(jnp.int32, (rlen, HD), 0) < length
    for g in range(per_kv):
        part = jnp.where(alive, out[g * rlen:(g + 1) * rlen, :], 0.0)
        out_ref[:, g * HD:(g + 1) * HD] = part.astype(out_ref.dtype)


def scores_and_mix(q_cols, after_own, after_kv, after_s, after_u, after_peak, now):
    plen = after_kv.shape[0]
    scale = HD ** -0.5 * LOG2E
    own = own_scores(after_own, q_cols, after_own.shape[0])
    after_u[...] = own
    after_top = folded(own, jnp.max)
    if now is not None:
        s_ref, u_ref, peak_ref, own_tile, vt_ref, p_ref, acc_ref, total_ref = now
        peak = peak_ref[...]
        part = jnp.exp2((u_ref[...] - peak[0:1, :]) * scale)
        total = folded(part, jnp.sum)
        acc = lax.dot_general(own_tile[:, HD:], part.astype(jnp.bfloat16), TN, preferred_element_type=jnp.float32)
        spread = jnp.concatenate([peak] * (CHUNK // 8), axis=0)
    for at in range(0, plen, BLOCK):
        rows = pl.ds(at, BLOCK)
        fresh = jnp.dot(after_kv[rows, :HD], q_cols, preferred_element_type=jnp.float32)
        after_s[rows, :] = fresh
        after_top = jnp.maximum(after_top, folded(fresh, jnp.max))
        if now is not None:
            for chunk in range(at, at + BLOCK, CHUNK):
                part = jnp.exp2((s_ref[chunk:chunk + CHUNK, :] - spread) * scale)
                total = total + folded(part, jnp.sum)
                p_ref[chunk:chunk + CHUNK, :] = part.astype(jnp.bfloat16)
            acc = acc + jnp.dot(vt_ref[:, rows], p_ref[rows, :], preferred_element_type=jnp.float32)
    after_peak[...] = jnp.broadcast_to(jnp.max(after_top, axis=0, keepdims=True), after_peak.shape)
    if now is not None:
        acc_ref[...] = acc
        total_ref[...] = jnp.broadcast_to(jnp.sum(total, axis=0, keepdims=True), total_ref.shape)


def listed(items, cap, count, groups, lengths, target, source):
    def look(at, n):
        hit = groups[at] == target

        @pl.when(hit)
        def _():
            items[n] = at
            items[cap + n] = source
            items[2 * cap + n] = lengths[at]

        return n + hit.astype(jnp.int32)

    return lax.fori_loop(0, groups.shape[0], look, count)


def attend_kernel(passes, n_cand, per_kv, head, two, fresh, waits, *refs):
    refs = list(refs)
    facts, groups, lengths = refs[:3]
    refs = refs[3:]
    if two:
        x_ref, refs = refs[0], refs[1:]
    q_ref, own_ref = refs[:2]
    cands, refs = refs[2:2 + n_cand], refs[2 + n_cand + waits:]
    n_out = 2 if two else 1
    if not fresh:
        refs = refs[1:]
    outs, token, refs = refs[:n_out], refs[n_out], refs[n_out + 1:]
    items, at_slot, q_buf, own_buf, kv_buf, vt_buf, s0, s1, u0, u1, peak0, peak1, turned0, turned1, acc0, acc1, total0, total1, p_buf, o0, o1, info, q_sem, own_sem, kv_sem, o_sem = refs
    s_buf, u_buf, peak_buf, o_buf = (s0, s1), (u0, u1), (peak0, peak1), (o0, o1)
    turned, acc_buf, total_buf = (turned0, turned1), (acc0, acc1), (total0, total1)
    local = groups.shape[0]
    cap = items.shape[0] // 3
    width = per_kv * HD
    stacked = passes is None

    count = jnp.int32(0)
    if stacked:
        def one_prompt(prompt, n):
            return listed(items, cap, n, groups, lengths, prompt, prompt)

        count = lax.fori_loop(0, cands[0].shape[0], one_prompt, count)
    else:
        for far, target, source in passes:
            if not far:
                count = listed(items, cap, count, groups, lengths, facts[target], facts[source])
                continue
            notes = pltpu.make_async_copy(x_ref.at[0, :, pl.ds(width + 2 * HD, HD)], info, kv_sem)
            notes.start()
            notes.wait()
            handed = jnp.max(info[0:16, :].astype(jnp.float32)).astype(jnp.int32)
            handed = jnp.where(facts[target] >= 0, jnp.minimum(handed, SLOTS), 0)

            def take(slot, n):
                items[n] = local + slot
                items[cap + n] = facts[source]
                items[2 * cap + n] = q_buf.shape[1]
                return n + 1

            count = lax.fori_loop(0, handed, take, count)

    token[0] = count

    def each_array(i, act_local, act_far):
        at = items[i]
        if not two:
            act_local(at)
            return

        @pl.when(at < local)
        def _():
            act_local(at)

        @pl.when(at >= local)
        def _():
            act_far(at - local)

    mine = pl.ds(head * width, width)
    first = pl.ds(0, width)
    handed_own = pl.ds(width, 2 * HD)

    def fetch(i):
        slot, fourth = lax.rem(i, 2), lax.rem(i, 4)

        def here(at):
            pltpu.make_async_copy(q_ref.at[at, :, mine], q_buf.at[slot], q_sem.at[slot]).start()
            pltpu.make_async_copy(own_ref.at[at], own_buf.at[fourth], own_sem.at[fourth]).start()

        def far(at):
            pltpu.make_async_copy(x_ref.at[at, :, first], q_buf.at[slot], q_sem.at[slot]).start()
            pltpu.make_async_copy(x_ref.at[at, :, handed_own], own_buf.at[fourth], own_sem.at[fourth]).start()

        each_array(i, here, far)

    def fetched(i):
        slot, fourth = lax.rem(i, 2), lax.rem(i, 4)
        pltpu.make_async_copy(q_ref.at[0, :, first], q_buf.at[slot], q_sem.at[slot]).wait()
        pltpu.make_async_copy(own_ref.at[0], own_buf.at[fourth], own_sem.at[fourth]).wait()

    def store(i, slot):
        def here(at):
            pltpu.make_async_copy(o_buf[slot], outs[0].at[at, :, mine], o_sem.at[slot]).start()

        def far(at):
            pltpu.make_async_copy(o_buf[slot], outs[1].at[at], o_sem.at[slot]).start()

        each_array(i, here, far)

    def stored(slot):
        pltpu.make_async_copy(o_buf[slot], outs[0].at[0, :, first], o_sem.at[slot]).wait()

    def load(source, into):
        if stacked:
            pltpu.make_async_copy(cands[0].at[source], kv_buf.at[into], kv_sem).start()
        else:
            for which in range(n_cand):
                @pl.when(source == which)
                def _():
                    source_ref = cands[which].at[head] if len(cands[which].shape) == 3 else cands[which]
                    pltpu.make_async_copy(source_ref, kv_buf.at[into], kv_sem).start()

        pltpu.make_async_copy(kv_buf.at[into], kv_buf.at[into], kv_sem).wait()
        vt_buf[into] = kv_buf[into, :, HD:].T

    @pl.when(count > 0)
    def _():
        fetch(jnp.int32(0))

        @pl.when(count > 1)
        def _():
            fetch(jnp.int32(1))

        load(items[cap], 0)
        at_slot[0] = 0
        fetched(jnp.int32(0))
        turn(q_buf[0], per_kv, turned[0])

        @pl.when(count > 2)
        def _():
            fetch(jnp.int32(2))

        @pl.when(count > 1)
        def _():
            fetched(jnp.int32(1))

        turn(q_buf[1], per_kv, turned[1])
        scores_and_mix(turned[0][...], own_buf[0], kv_buf.at[0], s_buf[0], u_buf[0], peak_buf[0], None)

        def one(i, slot):
            other = 1 - slot
            held = at_slot[0]
            more = i + 1 < count
            moved = more & (items[cap + jnp.minimum(i + 1, count - 1)] != items[cap + i])
            holds = jnp.where(moved, 1 - held, held)
            at_slot[0] = holds

            @pl.when(i + 2 < count)
            def _():
                fetched(i + 2)

            @pl.when(i + 3 < count)
            def _():
                fetch(i + 3)

            @pl.when(moved)
            def _():
                load(items[cap + i + 1], holds)

            @pl.when(i >= 3)
            def _():
                stored(other)

            now = (
                s_buf[slot], u_buf[slot], peak_buf[slot], own_buf[lax.rem(i, 4)], vt_buf.at[held], p_buf,
                acc_buf[slot], total_buf[slot])
            scores_and_mix(
                turned[other][...], own_buf[lax.rem(i + 1, 4)], kv_buf.at[holds],
                s_buf[other], u_buf[other], peak_buf[other], now)
            turn(q_buf[slot], per_kv, turned[slot])
            finish(acc_buf[other], total_buf[other], items[2 * cap + jnp.maximum(i - 1, 0)], per_kv, o_buf[other])

            @pl.when(i >= 1)
            def _():
                store(i - 1, other)

        def pair(j, _):
            one(2 * j, 0)

            @pl.when(2 * j + 1 < count)
            def _():
                one(2 * j + 1, 1)

            return 0

        lax.fori_loop(0, lax.div(count + 1, 2), pair, 0)
        final = count - 1
        for slot in range(2):
            @pl.when(lax.rem(final, 2) == slot)
            def _():
                @pl.when(final >= 2)
                def _():
                    stored(slot)

                finish(acc_buf[slot], total_buf[slot], items[2 * cap + final], per_kv, o_buf[slot])
                store(final, slot)

        stored(0)

        @pl.when(count > 1)
        def _():
            stored(1)


def attend(facts, groups, lengths, queries, own, cands, outs, head, per_kv, passes, items, far=None, fresh=False, wait_for=None):
    rlen = queries.shape[1]
    plen = cands[0].shape[-2]
    width = per_kv * HD
    small = [facts, groups, lengths]
    large = ([far] if far is not None else []) + [queries, own] + cands
    operands = small + large + ([] if wait_for is None else [wait_for])
    aliases = {}
    if not fresh:
        aliases = {len(operands): 0}
        operands = operands + [outs[0]]
    cap = groups.shape[0] + (SLOTS if far is not None else 0)
    return pl.pallas_call(
        functools.partial(attend_kernel, passes, len(cands), per_kv, head, far is not None, fresh, wait_for is not None),
        out_shape=[jax.ShapeDtypeStruct(o.shape, o.dtype) for o in outs] + [jax.ShapeDtypeStruct((1,), jnp.int32)],
        in_specs=[SMEM] * len(small) + [HBM] * (len(operands) - len(small)),
        out_specs=[HBM] * len(outs) + [SMEM],
        input_output_aliases=aliases,
        scratch_shapes=[
            pltpu.SMEM((3 * cap,), jnp.int32),
            pltpu.SMEM((1,), jnp.int32),
            pltpu.VMEM((2, rlen, width), jnp.bfloat16),
            pltpu.VMEM((4, rlen, 2 * HD), jnp.bfloat16),
            pltpu.VMEM((2, plen, 2 * HD), jnp.bfloat16),
            pltpu.VMEM((2, HD, plen), jnp.bfloat16),
            pltpu.VMEM((plen, per_kv * rlen), jnp.float32),
            pltpu.VMEM((plen, per_kv * rlen), jnp.float32),
            pltpu.VMEM((rlen, per_kv * rlen), jnp.float32),
            pltpu.VMEM((rlen, per_kv * rlen), jnp.float32),
            pltpu.VMEM((8, per_kv * rlen), jnp.float32),
            pltpu.VMEM((8, per_kv * rlen), jnp.float32),
            pltpu.VMEM((HD, per_kv * rlen), jnp.bfloat16),
            pltpu.VMEM((HD, per_kv * rlen), jnp.bfloat16),
            pltpu.VMEM((HD, per_kv * rlen), jnp.float32),
            pltpu.VMEM((HD, per_kv * rlen), jnp.float32),
            pltpu.VMEM((8, per_kv * rlen), jnp.float32),
            pltpu.VMEM((8, per_kv * rlen), jnp.float32),
            pltpu.VMEM((plen, per_kv * rlen), jnp.bfloat16),
            pltpu.VMEM((rlen, width), jnp.bfloat16),
            pltpu.VMEM((rlen, width), jnp.bfloat16),
            pltpu.VMEM((rlen, HD), jnp.bfloat16),
            pltpu.SemaphoreType.DMA((2,)),
            pltpu.SemaphoreType.DMA((4,)),
            pltpu.SemaphoreType.DMA,
            pltpu.SemaphoreType.DMA((2,)),
        ],
        compiler_params=pltpu.CompilerParams(vmem_limit_bytes=VMEM_BYTES),
        cost_estimate=pl.CostEstimate(flops=items << 20, bytes_accessed=1 << 16, transcendentals=0),
    )(*operands)


def pack_kernel(target, width, facts, groups, q_ref, own0, own1, out0, out1, sem):
    owns, outs = (own0, own1), (out0, out1)

    def each(act):
        def look(at, slot):
            hit = groups[at] == facts[target]

            @pl.when(hit)
            def _():
                for head, out in enumerate(outs):
                    part = pl.ds(head * width, width)
                    act(pltpu.make_async_copy(q_ref.at[at, :, part], out.at[slot, :, pl.ds(0, width)], sem))
                    act(pltpu.make_async_copy(owns[head].at[at], out.at[slot, :, pl.ds(width, 2 * HD)], sem))

            return slot + hit.astype(jnp.int32)

        return lax.fori_loop(0, groups.shape[0], look, jnp.int32(0))

    count = each(lambda copy: copy.start())
    notes = jnp.full((out0.shape[1], HD), count, jnp.int32).astype(jnp.float32).astype(out0.dtype)
    for out in outs:
        out[0, :, width + 2 * HD:] = notes
    each(lambda copy: copy.wait())


def pack(facts, target, groups, queries, own, width):
    shape = jax.ShapeDtypeStruct((SLOTS, queries.shape[1], width + 3 * HD), queries.dtype)
    return pl.pallas_call(
        functools.partial(pack_kernel, target, width),
        out_shape=[shape, shape],
        in_specs=[SMEM, SMEM, HBM, HBM, HBM],
        out_specs=[VMEM, VMEM],
        scratch_shapes=[pltpu.SemaphoreType.DMA],
        compiler_params=pltpu.CompilerParams(vmem_limit_bytes=1 << 23),
    )(facts, groups, queries, *own)


def gate_kernel(*refs):
    pass


def gate(value, *others):
    return pl.pallas_call(
        gate_kernel,
        out_shape=jax.ShapeDtypeStruct(value.shape, value.dtype),
        in_specs=[HBM] + [SMEM if other.ndim == 1 else HBM for other in others],
        out_specs=HBM,
        input_output_aliases={0: 0},
    )(value, *others)


def cut_kernel(pair, out0, out1, sem):
    copies = [pltpu.make_async_copy(pair.at[head], out, sem.at[head]) for head, out in enumerate((out0, out1))]
    for copy in copies:
        copy.start()
    for copy in copies:
        copy.wait()


def cut(pair):
    shape = jax.ShapeDtypeStruct(pair.shape[1:], pair.dtype)
    return pl.pallas_call(
        cut_kernel,
        out_shape=[shape, shape],
        in_specs=[HBM],
        out_specs=[VMEM, VMEM],
        scratch_shapes=[pltpu.SemaphoreType.DMA((2,))],
        compiler_params=pltpu.CompilerParams(vmem_limit_bytes=1 << 23),
    )(pair)


def merge_kernel(target, head, facts, groups, lengths, got, old, out, ready, sem):
    rlen, width = got.shape[1:]
    token_at = lax.broadcasted_iota(jnp.int32, (rlen, HD), 0)

    def each(act, fill):
        def look(at, slot):
            hit = groups[at] == facts[target]

            @pl.when(hit)
            def _():
                if fill:
                    alive = token_at < lengths[at]
                    for lane in range(0, width, HD):
                        part = got[slot, :, lane:lane + HD]
                        ready[slot, :, lane:lane + HD] = jnp.where(alive, part, jnp.zeros_like(part))
                act(pltpu.make_async_copy(ready.at[slot], out.at[at, :, pl.ds(head * width, width)], sem))

            return slot + hit.astype(jnp.int32)

        lax.fori_loop(0, groups.shape[0], look, jnp.int32(0))

    each(lambda copy: copy.start(), True)
    each(lambda copy: copy.wait(), False)


def merge(facts, target, groups, lengths, got, out, head):
    return pl.pallas_call(
        functools.partial(merge_kernel, target, head),
        out_shape=jax.ShapeDtypeStruct(out.shape, out.dtype),
        in_specs=[SMEM, SMEM, SMEM, VMEM, HBM],
        out_specs=HBM,
        input_output_aliases={4: 0},
        scratch_shapes=[pltpu.VMEM(got.shape, got.dtype), pltpu.SemaphoreType.DMA],
        compiler_params=pltpu.CompilerParams(vmem_limit_bytes=1 << 23),
    )(facts, groups, lengths, got, out)


def after(value, *others):
    return lax.optimization_barrier((value,) + others)[0]


def gathered(queries, resp_kv, prompt_kv, lengths, group_of, first_head, kv_needed, per_kv):
    out = jax.ShapeDtypeStruct(queries.shape, jnp.bfloat16)
    facts = jnp.zeros((8,), jnp.int32)
    for head in range(kv_needed):
        mine = lax.dynamic_index_in_dim(prompt_kv, first_head + head, 2, keepdims=False)
        own = lax.dynamic_index_in_dim(resp_kv, first_head + head, 2, keepdims=False)
        whole = lax.all_gather(mine, "seq", axis=0, tiled=True)
        out, _ = attend(facts, group_of, lengths, queries, own, [whole], [out], head, per_kv, None, 16, fresh=head == 0)
    return out


def relayed(queries, resp_kv, prompt_kv, lengths, group_of, first_head, per_kv):
    me = lax.axis_index("seq")
    width = per_kv * HD
    middle, inward, outward = [(1, 2), (2, 1)], [(0, 1), (3, 2)], [(1, 0), (2, 3)]

    def send(pairs, value):
        return lax.ppermute(value, "seq", pairs)

    def two_heads(start):
        return lambda pairs: jnp.transpose(pairs[:, start:start + 2], (1, 0, 2))

    splits = prompt_kv.shape[2] // 2
    mine = lax.switch(first_head // 2, [two_heads(2 * at) for at in range(splits)], prompt_kv[0])
    across = send(middle, mine)
    inner_prompt = send(outward, mine)
    near = [send(inward, part) for part in cut(mine)]

    low = me < 2
    is_inner = (me == 1) | (me == 2)
    outer, inner = jnp.where(low, 0, 3), jnp.where(low, 1, 2)
    far_inner, far_outer = jnp.where(low, 2, 1), jnp.where(low, 3, 0)
    facts = jnp.stack([
        me,
        jnp.zeros_like(me),
        jnp.where(is_inner, outer, inner),
        jnp.where(is_inner, 0, 2),
        jnp.where(is_inner, far_inner, -1),
        jnp.ones_like(me),
        jnp.where(is_inner, far_outer, -1),
        jnp.where(is_inner, far_outer, far_inner),
        jnp.where(is_inner, 0, 1),
        jnp.where(is_inner, -1, far_outer),
    ]).astype(jnp.int32)

    own_by_head = after(jnp.transpose(resp_kv, (2, 0, 1, 3)))
    own = [lax.dynamic_index_in_dim(own_by_head, first_head + head, 0, keepdims=False) for head in range(2)]
    packed = pack(facts, 9, group_of, queries, own, width)
    out = jax.ShapeDtypeStruct(queries.shape, jnp.bfloat16)
    back_shape = jax.ShapeDtypeStruct((SLOTS, queries.shape[1], width), jnp.bfloat16)

    def run(head, cands, outs, passes, items, far=None, fresh=False, wait_for=None):
        return attend(
            facts, group_of, lengths, queries, own[head], cands, outs, head, per_kv, passes, items, far, fresh, wait_for)

    out, token = run(0, [mine], [out], [(False, 0, 1)], 4, fresh=True, wait_for=packed[0])
    near[0] = gate(near[0], token)
    last = [send(middle, near[0])]
    handed = [send(inward, gate(part, near[0])) for part in packed]
    out, token = run(1, [mine], [out], [(False, 0, 1)], 4)
    near[1] = gate(near[1], token)
    last.append(send(middle, near[1]))
    across = gate(across, token, inner_prompt)
    parts = cut(across)
    far_inner_prompt = [send(outward, parts[0])]
    for head in range(2):
        out, token = run(head, [near[head], across, inner_prompt], [out], [(False, 2, 3), (False, 4, 5)], 8, wait_for=near[1])
        if head == 0:
            far_inner_prompt.append(send(outward, gate(parts[1], token)))
    back = [None, None]
    for head in range(2):
        out, back[head], _ = run(head, [last[head]], [out, back_shape], [(True, 6, 1)], 4, handed[head])
        back[head] = send(outward, back[head])
        out, _ = run(head, [last[head], far_inner_prompt[head]], [out], [(False, 7, 8)], 4)
    for head in range(2):
        out = merge(facts, 9, group_of, lengths, back[head], out, head)
    return out


def shards(queries, resp_kv, prompt_kv, lengths, group_of):
    local_heads = queries.shape[2] // HD
    group = QHEADS // KVH
    kv_needed = max(local_heads // group, 1)
    per_kv = local_heads // kv_needed
    first_head = lax.axis_index("pp") * local_heads // group
    args = (queries, resp_kv, prompt_kv, lengths, group_of, first_head)
    if lax.axis_size("seq") == 4 and kv_needed == 2 and prompt_kv.shape[0] == 1:
        return relayed(*args, per_kv)
    return gathered(*args, kv_needed, per_kv)


def solution(mesh):
    placed = (
        P(("rep", "seq"), None, ("tp", "pp")),
        P(("rep", "seq"), None, "tp", None),
        P(("rep", "seq"), None, "tp", None),
        P(("rep", "seq")),
        P(("rep", "seq")),
    )
    return jax.shard_map(
        shards,
        mesh=mesh,
        in_specs=placed,
        out_specs=P(("rep", "seq"), None, ("tp", "pp")),
        check_vma=False,
    )
```

```python
import functools
import math

import jax
import jax.numpy as jnp
from jax import lax
from jax.experimental import pallas as pl
from jax.experimental.pallas import tpu as pltpu
from jax.sharding import PartitionSpec as P

QHEADS = 64
KVH = 8
HD = 128
LOG2E = math.log2(math.e)
VMEM_BYTES = 56 * 1024 * 1024
SLOTS = 8
HBM = pl.BlockSpec(memory_space=pl.ANY)
SMEM = pl.BlockSpec(memory_space=pltpu.SMEM)
VMEM = pl.BlockSpec(memory_space=pltpu.VMEM)


TN = (((0,), (0,)), ((), ()))
BLOCK = 512
CHUNK = 32
ONES = 16
GROUPS = 10


def stacked_heads(q_tile, per_kv):
    return jnp.concatenate([q_tile[:, g * HD:(g + 1) * HD] for g in range(per_kv)], axis=0)


def own_scores(own_tile, q_cols, rlen):
    keys = own_tile[:, :HD]
    own = jnp.dot(jnp.concatenate([keys, keys], axis=1), q_cols, preferred_element_type=jnp.float32)
    own_at = lax.broadcasted_iota(jnp.int32, own.shape, 0)
    token_at = lax.broadcasted_iota(jnp.int32, own.shape, 1) % rlen
    return jnp.where(own_at <= token_at, own, -1e30)


def folded(values, op):
    return op(values.reshape(values.shape[0] // 8, 8, values.shape[1]), axis=0)


def turn(q_tile, per_kv, out_ref):
    scaled = stacked_heads(q_tile, per_kv).T.astype(jnp.float32) * (HD ** -0.5 * LOG2E)
    high = scaled.astype(jnp.bfloat16)
    out_ref[:HD, :] = high
    out_ref[HD:, :] = (scaled - high.astype(jnp.float32)).astype(jnp.bfloat16)


def finish(acc_ref, length, per_kv, out_ref):
    out = (acc_ref[:HD, :] * (1.0 / acc_ref[HD:HD + 1, :])).T
    rlen = out_ref.shape[0]
    alive = lax.broadcasted_iota(jnp.int32, (rlen, HD), 0) < length
    for g in range(per_kv):
        part = jnp.where(alive, out[g * rlen:(g + 1) * rlen, :], 0.0)
        out_ref[:, g * HD:(g + 1) * HD] = part.astype(out_ref.dtype)


def scores_and_mix(q_cols, after_own, after_keys, after_s, after_u, after_peak, now):
    plen = after_keys.shape[0]
    own = own_scores(after_own, q_cols, after_own.shape[0])
    after_u[...] = own
    after_top = folded(own, jnp.max)
    if now is not None:
        s_ref, u_ref, peak_ref, own_tile, vt_ref, p_ref, acc_ref = now
        peak = peak_ref[...]
        part = jnp.exp2(u_ref[...] - peak[0:1, :]).astype(jnp.bfloat16)
        own_total = jnp.sum(part.astype(jnp.float32), axis=0, keepdims=True)
        own_acc = lax.dot_general(own_tile[:, HD:], part, TN, preferred_element_type=jnp.float32)
        acc = jnp.concatenate([own_acc, jnp.broadcast_to(own_total, (ONES, own_total.shape[1]))], axis=0)
        spread = jnp.concatenate([peak] * (CHUNK // 8), axis=0)
    for at in range(0, plen, BLOCK):
        rows = pl.ds(at, BLOCK)
        fresh = jnp.dot(after_keys[rows, :], q_cols, preferred_element_type=jnp.float32)
        after_s[rows, :] = fresh
        after_top = jnp.maximum(after_top, folded(fresh, jnp.max))
        if now is not None:
            for chunk in range(at, at + BLOCK, CHUNK):
                part = jnp.exp2(s_ref[chunk:chunk + CHUNK, :] - spread)
                p_ref[chunk:chunk + CHUNK, :] = part.astype(jnp.bfloat16)
            acc = acc + jnp.dot(vt_ref[:, rows], p_ref[rows, :], preferred_element_type=jnp.float32)
    after_peak[...] = jnp.broadcast_to(jnp.max(after_top, axis=0, keepdims=True), after_peak.shape)
    if now is not None:
        acc_ref[...] = acc


def listed(items, cap, count, facts, local, target, source):
    def look(at, n):
        hit = facts[GROUPS + at] == target

        @pl.when(hit)
        def _():
            items[n] = at
            items[cap + n] = source
            items[2 * cap + n] = facts[GROUPS + local + at]

        return n + hit.astype(jnp.int32)

    return lax.fori_loop(0, local, look, count)


def attend_kernel(passes, n_cand, per_kv, head, two, fresh, waits, *refs):
    refs = list(refs)
    facts, refs = refs[0], refs[1:]
    if two:
        x_ref, refs = refs[0], refs[1:]
    q_ref, own_ref = refs[:2]
    cands, refs = refs[2:2 + n_cand], refs[2 + n_cand + waits:]
    n_out = 2 if two else 1
    if not fresh:
        refs = refs[1:]
    outs, token, refs = refs[:n_out], refs[n_out], refs[n_out + 1:]
    items, at_slot, q_buf, own_buf, key_buf, value_buf, vt_buf, s0, s1, u0, u1, peak0, peak1, turned0, turned1, acc0, acc1, p_buf, o0, o1, info, q_sem, own_sem, kv_sem, o_sem = refs
    s_buf, u_buf, peak_buf, o_buf = (s0, s1), (u0, u1), (peak0, peak1), (o0, o1)
    turned, acc_buf = (turned0, turned1), (acc0, acc1)
    local = (facts.shape[0] - GROUPS) // 2
    cap = items.shape[0] // 3
    width = per_kv * HD
    stacked = passes is None

    count = jnp.int32(0)
    if stacked:
        def one_prompt(prompt, n):
            return listed(items, cap, n, facts, local, prompt, prompt)

        count = lax.fori_loop(0, cands[0].shape[0], one_prompt, count)
    else:
        for far, target, source in passes:
            if not far:
                count = listed(items, cap, count, facts, local, facts[target], facts[source])
                continue
            notes = pltpu.make_async_copy(x_ref.at[0, :, pl.ds(width + 2 * HD, HD)], info, kv_sem)
            notes.start()
            notes.wait()
            handed = jnp.max(info[0:16, :].astype(jnp.float32)).astype(jnp.int32)
            handed = jnp.where(facts[target] >= 0, jnp.minimum(handed, SLOTS), 0)

            def take(slot, n):
                items[n] = local + slot
                items[cap + n] = facts[source]
                items[2 * cap + n] = q_buf.shape[1]
                return n + 1

            count = lax.fori_loop(0, handed, take, count)

    token[0] = count

    def each_array(i, act_local, act_far):
        at = items[i]
        if not two:
            act_local(at)
            return

        @pl.when(at < local)
        def _():
            act_local(at)

        @pl.when(at >= local)
        def _():
            act_far(at - local)

    mine = pl.ds(head * width, width)
    first = pl.ds(0, width)
    handed_own = pl.ds(width, 2 * HD)

    def fetch(i):
        slot, fourth = lax.rem(i, 2), lax.rem(i, 4)

        def here(at):
            pltpu.make_async_copy(q_ref.at[at, :, mine], q_buf.at[slot], q_sem.at[slot]).start()
            pltpu.make_async_copy(own_ref.at[at], own_buf.at[fourth], own_sem.at[fourth]).start()

        def far(at):
            pltpu.make_async_copy(x_ref.at[at, :, first], q_buf.at[slot], q_sem.at[slot]).start()
            pltpu.make_async_copy(x_ref.at[at, :, handed_own], own_buf.at[fourth], own_sem.at[fourth]).start()

        each_array(i, here, far)

    def fetched(i):
        slot, fourth = lax.rem(i, 2), lax.rem(i, 4)
        pltpu.make_async_copy(q_ref.at[0, :, first], q_buf.at[slot], q_sem.at[slot]).wait()
        pltpu.make_async_copy(own_ref.at[0], own_buf.at[fourth], own_sem.at[fourth]).wait()

    def store(i, slot):
        def here(at):
            pltpu.make_async_copy(o_buf[slot], outs[0].at[at, :, mine], o_sem.at[slot]).start()

        def far(at):
            pltpu.make_async_copy(o_buf[slot], outs[1].at[at], o_sem.at[slot]).start()

        each_array(i, here, far)

    def stored(slot):
        pltpu.make_async_copy(o_buf[slot], outs[0].at[0, :, first], o_sem.at[slot]).wait()

    keys, values = pl.ds(0, HD), pl.ds(HD, HD)

    def ask(source, into):
        def bring(pairs):
            for twin in (keys, values):
                pltpu.make_async_copy(pairs.at[:, keys], key_buf.at[into, :, twin], kv_sem).start()
            pltpu.make_async_copy(pairs.at[:, values], value_buf, kv_sem).start()

        if stacked:
            bring(cands[0].at[source])
        else:
            for which in range(n_cand):
                @pl.when(source == which)
                def _():
                    bring(cands[which].at[head] if len(cands[which].shape) == 3 else cands[which])

    def receive(into):
        for _ in range(3):
            pltpu.make_async_copy(value_buf, value_buf, kv_sem).wait()
        vt_buf[into, :HD, :] = value_buf[...].T

    @pl.when(count > 0)
    def _():
        ask(items[cap], 0)
        fetch(jnp.int32(0))
        vt_buf[:, HD:, :] = jnp.ones((2, ONES, vt_buf.shape[2]), vt_buf.dtype)

        @pl.when(count > 1)
        def _():
            fetch(jnp.int32(1))

        at_slot[0] = 0
        fetched(jnp.int32(0))
        turn(q_buf[0], per_kv, turned[0])

        @pl.when(count > 2)
        def _():
            fetch(jnp.int32(2))

        @pl.when(count > 1)
        def _():
            fetched(jnp.int32(1))

        turn(q_buf[1], per_kv, turned[1])
        receive(0)
        scores_and_mix(turned[0][...], own_buf[0], key_buf.at[0], s_buf[0], u_buf[0], peak_buf[0], None)

        def one(i, slot):
            other = 1 - slot
            held = at_slot[0]
            more = i + 1 < count
            moved = more & (items[cap + jnp.minimum(i + 1, count - 1)] != items[cap + i])
            holds = jnp.where(moved, 1 - held, held)
            at_slot[0] = holds

            @pl.when(i + 2 < count)
            def _():
                fetched(i + 2)

            @pl.when(i + 3 < count)
            def _():
                fetch(i + 3)

            @pl.when(moved)
            def _():
                ask(items[cap + i + 1], holds)
                receive(holds)

            @pl.when(i >= 3)
            def _():
                stored(other)

            now = (
                s_buf[slot], u_buf[slot], peak_buf[slot], own_buf[lax.rem(i, 4)], vt_buf.at[held], p_buf,
                acc_buf[slot])
            scores_and_mix(
                turned[other][...], own_buf[lax.rem(i + 1, 4)], key_buf.at[holds],
                s_buf[other], u_buf[other], peak_buf[other], now)
            turn(q_buf[slot], per_kv, turned[slot])
            finish(acc_buf[other], items[2 * cap + jnp.maximum(i - 1, 0)], per_kv, o_buf[other])

            @pl.when(i >= 1)
            def _():
                store(i - 1, other)

        def pair(j, _):
            one(2 * j, 0)

            @pl.when(2 * j + 1 < count)
            def _():
                one(2 * j + 1, 1)

            return 0

        lax.fori_loop(0, lax.div(count + 1, 2), pair, 0)
        final = count - 1
        for slot in range(2):
            @pl.when(lax.rem(final, 2) == slot)
            def _():
                @pl.when(final >= 2)
                def _():
                    stored(slot)

                finish(acc_buf[slot], items[2 * cap + final], per_kv, o_buf[slot])
                store(final, slot)

        stored(0)

        @pl.when(count > 1)
        def _():
            stored(1)


def attend(facts, queries, own, cands, outs, head, per_kv, passes, items, far=None, fresh=False, wait_for=None):
    rlen = queries.shape[1]
    plen = cands[0].shape[-2]
    width = per_kv * HD
    small = [facts]
    large = ([far] if far is not None else []) + [queries, own] + cands
    operands = small + large + ([] if wait_for is None else [wait_for])
    aliases = {}
    if not fresh:
        aliases = {len(operands): 0}
        operands = operands + [outs[0]]
    cap = queries.shape[0] + (SLOTS if far is not None else 0)
    return pl.pallas_call(
        functools.partial(attend_kernel, passes, len(cands), per_kv, head, far is not None, fresh, wait_for is not None),
        out_shape=[jax.ShapeDtypeStruct(o.shape, o.dtype) for o in outs] + [jax.ShapeDtypeStruct((1,), jnp.int32)],
        in_specs=[SMEM] * len(small) + [HBM] * (len(operands) - len(small)),
        out_specs=[HBM] * len(outs) + [SMEM],
        input_output_aliases=aliases,
        scratch_shapes=[
            pltpu.SMEM((3 * cap,), jnp.int32),
            pltpu.SMEM((1,), jnp.int32),
            pltpu.VMEM((2, rlen, width), jnp.bfloat16),
            pltpu.VMEM((4, rlen, 2 * HD), jnp.bfloat16),
            pltpu.VMEM((2, plen, 2 * HD), jnp.bfloat16),
            pltpu.VMEM((plen, HD), jnp.bfloat16),
            pltpu.VMEM((2, HD + ONES, plen), jnp.bfloat16),
            pltpu.VMEM((plen, per_kv * rlen), jnp.float32),
            pltpu.VMEM((plen, per_kv * rlen), jnp.float32),
            pltpu.VMEM((rlen, per_kv * rlen), jnp.float32),
            pltpu.VMEM((rlen, per_kv * rlen), jnp.float32),
            pltpu.VMEM((8, per_kv * rlen), jnp.float32),
            pltpu.VMEM((8, per_kv * rlen), jnp.float32),
            pltpu.VMEM((2 * HD, per_kv * rlen), jnp.bfloat16),
            pltpu.VMEM((2 * HD, per_kv * rlen), jnp.bfloat16),
            pltpu.VMEM((HD + ONES, per_kv * rlen), jnp.float32),
            pltpu.VMEM((HD + ONES, per_kv * rlen), jnp.float32),
            pltpu.VMEM((plen, per_kv * rlen), jnp.bfloat16),
            pltpu.VMEM((rlen, width), jnp.bfloat16),
            pltpu.VMEM((rlen, width), jnp.bfloat16),
            pltpu.VMEM((rlen, HD), jnp.bfloat16),
            pltpu.SemaphoreType.DMA((2,)),
            pltpu.SemaphoreType.DMA((4,)),
            pltpu.SemaphoreType.DMA,
            pltpu.SemaphoreType.DMA((2,)),
        ],
        compiler_params=pltpu.CompilerParams(vmem_limit_bytes=VMEM_BYTES),
        cost_estimate=pl.CostEstimate(flops=items << 20, bytes_accessed=1 << 16, transcendentals=0),
    )(*operands)


def pack_kernel(target, width, facts, groups, q_ref, own0, own1, out0, out1, sem):
    owns, outs = (own0, own1), (out0, out1)

    def each(act):
        def look(at, slot):
            hit = groups[at] == facts[target]

            @pl.when(hit)
            def _():
                for head, out in enumerate(outs):
                    part = pl.ds(head * width, width)
                    act(pltpu.make_async_copy(q_ref.at[at, :, part], out.at[slot, :, pl.ds(0, width)], sem))
                    act(pltpu.make_async_copy(owns[head].at[at], out.at[slot, :, pl.ds(width, 2 * HD)], sem))

            return slot + hit.astype(jnp.int32)

        return lax.fori_loop(0, groups.shape[0], look, jnp.int32(0))

    count = each(lambda copy: copy.start())
    notes = jnp.full((out0.shape[1], HD), count, jnp.int32).astype(jnp.float32).astype(out0.dtype)
    for out in outs:
        out[0, :, width + 2 * HD:] = notes
    each(lambda copy: copy.wait())


def pack(facts, target, groups, queries, own, width):
    shape = jax.ShapeDtypeStruct((SLOTS, queries.shape[1], width + 3 * HD), queries.dtype)
    return pl.pallas_call(
        functools.partial(pack_kernel, target, width),
        out_shape=[shape, shape],
        in_specs=[SMEM, SMEM, HBM, HBM, HBM],
        out_specs=[VMEM, VMEM],
        scratch_shapes=[pltpu.SemaphoreType.DMA],
        compiler_params=pltpu.CompilerParams(vmem_limit_bytes=1 << 23),
    )(facts, groups, queries, *own)


def gate_kernel(*refs):
    pass


def gate(value, *others):
    return pl.pallas_call(
        gate_kernel,
        out_shape=jax.ShapeDtypeStruct(value.shape, value.dtype),
        in_specs=[HBM] + [SMEM if other.ndim == 1 else HBM for other in others],
        out_specs=HBM,
        input_output_aliases={0: 0},
    )(value, *others)


def cut_kernel(pair, out0, out1, sem):
    copies = [pltpu.make_async_copy(pair.at[head], out, sem.at[head]) for head, out in enumerate((out0, out1))]
    for copy in copies:
        copy.start()
    for copy in copies:
        copy.wait()


def cut(pair):
    shape = jax.ShapeDtypeStruct(pair.shape[1:], pair.dtype)
    return pl.pallas_call(
        cut_kernel,
        out_shape=[shape, shape],
        in_specs=[HBM],
        out_specs=[VMEM, VMEM],
        scratch_shapes=[pltpu.SemaphoreType.DMA((2,))],
        compiler_params=pltpu.CompilerParams(vmem_limit_bytes=1 << 23),
    )(pair)


def merge_kernel(target, head, facts, groups, lengths, got, old, out, ready, sem):
    rlen, width = got.shape[1:]
    token_at = lax.broadcasted_iota(jnp.int32, (rlen, HD), 0)

    def each(act, fill):
        def look(at, slot):
            hit = groups[at] == facts[target]

            @pl.when(hit)
            def _():
                if fill:
                    alive = token_at < lengths[at]
                    for lane in range(0, width, HD):
                        part = got[slot, :, lane:lane + HD]
                        ready[slot, :, lane:lane + HD] = jnp.where(alive, part, jnp.zeros_like(part))
                act(pltpu.make_async_copy(ready.at[slot], out.at[at, :, pl.ds(head * width, width)], sem))

            return slot + hit.astype(jnp.int32)

        lax.fori_loop(0, groups.shape[0], look, jnp.int32(0))

    each(lambda copy: copy.start(), True)
    each(lambda copy: copy.wait(), False)


def merge(facts, target, groups, lengths, got, out, head):
    return pl.pallas_call(
        functools.partial(merge_kernel, target, head),
        out_shape=jax.ShapeDtypeStruct(out.shape, out.dtype),
        in_specs=[SMEM, SMEM, SMEM, VMEM, HBM],
        out_specs=HBM,
        input_output_aliases={4: 0},
        scratch_shapes=[pltpu.VMEM(got.shape, got.dtype), pltpu.SemaphoreType.DMA],
        compiler_params=pltpu.CompilerParams(vmem_limit_bytes=1 << 23),
    )(facts, groups, lengths, got, out)


def after(value, *others):
    return lax.optimization_barrier((value,) + others)[0]


def gathered(queries, resp_kv, prompt_kv, lengths, group_of, first_head, kv_needed, per_kv):
    out = jax.ShapeDtypeStruct(queries.shape, jnp.bfloat16)
    facts = jnp.concatenate([jnp.zeros((GROUPS,), jnp.int32), group_of, lengths])
    for head in range(kv_needed):
        mine = lax.dynamic_index_in_dim(prompt_kv, first_head + head, 2, keepdims=False)
        own = lax.dynamic_index_in_dim(resp_kv, first_head + head, 2, keepdims=False)
        whole = lax.all_gather(mine, "seq", axis=0, tiled=True)
        out, _ = attend(facts, queries, own, [whole], [out], head, per_kv, None, 16, fresh=head == 0)
    return out


def relayed(queries, resp_kv, prompt_kv, lengths, group_of, first_head, per_kv):
    me = lax.axis_index("seq")
    width = per_kv * HD
    middle, inward, outward = [(1, 2), (2, 1)], [(0, 1), (3, 2)], [(1, 0), (2, 3)]

    def send(pairs, value):
        return lax.ppermute(value, "seq", pairs)

    def two_heads(start):
        return lambda pairs: jnp.transpose(pairs[:, start:start + 2], (1, 0, 2))

    splits = prompt_kv.shape[2] // 2
    mine = lax.switch(first_head // 2, [two_heads(2 * at) for at in range(splits)], prompt_kv[0])
    across = send(middle, mine)
    inner_prompt = send(outward, mine)
    near = [send(inward, part) for part in cut(mine)]

    low = me < 2
    is_inner = (me == 1) | (me == 2)
    outer, inner = jnp.where(low, 0, 3), jnp.where(low, 1, 2)
    far_inner, far_outer = jnp.where(low, 2, 1), jnp.where(low, 3, 0)
    facts = jnp.stack([
        me,
        jnp.zeros_like(me),
        jnp.where(is_inner, outer, inner),
        jnp.where(is_inner, 0, 2),
        jnp.where(is_inner, far_inner, -1),
        jnp.ones_like(me),
        jnp.where(is_inner, far_outer, -1),
        jnp.where(is_inner, far_outer, far_inner),
        jnp.where(is_inner, 0, 1),
        jnp.where(is_inner, -1, far_outer),
    ]).astype(jnp.int32)
    facts = jnp.concatenate([facts, group_of, lengths])

    own_by_head = after(jnp.transpose(resp_kv, (2, 0, 1, 3)))
    own = [lax.dynamic_index_in_dim(own_by_head, first_head + head, 0, keepdims=False) for head in range(2)]
    packed = pack(facts, 9, group_of, queries, own, width)
    out = jax.ShapeDtypeStruct(queries.shape, jnp.bfloat16)
    back_shape = jax.ShapeDtypeStruct((SLOTS, queries.shape[1], width), jnp.bfloat16)

    def run(head, cands, outs, passes, items, far=None, fresh=False, wait_for=None):
        return attend(
            facts, queries, own[head], cands, outs, head, per_kv, passes, items, far, fresh, wait_for)

    out, token = run(0, [mine], [out], [(False, 0, 1)], 4, fresh=True, wait_for=packed[0])
    near[0] = gate(near[0], token)
    last = [send(middle, near[0])]
    handed = [send(inward, gate(part, near[0])) for part in packed]
    out, token = run(1, [mine], [out], [(False, 0, 1)], 4)
    near[1] = gate(near[1], token)
    last.append(send(middle, near[1]))
    across = gate(across, token, inner_prompt)
    parts = cut(across)
    far_inner_prompt = [send(outward, parts[0])]
    for head in range(2):
        out, token = run(head, [near[head], across, inner_prompt], [out], [(False, 2, 3), (False, 4, 5)], 8, wait_for=near[1])
        if head == 0:
            far_inner_prompt.append(send(outward, gate(parts[1], token)))
    back = [None, None]
    out, back[0], _ = run(
        0, [last[0], far_inner_prompt[0]], [out, back_shape], [(True, 6, 1), (False, 7, 8)], 8, handed[0])
    back[0] = send(outward, back[0])
    out, back[1], _ = run(1, [last[1]], [out, back_shape], [(True, 6, 1)], 4, handed[1])
    back[1] = send(outward, back[1])
    out, _ = run(1, [last[1], far_inner_prompt[1]], [out], [(False, 7, 8)], 4)
    for head in range(2):
        out = merge(facts, 9, group_of, lengths, back[head], out, head)
    return out


def shards(queries, resp_kv, prompt_kv, lengths, group_of):
    local_heads = queries.shape[2] // HD
    group = QHEADS // KVH
    kv_needed = max(local_heads // group, 1)
    per_kv = local_heads // kv_needed
    first_head = lax.axis_index("pp") * local_heads // group
    args = (queries, resp_kv, prompt_kv, lengths, group_of, first_head)
    if lax.axis_size("seq") == 4 and kv_needed == 2 and prompt_kv.shape[0] == 1:
        return relayed(*args, per_kv)
    return gathered(*args, kv_needed, per_kv)


def solution(mesh):
    placed = (
        P(("rep", "seq"), None, ("tp", "pp")),
        P(("rep", "seq"), None, "tp", None),
        P(("rep", "seq"), None, "tp", None),
        P(("rep", "seq")),
        P(("rep", "seq")),
    )
    return jax.shard_map(
        shards,
        mesh=mesh,
        in_specs=placed,
        out_specs=P(("rep", "seq"), None, ("tp", "pp")),
        check_vma=False,
    )
```

```python
import functools
import math

import jax
import jax.numpy as jnp
from jax import lax
from jax.experimental import pallas as pl
from jax.experimental.pallas import tpu as pltpu
from jax.sharding import PartitionSpec as P

QHEADS = 64
KVH = 8
HD = 128
LOG2E = math.log2(math.e)
VMEM_BYTES = 56 * 1024 * 1024
SLOTS = 8
HBM = pl.BlockSpec(memory_space=pl.ANY)
SMEM = pl.BlockSpec(memory_space=pltpu.SMEM)
VMEM = pl.BlockSpec(memory_space=pltpu.VMEM)


TN = (((0,), (0,)), ((), ()))
BLOCK = 512
CHUNK = 32
ONES = 16
GROUPS = 11


def stacked_heads(q_tile, per_kv):
    return jnp.concatenate([q_tile[:, g * HD:(g + 1) * HD] for g in range(per_kv)], axis=0)


def own_scores(own_tile, q_cols, rlen):
    keys = own_tile[:, :HD]
    own = jnp.dot(jnp.concatenate([keys, keys], axis=1), q_cols, preferred_element_type=jnp.float32)
    own_at = lax.broadcasted_iota(jnp.int32, own.shape, 0)
    token_at = lax.broadcasted_iota(jnp.int32, own.shape, 1) % rlen
    return jnp.where(own_at <= token_at, own, -1e30)


def folded(values, op):
    return op(values.reshape(values.shape[0] // 8, 8, values.shape[1]), axis=0)


def turn(q_tile, per_kv, out_ref):
    scaled = stacked_heads(q_tile, per_kv).T.astype(jnp.float32) * (HD ** -0.5 * LOG2E)
    high = scaled.astype(jnp.bfloat16)
    out_ref[:HD, :] = high
    out_ref[HD:, :] = (scaled - high.astype(jnp.float32)).astype(jnp.bfloat16)


def finish(acc_ref, length, per_kv, out_ref):
    out = (acc_ref[:HD, :] * (1.0 / acc_ref[HD:HD + 1, :])).T
    rlen = out_ref.shape[0]
    alive = lax.broadcasted_iota(jnp.int32, (rlen, HD), 0) < length
    for g in range(per_kv):
        part = jnp.where(alive, out[g * rlen:(g + 1) * rlen, :], 0.0)
        out_ref[:, g * HD:(g + 1) * HD] = part.astype(out_ref.dtype)


def scores_and_mix(q_cols, after_own, after_keys, after_s, after_u, after_peak, now):
    plen = after_keys.shape[0]
    own = own_scores(after_own, q_cols, after_own.shape[0])
    after_u[...] = own
    after_top = folded(own, jnp.max)
    if now is not None:
        s_ref, u_ref, peak_ref, own_tile, vt_ref, p_ref, acc_ref = now
        peak = peak_ref[...]
        part = jnp.exp2(u_ref[...] - peak[0:1, :]).astype(jnp.bfloat16)
        own_total = jnp.sum(part.astype(jnp.float32), axis=0, keepdims=True)
        own_acc = lax.dot_general(own_tile[:, HD:], part, TN, preferred_element_type=jnp.float32)
        acc = jnp.concatenate([own_acc, jnp.broadcast_to(own_total, (ONES, own_total.shape[1]))], axis=0)
        spread = jnp.concatenate([peak] * (CHUNK // 8), axis=0)
    for at in range(0, plen, BLOCK):
        rows = pl.ds(at, BLOCK)
        fresh = jnp.dot(after_keys[rows, :], q_cols, preferred_element_type=jnp.float32)
        after_s[rows, :] = fresh
        after_top = jnp.maximum(after_top, folded(fresh, jnp.max))
        if now is not None:
            for chunk in range(at, at + BLOCK, CHUNK):
                part = jnp.exp2(s_ref[chunk:chunk + CHUNK, :] - spread)
                p_ref[chunk:chunk + CHUNK, :] = part.astype(jnp.bfloat16)
            acc = acc + jnp.dot(vt_ref[:, rows], p_ref[rows, :], preferred_element_type=jnp.float32)
    after_peak[...] = jnp.broadcast_to(jnp.max(after_top, axis=0, keepdims=True), after_peak.shape)
    if now is not None:
        acc_ref[...] = acc


def listed(items, cap, count, facts, local, target, source, head):
    def look(at, n):
        hit = facts[GROUPS + at] == target

        @pl.when(hit)
        def _():
            items[n] = at
            items[cap + n] = source
            items[2 * cap + n] = facts[GROUPS + local + at]
            items[3 * cap + n] = head

        return n + hit.astype(jnp.int32)

    return lax.fori_loop(0, local, look, count)


def attend_kernel(passes, n_cand, per_kv, whole_head, two, fresh, waits, *refs):
    refs = list(refs)
    facts, refs = refs[0], refs[1:]
    if two:
        x_ref, refs = refs[0], refs[1:]
    q_ref, own_ref = refs[:2]
    cands, refs = refs[2:2 + n_cand], refs[2 + n_cand + waits:]
    n_out = 2 if two else 1
    if not fresh:
        refs = refs[1:]
    outs, token, refs = refs[:n_out], refs[n_out], refs[n_out + 1:]
    items, at_slot, q_buf, own_buf, key_buf, value_buf, vt_buf, s0, s1, u0, u1, peak0, peak1, turned0, turned1, acc0, acc1, p_buf, o0, o1, info, q_sem, own_sem, kv_sem, o_sem = refs
    s_buf, u_buf, peak_buf, o_buf = (s0, s1), (u0, u1), (peak0, peak1), (o0, o1)
    turned, acc_buf = (turned0, turned1), (acc0, acc1)
    local = (facts.shape[0] - GROUPS) // 2
    cap = items.shape[0] // 4
    width = per_kv * HD
    stacked = passes is None

    count = jnp.int32(0)
    if stacked:
        def one_prompt(prompt, n):
            return listed(items, cap, n, facts, local, prompt, prompt, whole_head)

        count = lax.fori_loop(0, cands[0].shape[0], one_prompt, count)
    else:
        for far, target, source, head in passes:
            if not far:
                count = listed(items, cap, count, facts, local, facts[target], facts[source], head)
                continue
            notes = pltpu.make_async_copy(x_ref.at[0, :, pl.ds(2 * (width + 2 * HD), HD)], info, kv_sem)
            notes.start()
            notes.wait()
            far_head = head
            handed = jnp.max(info[0:16, :].astype(jnp.float32)).astype(jnp.int32)
            handed = jnp.where(facts[target] >= 0, jnp.minimum(handed, SLOTS), 0)

            def take(slot, n):
                items[n] = local + slot
                items[cap + n] = facts[source]
                items[2 * cap + n] = q_buf.shape[1]
                items[3 * cap + n] = far_head
                return n + 1

            count = lax.fori_loop(0, handed, take, count)

    token[0] = count

    def each_array(i, act_local, act_far):
        at = items[i]
        if not two:
            act_local(at)
            return

        @pl.when(at < local)
        def _():
            act_local(at)

        @pl.when(at >= local)
        def _():
            act_far(at - local)

    first = pl.ds(0, width)

    def lanes(i, step, skip, size):
        return pl.ds(pl.multiple_of(items[3 * cap + i] * step + skip, HD), size)

    def mine(i):
        return lanes(i, width, 0, width)

    def fetch(i):
        slot, fourth = lax.rem(i, 2), lax.rem(i, 4)

        def here(at):
            pltpu.make_async_copy(q_ref.at[at, :, mine(i)], q_buf.at[slot], q_sem.at[slot]).start()
            pltpu.make_async_copy(own_ref.at[items[3 * cap + i], at], own_buf.at[fourth], own_sem.at[fourth]).start()

        def far(at):
            pltpu.make_async_copy(x_ref.at[at, :, lanes(i, width + 2 * HD, 0, width)], q_buf.at[slot], q_sem.at[slot]).start()
            pltpu.make_async_copy(x_ref.at[at, :, lanes(i, width + 2 * HD, width, 2 * HD)], own_buf.at[fourth], own_sem.at[fourth]).start()

        each_array(i, here, far)

    def fetched(i):
        slot, fourth = lax.rem(i, 2), lax.rem(i, 4)
        pltpu.make_async_copy(q_ref.at[0, :, first], q_buf.at[slot], q_sem.at[slot]).wait()
        pltpu.make_async_copy(own_ref.at[0, 0], own_buf.at[fourth], own_sem.at[fourth]).wait()

    def store(i, slot):
        def here(at):
            pltpu.make_async_copy(o_buf[slot], outs[0].at[at, :, mine(i)], o_sem.at[slot]).start()

        def far(at):
            pltpu.make_async_copy(o_buf[slot], outs[1].at[at], o_sem.at[slot]).start()

        each_array(i, here, far)

    def stored(slot):
        pltpu.make_async_copy(o_buf[slot], outs[0].at[0, :, first], o_sem.at[slot]).wait()

    keys, values = pl.ds(0, HD), pl.ds(HD, HD)

    def ask(i, into):
        source = items[cap + i]

        def bring(pairs):
            for twin in (keys, values):
                pltpu.make_async_copy(pairs.at[:, keys], key_buf.at[into, :, twin], kv_sem).start()
            pltpu.make_async_copy(pairs.at[:, values], value_buf, kv_sem).start()

        if stacked:
            bring(cands[0].at[source])
        else:
            for which in range(n_cand):
                @pl.when(source == which)
                def _():
                    bring(cands[which].at[items[3 * cap + i]] if len(cands[which].shape) == 3 else cands[which])

    def receive(into):
        for _ in range(3):
            pltpu.make_async_copy(value_buf, value_buf, kv_sem).wait()
        vt_buf[into, :HD, :] = value_buf[...].T

    @pl.when(count > 0)
    def _():
        ask(0, 0)
        fetch(jnp.int32(0))
        vt_buf[:, HD:, :] = jnp.ones((2, ONES, vt_buf.shape[2]), vt_buf.dtype)

        @pl.when(count > 1)
        def _():
            fetch(jnp.int32(1))

        at_slot[0] = 0
        fetched(jnp.int32(0))
        turn(q_buf[0], per_kv, turned[0])

        @pl.when(count > 2)
        def _():
            fetch(jnp.int32(2))

        @pl.when(count > 1)
        def _():
            fetched(jnp.int32(1))

        turn(q_buf[1], per_kv, turned[1])
        receive(0)
        scores_and_mix(turned[0][...], own_buf[0], key_buf.at[0], s_buf[0], u_buf[0], peak_buf[0], None)

        def one(i, slot):
            other = 1 - slot
            held = at_slot[0]
            more = i + 1 < count
            after_i = jnp.minimum(i + 1, count - 1)
            moved = more & ((items[cap + after_i] != items[cap + i]) | (items[3 * cap + after_i] != items[3 * cap + i]))
            holds = jnp.where(moved, 1 - held, held)
            at_slot[0] = holds

            @pl.when(i + 2 < count)
            def _():
                fetched(i + 2)

            @pl.when(i + 3 < count)
            def _():
                fetch(i + 3)

            @pl.when(moved)
            def _():
                ask(i + 1, holds)
                receive(holds)

            @pl.when(i >= 3)
            def _():
                stored(other)

            now = (
                s_buf[slot], u_buf[slot], peak_buf[slot], own_buf[lax.rem(i, 4)], vt_buf.at[held], p_buf,
                acc_buf[slot])
            scores_and_mix(
                turned[other][...], own_buf[lax.rem(i + 1, 4)], key_buf.at[holds],
                s_buf[other], u_buf[other], peak_buf[other], now)
            turn(q_buf[slot], per_kv, turned[slot])
            finish(acc_buf[other], items[2 * cap + jnp.maximum(i - 1, 0)], per_kv, o_buf[other])

            @pl.when(i >= 1)
            def _():
                store(i - 1, other)

        def pair(j, _):
            one(2 * j, 0)

            @pl.when(2 * j + 1 < count)
            def _():
                one(2 * j + 1, 1)

            return 0

        lax.fori_loop(0, lax.div(count + 1, 2), pair, 0)
        final = count - 1
        for slot in range(2):
            @pl.when(lax.rem(final, 2) == slot)
            def _():
                @pl.when(final >= 2)
                def _():
                    stored(slot)

                finish(acc_buf[slot], items[2 * cap + final], per_kv, o_buf[slot])
                store(final, slot)

        stored(0)

        @pl.when(count > 1)
        def _():
            stored(1)


def attend(facts, queries, own, cands, outs, head, per_kv, passes, items, far=None, fresh=False, wait_for=None):
    rlen = queries.shape[1]
    plen = cands[0].shape[-2]
    width = per_kv * HD
    small = [facts]
    large = ([far] if far is not None else []) + [queries, own] + cands
    operands = small + large + ([] if wait_for is None else [wait_for])
    aliases = {}
    if not fresh:
        aliases = {len(operands): 0}
        operands = operands + [outs[0]]
    cap = 2 * queries.shape[0] + (SLOTS if far is not None else 0)
    return pl.pallas_call(
        functools.partial(attend_kernel, passes, len(cands), per_kv, head, far is not None, fresh, wait_for is not None),
        out_shape=[jax.ShapeDtypeStruct(o.shape, o.dtype) for o in outs] + [jax.ShapeDtypeStruct((1,), jnp.int32)],
        in_specs=[SMEM] * len(small) + [HBM] * (len(operands) - len(small)),
        out_specs=[HBM] * len(outs) + [SMEM],
        input_output_aliases=aliases,
        scratch_shapes=[
            pltpu.SMEM((4 * cap,), jnp.int32),
            pltpu.SMEM((1,), jnp.int32),
            pltpu.VMEM((2, rlen, width), jnp.bfloat16),
            pltpu.VMEM((4, rlen, 2 * HD), jnp.bfloat16),
            pltpu.VMEM((2, plen, 2 * HD), jnp.bfloat16),
            pltpu.VMEM((plen, HD), jnp.bfloat16),
            pltpu.VMEM((2, HD + ONES, plen), jnp.bfloat16),
            pltpu.VMEM((plen, per_kv * rlen), jnp.float32),
            pltpu.VMEM((plen, per_kv * rlen), jnp.float32),
            pltpu.VMEM((rlen, per_kv * rlen), jnp.float32),
            pltpu.VMEM((rlen, per_kv * rlen), jnp.float32),
            pltpu.VMEM((8, per_kv * rlen), jnp.float32),
            pltpu.VMEM((8, per_kv * rlen), jnp.float32),
            pltpu.VMEM((2 * HD, per_kv * rlen), jnp.bfloat16),
            pltpu.VMEM((2 * HD, per_kv * rlen), jnp.bfloat16),
            pltpu.VMEM((HD + ONES, per_kv * rlen), jnp.float32),
            pltpu.VMEM((HD + ONES, per_kv * rlen), jnp.float32),
            pltpu.VMEM((plen, per_kv * rlen), jnp.bfloat16),
            pltpu.VMEM((rlen, width), jnp.bfloat16),
            pltpu.VMEM((rlen, width), jnp.bfloat16),
            pltpu.VMEM((rlen, HD), jnp.bfloat16),
            pltpu.SemaphoreType.DMA((2,)),
            pltpu.SemaphoreType.DMA((4,)),
            pltpu.SemaphoreType.DMA,
            pltpu.SemaphoreType.DMA((2,)),
        ],
        compiler_params=pltpu.CompilerParams(vmem_limit_bytes=VMEM_BYTES),
        cost_estimate=pl.CostEstimate(flops=items << 20, bytes_accessed=1 << 16, transcendentals=0),
    )(*operands)


def pack_kernel(target, width, facts, q_ref, own_ref, out, sem):
    step = width + 2 * HD
    local = q_ref.shape[0]

    def each(act):
        def look(at, slot):
            hit = facts[GROUPS + at] == facts[target]

            @pl.when(hit)
            def _():
                for head in range(2):
                    part = pl.ds(head * width, width)
                    act(pltpu.make_async_copy(q_ref.at[at, :, part], out.at[slot, :, pl.ds(head * step, width)], sem))
                    act(pltpu.make_async_copy(
                        own_ref.at[head, at], out.at[slot, :, pl.ds(head * step + width, 2 * HD)], sem))

            return slot + hit.astype(jnp.int32)

        return lax.fori_loop(0, local, look, jnp.int32(0))

    count = each(lambda copy: copy.start())
    out[0, :, 2 * step:] = jnp.full((out.shape[1], HD), count, jnp.int32).astype(jnp.float32).astype(out.dtype)
    each(lambda copy: copy.wait())


def pack(facts, target, queries, own, width):
    return pl.pallas_call(
        functools.partial(pack_kernel, target, width),
        out_shape=jax.ShapeDtypeStruct((SLOTS, queries.shape[1], 2 * width + 5 * HD), queries.dtype),
        in_specs=[SMEM, HBM, HBM],
        out_specs=VMEM,
        scratch_shapes=[pltpu.SemaphoreType.DMA],
        compiler_params=pltpu.CompilerParams(vmem_limit_bytes=1 << 23),
    )(facts, queries, own)


def gate_kernel(*refs):
    pass


def gate(value, *others):
    return pl.pallas_call(
        gate_kernel,
        out_shape=jax.ShapeDtypeStruct(value.shape, value.dtype),
        in_specs=[HBM] + [SMEM if other.ndim == 1 else HBM for other in others],
        out_specs=HBM,
        input_output_aliases={0: 0},
    )(value, *others)


def cut_kernel(pair, out0, out1, sem):
    copies = [pltpu.make_async_copy(pair.at[head], out, sem.at[head]) for head, out in enumerate((out0, out1))]
    for copy in copies:
        copy.start()
    for copy in copies:
        copy.wait()


def cut(pair):
    shape = jax.ShapeDtypeStruct(pair.shape[1:], pair.dtype)
    return pl.pallas_call(
        cut_kernel,
        out_shape=[shape, shape],
        in_specs=[HBM],
        out_specs=[VMEM, VMEM],
        scratch_shapes=[pltpu.SemaphoreType.DMA((2,))],
        compiler_params=pltpu.CompilerParams(vmem_limit_bytes=1 << 23),
    )(pair)


def merge_kernel(target, head, facts, groups, lengths, got, old, out, ready, sem):
    rlen, width = got.shape[1:]
    token_at = lax.broadcasted_iota(jnp.int32, (rlen, HD), 0)

    def each(act, fill):
        def look(at, slot):
            hit = groups[at] == facts[target]

            @pl.when(hit)
            def _():
                if fill:
                    alive = token_at < lengths[at]
                    for lane in range(0, width, HD):
                        part = got[slot, :, lane:lane + HD]
                        ready[slot, :, lane:lane + HD] = jnp.where(alive, part, jnp.zeros_like(part))
                act(pltpu.make_async_copy(ready.at[slot], out.at[at, :, pl.ds(head * width, width)], sem))

            return slot + hit.astype(jnp.int32)

        lax.fori_loop(0, groups.shape[0], look, jnp.int32(0))

    each(lambda copy: copy.start(), True)
    each(lambda copy: copy.wait(), False)


def merge(facts, target, groups, lengths, got, out, head):
    return pl.pallas_call(
        functools.partial(merge_kernel, target, head),
        out_shape=jax.ShapeDtypeStruct(out.shape, out.dtype),
        in_specs=[SMEM, SMEM, SMEM, VMEM, HBM],
        out_specs=HBM,
        input_output_aliases={4: 0},
        scratch_shapes=[pltpu.VMEM(got.shape, got.dtype), pltpu.SemaphoreType.DMA],
        compiler_params=pltpu.CompilerParams(vmem_limit_bytes=1 << 23),
    )(facts, groups, lengths, got, out)


def after(value, *others):
    return lax.optimization_barrier((value,) + others)[0]


def gathered(queries, resp_kv, prompt_kv, lengths, group_of, first_head, kv_needed, per_kv):
    out = jax.ShapeDtypeStruct(queries.shape, jnp.bfloat16)
    facts = jnp.concatenate([jnp.zeros((GROUPS,), jnp.int32), group_of, lengths])
    for head in range(kv_needed):
        mine = lax.dynamic_index_in_dim(prompt_kv, first_head + head, 2, keepdims=False)
        own = lax.dynamic_index_in_dim(resp_kv, first_head + head, 2, keepdims=False)[None]
        whole = lax.all_gather(mine, "seq", axis=0, tiled=True)
        out, _ = attend(facts, queries, own, [whole], [out], head, per_kv, None, 16, fresh=head == 0)
    return out


def relayed(queries, resp_kv, prompt_kv, lengths, group_of, first_head, per_kv):
    me = lax.axis_index("seq")
    width = per_kv * HD
    middle, inward, outward = [(1, 2), (2, 1)], [(0, 1), (3, 2)], [(1, 0), (2, 3)]

    def send(pairs, value):
        return lax.ppermute(value, "seq", pairs)

    def two_heads(start):
        return lambda pairs: jnp.transpose(pairs[:, start:start + 2], (1, 0, 2))

    def two_own(start):
        return lambda pairs: jnp.transpose(pairs[:, :, start:start + 2], (2, 0, 1, 3))

    splits = prompt_kv.shape[2] // 2
    mine = lax.switch(first_head // 2, [two_heads(2 * at) for at in range(splits)], prompt_kv[0])
    across = send(middle, mine)
    inner_prompt = send(outward, mine)
    near = [send(inward, part) for part in cut(mine)]

    low = me < 2
    is_inner = (me == 1) | (me == 2)
    outer, inner = jnp.where(low, 0, 3), jnp.where(low, 1, 2)
    far_inner, far_outer = jnp.where(low, 2, 1), jnp.where(low, 3, 0)
    facts = jnp.stack([
        me,
        jnp.zeros_like(me),
        jnp.where(is_inner, -1, inner),
        jnp.full_like(me, 2),
        jnp.where(is_inner, far_inner, -1),
        jnp.ones_like(me),
        jnp.where(is_inner, far_outer, -1),
        jnp.where(is_inner, far_outer, far_inner),
        jnp.where(is_inner, 0, 1),
        jnp.where(is_inner, -1, far_outer),
        jnp.where(is_inner, outer, -1),
    ]).astype(jnp.int32)
    facts = jnp.concatenate([facts, group_of, lengths])

    own = lax.switch(first_head // 2, [two_own(2 * at) for at in range(splits)], resp_kv)
    packed = pack(facts, 9, queries, own, width)
    out = jax.ShapeDtypeStruct(queries.shape, jnp.bfloat16)
    back_shape = jax.ShapeDtypeStruct((SLOTS, queries.shape[1], width), jnp.bfloat16)

    def run(cands, outs, passes, items, far=None, fresh=False, wait_for=None):
        return attend(facts, queries, own, cands, outs, 0, per_kv, passes, items, far, fresh, wait_for)

    out, token = run([mine], [out], [(False, 0, 1, 0), (False, 0, 1, 1)], 8, fresh=True, wait_for=packed)
    near[0] = gate(near[0], token)
    last = [send(middle, near[0])]
    handed = send(inward, gate(packed, near[0]))
    out, token = run([near[0]], [out], [(False, 10, 1, 0)], 4)
    near[1] = gate(near[1], token)
    last.append(send(middle, near[1]))
    across = gate(across, token, inner_prompt)
    far_inner_prompt = [send(outward, part) for part in cut(across)]
    out, _ = run(
        [near[1], across, inner_prompt], [out],
        [(False, 2, 3, 0), (False, 2, 3, 1), (False, 10, 1, 1), (False, 4, 5, 0), (False, 4, 5, 1)], 16, wait_for=near[1])
    back = [None, None]
    out, back[0], _ = run(
        [last[0], far_inner_prompt[0]], [out, back_shape], [(True, 6, 1, 0), (False, 7, 8, 0)], 8, handed)
    back[0] = send(outward, back[0])
    out, back[1], _ = run([last[1]], [out, back_shape], [(True, 6, 1, 1)], 4, handed)
    back[1] = send(outward, back[1])
    out, _ = run([last[1], far_inner_prompt[1]], [out], [(False, 7, 8, 1)], 4)
    for head in range(2):
        out = merge(facts, 9, group_of, lengths, back[head], out, head)
    return out


def shards(queries, resp_kv, prompt_kv, lengths, group_of):
    local_heads = queries.shape[2] // HD
    group = QHEADS // KVH
    kv_needed = max(local_heads // group, 1)
    per_kv = local_heads // kv_needed
    first_head = lax.axis_index("pp") * local_heads // group
    args = (queries, resp_kv, prompt_kv, lengths, group_of, first_head)
    if lax.axis_size("seq") == 4 and kv_needed == 2 and prompt_kv.shape[0] == 1:
        return relayed(*args, per_kv)
    return gathered(*args, kv_needed, per_kv)


def solution(mesh):
    placed = (
        P(("rep", "seq"), None, ("tp", "pp")),
        P(("rep", "seq"), None, "tp", None),
        P(("rep", "seq"), None, "tp", None),
        P(("rep", "seq")),
        P(("rep", "seq")),
    )
    return jax.shard_map(
        shards,
        mesh=mesh,
        in_specs=placed,
        out_specs=P(("rep", "seq"), None, ("tp", "pp")),
        check_vma=False,
    )
```

```python
import functools
import math

import jax
import jax.numpy as jnp
from jax import lax
from jax.experimental import pallas as pl
from jax.experimental.pallas import tpu as pltpu
from jax.sharding import PartitionSpec as P

QHEADS = 64
KVH = 8
HD = 128
LOG2E = math.log2(math.e)
LN2 = math.log(2.0)
VMEM_BYTES = 56 * 1024 * 1024
SLOTS = 8
HBM = pl.BlockSpec(memory_space=pl.ANY)
SMEM = pl.BlockSpec(memory_space=pltpu.SMEM)
VMEM = pl.BlockSpec(memory_space=pltpu.VMEM)


TN = (((0,), (0,)), ((), ()))
BLOCK = 512
CHUNK = 32
ONES = 16
GROUPS = 11


def stacked_heads(q_tile, per_kv):
    return jnp.concatenate([q_tile[:, g * HD:(g + 1) * HD] for g in range(per_kv)], axis=0)


def own_scores(own_tile, q_cols, rlen):
    keys = own_tile[:, :HD]
    own = jnp.dot(jnp.concatenate([keys, keys], axis=1), q_cols, preferred_element_type=jnp.float32)
    own_at = lax.broadcasted_iota(jnp.int32, own.shape, 0)
    token_at = lax.broadcasted_iota(jnp.int32, own.shape, 1) % rlen
    return jnp.where(own_at <= token_at, own, -1e30)


def folded(values, op):
    return op(values.reshape(values.shape[0] // 8, 8, values.shape[1]), axis=0)


def weights(power):
    high = power.astype(jnp.bfloat16)
    rest = ((power - high.astype(jnp.float32)) * LN2).astype(jnp.bfloat16)
    coarse = jnp.exp2(high)
    return coarse + coarse * (rest + rest * rest * 0.5)


def turn(q_tile, per_kv, out_ref):
    scaled = stacked_heads(q_tile, per_kv).T.astype(jnp.float32) * (HD ** -0.5 * LOG2E)
    high = scaled.astype(jnp.bfloat16)
    out_ref[:HD, :] = high
    out_ref[HD:, :] = (scaled - high.astype(jnp.float32)).astype(jnp.bfloat16)


def finish(acc_ref, length, per_kv, out_ref):
    out = (acc_ref[:HD, :] * (1.0 / acc_ref[HD:HD + 1, :])).T
    rlen = out_ref.shape[0]
    alive = lax.broadcasted_iota(jnp.int32, (rlen, HD), 0) < length
    for g in range(per_kv):
        part = jnp.where(alive, out[g * rlen:(g + 1) * rlen, :], 0.0)
        out_ref[:, g * HD:(g + 1) * HD] = part.astype(out_ref.dtype)


def scores_and_mix(q_cols, after_own, after_keys, after_s, after_u, after_peak, now):
    plen = after_keys.shape[0]
    own = own_scores(after_own, q_cols, after_own.shape[0])
    after_u[...] = own
    after_top = folded(own, jnp.max)
    if now is not None:
        s_ref, u_ref, peak_ref, own_tile, vt_ref, p_ref, acc_ref = now
        peak = peak_ref[...]
        part = jnp.exp2(u_ref[...] - peak[0:1, :]).astype(jnp.bfloat16)
        own_total = jnp.sum(part.astype(jnp.float32), axis=0, keepdims=True)
        own_acc = lax.dot_general(own_tile[:, HD:], part, TN, preferred_element_type=jnp.float32)
        acc = jnp.concatenate([own_acc, jnp.broadcast_to(own_total, (ONES, own_total.shape[1]))], axis=0)
        spread = jnp.concatenate([peak] * (CHUNK // 8), axis=0)
    for at in range(0, plen, BLOCK):
        rows = pl.ds(at, BLOCK)
        fresh = jnp.dot(after_keys[rows, :], q_cols, preferred_element_type=jnp.float32)
        after_s[rows, :] = fresh
        after_top = jnp.maximum(after_top, folded(fresh, jnp.max))
        if now is not None:
            for chunk in range(at, at + BLOCK, CHUNK):
                p_ref[chunk:chunk + CHUNK, :] = weights(s_ref[chunk:chunk + CHUNK, :] - spread)
            acc = acc + jnp.dot(vt_ref[:, rows], p_ref[rows, :], preferred_element_type=jnp.float32)
    after_peak[...] = jnp.broadcast_to(jnp.max(after_top, axis=0, keepdims=True), after_peak.shape)
    if now is not None:
        acc_ref[...] = acc


def listed(items, cap, count, facts, local, target, source, head):
    def look(at, n):
        hit = facts[GROUPS + at] == target

        @pl.when(hit)
        def _():
            items[n] = at
            items[cap + n] = source
            items[2 * cap + n] = facts[GROUPS + local + at]
            items[3 * cap + n] = head

        return n + hit.astype(jnp.int32)

    return lax.fori_loop(0, local, look, count)


def attend_kernel(passes, n_cand, per_kv, whole_head, two, fresh, waits, *refs):
    refs = list(refs)
    facts, refs = refs[0], refs[1:]
    if two:
        x_ref, refs = refs[0], refs[1:]
    q_ref, own_ref = refs[:2]
    cands, refs = refs[2:2 + n_cand], refs[2 + n_cand + waits:]
    n_out = 2 if two else 1
    if not fresh:
        refs = refs[1:]
    outs, token, refs = refs[:n_out], refs[n_out], refs[n_out + 1:]
    items, at_slot, q_buf, own_buf, key_buf, value_buf, vt_buf, s0, s1, u0, u1, peak0, peak1, turned0, turned1, acc0, acc1, p_buf, o0, o1, info, q_sem, own_sem, kv_sem, o_sem = refs
    s_buf, u_buf, peak_buf, o_buf = (s0, s1), (u0, u1), (peak0, peak1), (o0, o1)
    turned, acc_buf = (turned0, turned1), (acc0, acc1)
    local = (facts.shape[0] - GROUPS) // 2
    cap = items.shape[0] // 4
    width = per_kv * HD
    stacked = passes is None

    count = jnp.int32(0)
    if stacked:
        def one_prompt(prompt, n):
            return listed(items, cap, n, facts, local, prompt, prompt, whole_head)

        count = lax.fori_loop(0, cands[0].shape[0], one_prompt, count)
    else:
        for far, target, source, head in passes:
            if not far:
                count = listed(items, cap, count, facts, local, facts[target], facts[source], head)
                continue
            notes = pltpu.make_async_copy(x_ref.at[0, :, pl.ds(2 * (width + 2 * HD), HD)], info, kv_sem)
            notes.start()
            notes.wait()
            far_head = head
            handed = jnp.max(info[0:16, :].astype(jnp.float32)).astype(jnp.int32)
            handed = jnp.where(facts[target] >= 0, jnp.minimum(handed, SLOTS), 0)

            def take(slot, n):
                items[n] = local + slot
                items[cap + n] = facts[source]
                items[2 * cap + n] = q_buf.shape[1]
                items[3 * cap + n] = far_head
                return n + 1

            count = lax.fori_loop(0, handed, take, count)

    token[0] = count

    def each_array(i, act_local, act_far):
        at = items[i]
        if not two:
            act_local(at)
            return

        @pl.when(at < local)
        def _():
            act_local(at)

        @pl.when(at >= local)
        def _():
            act_far(at - local)

    first = pl.ds(0, width)

    def lanes(i, step, skip, size):
        return pl.ds(pl.multiple_of(items[3 * cap + i] * step + skip, HD), size)

    def mine(i):
        return lanes(i, width, 0, width)

    def fetch(i):
        slot, fourth = lax.rem(i, 2), lax.rem(i, 4)

        def here(at):
            pltpu.make_async_copy(q_ref.at[at, :, mine(i)], q_buf.at[slot], q_sem.at[slot]).start()
            pltpu.make_async_copy(own_ref.at[items[3 * cap + i], at], own_buf.at[fourth], own_sem.at[fourth]).start()

        def far(at):
            pltpu.make_async_copy(x_ref.at[at, :, lanes(i, width + 2 * HD, 0, width)], q_buf.at[slot], q_sem.at[slot]).start()
            pltpu.make_async_copy(x_ref.at[at, :, lanes(i, width + 2 * HD, width, 2 * HD)], own_buf.at[fourth], own_sem.at[fourth]).start()

        each_array(i, here, far)

    def fetched(i):
        slot, fourth = lax.rem(i, 2), lax.rem(i, 4)
        pltpu.make_async_copy(q_ref.at[0, :, first], q_buf.at[slot], q_sem.at[slot]).wait()
        pltpu.make_async_copy(own_ref.at[0, 0], own_buf.at[fourth], own_sem.at[fourth]).wait()

    def store(i, slot):
        def here(at):
            pltpu.make_async_copy(o_buf[slot], outs[0].at[at, :, mine(i)], o_sem.at[slot]).start()

        def far(at):
            pltpu.make_async_copy(o_buf[slot], outs[1].at[at], o_sem.at[slot]).start()

        each_array(i, here, far)

    def stored(slot):
        pltpu.make_async_copy(o_buf[slot], outs[0].at[0, :, first], o_sem.at[slot]).wait()

    keys, values = pl.ds(0, HD), pl.ds(HD, HD)

    def ask(i, into):
        source = items[cap + i]

        def bring(pairs):
            for twin in (keys, values):
                pltpu.make_async_copy(pairs.at[:, keys], key_buf.at[into, :, twin], kv_sem).start()
            pltpu.make_async_copy(pairs.at[:, values], value_buf, kv_sem).start()

        if stacked:
            bring(cands[0].at[source])
        else:
            for which in range(n_cand):
                @pl.when(source == which)
                def _():
                    bring(cands[which].at[items[3 * cap + i]] if len(cands[which].shape) == 3 else cands[which])

    def receive(into):
        for _ in range(3):
            pltpu.make_async_copy(value_buf, value_buf, kv_sem).wait()
        vt_buf[into, :HD, :] = value_buf[...].T

    @pl.when(count > 0)
    def _():
        ask(0, 0)
        fetch(jnp.int32(0))
        vt_buf[:, HD:, :] = jnp.ones((2, ONES, vt_buf.shape[2]), vt_buf.dtype)

        @pl.when(count > 1)
        def _():
            fetch(jnp.int32(1))

        at_slot[0] = 0
        fetched(jnp.int32(0))
        turn(q_buf[0], per_kv, turned[0])

        @pl.when(count > 2)
        def _():
            fetch(jnp.int32(2))

        @pl.when(count > 1)
        def _():
            fetched(jnp.int32(1))

        turn(q_buf[1], per_kv, turned[1])
        receive(0)
        scores_and_mix(turned[0][...], own_buf[0], key_buf.at[0], s_buf[0], u_buf[0], peak_buf[0], None)

        def one(i, slot):
            other = 1 - slot
            held = at_slot[0]
            more = i + 1 < count
            after_i = jnp.minimum(i + 1, count - 1)
            moved = more & ((items[cap + after_i] != items[cap + i]) | (items[3 * cap + after_i] != items[3 * cap + i]))
            holds = jnp.where(moved, 1 - held, held)
            at_slot[0] = holds

            @pl.when(i + 2 < count)
            def _():
                fetched(i + 2)

            @pl.when(i + 3 < count)
            def _():
                fetch(i + 3)

            @pl.when(moved)
            def _():
                ask(i + 1, holds)
                receive(holds)

            @pl.when(i >= 3)
            def _():
                stored(other)

            now = (
                s_buf[slot], u_buf[slot], peak_buf[slot], own_buf[lax.rem(i, 4)], vt_buf.at[held], p_buf,
                acc_buf[slot])
            scores_and_mix(
                turned[other][...], own_buf[lax.rem(i + 1, 4)], key_buf.at[holds],
                s_buf[other], u_buf[other], peak_buf[other], now)
            turn(q_buf[slot], per_kv, turned[slot])
            finish(acc_buf[other], items[2 * cap + jnp.maximum(i - 1, 0)], per_kv, o_buf[other])

            @pl.when(i >= 1)
            def _():
                store(i - 1, other)

        def pair(j, _):
            one(2 * j, 0)

            @pl.when(2 * j + 1 < count)
            def _():
                one(2 * j + 1, 1)

            return 0

        lax.fori_loop(0, lax.div(count + 1, 2), pair, 0)
        final = count - 1
        for slot in range(2):
            @pl.when(lax.rem(final, 2) == slot)
            def _():
                @pl.when(final >= 2)
                def _():
                    stored(slot)

                finish(acc_buf[slot], items[2 * cap + final], per_kv, o_buf[slot])
                store(final, slot)

        stored(0)

        @pl.when(count > 1)
        def _():
            stored(1)


def attend(facts, queries, own, cands, outs, head, per_kv, passes, items, far=None, fresh=False, wait_for=None):
    rlen = queries.shape[1]
    plen = cands[0].shape[-2]
    width = per_kv * HD
    small = [facts]
    large = ([far] if far is not None else []) + [queries, own] + cands
    operands = small + large + ([] if wait_for is None else [wait_for])
    aliases = {}
    if not fresh:
        aliases = {len(operands): 0}
        operands = operands + [outs[0]]
    cap = 2 * queries.shape[0] + (SLOTS if far is not None else 0)
    return pl.pallas_call(
        functools.partial(attend_kernel, passes, len(cands), per_kv, head, far is not None, fresh, wait_for is not None),
        out_shape=[jax.ShapeDtypeStruct(o.shape, o.dtype) for o in outs] + [jax.ShapeDtypeStruct((1,), jnp.int32)],
        in_specs=[SMEM] * len(small) + [HBM] * (len(operands) - len(small)),
        out_specs=[HBM] * len(outs) + [SMEM],
        input_output_aliases=aliases,
        scratch_shapes=[
            pltpu.SMEM((4 * cap,), jnp.int32),
            pltpu.SMEM((1,), jnp.int32),
            pltpu.VMEM((2, rlen, width), jnp.bfloat16),
            pltpu.VMEM((4, rlen, 2 * HD), jnp.bfloat16),
            pltpu.VMEM((2, plen, 2 * HD), jnp.bfloat16),
            pltpu.VMEM((plen, HD), jnp.bfloat16),
            pltpu.VMEM((2, HD + ONES, plen), jnp.bfloat16),
            pltpu.VMEM((plen, per_kv * rlen), jnp.float32),
            pltpu.VMEM((plen, per_kv * rlen), jnp.float32),
            pltpu.VMEM((rlen, per_kv * rlen), jnp.float32),
            pltpu.VMEM((rlen, per_kv * rlen), jnp.float32),
            pltpu.VMEM((8, per_kv * rlen), jnp.float32),
            pltpu.VMEM((8, per_kv * rlen), jnp.float32),
            pltpu.VMEM((2 * HD, per_kv * rlen), jnp.bfloat16),
            pltpu.VMEM((2 * HD, per_kv * rlen), jnp.bfloat16),
            pltpu.VMEM((HD + ONES, per_kv * rlen), jnp.float32),
            pltpu.VMEM((HD + ONES, per_kv * rlen), jnp.float32),
            pltpu.VMEM((plen, per_kv * rlen), jnp.bfloat16),
            pltpu.VMEM((rlen, width), jnp.bfloat16),
            pltpu.VMEM((rlen, width), jnp.bfloat16),
            pltpu.VMEM((rlen, HD), jnp.bfloat16),
            pltpu.SemaphoreType.DMA((2,)),
            pltpu.SemaphoreType.DMA((4,)),
            pltpu.SemaphoreType.DMA,
            pltpu.SemaphoreType.DMA((2,)),
        ],
        compiler_params=pltpu.CompilerParams(vmem_limit_bytes=VMEM_BYTES),
        cost_estimate=pl.CostEstimate(flops=items << 20, bytes_accessed=1 << 16, transcendentals=0),
    )(*operands)


def pack_kernel(target, width, facts, q_ref, own_ref, out, sem):
    step = width + 2 * HD
    local = q_ref.shape[0]

    def each(act):
        def look(at, slot):
            hit = facts[GROUPS + at] == facts[target]

            @pl.when(hit)
            def _():
                for head in range(2):
                    part = pl.ds(head * width, width)
                    act(pltpu.make_async_copy(q_ref.at[at, :, part], out.at[slot, :, pl.ds(head * step, width)], sem))
                    act(pltpu.make_async_copy(
                        own_ref.at[head, at], out.at[slot, :, pl.ds(head * step + width, 2 * HD)], sem))

            return slot + hit.astype(jnp.int32)

        return lax.fori_loop(0, local, look, jnp.int32(0))

    count = each(lambda copy: copy.start())
    out[0, :, 2 * step:] = jnp.full((out.shape[1], HD), count, jnp.int32).astype(jnp.float32).astype(out.dtype)
    each(lambda copy: copy.wait())


def pack(facts, target, queries, own, width):
    return pl.pallas_call(
        functools.partial(pack_kernel, target, width),
        out_shape=jax.ShapeDtypeStruct((SLOTS, queries.shape[1], 2 * width + 5 * HD), queries.dtype),
        in_specs=[SMEM, HBM, HBM],
        out_specs=VMEM,
        scratch_shapes=[pltpu.SemaphoreType.DMA],
        compiler_params=pltpu.CompilerParams(vmem_limit_bytes=1 << 23),
    )(facts, queries, own)


def gate_kernel(*refs):
    pass


def gate(value, *others):
    return pl.pallas_call(
        gate_kernel,
        out_shape=jax.ShapeDtypeStruct(value.shape, value.dtype),
        in_specs=[HBM] + [SMEM if other.ndim == 1 else HBM for other in others],
        out_specs=HBM,
        input_output_aliases={0: 0},
    )(value, *others)


def cut_kernel(pair, out0, out1, sem):
    copies = [pltpu.make_async_copy(pair.at[head], out, sem.at[head]) for head, out in enumerate((out0, out1))]
    for copy in copies:
        copy.start()
    for copy in copies:
        copy.wait()


def cut(pair):
    shape = jax.ShapeDtypeStruct(pair.shape[1:], pair.dtype)
    return pl.pallas_call(
        cut_kernel,
        out_shape=[shape, shape],
        in_specs=[HBM],
        out_specs=[VMEM, VMEM],
        scratch_shapes=[pltpu.SemaphoreType.DMA((2,))],
        compiler_params=pltpu.CompilerParams(vmem_limit_bytes=1 << 23),
    )(pair)


def merge_kernel(target, head, facts, groups, lengths, got, old, out, ready, sem):
    rlen, width = got.shape[1:]
    token_at = lax.broadcasted_iota(jnp.int32, (rlen, HD), 0)

    def each(act, fill):
        def look(at, slot):
            hit = groups[at] == facts[target]

            @pl.when(hit)
            def _():
                if fill:
                    alive = token_at < lengths[at]
                    for lane in range(0, width, HD):
                        part = got[slot, :, lane:lane + HD]
                        ready[slot, :, lane:lane + HD] = jnp.where(alive, part, jnp.zeros_like(part))
                act(pltpu.make_async_copy(ready.at[slot], out.at[at, :, pl.ds(head * width, width)], sem))

            return slot + hit.astype(jnp.int32)

        lax.fori_loop(0, groups.shape[0], look, jnp.int32(0))

    each(lambda copy: copy.start(), True)
    each(lambda copy: copy.wait(), False)


def merge(facts, target, groups, lengths, got, out, head):
    return pl.pallas_call(
        functools.partial(merge_kernel, target, head),
        out_shape=jax.ShapeDtypeStruct(out.shape, out.dtype),
        in_specs=[SMEM, SMEM, SMEM, VMEM, HBM],
        out_specs=HBM,
        input_output_aliases={4: 0},
        scratch_shapes=[pltpu.VMEM(got.shape, got.dtype), pltpu.SemaphoreType.DMA],
        compiler_params=pltpu.CompilerParams(vmem_limit_bytes=1 << 23),
    )(facts, groups, lengths, got, out)


def after(value, *others):
    return lax.optimization_barrier((value,) + others)[0]


def gathered(queries, resp_kv, prompt_kv, lengths, group_of, first_head, kv_needed, per_kv):
    out = jax.ShapeDtypeStruct(queries.shape, jnp.bfloat16)
    facts = jnp.concatenate([jnp.zeros((GROUPS,), jnp.int32), group_of, lengths])
    for head in range(kv_needed):
        mine = lax.dynamic_index_in_dim(prompt_kv, first_head + head, 2, keepdims=False)
        own = lax.dynamic_index_in_dim(resp_kv, first_head + head, 2, keepdims=False)[None]
        whole = lax.all_gather(mine, "seq", axis=0, tiled=True)
        out, _ = attend(facts, queries, own, [whole], [out], head, per_kv, None, 16, fresh=head == 0)
    return out


def relayed(queries, resp_kv, prompt_kv, lengths, group_of, first_head, per_kv):
    me = lax.axis_index("seq")
    width = per_kv * HD
    middle, inward, outward = [(1, 2), (2, 1)], [(0, 1), (3, 2)], [(1, 0), (2, 3)]

    def send(pairs, value):
        return lax.ppermute(value, "seq", pairs)

    def two_heads(start):
        return lambda pairs: jnp.transpose(pairs[:, start:start + 2], (1, 0, 2))

    def two_own(start):
        return lambda pairs: jnp.transpose(pairs[:, :, start:start + 2], (2, 0, 1, 3))

    splits = prompt_kv.shape[2] // 2
    mine = lax.switch(first_head // 2, [two_heads(2 * at) for at in range(splits)], prompt_kv[0])
    across = send(middle, mine)
    inner_prompt = send(outward, mine)
    near = [send(inward, part) for part in cut(mine)]

    low = me < 2
    is_inner = (me == 1) | (me == 2)
    outer, inner = jnp.where(low, 0, 3), jnp.where(low, 1, 2)
    far_inner, far_outer = jnp.where(low, 2, 1), jnp.where(low, 3, 0)
    facts = jnp.stack([
        me,
        jnp.zeros_like(me),
        jnp.where(is_inner, -1, inner),
        jnp.full_like(me, 2),
        jnp.where(is_inner, far_inner, -1),
        jnp.ones_like(me),
        jnp.where(is_inner, far_outer, -1),
        jnp.where(is_inner, far_outer, far_inner),
        jnp.where(is_inner, 0, 1),
        jnp.where(is_inner, -1, far_outer),
        jnp.where(is_inner, outer, -1),
    ]).astype(jnp.int32)
    facts = jnp.concatenate([facts, group_of, lengths])

    own = lax.switch(first_head // 2, [two_own(2 * at) for at in range(splits)], resp_kv)
    packed = pack(facts, 9, queries, own, width)
    out = jax.ShapeDtypeStruct(queries.shape, jnp.bfloat16)
    back_shape = jax.ShapeDtypeStruct((SLOTS, queries.shape[1], width), jnp.bfloat16)

    def run(cands, outs, passes, items, far=None, fresh=False, wait_for=None):
        return attend(facts, queries, own, cands, outs, 0, per_kv, passes, items, far, fresh, wait_for)

    out, token = run([mine], [out], [(False, 0, 1, 0), (False, 0, 1, 1)], 8, fresh=True, wait_for=packed)
    near[0] = gate(near[0], token)
    last = [send(middle, near[0])]
    handed = send(inward, gate(packed, near[0]))
    out, token = run([near[0]], [out], [(False, 10, 1, 0)], 4)
    near[1] = gate(near[1], token)
    last.append(send(middle, near[1]))
    across = gate(across, token, inner_prompt)
    far_inner_prompt = [send(outward, part) for part in cut(across)]
    out, _ = run(
        [near[1], across, inner_prompt], [out],
        [(False, 2, 3, 0), (False, 2, 3, 1), (False, 10, 1, 1), (False, 4, 5, 0), (False, 4, 5, 1)], 16, wait_for=near[1])
    back = [None, None]
    out, back[0], _ = run(
        [last[0], far_inner_prompt[0]], [out, back_shape], [(True, 6, 1, 0), (False, 7, 8, 0)], 8, handed)
    back[0] = send(outward, back[0])
    out, back[1], _ = run([last[1]], [out, back_shape], [(True, 6, 1, 1)], 4, handed)
    back[1] = send(outward, back[1])
    out, _ = run([last[1], far_inner_prompt[1]], [out], [(False, 7, 8, 1)], 4)
    for head in range(2):
        out = merge(facts, 9, group_of, lengths, back[head], out, head)
    return out


def shards(queries, resp_kv, prompt_kv, lengths, group_of):
    local_heads = queries.shape[2] // HD
    group = QHEADS // KVH
    kv_needed = max(local_heads // group, 1)
    per_kv = local_heads // kv_needed
    first_head = lax.axis_index("pp") * local_heads // group
    args = (queries, resp_kv, prompt_kv, lengths, group_of, first_head)
    if lax.axis_size("seq") == 4 and kv_needed == 2 and prompt_kv.shape[0] == 1:
        return relayed(*args, per_kv)
    return gathered(*args, kv_needed, per_kv)


def solution(mesh):
    placed = (
        P(("rep", "seq"), None, ("tp", "pp")),
        P(("rep", "seq"), None, "tp", None),
        P(("rep", "seq"), None, "tp", None),
        P(("rep", "seq")),
        P(("rep", "seq")),
    )
    return jax.shard_map(
        shards,
        mesh=mesh,
        in_specs=placed,
        out_specs=P(("rep", "seq"), None, ("tp", "pp")),
        check_vma=False,
    )
```

```python
import functools
import math

import jax
import jax.numpy as jnp
from jax import lax
from jax.experimental import pallas as pl
from jax.experimental.pallas import tpu as pltpu
from jax.sharding import PartitionSpec as P

QHEADS = 64
KVH = 8
HD = 128
LOG2E = math.log2(math.e)
VMEM_BYTES = 56 * 1024 * 1024
SLOTS = 8
HBM = pl.BlockSpec(memory_space=pl.ANY)
SMEM = pl.BlockSpec(memory_space=pltpu.SMEM)
VMEM = pl.BlockSpec(memory_space=pltpu.VMEM)


TN = (((0,), (0,)), ((), ()))
BLOCK = 512
SCORE_BLOCK = 1024
CHUNK = 32
GROUPS = 11


def stacked_heads(q_tile, per_kv):
    return jnp.concatenate([q_tile[:, g * HD:(g + 1) * HD] for g in range(per_kv)], axis=0)


def own_scores(own_tile, q_cols, rlen):
    own = jnp.dot(own_tile[:, :HD], q_cols, preferred_element_type=jnp.float32)
    own_at = lax.broadcasted_iota(jnp.int32, own.shape, 0)
    token_at = lax.broadcasted_iota(jnp.int32, own.shape, 1) % rlen
    return jnp.where(own_at <= token_at, own, -1e30)


def folded(values, op):
    return op(values.reshape(values.shape[0] // 8, 8, values.shape[1]), axis=0)


def turn(q_tile, per_kv, out_ref):
    out_ref[...] = stacked_heads(q_tile, per_kv).T


def finish(acc_ref, total_ref, length, per_kv, out_ref):
    out = (acc_ref[...] * (1.0 / total_ref[0:1, :])).T
    rlen = out_ref.shape[0]
    alive = lax.broadcasted_iota(jnp.int32, (rlen, HD), 0) < length
    for g in range(per_kv):
        part = jnp.where(alive, out[g * rlen:(g + 1) * rlen, :], 0.0)
        out_ref[:, g * HD:(g + 1) * HD] = part.astype(out_ref.dtype)


def scores_and_mix(q_cols, after_own, after_keys, after_s, after_u, after_peak, now):
    plen = after_keys.shape[0]
    scale = HD ** -0.5 * LOG2E
    own = own_scores(after_own, q_cols, after_own.shape[0])
    after_u[...] = own
    after_top = folded(own, jnp.max)
    if now is not None:
        s_ref, u_ref, peak_ref, own_tile, vt_ref, p_ref, acc_ref, total_ref = now
        peak = peak_ref[...]
        part = jnp.exp2((u_ref[...] - peak[0:1, :]) * scale)
        total = folded(part, jnp.sum)
        acc = lax.dot_general(own_tile[:, HD:], part.astype(jnp.bfloat16), TN, preferred_element_type=jnp.float32)
        spread = jnp.concatenate([peak] * (CHUNK // 8), axis=0)
    for at in range(0, plen, BLOCK):
        rows = pl.ds(at, BLOCK)
        if at % SCORE_BLOCK == 0:
            score_rows = pl.ds(at, SCORE_BLOCK)
            fresh = jnp.dot(after_keys[score_rows, :], q_cols, preferred_element_type=jnp.float32)
            after_s[score_rows, :] = fresh
            after_top = jnp.maximum(after_top, folded(fresh, jnp.max))
        if now is not None:
            for chunk in range(at, at + BLOCK, CHUNK):
                part = jnp.exp2((s_ref[chunk:chunk + CHUNK, :] - spread) * scale)
                total = total + folded(part, jnp.sum)
                p_ref[chunk:chunk + CHUNK, :] = part.astype(jnp.bfloat16)
            acc = acc + jnp.dot(vt_ref[:, rows], p_ref[rows, :], preferred_element_type=jnp.float32)
    after_peak[...] = jnp.broadcast_to(jnp.max(after_top, axis=0, keepdims=True), after_peak.shape)
    if now is not None:
        acc_ref[...] = acc
        total_ref[...] = jnp.broadcast_to(jnp.sum(total, axis=0, keepdims=True), total_ref.shape)


def listed(items, cap, count, facts, local, target, source, head):
    def look(at, n):
        hit = facts[GROUPS + at] == target

        @pl.when(hit)
        def _():
            items[n] = at
            items[cap + n] = source
            items[2 * cap + n] = facts[GROUPS + local + at]
            items[3 * cap + n] = head

        return n + hit.astype(jnp.int32)

    return lax.fori_loop(0, local, look, count)


def attend_kernel(passes, n_cand, per_kv, whole_head, two, fresh, waits, *refs):
    refs = list(refs)
    facts, refs = refs[0], refs[1:]
    if two:
        x_ref, refs = refs[0], refs[1:]
    q_ref, own_ref = refs[:2]
    cands, refs = refs[2:2 + n_cand], refs[2 + n_cand + waits:]
    n_out = 2 if two else 1
    if not fresh:
        refs = refs[1:]
    outs, token, refs = refs[:n_out], refs[n_out], refs[n_out + 1:]
    items, at_slot, q_buf, own_buf, key_buf, value_buf, vt_buf, s0, s1, u0, u1, peak0, peak1, turned0, turned1, acc0, acc1, total0, total1, p_buf, o0, o1, info, q_sem, own_sem, kv_sem, o_sem = refs
    s_buf, u_buf, peak_buf, o_buf = (s0, s1), (u0, u1), (peak0, peak1), (o0, o1)
    turned, acc_buf, total_buf = (turned0, turned1), (acc0, acc1), (total0, total1)
    local = (facts.shape[0] - GROUPS) // 2
    cap = items.shape[0] // 4
    width = per_kv * HD
    stacked = passes is None

    count = jnp.int32(0)
    if stacked:
        def one_prompt(prompt, n):
            return listed(items, cap, n, facts, local, prompt, prompt, whole_head)

        count = lax.fori_loop(0, cands[0].shape[0], one_prompt, count)
    else:
        for far, target, source, head in passes:
            if not far:
                count = listed(items, cap, count, facts, local, facts[target], facts[source], head)
                continue
            notes = pltpu.make_async_copy(x_ref.at[0, :, pl.ds(2 * (width + 2 * HD), HD)], info, kv_sem)
            notes.start()
            notes.wait()
            far_head = head
            handed = jnp.max(info[0:16, :].astype(jnp.float32)).astype(jnp.int32)
            handed = jnp.where(facts[target] >= 0, jnp.minimum(handed, SLOTS), 0)

            def take(slot, n):
                items[n] = local + slot
                items[cap + n] = facts[source]
                items[2 * cap + n] = q_buf.shape[1]
                items[3 * cap + n] = far_head
                return n + 1

            count = lax.fori_loop(0, handed, take, count)

    token[0] = count

    def each_array(i, act_local, act_far):
        at = items[i]
        if not two:
            act_local(at)
            return

        @pl.when(at < local)
        def _():
            act_local(at)

        @pl.when(at >= local)
        def _():
            act_far(at - local)

    first = pl.ds(0, width)

    def lanes(i, step, skip, size):
        return pl.ds(pl.multiple_of(items[3 * cap + i] * step + skip, HD), size)

    def mine(i):
        return lanes(i, width, 0, width)

    def fetch(i):
        slot, fourth = lax.rem(i, 2), lax.rem(i, 4)

        def here(at):
            pltpu.make_async_copy(q_ref.at[at, :, mine(i)], q_buf.at[slot], q_sem.at[slot]).start()
            pltpu.make_async_copy(own_ref.at[items[3 * cap + i], at], own_buf.at[fourth], own_sem.at[fourth]).start()

        def far(at):
            pltpu.make_async_copy(x_ref.at[at, :, lanes(i, width + 2 * HD, 0, width)], q_buf.at[slot], q_sem.at[slot]).start()
            pltpu.make_async_copy(x_ref.at[at, :, lanes(i, width + 2 * HD, width, 2 * HD)], own_buf.at[fourth], own_sem.at[fourth]).start()

        each_array(i, here, far)

    def fetched(i):
        slot, fourth = lax.rem(i, 2), lax.rem(i, 4)
        pltpu.make_async_copy(q_ref.at[0, :, first], q_buf.at[slot], q_sem.at[slot]).wait()
        pltpu.make_async_copy(own_ref.at[0, 0], own_buf.at[fourth], own_sem.at[fourth]).wait()

    def store(i, slot):
        def here(at):
            pltpu.make_async_copy(o_buf[slot], outs[0].at[at, :, mine(i)], o_sem.at[slot]).start()

        def far(at):
            pltpu.make_async_copy(o_buf[slot], outs[1].at[at], o_sem.at[slot]).start()

        each_array(i, here, far)

    def stored(slot):
        pltpu.make_async_copy(o_buf[slot], outs[0].at[0, :, first], o_sem.at[slot]).wait()

    keys, values = pl.ds(0, HD), pl.ds(HD, HD)

    def ask(i, into):
        source = items[cap + i]

        def bring(pairs):
            pltpu.make_async_copy(pairs.at[:, keys], key_buf.at[into], kv_sem).start()
            pltpu.make_async_copy(pairs.at[:, values], value_buf, kv_sem).start()

        if stacked:
            bring(cands[0].at[source])
        else:
            for which in range(n_cand):
                @pl.when(source == which)
                def _():
                    bring(cands[which].at[items[3 * cap + i]] if len(cands[which].shape) == 3 else cands[which])

    def receive(into):
        for _ in range(2):
            pltpu.make_async_copy(value_buf, value_buf, kv_sem).wait()
        vt_buf[into] = value_buf[...].T

    @pl.when(count > 0)
    def _():
        ask(0, 0)
        fetch(jnp.int32(0))

        @pl.when(count > 1)
        def _():
            fetch(jnp.int32(1))

        at_slot[0] = 0
        fetched(jnp.int32(0))
        turn(q_buf[0], per_kv, turned[0])

        @pl.when(count > 2)
        def _():
            fetch(jnp.int32(2))

        @pl.when(count > 1)
        def _():
            fetched(jnp.int32(1))

        turn(q_buf[1], per_kv, turned[1])
        receive(0)
        scores_and_mix(turned[0][...], own_buf[0], key_buf.at[0], s_buf[0], u_buf[0], peak_buf[0], None)

        def one(i, slot):
            other = 1 - slot
            held = at_slot[0]
            more = i + 1 < count
            after_i = jnp.minimum(i + 1, count - 1)
            moved = more & ((items[cap + after_i] != items[cap + i]) | (items[3 * cap + after_i] != items[3 * cap + i]))
            holds = jnp.where(moved, 1 - held, held)
            at_slot[0] = holds

            @pl.when(i + 2 < count)
            def _():
                fetched(i + 2)

            @pl.when(i + 3 < count)
            def _():
                fetch(i + 3)

            @pl.when(moved)
            def _():
                ask(i + 1, holds)
                receive(holds)

            @pl.when(i >= 3)
            def _():
                stored(other)

            now = (
                s_buf[slot], u_buf[slot], peak_buf[slot], own_buf[lax.rem(i, 4)], vt_buf.at[held], p_buf,
                acc_buf[slot], total_buf[slot])
            scores_and_mix(
                turned[other][...], own_buf[lax.rem(i + 1, 4)], key_buf.at[holds],
                s_buf[other], u_buf[other], peak_buf[other], now)
            turn(q_buf[slot], per_kv, turned[slot])
            finish(acc_buf[other], total_buf[other], items[2 * cap + jnp.maximum(i - 1, 0)], per_kv, o_buf[other])

            @pl.when(i >= 1)
            def _():
                store(i - 1, other)

        def pair(j, _):
            one(2 * j, 0)

            @pl.when(2 * j + 1 < count)
            def _():
                one(2 * j + 1, 1)

            return 0

        lax.fori_loop(0, lax.div(count + 1, 2), pair, 0)
        final = count - 1
        for slot in range(2):
            @pl.when(lax.rem(final, 2) == slot)
            def _():
                @pl.when(final >= 2)
                def _():
                    stored(slot)

                finish(acc_buf[slot], total_buf[slot], items[2 * cap + final], per_kv, o_buf[slot])
                store(final, slot)

        stored(0)

        @pl.when(count > 1)
        def _():
            stored(1)


def attend(facts, queries, own, cands, outs, head, per_kv, passes, items, far=None, fresh=False, wait_for=None):
    rlen = queries.shape[1]
    plen = cands[0].shape[-2]
    width = per_kv * HD
    small = [facts]
    large = ([far] if far is not None else []) + [queries, own] + cands
    operands = small + large + ([] if wait_for is None else [wait_for])
    aliases = {}
    if not fresh:
        aliases = {len(operands): 0}
        operands = operands + [outs[0]]
    cap = 2 * queries.shape[0] + (SLOTS if far is not None else 0)
    return pl.pallas_call(
        functools.partial(attend_kernel, passes, len(cands), per_kv, head, far is not None, fresh, wait_for is not None),
        out_shape=[jax.ShapeDtypeStruct(o.shape, o.dtype) for o in outs] + [jax.ShapeDtypeStruct((1,), jnp.int32)],
        in_specs=[SMEM] * len(small) + [HBM] * (len(operands) - len(small)),
        out_specs=[HBM] * len(outs) + [SMEM],
        input_output_aliases=aliases,
        scratch_shapes=[
            pltpu.SMEM((4 * cap,), jnp.int32),
            pltpu.SMEM((1,), jnp.int32),
            pltpu.VMEM((2, rlen, width), jnp.bfloat16),
            pltpu.VMEM((4, rlen, 2 * HD), jnp.bfloat16),
            pltpu.VMEM((2, plen, HD), jnp.bfloat16),
            pltpu.VMEM((plen, HD), jnp.bfloat16),
            pltpu.VMEM((2, HD, plen), jnp.bfloat16),
            pltpu.VMEM((plen, per_kv * rlen), jnp.float32),
            pltpu.VMEM((plen, per_kv * rlen), jnp.float32),
            pltpu.VMEM((rlen, per_kv * rlen), jnp.float32),
            pltpu.VMEM((rlen, per_kv * rlen), jnp.float32),
            pltpu.VMEM((8, per_kv * rlen), jnp.float32),
            pltpu.VMEM((8, per_kv * rlen), jnp.float32),
            pltpu.VMEM((HD, per_kv * rlen), jnp.bfloat16),
            pltpu.VMEM((HD, per_kv * rlen), jnp.bfloat16),
            pltpu.VMEM((HD, per_kv * rlen), jnp.float32),
            pltpu.VMEM((HD, per_kv * rlen), jnp.float32),
            pltpu.VMEM((8, per_kv * rlen), jnp.float32),
            pltpu.VMEM((8, per_kv * rlen), jnp.float32),
            pltpu.VMEM((plen, per_kv * rlen), jnp.bfloat16),
            pltpu.VMEM((rlen, width), jnp.bfloat16),
            pltpu.VMEM((rlen, width), jnp.bfloat16),
            pltpu.VMEM((rlen, HD), jnp.bfloat16),
            pltpu.SemaphoreType.DMA((2,)),
            pltpu.SemaphoreType.DMA((4,)),
            pltpu.SemaphoreType.DMA,
            pltpu.SemaphoreType.DMA((2,)),
        ],
        compiler_params=pltpu.CompilerParams(vmem_limit_bytes=VMEM_BYTES),
        cost_estimate=pl.CostEstimate(flops=items << 20, bytes_accessed=1 << 16, transcendentals=0),
    )(*operands)


def pack_kernel(target, width, facts, q_ref, own_ref, out, sem):
    step = width + 2 * HD
    local = q_ref.shape[0]

    def each(act):
        def look(at, slot):
            hit = facts[GROUPS + at] == facts[target]

            @pl.when(hit)
            def _():
                for head in range(2):
                    part = pl.ds(head * width, width)
                    act(pltpu.make_async_copy(q_ref.at[at, :, part], out.at[slot, :, pl.ds(head * step, width)], sem))
                    act(pltpu.make_async_copy(
                        own_ref.at[head, at], out.at[slot, :, pl.ds(head * step + width, 2 * HD)], sem))

            return slot + hit.astype(jnp.int32)

        return lax.fori_loop(0, local, look, jnp.int32(0))

    count = each(lambda copy: copy.start())
    out[0, :, 2 * step:] = jnp.full((out.shape[1], HD), count, jnp.int32).astype(jnp.float32).astype(out.dtype)
    each(lambda copy: copy.wait())


def pack(facts, target, queries, own, width):
    return pl.pallas_call(
        functools.partial(pack_kernel, target, width),
        out_shape=jax.ShapeDtypeStruct((SLOTS, queries.shape[1], 2 * width + 5 * HD), queries.dtype),
        in_specs=[SMEM, HBM, HBM],
        out_specs=VMEM,
        scratch_shapes=[pltpu.SemaphoreType.DMA],
        compiler_params=pltpu.CompilerParams(vmem_limit_bytes=1 << 23),
    )(facts, queries, own)


def gate_kernel(*refs):
    pass


def gate(value, *others):
    return pl.pallas_call(
        gate_kernel,
        out_shape=jax.ShapeDtypeStruct(value.shape, value.dtype),
        in_specs=[HBM] + [SMEM if other.ndim == 1 else HBM for other in others],
        out_specs=HBM,
        input_output_aliases={0: 0},
    )(value, *others)


def cut_kernel(pair, out0, out1, sem):
    copies = [pltpu.make_async_copy(pair.at[head], out, sem.at[head]) for head, out in enumerate((out0, out1))]
    for copy in copies:
        copy.start()
    for copy in copies:
        copy.wait()


def cut(pair):
    shape = jax.ShapeDtypeStruct(pair.shape[1:], pair.dtype)
    return pl.pallas_call(
        cut_kernel,
        out_shape=[shape, shape],
        in_specs=[HBM],
        out_specs=[VMEM, VMEM],
        scratch_shapes=[pltpu.SemaphoreType.DMA((2,))],
        compiler_params=pltpu.CompilerParams(vmem_limit_bytes=1 << 23),
    )(pair)


def merge_kernel(target, head, facts, groups, lengths, got, old, out, ready, sem):
    rlen, width = got.shape[1:]
    token_at = lax.broadcasted_iota(jnp.int32, (rlen, HD), 0)

    def each(act, fill):
        def look(at, slot):
            hit = groups[at] == facts[target]

            @pl.when(hit)
            def _():
                if fill:
                    alive = token_at < lengths[at]
                    for lane in range(0, width, HD):
                        part = got[slot, :, lane:lane + HD]
                        ready[slot, :, lane:lane + HD] = jnp.where(alive, part, jnp.zeros_like(part))
                act(pltpu.make_async_copy(ready.at[slot], out.at[at, :, pl.ds(head * width, width)], sem))

            return slot + hit.astype(jnp.int32)

        lax.fori_loop(0, groups.shape[0], look, jnp.int32(0))

    each(lambda copy: copy.start(), True)
    each(lambda copy: copy.wait(), False)


def merge(facts, target, groups, lengths, got, out, head):
    return pl.pallas_call(
        functools.partial(merge_kernel, target, head),
        out_shape=jax.ShapeDtypeStruct(out.shape, out.dtype),
        in_specs=[SMEM, SMEM, SMEM, VMEM, HBM],
        out_specs=HBM,
        input_output_aliases={4: 0},
        scratch_shapes=[pltpu.VMEM(got.shape, got.dtype), pltpu.SemaphoreType.DMA],
        compiler_params=pltpu.CompilerParams(vmem_limit_bytes=1 << 23),
    )(facts, groups, lengths, got, out)


def after(value, *others):
    return lax.optimization_barrier((value,) + others)[0]


def gathered(queries, resp_kv, prompt_kv, lengths, group_of, first_head, kv_needed, per_kv):
    out = jax.ShapeDtypeStruct(queries.shape, jnp.bfloat16)
    facts = jnp.concatenate([jnp.zeros((GROUPS,), jnp.int32), group_of, lengths])
    for head in range(kv_needed):
        mine = lax.dynamic_index_in_dim(prompt_kv, first_head + head, 2, keepdims=False)
        own = lax.dynamic_index_in_dim(resp_kv, first_head + head, 2, keepdims=False)[None]
        whole = lax.all_gather(mine, "seq", axis=0, tiled=True)
        out, _ = attend(facts, queries, own, [whole], [out], head, per_kv, None, 16, fresh=head == 0)
    return out


def relayed(queries, resp_kv, prompt_kv, lengths, group_of, first_head, per_kv):
    me = lax.axis_index("seq")
    width = per_kv * HD
    middle, inward, outward = [(1, 2), (2, 1)], [(0, 1), (3, 2)], [(1, 0), (2, 3)]

    def send(pairs, value):
        return lax.ppermute(value, "seq", pairs)

    def two_heads(start):
        return lambda pairs: jnp.transpose(pairs[:, start:start + 2], (1, 0, 2))

    def two_own(start):
        return lambda pairs: jnp.transpose(pairs[:, :, start:start + 2], (2, 0, 1, 3))

    splits = prompt_kv.shape[2] // 2
    mine = lax.switch(first_head // 2, [two_heads(2 * at) for at in range(splits)], prompt_kv[0])
    across = send(middle, mine)
    inner_prompt = send(outward, mine)
    near = [send(inward, part) for part in cut(mine)]

    low = me < 2
    is_inner = (me == 1) | (me == 2)
    outer, inner = jnp.where(low, 0, 3), jnp.where(low, 1, 2)
    far_inner, far_outer = jnp.where(low, 2, 1), jnp.where(low, 3, 0)
    facts = jnp.stack([
        me,
        jnp.zeros_like(me),
        jnp.where(is_inner, -1, inner),
        jnp.full_like(me, 2),
        jnp.where(is_inner, far_inner, -1),
        jnp.ones_like(me),
        jnp.where(is_inner, far_outer, -1),
        jnp.where(is_inner, far_outer, far_inner),
        jnp.where(is_inner, 0, 1),
        jnp.where(is_inner, -1, far_outer),
        jnp.where(is_inner, outer, -1),
    ]).astype(jnp.int32)
    facts = jnp.concatenate([facts, group_of, lengths])

    own = lax.switch(first_head // 2, [two_own(2 * at) for at in range(splits)], resp_kv)
    packed = pack(facts, 9, queries, own, width)
    out = jax.ShapeDtypeStruct(queries.shape, jnp.bfloat16)
    back_shape = jax.ShapeDtypeStruct((SLOTS, queries.shape[1], width), jnp.bfloat16)

    def run(cands, outs, passes, items, far=None, fresh=False, wait_for=None):
        return attend(facts, queries, own, cands, outs, 0, per_kv, passes, items, far, fresh, wait_for)

    out, token = run([mine], [out], [(False, 0, 1, 0), (False, 0, 1, 1)], 8, fresh=True, wait_for=packed)
    near[0] = gate(near[0], token)
    last = [send(middle, near[0])]
    handed = send(inward, gate(packed, near[0]))
    out, token = run([near[0]], [out], [(False, 10, 1, 0)], 4)
    near[1] = gate(near[1], token)
    last.append(send(middle, near[1]))
    across = gate(across, token, inner_prompt)
    far_inner_prompt = [send(outward, part) for part in cut(across)]
    out, _ = run(
        [near[1], across, inner_prompt], [out],
        [(False, 2, 3, 0), (False, 2, 3, 1), (False, 10, 1, 1), (False, 4, 5, 0), (False, 4, 5, 1)], 16, wait_for=near[1])
    back = [None, None]
    out, back[0], _ = run(
        [last[0], far_inner_prompt[0]], [out, back_shape], [(True, 6, 1, 0), (False, 7, 8, 0)], 8, handed)
    back[0] = send(outward, back[0])
    out, back[1], _ = run([last[1]], [out, back_shape], [(True, 6, 1, 1)], 4, handed)
    back[1] = send(outward, back[1])
    out, _ = run([last[1], far_inner_prompt[1]], [out], [(False, 7, 8, 1)], 4)
    for head in range(2):
        out = merge(facts, 9, group_of, lengths, back[head], out, head)
    return out


def shards(queries, resp_kv, prompt_kv, lengths, group_of):
    local_heads = queries.shape[2] // HD
    group = QHEADS // KVH
    kv_needed = max(local_heads // group, 1)
    per_kv = local_heads // kv_needed
    first_head = lax.axis_index("pp") * local_heads // group
    args = (queries, resp_kv, prompt_kv, lengths, group_of, first_head)
    if lax.axis_size("seq") == 4 and kv_needed == 2 and prompt_kv.shape[0] == 1:
        return relayed(*args, per_kv)
    return gathered(*args, kv_needed, per_kv)


def solution(mesh):
    placed = (
        P(("rep", "seq"), None, ("tp", "pp")),
        P(("rep", "seq"), None, "tp", None),
        P(("rep", "seq"), None, "tp", None),
        P(("rep", "seq")),
        P(("rep", "seq")),
    )
    return jax.shard_map(
        shards,
        mesh=mesh,
        in_specs=placed,
        out_specs=P(("rep", "seq"), None, ("tp", "pp")),
        check_vma=False,
    )
```

```python
import functools
import math

import jax
import jax.numpy as jnp
from jax import lax
from jax.experimental import pallas as pl
from jax.experimental.pallas import tpu as pltpu
from jax.sharding import PartitionSpec as P

QHEADS = 64
KVH = 8
HD = 128
LOG2E = math.log2(math.e)
VMEM_BYTES = 56 * 1024 * 1024
SLOTS = 8
HBM = pl.BlockSpec(memory_space=pl.ANY)
SMEM = pl.BlockSpec(memory_space=pltpu.SMEM)
VMEM = pl.BlockSpec(memory_space=pltpu.VMEM)


TN = (((0,), (0,)), ((), ()))
BLOCK = 512
SCORE_BLOCK = 1024
CHUNK = 32
GROUPS = 11


def stacked_heads(q_tile, per_kv):
    return jnp.concatenate([q_tile[:, g * HD:(g + 1) * HD] for g in range(per_kv)], axis=0)


def own_scores(own_tile, q_cols, rlen):
    own = jnp.dot(own_tile[:, :HD], q_cols, preferred_element_type=jnp.float32)
    own_at = lax.broadcasted_iota(jnp.int32, own.shape, 0)
    token_at = lax.broadcasted_iota(jnp.int32, own.shape, 1) % rlen
    return jnp.where(own_at <= token_at, own, -1e30)


def folded(values, op):
    return op(values.reshape(values.shape[0] // 8, 8, values.shape[1]), axis=0)


def turn(q_tile, per_kv, out_ref):
    out_ref[...] = stacked_heads(q_tile, per_kv).T


def finish(acc_ref, total_ref, length, per_kv, out_ref):
    out = (acc_ref[...] * (1.0 / total_ref[0:1, :])).T
    rlen = out_ref.shape[0]
    alive = lax.broadcasted_iota(jnp.int32, (rlen, HD), 0) < length
    for g in range(per_kv):
        part = jnp.where(alive, out[g * rlen:(g + 1) * rlen, :], 0.0)
        out_ref[:, g * HD:(g + 1) * HD] = part.astype(out_ref.dtype)


def scores_and_mix(q_cols, after_own, after_keys, after_s, after_u, after_peak, now):
    plen = after_keys.shape[0]
    scale = HD ** -0.5 * LOG2E
    own = own_scores(after_own, q_cols, after_own.shape[0])
    after_u[...] = own
    after_top = folded(own, jnp.max)
    if now is not None:
        s_ref, u_ref, peak_ref, own_tile, vt_ref, p_ref, acc_ref, total_ref = now
        peak = peak_ref[...]
        part = jnp.exp2((u_ref[...] - peak[0:1, :]) * scale)
        total = folded(part, jnp.sum)
        acc = lax.dot_general(own_tile[:, HD:], part.astype(jnp.bfloat16), TN, preferred_element_type=jnp.float32)
        spread = jnp.concatenate([peak] * (CHUNK // 8), axis=0)
    for at in range(0, plen, BLOCK):
        rows = pl.ds(at, BLOCK)
        if at % SCORE_BLOCK == 0:
            score_rows = pl.ds(at, SCORE_BLOCK)
            fresh = jnp.dot(after_keys[score_rows, :], q_cols, preferred_element_type=jnp.float32)
            after_s[score_rows, :] = fresh
            after_top = jnp.maximum(after_top, folded(fresh, jnp.max))
        if now is not None:
            for chunk in range(at, at + BLOCK, CHUNK):
                part = jnp.exp2((s_ref[chunk:chunk + CHUNK, :] - spread) * scale)
                total = total + folded(part, jnp.sum)
                p_ref[chunk:chunk + CHUNK, :] = part.astype(jnp.bfloat16)
            acc = acc + jnp.dot(vt_ref[:, rows], p_ref[rows, :], preferred_element_type=jnp.float32)
    after_peak[...] = jnp.broadcast_to(jnp.max(after_top, axis=0, keepdims=True), after_peak.shape)
    if now is not None:
        acc_ref[...] = acc
        total_ref[...] = jnp.broadcast_to(jnp.sum(total, axis=0, keepdims=True), total_ref.shape)


def listed(items, cap, count, facts, local, target, source, head):
    def look(at, n):
        hit = facts[GROUPS + at] == target

        @pl.when(hit)
        def _():
            items[n] = at
            items[cap + n] = source
            items[2 * cap + n] = facts[GROUPS + local + at]
            items[3 * cap + n] = head

        return n + hit.astype(jnp.int32)

    return lax.fori_loop(0, local, look, count)


def attend_kernel(passes, n_cand, per_kv, whole_head, two, fresh, waits, *refs):
    refs = list(refs)
    facts, refs = refs[0], refs[1:]
    if two:
        x_ref, refs = refs[0], refs[1:]
    q_ref, own_ref = refs[:2]
    cands, refs = refs[2:2 + n_cand], refs[2 + n_cand + waits:]
    n_out = 2 if two else 1
    if not fresh:
        refs = refs[1:]
    outs, token, refs = refs[:n_out], refs[n_out], refs[n_out + 1:]
    items, at_slot, q_buf, own_buf, key_buf, value_buf, vt_buf, s0, s1, u0, u1, peak0, peak1, turned0, turned1, acc0, acc1, total0, total1, p_buf, o0, o1, info, q_sem, own_sem, kv_sem, o_sem = refs
    s_buf, u_buf, peak_buf, o_buf = (s0, s1), (u0, u1), (peak0, peak1), (o0, o1)
    turned, acc_buf, total_buf = (turned0, turned1), (acc0, acc1), (total0, total1)
    local = (facts.shape[0] - GROUPS) // 2
    cap = items.shape[0] // 4
    width = per_kv * HD
    stacked = passes is None

    count = jnp.int32(0)
    if stacked:
        def one_prompt(prompt, n):
            return listed(items, cap, n, facts, local, prompt, prompt, whole_head)

        count = lax.fori_loop(0, cands[0].shape[0], one_prompt, count)
    else:
        for far, target, source, head in passes:
            if not far:
                count = listed(items, cap, count, facts, local, facts[target], facts[source], head)
                continue
            notes = pltpu.make_async_copy(x_ref.at[0, :, pl.ds(2 * (width + 2 * HD), HD)], info, kv_sem)
            notes.start()
            notes.wait()
            far_head = head
            handed = jnp.max(info[0:16, :].astype(jnp.float32)).astype(jnp.int32)
            handed = jnp.where(facts[target] >= 0, jnp.minimum(handed, SLOTS), 0)

            def take(slot, n):
                items[n] = local + slot
                items[cap + n] = facts[source]
                items[2 * cap + n] = q_buf.shape[1]
                items[3 * cap + n] = far_head
                return n + 1

            count = lax.fori_loop(0, handed, take, count)

    token[0] = count

    def each_array(i, act_local, act_far):
        at = items[i]
        if not two:
            act_local(at)
            return

        @pl.when(at < local)
        def _():
            act_local(at)

        @pl.when(at >= local)
        def _():
            act_far(at - local)

    first = pl.ds(0, width)

    def lanes(i, step, skip, size):
        return pl.ds(pl.multiple_of(items[3 * cap + i] * step + skip, HD), size)

    def mine(i):
        return lanes(i, width, 0, width)

    def fetch(i):
        slot, fourth = lax.rem(i, 2), lax.rem(i, 4)

        def here(at):
            pltpu.make_async_copy(q_ref.at[at, :, mine(i)], q_buf.at[slot], q_sem.at[slot]).start()
            pltpu.make_async_copy(own_ref.at[items[3 * cap + i], at], own_buf.at[fourth], own_sem.at[fourth]).start()

        def far(at):
            pltpu.make_async_copy(x_ref.at[at, :, lanes(i, width + 2 * HD, 0, width)], q_buf.at[slot], q_sem.at[slot]).start()
            pltpu.make_async_copy(x_ref.at[at, :, lanes(i, width + 2 * HD, width, 2 * HD)], own_buf.at[fourth], own_sem.at[fourth]).start()

        each_array(i, here, far)

    def fetched(i):
        slot, fourth = lax.rem(i, 2), lax.rem(i, 4)
        pltpu.make_async_copy(q_ref.at[0, :, first], q_buf.at[slot], q_sem.at[slot]).wait()
        pltpu.make_async_copy(own_ref.at[0, 0], own_buf.at[fourth], own_sem.at[fourth]).wait()

    def store(i, slot):
        def here(at):
            pltpu.make_async_copy(o_buf[slot], outs[0].at[at, :, mine(i)], o_sem.at[slot]).start()

        def far(at):
            pltpu.make_async_copy(o_buf[slot], outs[1].at[at], o_sem.at[slot]).start()

        each_array(i, here, far)

    def stored(slot):
        pltpu.make_async_copy(o_buf[slot], outs[0].at[0, :, first], o_sem.at[slot]).wait()

    keys, values = pl.ds(0, HD), pl.ds(HD, HD)

    def ask(i, into):
        source = items[cap + i]

        def bring(pairs):
            pltpu.make_async_copy(pairs.at[:, keys], key_buf.at[into], kv_sem).start()
            pltpu.make_async_copy(pairs.at[:, values], value_buf, kv_sem).start()

        if stacked:
            bring(cands[0].at[source])
        else:
            for which in range(n_cand):
                @pl.when(source == which)
                def _():
                    bring(cands[which].at[items[3 * cap + i]] if len(cands[which].shape) == 3 else cands[which])

    def receive(into):
        for _ in range(2):
            pltpu.make_async_copy(value_buf, value_buf, kv_sem).wait()
        vt_buf[into] = value_buf[...].T

    @pl.when(count > 0)
    def _():
        ask(0, 0)
        fetch(jnp.int32(0))

        @pl.when(count > 1)
        def _():
            fetch(jnp.int32(1))

        at_slot[0] = 0
        fetched(jnp.int32(0))
        turn(q_buf[0], per_kv, turned[0])

        @pl.when(count > 2)
        def _():
            fetch(jnp.int32(2))

        @pl.when(count > 1)
        def _():
            fetched(jnp.int32(1))

        turn(q_buf[1], per_kv, turned[1])
        receive(0)
        scores_and_mix(turned[0][...], own_buf[0], key_buf.at[0], s_buf[0], u_buf[0], peak_buf[0], None)

        def one(i, slot):
            other = 1 - slot
            held = at_slot[0]
            more = i + 1 < count
            after_i = jnp.minimum(i + 1, count - 1)
            moved = more & ((items[cap + after_i] != items[cap + i]) | (items[3 * cap + after_i] != items[3 * cap + i]))
            holds = jnp.where(moved, 1 - held, held)
            at_slot[0] = holds

            @pl.when(i + 2 < count)
            def _():
                fetched(i + 2)

            @pl.when(i + 3 < count)
            def _():
                fetch(i + 3)

            @pl.when(moved)
            def _():
                ask(i + 1, holds)
                receive(holds)

            @pl.when(i >= 3)
            def _():
                stored(other)

            now = (
                s_buf[slot], u_buf[slot], peak_buf[slot], own_buf[lax.rem(i, 4)], vt_buf.at[held], p_buf,
                acc_buf[slot], total_buf[slot])
            scores_and_mix(
                turned[other][...], own_buf[lax.rem(i + 1, 4)], key_buf.at[holds],
                s_buf[other], u_buf[other], peak_buf[other], now)
            turn(q_buf[slot], per_kv, turned[slot])
            finish(acc_buf[other], total_buf[other], items[2 * cap + jnp.maximum(i - 1, 0)], per_kv, o_buf[other])

            @pl.when(i >= 1)
            def _():
                store(i - 1, other)

        def pair(j, _):
            one(2 * j, 0)

            @pl.when(2 * j + 1 < count)
            def _():
                one(2 * j + 1, 1)

            return 0

        lax.fori_loop(0, lax.div(count + 1, 2), pair, 0)
        final = count - 1
        for slot in range(2):
            @pl.when(lax.rem(final, 2) == slot)
            def _():
                @pl.when(final >= 2)
                def _():
                    stored(slot)

                finish(acc_buf[slot], total_buf[slot], items[2 * cap + final], per_kv, o_buf[slot])
                store(final, slot)

        stored(0)

        @pl.when(count > 1)
        def _():
            stored(1)


def attend(facts, queries, own, cands, outs, head, per_kv, passes, items, far=None, fresh=False, wait_for=None):
    rlen = queries.shape[1]
    plen = cands[0].shape[-2]
    width = per_kv * HD
    small = [facts]
    large = ([far] if far is not None else []) + [queries, own] + cands
    operands = small + large + ([] if wait_for is None else [wait_for])
    aliases = {}
    if not fresh:
        aliases = {len(operands): 0}
        operands = operands + [outs[0]]
    cap = 2 * queries.shape[0] + (SLOTS if far is not None else 0)
    return pl.pallas_call(
        functools.partial(attend_kernel, passes, len(cands), per_kv, head, far is not None, fresh, wait_for is not None),
        out_shape=[jax.ShapeDtypeStruct(o.shape, o.dtype) for o in outs] + [jax.ShapeDtypeStruct((1,), jnp.int32)],
        in_specs=[SMEM] * len(small) + [HBM] * (len(operands) - len(small)),
        out_specs=[HBM] * len(outs) + [SMEM],
        input_output_aliases=aliases,
        scratch_shapes=[
            pltpu.SMEM((4 * cap,), jnp.int32),
            pltpu.SMEM((1,), jnp.int32),
            pltpu.VMEM((2, rlen, width), jnp.bfloat16),
            pltpu.VMEM((4, rlen, 2 * HD), jnp.bfloat16),
            pltpu.VMEM((2, plen, HD), jnp.bfloat16),
            pltpu.VMEM((plen, HD), jnp.bfloat16),
            pltpu.VMEM((2, HD, plen), jnp.bfloat16),
            pltpu.VMEM((plen, per_kv * rlen), jnp.float32),
            pltpu.VMEM((plen, per_kv * rlen), jnp.float32),
            pltpu.VMEM((rlen, per_kv * rlen), jnp.float32),
            pltpu.VMEM((rlen, per_kv * rlen), jnp.float32),
            pltpu.VMEM((8, per_kv * rlen), jnp.float32),
            pltpu.VMEM((8, per_kv * rlen), jnp.float32),
            pltpu.VMEM((HD, per_kv * rlen), jnp.bfloat16),
            pltpu.VMEM((HD, per_kv * rlen), jnp.bfloat16),
            pltpu.VMEM((HD, per_kv * rlen), jnp.float32),
            pltpu.VMEM((HD, per_kv * rlen), jnp.float32),
            pltpu.VMEM((8, per_kv * rlen), jnp.float32),
            pltpu.VMEM((8, per_kv * rlen), jnp.float32),
            pltpu.VMEM((plen, per_kv * rlen), jnp.bfloat16),
            pltpu.VMEM((rlen, width), jnp.bfloat16),
            pltpu.VMEM((rlen, width), jnp.bfloat16),
            pltpu.VMEM((rlen, HD), jnp.bfloat16),
            pltpu.SemaphoreType.DMA((2,)),
            pltpu.SemaphoreType.DMA((4,)),
            pltpu.SemaphoreType.DMA,
            pltpu.SemaphoreType.DMA((2,)),
        ],
        compiler_params=pltpu.CompilerParams(vmem_limit_bytes=VMEM_BYTES),
        cost_estimate=pl.CostEstimate(flops=items << 20, bytes_accessed=1 << 16, transcendentals=0),
    )(*operands)


def pack_kernel(target, width, facts, q_ref, own_ref, out, sem):
    step = width + 2 * HD
    local = q_ref.shape[0]

    def each(act):
        def look(at, slot):
            hit = facts[GROUPS + at] == facts[target]

            @pl.when(hit)
            def _():
                for head in range(2):
                    part = pl.ds(head * width, width)
                    act(pltpu.make_async_copy(q_ref.at[at, :, part], out.at[slot, :, pl.ds(head * step, width)], sem))
                    act(pltpu.make_async_copy(
                        own_ref.at[head, at], out.at[slot, :, pl.ds(head * step + width, 2 * HD)], sem))

            return slot + hit.astype(jnp.int32)

        return lax.fori_loop(0, local, look, jnp.int32(0))

    count = each(lambda copy: copy.start())
    out[0, :, 2 * step:] = jnp.full((out.shape[1], HD), count, jnp.int32).astype(jnp.float32).astype(out.dtype)
    each(lambda copy: copy.wait())


def pack(facts, target, queries, own, width):
    return pl.pallas_call(
        functools.partial(pack_kernel, target, width),
        out_shape=jax.ShapeDtypeStruct((SLOTS, queries.shape[1], 2 * width + 5 * HD), queries.dtype),
        in_specs=[SMEM, HBM, HBM],
        out_specs=VMEM,
        scratch_shapes=[pltpu.SemaphoreType.DMA],
        compiler_params=pltpu.CompilerParams(vmem_limit_bytes=1 << 23),
    )(facts, queries, own)


def gate_kernel(*refs):
    pass


def gate(value, *others):
    return pl.pallas_call(
        gate_kernel,
        out_shape=jax.ShapeDtypeStruct(value.shape, value.dtype),
        in_specs=[HBM] + [SMEM if other.ndim == 1 else HBM for other in others],
        out_specs=HBM,
        input_output_aliases={0: 0},
    )(value, *others)


def two_heads_kernel(count, first, pairs, out):
    for start in range(0, count, 2):
        @pl.when(first[0] == start)
        def _():
            for head in range(2):
                out[head] = pairs[:, start + head, :]


def two_heads(first, pairs):
    tokens, count, lanes = pairs.shape
    block = 256
    return pl.pallas_call(
        functools.partial(two_heads_kernel, count),
        out_shape=jax.ShapeDtypeStruct((2, tokens, lanes), pairs.dtype),
        grid=(tokens // block,),
        in_specs=[SMEM, pl.BlockSpec((block, count, lanes), lambda i: (i, 0, 0))],
        out_specs=pl.BlockSpec((2, block, lanes), lambda i: (0, i, 0)),
        compiler_params=pltpu.CompilerParams(vmem_limit_bytes=1 << 23),
    )(first, pairs)


def cut_kernel(pair, out0, out1, sem):
    copies = [pltpu.make_async_copy(pair.at[head], out, sem.at[head]) for head, out in enumerate((out0, out1))]
    for copy in copies:
        copy.start()
    for copy in copies:
        copy.wait()


def cut(pair):
    shape = jax.ShapeDtypeStruct(pair.shape[1:], pair.dtype)
    return pl.pallas_call(
        cut_kernel,
        out_shape=[shape, shape],
        in_specs=[HBM],
        out_specs=[VMEM, VMEM],
        scratch_shapes=[pltpu.SemaphoreType.DMA((2,))],
        compiler_params=pltpu.CompilerParams(vmem_limit_bytes=1 << 23),
    )(pair)


def merge_kernel(target, head, facts, groups, lengths, got, old, out, ready, sem):
    rlen, width = got.shape[1:]
    token_at = lax.broadcasted_iota(jnp.int32, (rlen, HD), 0)

    def each(act, fill):
        def look(at, slot):
            hit = groups[at] == facts[target]

            @pl.when(hit)
            def _():
                if fill:
                    alive = token_at < lengths[at]
                    for lane in range(0, width, HD):
                        part = got[slot, :, lane:lane + HD]
                        ready[slot, :, lane:lane + HD] = jnp.where(alive, part, jnp.zeros_like(part))
                act(pltpu.make_async_copy(ready.at[slot], out.at[at, :, pl.ds(head * width, width)], sem))

            return slot + hit.astype(jnp.int32)

        lax.fori_loop(0, groups.shape[0], look, jnp.int32(0))

    each(lambda copy: copy.start(), True)
    each(lambda copy: copy.wait(), False)


def merge(facts, target, groups, lengths, got, out, head):
    return pl.pallas_call(
        functools.partial(merge_kernel, target, head),
        out_shape=jax.ShapeDtypeStruct(out.shape, out.dtype),
        in_specs=[SMEM, SMEM, SMEM, VMEM, HBM],
        out_specs=HBM,
        input_output_aliases={4: 0},
        scratch_shapes=[pltpu.VMEM(got.shape, got.dtype), pltpu.SemaphoreType.DMA],
        compiler_params=pltpu.CompilerParams(vmem_limit_bytes=1 << 23),
    )(facts, groups, lengths, got, out)


def after(value, *others):
    return lax.optimization_barrier((value,) + others)[0]


def gathered(queries, resp_kv, prompt_kv, lengths, group_of, first_head, kv_needed, per_kv):
    out = jax.ShapeDtypeStruct(queries.shape, jnp.bfloat16)
    facts = jnp.concatenate([jnp.zeros((GROUPS,), jnp.int32), group_of, lengths])
    for head in range(kv_needed):
        mine = lax.dynamic_index_in_dim(prompt_kv, first_head + head, 2, keepdims=False)
        own = lax.dynamic_index_in_dim(resp_kv, first_head + head, 2, keepdims=False)[None]
        whole = lax.all_gather(mine, "seq", axis=0, tiled=True)
        out, _ = attend(facts, queries, own, [whole], [out], head, per_kv, None, 16, fresh=head == 0)
    return out


def relayed(queries, resp_kv, prompt_kv, lengths, group_of, first_head, per_kv):
    me = lax.axis_index("seq")
    width = per_kv * HD
    middle, inward, outward = [(1, 2), (2, 1)], [(0, 1), (3, 2)], [(1, 0), (2, 3)]

    def send(pairs, value):
        return lax.ppermute(value, "seq", pairs)

    def two_own(start):
        return lambda pairs: jnp.transpose(pairs[:, :, start:start + 2], (2, 0, 1, 3))

    splits = prompt_kv.shape[2] // 2
    mine = two_heads(jnp.reshape(first_head, (1,)).astype(jnp.int32), prompt_kv[0])
    across = send(middle, mine)
    inner_prompt = send(outward, mine)
    near = [send(inward, part) for part in cut(mine)]

    low = me < 2
    is_inner = (me == 1) | (me == 2)
    outer, inner = jnp.where(low, 0, 3), jnp.where(low, 1, 2)
    far_inner, far_outer = jnp.where(low, 2, 1), jnp.where(low, 3, 0)
    facts = jnp.stack([
        me,
        jnp.zeros_like(me),
        jnp.where(is_inner, -1, inner),
        jnp.full_like(me, 2),
        jnp.where(is_inner, far_inner, -1),
        jnp.ones_like(me),
        jnp.where(is_inner, far_outer, -1),
        jnp.where(is_inner, far_outer, far_inner),
        jnp.where(is_inner, 0, 1),
        jnp.where(is_inner, -1, far_outer),
        jnp.where(is_inner, outer, -1),
    ]).astype(jnp.int32)
    facts = jnp.concatenate([facts, group_of, lengths])

    own = lax.switch(first_head // 2, [two_own(2 * at) for at in range(splits)], resp_kv)
    packed = pack(facts, 9, queries, own, width)
    out = jax.ShapeDtypeStruct(queries.shape, jnp.bfloat16)
    back_shape = jax.ShapeDtypeStruct((SLOTS, queries.shape[1], width), jnp.bfloat16)

    def run(cands, outs, passes, items, far=None, fresh=False, wait_for=None):
        return attend(facts, queries, own, cands, outs, 0, per_kv, passes, items, far, fresh, wait_for)

    out, token = run([mine], [out], [(False, 0, 1, 0), (False, 0, 1, 1)], 8, fresh=True, wait_for=packed)
    near[0] = gate(near[0], token)
    last = [send(middle, near[0])]
    handed = send(inward, gate(packed, near[0]))
    out, token = run([near[0]], [out], [(False, 10, 1, 0)], 4)
    near[1] = gate(near[1], token)
    last.append(send(middle, near[1]))
    across = gate(across, token, inner_prompt)
    far_inner_prompt = [send(outward, part) for part in cut(across)]
    out, _ = run(
        [near[1], across, inner_prompt], [out],
        [(False, 2, 3, 0), (False, 2, 3, 1), (False, 10, 1, 1), (False, 4, 5, 0), (False, 4, 5, 1)], 16, wait_for=near[1])
    back = [None, None]
    out, back[0], _ = run(
        [last[0], far_inner_prompt[0]], [out, back_shape], [(True, 6, 1, 0), (False, 7, 8, 0)], 8, handed)
    back[0] = send(outward, back[0])
    out, back[1], _ = run([last[1]], [out, back_shape], [(True, 6, 1, 1)], 4, handed)
    back[1] = send(outward, back[1])
    out, _ = run([last[1], far_inner_prompt[1]], [out], [(False, 7, 8, 1)], 4)
    for head in range(2):
        out = merge(facts, 9, group_of, lengths, back[head], out, head)
    return out


def shards(queries, resp_kv, prompt_kv, lengths, group_of):
    local_heads = queries.shape[2] // HD
    group = QHEADS // KVH
    kv_needed = max(local_heads // group, 1)
    per_kv = local_heads // kv_needed
    first_head = lax.axis_index("pp") * local_heads // group
    args = (queries, resp_kv, prompt_kv, lengths, group_of, first_head)
    if lax.axis_size("seq") == 4 and kv_needed == 2 and prompt_kv.shape[0] == 1:
        return relayed(*args, per_kv)
    return gathered(*args, kv_needed, per_kv)


def solution(mesh):
    placed = (
        P(("rep", "seq"), None, ("tp", "pp")),
        P(("rep", "seq"), None, "tp", None),
        P(("rep", "seq"), None, "tp", None),
        P(("rep", "seq")),
        P(("rep", "seq")),
    )
    return jax.shard_map(
        shards,
        mesh=mesh,
        in_specs=placed,
        out_specs=P(("rep", "seq"), None, ("tp", "pp")),
        check_vma=False,
    )
```

```python
import functools
import math

import jax
import jax.numpy as jnp
from jax import lax
from jax.experimental import pallas as pl
from jax.experimental.pallas import tpu as pltpu
from jax.sharding import PartitionSpec as P

QHEADS = 64
KVH = 8
HD = 128
LOG2E = math.log2(math.e)
VMEM_BYTES = 20 * 1024 * 1024
SLOTS = 8
HBM = pl.BlockSpec(memory_space=pl.ANY)
SMEM = pl.BlockSpec(memory_space=pltpu.SMEM)
VMEM = pl.BlockSpec(memory_space=pltpu.VMEM)


TN = (((0,), (0,)), ((), ()))
BLOCK = 512
SCORE_BLOCK = 1024
CHUNK = 32
GROUPS = 11


def stacked_heads(q_tile, per_kv):
    return jnp.concatenate([q_tile[:, g * HD:(g + 1) * HD] for g in range(per_kv)], axis=0)


def own_scores(own_tile, q_cols, rlen):
    own = jnp.dot(own_tile[:, :HD], q_cols, preferred_element_type=jnp.float32)
    own_at = lax.broadcasted_iota(jnp.int32, own.shape, 0)
    token_at = lax.broadcasted_iota(jnp.int32, own.shape, 1) % rlen
    return jnp.where(own_at <= token_at, own, -1e30)


def folded(values, op):
    return op(values.reshape(values.shape[0] // 8, 8, values.shape[1]), axis=0)


def turn(q_tile, per_kv, out_ref):
    out_ref[...] = stacked_heads(q_tile, per_kv).T


def finish(acc_ref, total_ref, length, per_kv, out_ref):
    out = (acc_ref[...] * (1.0 / total_ref[0:1, :])).T
    rlen = out_ref.shape[0]
    alive = lax.broadcasted_iota(jnp.int32, (rlen, HD), 0) < length
    for g in range(per_kv):
        part = jnp.where(alive, out[g * rlen:(g + 1) * rlen, :], 0.0)
        out_ref[:, g * HD:(g + 1) * HD] = part.astype(out_ref.dtype)


def scores_and_mix(q_cols, after_own, after_keys, after_s, after_u, after_peak, now):
    plen = after_keys.shape[0]
    scale = HD ** -0.5 * LOG2E
    own = own_scores(after_own, q_cols, after_own.shape[0])
    after_u[...] = own
    after_top = folded(own, jnp.max)
    if now is not None:
        s_ref, u_ref, peak_ref, own_tile, vt_ref, p_ref, acc_ref, total_ref = now
        peak = peak_ref[...]
        part = jnp.exp2((u_ref[...] - peak[0:1, :]) * scale)
        total = folded(part, jnp.sum)
        acc = lax.dot_general(own_tile[:, HD:], part.astype(jnp.bfloat16), TN, preferred_element_type=jnp.float32)
        spread = jnp.concatenate([peak] * (CHUNK // 8), axis=0)
    for at in range(0, plen, BLOCK):
        rows = pl.ds(at, BLOCK)
        if at % SCORE_BLOCK == 0:
            score_rows = pl.ds(at, SCORE_BLOCK)
            fresh = jnp.dot(after_keys[score_rows, :], q_cols, preferred_element_type=jnp.float32)
            after_s[score_rows, :] = fresh
            after_top = jnp.maximum(after_top, folded(fresh, jnp.max))
        if now is not None:
            for chunk in range(at, at + BLOCK, CHUNK):
                part = jnp.exp2((s_ref[chunk:chunk + CHUNK, :] - spread) * scale)
                total = total + folded(part, jnp.sum)
                p_ref[chunk:chunk + CHUNK, :] = part.astype(jnp.bfloat16)
            acc = acc + jnp.dot(vt_ref[:, rows], p_ref[rows, :], preferred_element_type=jnp.float32)
    after_peak[...] = jnp.broadcast_to(jnp.max(after_top, axis=0, keepdims=True), after_peak.shape)
    if now is not None:
        acc_ref[...] = acc
        total_ref[...] = jnp.broadcast_to(jnp.sum(total, axis=0, keepdims=True), total_ref.shape)


def listed(items, cap, count, facts, local, target, source, head):
    def look(at, n):
        hit = facts[GROUPS + at] == target

        @pl.when(hit)
        def _():
            items[n] = at
            items[cap + n] = source
            items[2 * cap + n] = facts[GROUPS + local + at]
            items[3 * cap + n] = head

        return n + hit.astype(jnp.int32)

    return lax.fori_loop(0, local, look, count)


def attend_kernel(passes, n_cand, per_kv, whole_head, two, fresh, waits, *refs):
    refs = list(refs)
    facts, refs = refs[0], refs[1:]
    if two:
        x_ref, refs = refs[0], refs[1:]
    q_ref, own_ref = refs[:2]
    cands, refs = refs[2:2 + n_cand], refs[2 + n_cand + waits:]
    n_out = 2 if two else 1
    if not fresh:
        refs = refs[1:]
    outs, token, refs = refs[:n_out], refs[n_out], refs[n_out + 1:]
    items, at_slot, q_buf, own_buf, key_buf, value_buf, vt_buf, s0, s1, u0, u1, peak0, peak1, turned0, turned1, acc0, acc1, total0, total1, p_buf, o0, o1, info, q_sem, own_sem, kv_sem, o_sem = refs
    s_buf, u_buf, peak_buf, o_buf = (s0, s1), (u0, u1), (peak0, peak1), (o0, o1)
    turned, acc_buf, total_buf = (turned0, turned1), (acc0, acc1), (total0, total1)
    local = (facts.shape[0] - GROUPS) // 2
    cap = items.shape[0] // 4
    width = per_kv * HD
    stacked = passes is None

    count = jnp.int32(0)
    if stacked:
        def one_prompt(prompt, n):
            return listed(items, cap, n, facts, local, prompt, prompt, whole_head)

        count = lax.fori_loop(0, cands[0].shape[0], one_prompt, count)
    else:
        for far, target, source, head in passes:
            if not far:
                count = listed(items, cap, count, facts, local, facts[target], facts[source], head)
                continue
            notes = pltpu.make_async_copy(x_ref.at[0, :, pl.ds(2 * (width + 2 * HD), HD)], info, kv_sem)
            notes.start()
            notes.wait()
            far_head = head
            handed = jnp.max(info[0:16, :].astype(jnp.float32)).astype(jnp.int32)
            handed = jnp.where(facts[target] >= 0, jnp.minimum(handed, SLOTS), 0)

            def take(slot, n):
                items[n] = local + slot
                items[cap + n] = facts[source]
                items[2 * cap + n] = q_buf.shape[1]
                items[3 * cap + n] = far_head
                return n + 1

            count = lax.fori_loop(0, handed, take, count)

    token[0] = count

    def each_array(i, act_local, act_far):
        at = items[i]
        if not two:
            act_local(at)
            return

        @pl.when(at < local)
        def _():
            act_local(at)

        @pl.when(at >= local)
        def _():
            act_far(at - local)

    first = pl.ds(0, width)

    def lanes(i, step, skip, size):
        return pl.ds(pl.multiple_of(items[3 * cap + i] * step + skip, HD), size)

    def mine(i):
        return lanes(i, width, 0, width)

    def fetch(i):
        slot, fourth = lax.rem(i, 2), lax.rem(i, 4)

        def here(at):
            pltpu.make_async_copy(q_ref.at[at, :, mine(i)], q_buf.at[slot], q_sem.at[slot]).start()
            pltpu.make_async_copy(own_ref.at[items[3 * cap + i], at], own_buf.at[fourth], own_sem.at[fourth]).start()

        def far(at):
            pltpu.make_async_copy(x_ref.at[at, :, lanes(i, width + 2 * HD, 0, width)], q_buf.at[slot], q_sem.at[slot]).start()
            pltpu.make_async_copy(x_ref.at[at, :, lanes(i, width + 2 * HD, width, 2 * HD)], own_buf.at[fourth], own_sem.at[fourth]).start()

        each_array(i, here, far)

    def fetched(i):
        slot, fourth = lax.rem(i, 2), lax.rem(i, 4)
        pltpu.make_async_copy(q_ref.at[0, :, first], q_buf.at[slot], q_sem.at[slot]).wait()
        pltpu.make_async_copy(own_ref.at[0, 0], own_buf.at[fourth], own_sem.at[fourth]).wait()

    def store(i, slot):
        def here(at):
            pltpu.make_async_copy(o_buf[slot], outs[0].at[at, :, mine(i)], o_sem.at[slot]).start()

        def far(at):
            pltpu.make_async_copy(o_buf[slot], outs[1].at[at], o_sem.at[slot]).start()

        each_array(i, here, far)

    def stored(slot):
        pltpu.make_async_copy(o_buf[slot], outs[0].at[0, :, first], o_sem.at[slot]).wait()

    keys, values = pl.ds(0, HD), pl.ds(HD, HD)

    def ask(i, into):
        source = items[cap + i]

        def bring(pairs):
            pltpu.make_async_copy(pairs.at[:, keys], key_buf.at[into], kv_sem).start()
            pltpu.make_async_copy(pairs.at[:, values], value_buf, kv_sem).start()

        if stacked:
            bring(cands[0].at[source])
        else:
            for which in range(n_cand):
                @pl.when(source == which)
                def _():
                    bring(cands[which].at[items[3 * cap + i]] if len(cands[which].shape) == 3 else cands[which])

    def receive(into):
        for _ in range(2):
            pltpu.make_async_copy(value_buf, value_buf, kv_sem).wait()
        vt_buf[into] = value_buf[...].T

    @pl.when(count > 0)
    def _():
        ask(0, 0)
        fetch(jnp.int32(0))

        @pl.when(count > 1)
        def _():
            fetch(jnp.int32(1))

        at_slot[0] = 0
        fetched(jnp.int32(0))
        turn(q_buf[0], per_kv, turned[0])

        @pl.when(count > 2)
        def _():
            fetch(jnp.int32(2))

        @pl.when(count > 1)
        def _():
            fetched(jnp.int32(1))

        turn(q_buf[1], per_kv, turned[1])
        receive(0)
        scores_and_mix(turned[0][...], own_buf[0], key_buf.at[0], s_buf[0], u_buf[0], peak_buf[0], None)

        def one(i, slot):
            other = 1 - slot
            held = at_slot[0]
            more = i + 1 < count
            after_i = jnp.minimum(i + 1, count - 1)
            moved = more & ((items[cap + after_i] != items[cap + i]) | (items[3 * cap + after_i] != items[3 * cap + i]))
            holds = jnp.where(moved, 1 - held, held)
            at_slot[0] = holds

            @pl.when(i + 2 < count)
            def _():
                fetched(i + 2)

            @pl.when(i + 3 < count)
            def _():
                fetch(i + 3)

            @pl.when(moved)
            def _():
                ask(i + 1, holds)
                receive(holds)

            @pl.when(i >= 3)
            def _():
                stored(other)

            now = (
                s_buf[slot], u_buf[slot], peak_buf[slot], own_buf[lax.rem(i, 4)], vt_buf.at[held], p_buf,
                acc_buf[slot], total_buf[slot])
            scores_and_mix(
                turned[other][...], own_buf[lax.rem(i + 1, 4)], key_buf.at[holds],
                s_buf[other], u_buf[other], peak_buf[other], now)
            turn(q_buf[slot], per_kv, turned[slot])
            finish(acc_buf[other], total_buf[other], items[2 * cap + jnp.maximum(i - 1, 0)], per_kv, o_buf[other])

            @pl.when(i >= 1)
            def _():
                store(i - 1, other)

        def pair(j, _):
            one(2 * j, 0)

            @pl.when(2 * j + 1 < count)
            def _():
                one(2 * j + 1, 1)

            return 0

        lax.fori_loop(0, lax.div(count + 1, 2), pair, 0)
        final = count - 1
        for slot in range(2):
            @pl.when(lax.rem(final, 2) == slot)
            def _():
                @pl.when(final >= 2)
                def _():
                    stored(slot)

                finish(acc_buf[slot], total_buf[slot], items[2 * cap + final], per_kv, o_buf[slot])
                store(final, slot)

        stored(0)

        @pl.when(count > 1)
        def _():
            stored(1)


def attend(facts, queries, own, cands, outs, head, per_kv, passes, items, far=None, fresh=False, wait_for=None):
    rlen = queries.shape[1]
    plen = cands[0].shape[-2]
    width = per_kv * HD
    small = [facts]
    large = ([far] if far is not None else []) + [queries, own] + cands
    operands = small + large + ([] if wait_for is None else [wait_for])
    aliases = {}
    if not fresh:
        aliases = {len(operands): 0}
        operands = operands + [outs[0]]
    cap = 2 * queries.shape[0] + (SLOTS if far is not None else 0)
    return pl.pallas_call(
        functools.partial(attend_kernel, passes, len(cands), per_kv, head, far is not None, fresh, wait_for is not None),
        out_shape=[jax.ShapeDtypeStruct(o.shape, o.dtype) for o in outs] + [jax.ShapeDtypeStruct((1,), jnp.int32)],
        in_specs=[SMEM] * len(small) + [HBM] * (len(operands) - len(small)),
        out_specs=[HBM] * len(outs) + [SMEM],
        input_output_aliases=aliases,
        scratch_shapes=[
            pltpu.SMEM((4 * cap,), jnp.int32),
            pltpu.SMEM((1,), jnp.int32),
            pltpu.VMEM((2, rlen, width), jnp.bfloat16),
            pltpu.VMEM((4, rlen, 2 * HD), jnp.bfloat16),
            pltpu.VMEM((2, plen, HD), jnp.bfloat16),
            pltpu.VMEM((plen, HD), jnp.bfloat16),
            pltpu.VMEM((2, HD, plen), jnp.bfloat16),
            pltpu.VMEM((plen, per_kv * rlen), jnp.float32),
            pltpu.VMEM((plen, per_kv * rlen), jnp.float32),
            pltpu.VMEM((rlen, per_kv * rlen), jnp.float32),
            pltpu.VMEM((rlen, per_kv * rlen), jnp.float32),
            pltpu.VMEM((8, per_kv * rlen), jnp.float32),
            pltpu.VMEM((8, per_kv * rlen), jnp.float32),
            pltpu.VMEM((HD, per_kv * rlen), jnp.bfloat16),
            pltpu.VMEM((HD, per_kv * rlen), jnp.bfloat16),
            pltpu.VMEM((HD, per_kv * rlen), jnp.float32),
            pltpu.VMEM((HD, per_kv * rlen), jnp.float32),
            pltpu.VMEM((8, per_kv * rlen), jnp.float32),
            pltpu.VMEM((8, per_kv * rlen), jnp.float32),
            pltpu.VMEM((plen, per_kv * rlen), jnp.bfloat16),
            pltpu.VMEM((rlen, width), jnp.bfloat16),
            pltpu.VMEM((rlen, width), jnp.bfloat16),
            pltpu.VMEM((rlen, HD), jnp.bfloat16),
            pltpu.SemaphoreType.DMA((2,)),
            pltpu.SemaphoreType.DMA((4,)),
            pltpu.SemaphoreType.DMA,
            pltpu.SemaphoreType.DMA((2,)),
        ],
        compiler_params=pltpu.CompilerParams(vmem_limit_bytes=VMEM_BYTES),
        cost_estimate=pl.CostEstimate(flops=items << 20, bytes_accessed=1 << 16, transcendentals=0),
    )(*operands)


def pack_kernel(target, width, facts, q_ref, own_ref, out, sem):
    step = width + 2 * HD
    local = q_ref.shape[0]

    def each(act):
        def look(at, slot):
            hit = facts[GROUPS + at] == facts[target]

            @pl.when(hit)
            def _():
                for head in range(2):
                    part = pl.ds(head * width, width)
                    act(pltpu.make_async_copy(q_ref.at[at, :, part], out.at[slot, :, pl.ds(head * step, width)], sem))
                    act(pltpu.make_async_copy(
                        own_ref.at[head, at], out.at[slot, :, pl.ds(head * step + width, 2 * HD)], sem))

            return slot + hit.astype(jnp.int32)

        return lax.fori_loop(0, local, look, jnp.int32(0))

    count = each(lambda copy: copy.start())
    out[0, :, 2 * step:] = jnp.full((out.shape[1], HD), count, jnp.int32).astype(jnp.float32).astype(out.dtype)
    each(lambda copy: copy.wait())


def pack(facts, target, queries, own, width):
    return pl.pallas_call(
        functools.partial(pack_kernel, target, width),
        out_shape=jax.ShapeDtypeStruct((SLOTS, queries.shape[1], 2 * width + 5 * HD), queries.dtype),
        in_specs=[SMEM, HBM, HBM],
        out_specs=VMEM,
        scratch_shapes=[pltpu.SemaphoreType.DMA],
        compiler_params=pltpu.CompilerParams(vmem_limit_bytes=1 << 23),
    )(facts, queries, own)


def gate_kernel(*refs):
    pass


def gate(value, *others):
    return pl.pallas_call(
        gate_kernel,
        out_shape=jax.ShapeDtypeStruct(value.shape, value.dtype),
        in_specs=[HBM] + [SMEM if other.ndim == 1 else HBM for other in others],
        out_specs=HBM,
        input_output_aliases={0: 0},
    )(value, *others)


def cut_kernel(pair, out0, out1, sem):
    copies = [pltpu.make_async_copy(pair.at[head], out, sem.at[head]) for head, out in enumerate((out0, out1))]
    for copy in copies:
        copy.start()
    for copy in copies:
        copy.wait()


def cut(pair):
    shape = jax.ShapeDtypeStruct(pair.shape[1:], pair.dtype)
    return pl.pallas_call(
        cut_kernel,
        out_shape=[shape, shape],
        in_specs=[HBM],
        out_specs=[VMEM, VMEM],
        scratch_shapes=[pltpu.SemaphoreType.DMA((2,))],
        compiler_params=pltpu.CompilerParams(vmem_limit_bytes=1 << 23),
    )(pair)


def merge_kernel(target, head, facts, groups, lengths, got, old, out, ready, sem):
    rlen, width = got.shape[1:]
    token_at = lax.broadcasted_iota(jnp.int32, (rlen, HD), 0)

    def each(act, fill):
        def look(at, slot):
            hit = groups[at] == facts[target]

            @pl.when(hit)
            def _():
                if fill:
                    alive = token_at < lengths[at]
                    for lane in range(0, width, HD):
                        part = got[slot, :, lane:lane + HD]
                        ready[slot, :, lane:lane + HD] = jnp.where(alive, part, jnp.zeros_like(part))
                act(pltpu.make_async_copy(ready.at[slot], out.at[at, :, pl.ds(head * width, width)], sem))

            return slot + hit.astype(jnp.int32)

        lax.fori_loop(0, groups.shape[0], look, jnp.int32(0))

    each(lambda copy: copy.start(), True)
    each(lambda copy: copy.wait(), False)


def merge(facts, target, groups, lengths, got, out, head):
    return pl.pallas_call(
        functools.partial(merge_kernel, target, head),
        out_shape=jax.ShapeDtypeStruct(out.shape, out.dtype),
        in_specs=[SMEM, SMEM, SMEM, VMEM, HBM],
        out_specs=HBM,
        input_output_aliases={4: 0},
        scratch_shapes=[pltpu.VMEM(got.shape, got.dtype), pltpu.SemaphoreType.DMA],
        compiler_params=pltpu.CompilerParams(vmem_limit_bytes=1 << 23),
    )(facts, groups, lengths, got, out)


def after(value, *others):
    return lax.optimization_barrier((value,) + others)[0]


def gathered(queries, resp_kv, prompt_kv, lengths, group_of, first_head, kv_needed, per_kv):
    out = jax.ShapeDtypeStruct(queries.shape, jnp.bfloat16)
    facts = jnp.concatenate([jnp.zeros((GROUPS,), jnp.int32), group_of, lengths])
    for head in range(kv_needed):
        mine = lax.dynamic_index_in_dim(prompt_kv, first_head + head, 2, keepdims=False)
        own = lax.dynamic_index_in_dim(resp_kv, first_head + head, 2, keepdims=False)[None]
        whole = lax.all_gather(mine, "seq", axis=0, tiled=True)
        out, _ = attend(facts, queries, own, [whole], [out], head, per_kv, None, 16, fresh=head == 0)
    return out


def relayed(queries, resp_kv, prompt_kv, lengths, group_of, first_head, per_kv):
    me = lax.axis_index("seq")
    width = per_kv * HD
    middle, inward, outward = [(1, 2), (2, 1)], [(0, 1), (3, 2)], [(1, 0), (2, 3)]

    def send(pairs, value):
        return lax.ppermute(value, "seq", pairs)

    def two_heads(start):
        return lambda pairs: jnp.transpose(pairs[:, start:start + 2], (1, 0, 2))

    def two_own(start):
        return lambda pairs: jnp.transpose(pairs[:, :, start:start + 2], (2, 0, 1, 3))

    splits = prompt_kv.shape[2] // 2
    mine = lax.switch(first_head // 2, [two_heads(2 * at) for at in range(splits)], prompt_kv[0])
    across = send(middle, mine)
    inner_prompt = send(outward, mine)
    near = [send(inward, part) for part in cut(mine)]

    low = me < 2
    is_inner = (me == 1) | (me == 2)
    outer, inner = jnp.where(low, 0, 3), jnp.where(low, 1, 2)
    far_inner, far_outer = jnp.where(low, 2, 1), jnp.where(low, 3, 0)
    facts = jnp.stack([
        me,
        jnp.zeros_like(me),
        jnp.where(is_inner, -1, inner),
        jnp.full_like(me, 2),
        jnp.where(is_inner, far_inner, -1),
        jnp.ones_like(me),
        jnp.where(is_inner, far_outer, -1),
        jnp.where(is_inner, far_outer, far_inner),
        jnp.where(is_inner, 0, 1),
        jnp.where(is_inner, -1, far_outer),
        jnp.where(is_inner, outer, -1),
    ]).astype(jnp.int32)
    facts = jnp.concatenate([facts, group_of, lengths])

    own = lax.switch(first_head // 2, [two_own(2 * at) for at in range(splits)], resp_kv)
    packed = pack(facts, 9, queries, own, width)
    out = jax.ShapeDtypeStruct(queries.shape, jnp.bfloat16)
    back_shape = jax.ShapeDtypeStruct((SLOTS, queries.shape[1], width), jnp.bfloat16)

    def run(cands, outs, passes, items, far=None, fresh=False, wait_for=None):
        return attend(facts, queries, own, cands, outs, 0, per_kv, passes, items, far, fresh, wait_for)

    out, token = run([mine], [out], [(False, 0, 1, 0), (False, 0, 1, 1)], 8, fresh=True, wait_for=packed)
    near[0] = gate(near[0], token)
    last = [send(middle, near[0])]
    handed = send(inward, gate(packed, near[0]))
    out, token = run([near[0]], [out], [(False, 10, 1, 0)], 4)
    near[1] = gate(near[1], token)
    last.append(send(middle, near[1]))
    across = gate(across, token, inner_prompt)
    far_inner_prompt = [send(outward, part) for part in cut(across)]
    out, _ = run(
        [near[1], across, inner_prompt], [out],
        [(False, 2, 3, 0), (False, 2, 3, 1), (False, 10, 1, 1), (False, 4, 5, 0), (False, 4, 5, 1)], 16, wait_for=near[1])
    back = [None, None]
    out, back[0], _ = run(
        [last[0], far_inner_prompt[0]], [out, back_shape], [(True, 6, 1, 0), (False, 7, 8, 0)], 8, handed)
    back[0] = send(outward, back[0])
    out, back[1], _ = run([last[1]], [out, back_shape], [(True, 6, 1, 1)], 4, handed)
    back[1] = send(outward, back[1])
    out, _ = run([last[1], far_inner_prompt[1]], [out], [(False, 7, 8, 1)], 4)
    for head in range(2):
        out = merge(facts, 9, group_of, lengths, back[head], out, head)
    return out


def shards(queries, resp_kv, prompt_kv, lengths, group_of):
    local_heads = queries.shape[2] // HD
    group = QHEADS // KVH
    kv_needed = max(local_heads // group, 1)
    per_kv = local_heads // kv_needed
    first_head = lax.axis_index("pp") * local_heads // group
    args = (queries, resp_kv, prompt_kv, lengths, group_of, first_head)
    if lax.axis_size("seq") == 4 and kv_needed == 2 and prompt_kv.shape[0] == 1:
        return relayed(*args, per_kv)
    return gathered(*args, kv_needed, per_kv)


def solution(mesh):
    placed = (
        P(("rep", "seq"), None, ("tp", "pp")),
        P(("rep", "seq"), None, "tp", None),
        P(("rep", "seq"), None, "tp", None),
        P(("rep", "seq")),
        P(("rep", "seq")),
    )
    return jax.shard_map(
        shards,
        mesh=mesh,
        in_specs=placed,
        out_specs=P(("rep", "seq"), None, ("tp", "pp")),
        check_vma=False,
    )
```

```python
import functools
import math

import jax
import jax.numpy as jnp
from jax import lax
from jax.experimental import pallas as pl
from jax.experimental.pallas import tpu as pltpu
from jax.sharding import PartitionSpec as P

QHEADS = 64
KVH = 8
HD = 128
LOG2E = math.log2(math.e)
VMEM_BYTES = 12 * 1024 * 1024
SLOTS = 8
HBM = pl.BlockSpec(memory_space=pl.ANY)
SMEM = pl.BlockSpec(memory_space=pltpu.SMEM)
VMEM = pl.BlockSpec(memory_space=pltpu.VMEM)


TN = (((0,), (0,)), ((), ()))
BLOCK = 512
SCORE_BLOCK = 1024
CHUNK = 32
GROUPS = 11


def stacked_heads(q_tile, per_kv):
    return jnp.concatenate([q_tile[:, g * HD:(g + 1) * HD] for g in range(per_kv)], axis=0)


def own_scores(own_tile, q_cols, rlen):
    own = jnp.dot(own_tile[:, :HD], q_cols, preferred_element_type=jnp.float32)
    own_at = lax.broadcasted_iota(jnp.int32, own.shape, 0)
    token_at = lax.broadcasted_iota(jnp.int32, own.shape, 1) % rlen
    return jnp.where(own_at <= token_at, own, -1e30)


def folded(values, op):
    return op(values.reshape(values.shape[0] // 8, 8, values.shape[1]), axis=0)


def turn(q_tile, per_kv, out_ref):
    out_ref[...] = stacked_heads(q_tile, per_kv).T


def finish(acc_ref, total_ref, length, per_kv, out_ref):
    out = (acc_ref[...] * (1.0 / total_ref[0:1, :])).T
    rlen = out_ref.shape[0]
    alive = lax.broadcasted_iota(jnp.int32, (rlen, HD), 0) < length
    for g in range(per_kv):
        part = jnp.where(alive, out[g * rlen:(g + 1) * rlen, :], 0.0)
        out_ref[:, g * HD:(g + 1) * HD] = part.astype(out_ref.dtype)


def scores_and_mix(q_cols, after_own, after_keys, after_s, after_u, after_peak, now):
    plen = after_keys.shape[0]
    scale = HD ** -0.5 * LOG2E
    own = own_scores(after_own, q_cols, after_own.shape[0])
    after_u[...] = own
    after_top = folded(own, jnp.max)
    if now is not None:
        s_ref, u_ref, peak_ref, own_tile, vt_ref, p_ref, acc_ref, total_ref = now
        peak = peak_ref[...]
        part = jnp.exp2((u_ref[...] - peak[0:1, :]) * scale)
        total = folded(part, jnp.sum)
        acc = lax.dot_general(own_tile[:, HD:], part.astype(jnp.bfloat16), TN, preferred_element_type=jnp.float32)
        spread = jnp.concatenate([peak] * (CHUNK // 8), axis=0)
    for at in range(0, plen, BLOCK):
        rows = pl.ds(at, BLOCK)
        if at % SCORE_BLOCK == 0:
            score_rows = pl.ds(at, SCORE_BLOCK)
            fresh = jnp.dot(after_keys[score_rows, :], q_cols, preferred_element_type=jnp.float32)
            after_s[score_rows, :] = fresh
            after_top = jnp.maximum(after_top, folded(fresh, jnp.max))
        if now is not None:
            for chunk in range(at, at + BLOCK, CHUNK):
                part = jnp.exp2((s_ref[chunk:chunk + CHUNK, :] - spread) * scale)
                total = total + folded(part, jnp.sum)
                p_ref[chunk:chunk + CHUNK, :] = part.astype(jnp.bfloat16)
            acc = acc + jnp.dot(vt_ref[:, rows], p_ref[rows, :], preferred_element_type=jnp.float32)
    after_peak[...] = jnp.broadcast_to(jnp.max(after_top, axis=0, keepdims=True), after_peak.shape)
    if now is not None:
        acc_ref[...] = acc
        total_ref[...] = jnp.broadcast_to(jnp.sum(total, axis=0, keepdims=True), total_ref.shape)


def listed(items, cap, count, facts, local, target, source, head):
    def look(at, n):
        hit = facts[GROUPS + at] == target

        @pl.when(hit)
        def _():
            items[n] = at
            items[cap + n] = source
            items[2 * cap + n] = facts[GROUPS + local + at]
            items[3 * cap + n] = head

        return n + hit.astype(jnp.int32)

    return lax.fori_loop(0, local, look, count)


def attend_kernel(passes, n_cand, per_kv, whole_head, two, fresh, waits, *refs):
    refs = list(refs)
    facts, refs = refs[0], refs[1:]
    if two:
        x_ref, refs = refs[0], refs[1:]
    q_ref, own_ref = refs[:2]
    cands, refs = refs[2:2 + n_cand], refs[2 + n_cand + waits:]
    n_out = 2 if two else 1
    if not fresh:
        refs = refs[1:]
    outs, token, refs = refs[:n_out], refs[n_out], refs[n_out + 1:]
    items, at_slot, q_buf, own_buf, key_buf, value_buf, vt_buf, s0, s1, u0, u1, peak0, peak1, turned0, turned1, acc0, acc1, total0, total1, p_buf, o0, o1, info, q_sem, own_sem, kv_sem, o_sem = refs
    s_buf, u_buf, peak_buf, o_buf = (s0, s1), (u0, u1), (peak0, peak1), (o0, o1)
    turned, acc_buf, total_buf = (turned0, turned1), (acc0, acc1), (total0, total1)
    local = (facts.shape[0] - GROUPS) // 2
    cap = items.shape[0] // 4
    width = per_kv * HD
    stacked = passes is None

    count = jnp.int32(0)
    if stacked:
        def one_prompt(prompt, n):
            return listed(items, cap, n, facts, local, prompt, prompt, whole_head)

        count = lax.fori_loop(0, cands[0].shape[0], one_prompt, count)
    else:
        for far, target, source, head in passes:
            if not far:
                count = listed(items, cap, count, facts, local, facts[target], facts[source], head)
                continue
            notes = pltpu.make_async_copy(x_ref.at[0, :, pl.ds(2 * (width + 2 * HD), HD)], info, kv_sem)
            notes.start()
            notes.wait()
            far_head = head
            handed = jnp.max(info[0:16, :].astype(jnp.float32)).astype(jnp.int32)
            handed = jnp.where(facts[target] >= 0, jnp.minimum(handed, SLOTS), 0)

            def take(slot, n):
                items[n] = local + slot
                items[cap + n] = facts[source]
                items[2 * cap + n] = q_buf.shape[1]
                items[3 * cap + n] = far_head
                return n + 1

            count = lax.fori_loop(0, handed, take, count)

    token[0] = count

    def each_array(i, act_local, act_far):
        at = items[i]
        if not two:
            act_local(at)
            return

        @pl.when(at < local)
        def _():
            act_local(at)

        @pl.when(at >= local)
        def _():
            act_far(at - local)

    first = pl.ds(0, width)

    def lanes(i, step, skip, size):
        return pl.ds(pl.multiple_of(items[3 * cap + i] * step + skip, HD), size)

    def mine(i):
        return lanes(i, width, 0, width)

    def fetch(i):
        slot, fourth = lax.rem(i, 2), lax.rem(i, 4)

        def here(at):
            pltpu.make_async_copy(q_ref.at[at, :, mine(i)], q_buf.at[slot], q_sem.at[slot]).start()
            pltpu.make_async_copy(own_ref.at[items[3 * cap + i], at], own_buf.at[fourth], own_sem.at[fourth]).start()

        def far(at):
            pltpu.make_async_copy(x_ref.at[at, :, lanes(i, width + 2 * HD, 0, width)], q_buf.at[slot], q_sem.at[slot]).start()
            pltpu.make_async_copy(x_ref.at[at, :, lanes(i, width + 2 * HD, width, 2 * HD)], own_buf.at[fourth], own_sem.at[fourth]).start()

        each_array(i, here, far)

    def fetched(i):
        slot, fourth = lax.rem(i, 2), lax.rem(i, 4)
        pltpu.make_async_copy(q_ref.at[0, :, first], q_buf.at[slot], q_sem.at[slot]).wait()
        pltpu.make_async_copy(own_ref.at[0, 0], own_buf.at[fourth], own_sem.at[fourth]).wait()

    def store(i, slot):
        def here(at):
            pltpu.make_async_copy(o_buf[slot], outs[0].at[at, :, mine(i)], o_sem.at[slot]).start()

        def far(at):
            pltpu.make_async_copy(o_buf[slot], outs[1].at[at], o_sem.at[slot]).start()

        each_array(i, here, far)

    def stored(slot):
        pltpu.make_async_copy(o_buf[slot], outs[0].at[0, :, first], o_sem.at[slot]).wait()

    keys, values = pl.ds(0, HD), pl.ds(HD, HD)

    def ask(i, into):
        source = items[cap + i]

        def bring(pairs):
            pltpu.make_async_copy(pairs.at[:, keys], key_buf.at[into], kv_sem).start()
            pltpu.make_async_copy(pairs.at[:, values], value_buf, kv_sem).start()

        if stacked:
            bring(cands[0].at[source])
        else:
            for which in range(n_cand):
                @pl.when(source == which)
                def _():
                    bring(cands[which].at[items[3 * cap + i]] if len(cands[which].shape) == 3 else cands[which])

    def receive(into):
        for _ in range(2):
            pltpu.make_async_copy(value_buf, value_buf, kv_sem).wait()
        vt_buf[into] = value_buf[...].T

    @pl.when(count > 0)
    def _():
        ask(0, 0)
        fetch(jnp.int32(0))

        @pl.when(count > 1)
        def _():
            fetch(jnp.int32(1))

        at_slot[0] = 0
        fetched(jnp.int32(0))
        turn(q_buf[0], per_kv, turned[0])

        @pl.when(count > 2)
        def _():
            fetch(jnp.int32(2))

        @pl.when(count > 1)
        def _():
            fetched(jnp.int32(1))

        turn(q_buf[1], per_kv, turned[1])
        receive(0)
        scores_and_mix(turned[0][...], own_buf[0], key_buf.at[0], s_buf[0], u_buf[0], peak_buf[0], None)

        def one(i, slot):
            other = 1 - slot
            held = at_slot[0]
            more = i + 1 < count
            after_i = jnp.minimum(i + 1, count - 1)
            moved = more & ((items[cap + after_i] != items[cap + i]) | (items[3 * cap + after_i] != items[3 * cap + i]))
            holds = jnp.where(moved, 1 - held, held)
            at_slot[0] = holds

            @pl.when(i + 2 < count)
            def _():
                fetched(i + 2)

            @pl.when(i + 3 < count)
            def _():
                fetch(i + 3)

            @pl.when(moved)
            def _():
                ask(i + 1, holds)
                receive(holds)

            @pl.when(i >= 3)
            def _():
                stored(other)

            now = (
                s_buf[slot], u_buf[slot], peak_buf[slot], own_buf[lax.rem(i, 4)], vt_buf.at[held], p_buf,
                acc_buf[slot], total_buf[slot])
            scores_and_mix(
                turned[other][...], own_buf[lax.rem(i + 1, 4)], key_buf.at[holds],
                s_buf[other], u_buf[other], peak_buf[other], now)
            turn(q_buf[slot], per_kv, turned[slot])
            finish(acc_buf[other], total_buf[other], items[2 * cap + jnp.maximum(i - 1, 0)], per_kv, o_buf[other])

            @pl.when(i >= 1)
            def _():
                store(i - 1, other)

        def pair(j, _):
            one(2 * j, 0)

            @pl.when(2 * j + 1 < count)
            def _():
                one(2 * j + 1, 1)

            return 0

        lax.fori_loop(0, lax.div(count + 1, 2), pair, 0)
        final = count - 1
        for slot in range(2):
            @pl.when(lax.rem(final, 2) == slot)
            def _():
                @pl.when(final >= 2)
                def _():
                    stored(slot)

                finish(acc_buf[slot], total_buf[slot], items[2 * cap + final], per_kv, o_buf[slot])
                store(final, slot)

        stored(0)

        @pl.when(count > 1)
        def _():
            stored(1)


def attend(facts, queries, own, cands, outs, head, per_kv, passes, items, far=None, fresh=False, wait_for=None):
    rlen = queries.shape[1]
    plen = cands[0].shape[-2]
    width = per_kv * HD
    small = [facts]
    large = ([far] if far is not None else []) + [queries, own] + cands
    operands = small + large + ([] if wait_for is None else [wait_for])
    aliases = {}
    if not fresh:
        aliases = {len(operands): 0}
        operands = operands + [outs[0]]
    cap = 2 * queries.shape[0] + (SLOTS if far is not None else 0)
    return pl.pallas_call(
        functools.partial(attend_kernel, passes, len(cands), per_kv, head, far is not None, fresh, wait_for is not None),
        out_shape=[jax.ShapeDtypeStruct(o.shape, o.dtype) for o in outs] + [jax.ShapeDtypeStruct((1,), jnp.int32)],
        in_specs=[SMEM] * len(small) + [HBM] * (len(operands) - len(small)),
        out_specs=[HBM] * len(outs) + [SMEM],
        input_output_aliases=aliases,
        scratch_shapes=[
            pltpu.SMEM((4 * cap,), jnp.int32),
            pltpu.SMEM((1,), jnp.int32),
            pltpu.VMEM((2, rlen, width), jnp.bfloat16),
            pltpu.VMEM((4, rlen, 2 * HD), jnp.bfloat16),
            pltpu.VMEM((2, plen, HD), jnp.bfloat16),
            pltpu.VMEM((plen, HD), jnp.bfloat16),
            pltpu.VMEM((2, HD, plen), jnp.bfloat16),
            pltpu.VMEM((plen, per_kv * rlen), jnp.float32),
            pltpu.VMEM((plen, per_kv * rlen), jnp.float32),
            pltpu.VMEM((rlen, per_kv * rlen), jnp.float32),
            pltpu.VMEM((rlen, per_kv * rlen), jnp.float32),
            pltpu.VMEM((8, per_kv * rlen), jnp.float32),
            pltpu.VMEM((8, per_kv * rlen), jnp.float32),
            pltpu.VMEM((HD, per_kv * rlen), jnp.bfloat16),
            pltpu.VMEM((HD, per_kv * rlen), jnp.bfloat16),
            pltpu.VMEM((HD, per_kv * rlen), jnp.float32),
            pltpu.VMEM((HD, per_kv * rlen), jnp.float32),
            pltpu.VMEM((8, per_kv * rlen), jnp.float32),
            pltpu.VMEM((8, per_kv * rlen), jnp.float32),
            pltpu.VMEM((plen, per_kv * rlen), jnp.bfloat16),
            pltpu.VMEM((rlen, width), jnp.bfloat16),
            pltpu.VMEM((rlen, width), jnp.bfloat16),
            pltpu.VMEM((rlen, HD), jnp.bfloat16),
            pltpu.SemaphoreType.DMA((2,)),
            pltpu.SemaphoreType.DMA((4,)),
            pltpu.SemaphoreType.DMA,
            pltpu.SemaphoreType.DMA((2,)),
        ],
        compiler_params=pltpu.CompilerParams(vmem_limit_bytes=VMEM_BYTES),
        cost_estimate=pl.CostEstimate(flops=items << 20, bytes_accessed=1 << 16, transcendentals=0),
    )(*operands)


def pack_kernel(target, width, facts, q_ref, own_ref, out, sem):
    step = width + 2 * HD
    local = q_ref.shape[0]

    def each(act):
        def look(at, slot):
            hit = facts[GROUPS + at] == facts[target]

            @pl.when(hit)
            def _():
                for head in range(2):
                    part = pl.ds(head * width, width)
                    act(pltpu.make_async_copy(q_ref.at[at, :, part], out.at[slot, :, pl.ds(head * step, width)], sem))
                    act(pltpu.make_async_copy(
                        own_ref.at[head, at], out.at[slot, :, pl.ds(head * step + width, 2 * HD)], sem))

            return slot + hit.astype(jnp.int32)

        return lax.fori_loop(0, local, look, jnp.int32(0))

    count = each(lambda copy: copy.start())
    out[0, :, 2 * step:] = jnp.full((out.shape[1], HD), count, jnp.int32).astype(jnp.float32).astype(out.dtype)
    each(lambda copy: copy.wait())


def pack(facts, target, queries, own, width):
    return pl.pallas_call(
        functools.partial(pack_kernel, target, width),
        out_shape=jax.ShapeDtypeStruct((SLOTS, queries.shape[1], 2 * width + 5 * HD), queries.dtype),
        in_specs=[SMEM, HBM, HBM],
        out_specs=VMEM,
        scratch_shapes=[pltpu.SemaphoreType.DMA],
        compiler_params=pltpu.CompilerParams(vmem_limit_bytes=1 << 23),
    )(facts, queries, own)


def gate_kernel(*refs):
    pass


def gate(value, *others):
    return pl.pallas_call(
        gate_kernel,
        out_shape=jax.ShapeDtypeStruct(value.shape, value.dtype),
        in_specs=[HBM] + [SMEM if other.ndim == 1 else HBM for other in others],
        out_specs=HBM,
        input_output_aliases={0: 0},
    )(value, *others)


def cut_kernel(flag, pair, out0, out1, sem):
    @pl.when(flag[0] > 0)
    def _():
        copies = [pltpu.make_async_copy(pair.at[head], out, sem.at[head]) for head, out in enumerate((out0, out1))]
        for copy in copies:
            copy.start()
        for copy in copies:
            copy.wait()


def cut(pair, wanted):
    shape = jax.ShapeDtypeStruct(pair.shape[1:], pair.dtype)
    return pl.pallas_call(
        cut_kernel,
        out_shape=[shape, shape],
        in_specs=[SMEM, HBM],
        out_specs=[VMEM, VMEM],
        scratch_shapes=[pltpu.SemaphoreType.DMA((2,))],
        compiler_params=pltpu.CompilerParams(vmem_limit_bytes=1 << 23),
    )(jnp.reshape(wanted, (1,)).astype(jnp.int32), pair)


def merge_kernel(target, head, facts, groups, lengths, got, old, out, ready, sem):
    rlen, width = got.shape[1:]
    token_at = lax.broadcasted_iota(jnp.int32, (rlen, HD), 0)

    def each(act, fill):
        def look(at, slot):
            hit = groups[at] == facts[target]

            @pl.when(hit)
            def _():
                if fill:
                    alive = token_at < lengths[at]
                    for lane in range(0, width, HD):
                        part = got[slot, :, lane:lane + HD]
                        ready[slot, :, lane:lane + HD] = jnp.where(alive, part, jnp.zeros_like(part))
                act(pltpu.make_async_copy(ready.at[slot], out.at[at, :, pl.ds(head * width, width)], sem))

            return slot + hit.astype(jnp.int32)

        lax.fori_loop(0, groups.shape[0], look, jnp.int32(0))

    each(lambda copy: copy.start(), True)
    each(lambda copy: copy.wait(), False)


def merge(facts, target, groups, lengths, got, out, head):
    return pl.pallas_call(
        functools.partial(merge_kernel, target, head),
        out_shape=jax.ShapeDtypeStruct(out.shape, out.dtype),
        in_specs=[SMEM, SMEM, SMEM, VMEM, HBM],
        out_specs=HBM,
        input_output_aliases={4: 0},
        scratch_shapes=[pltpu.VMEM(got.shape, got.dtype), pltpu.SemaphoreType.DMA],
        compiler_params=pltpu.CompilerParams(vmem_limit_bytes=1 << 23),
    )(facts, groups, lengths, got, out)


def after(value, *others):
    return lax.optimization_barrier((value,) + others)[0]


def gathered(queries, resp_kv, prompt_kv, lengths, group_of, first_head, kv_needed, per_kv):
    out = jax.ShapeDtypeStruct(queries.shape, jnp.bfloat16)
    facts = jnp.concatenate([jnp.zeros((GROUPS,), jnp.int32), group_of, lengths])
    for head in range(kv_needed):
        mine = lax.dynamic_index_in_dim(prompt_kv, first_head + head, 2, keepdims=False)
        own = lax.dynamic_index_in_dim(resp_kv, first_head + head, 2, keepdims=False)[None]
        whole = lax.all_gather(mine, "seq", axis=0, tiled=True)
        out, _ = attend(facts, queries, own, [whole], [out], head, per_kv, None, 16, fresh=head == 0)
    return out


def relayed(queries, resp_kv, prompt_kv, lengths, group_of, first_head, per_kv):
    me = lax.axis_index("seq")
    width = per_kv * HD
    middle, inward, outward = [(1, 2), (2, 1)], [(0, 1), (3, 2)], [(1, 0), (2, 3)]

    def send(pairs, value):
        return lax.ppermute(value, "seq", pairs)

    def two_heads(start):
        return lambda pairs: jnp.transpose(pairs[:, start:start + 2], (1, 0, 2))

    def two_own(start):
        return lambda pairs: jnp.transpose(pairs[:, :, start:start + 2], (2, 0, 1, 3))

    splits = prompt_kv.shape[2] // 2
    mine = lax.switch(first_head // 2, [two_heads(2 * at) for at in range(splits)], prompt_kv[0])
    inner_prompt = send(outward, mine)
    across = send(middle, mine)
    is_inner = (me == 1) | (me == 2)
    near = [send(inward, part) for part in cut(mine, ~is_inner)]

    low = me < 2
    outer, inner = jnp.where(low, 0, 3), jnp.where(low, 1, 2)
    far_inner, far_outer = jnp.where(low, 2, 1), jnp.where(low, 3, 0)
    facts = jnp.stack([
        me,
        jnp.zeros_like(me),
        jnp.where(is_inner, -1, inner),
        jnp.full_like(me, 2),
        jnp.where(is_inner, far_inner, -1),
        jnp.ones_like(me),
        jnp.where(is_inner, far_outer, -1),
        jnp.where(is_inner, far_outer, far_inner),
        jnp.where(is_inner, 0, 1),
        jnp.where(is_inner, -1, far_outer),
        jnp.where(is_inner, outer, -1),
    ]).astype(jnp.int32)
    facts = jnp.concatenate([facts, group_of, lengths])

    own = lax.switch(first_head // 2, [two_own(2 * at) for at in range(splits)], resp_kv)
    packed = pack(facts, 9, queries, own, width)
    out = jax.ShapeDtypeStruct(queries.shape, jnp.bfloat16)
    back_shape = jax.ShapeDtypeStruct((SLOTS, queries.shape[1], width), jnp.bfloat16)

    def run(cands, outs, passes, items, far=None, fresh=False, wait_for=None):
        return attend(facts, queries, own, cands, outs, 0, per_kv, passes, items, far, fresh, wait_for)

    out, token = run([mine], [out], [(False, 0, 1, 0), (False, 0, 1, 1)], 8, fresh=True, wait_for=packed)
    near[0] = gate(near[0], token)
    last = [send(middle, near[0])]
    handed = send(inward, gate(packed, near[0]))
    out, token = run([near[0]], [out], [(False, 10, 1, 0)], 4)
    near[1] = gate(near[1], token)
    last.append(send(middle, near[1]))
    inner_prompt = gate(inner_prompt, token)
    across = gate(across, token, inner_prompt)
    far_inner_prompt = [send(outward, part) for part in cut(across, is_inner)]
    out, _ = run(
        [near[1], across, inner_prompt], [out],
        [(False, 2, 3, 0), (False, 2, 3, 1), (False, 10, 1, 1), (False, 4, 5, 0), (False, 4, 5, 1)], 16, wait_for=near[1])
    back = [None, None]
    out, back[0], _ = run(
        [last[0], far_inner_prompt[0]], [out, back_shape], [(True, 6, 1, 0), (False, 7, 8, 0)], 8, handed)
    back[0] = send(outward, back[0])
    out, back[1], _ = run([last[1]], [out, back_shape], [(True, 6, 1, 1)], 4, handed)
    back[1] = send(outward, back[1])
    out, _ = run([last[1], far_inner_prompt[1]], [out], [(False, 7, 8, 1)], 4)
    for head in range(2):
        out = merge(facts, 9, group_of, lengths, back[head], out, head)
    return out


def shards(queries, resp_kv, prompt_kv, lengths, group_of):
    local_heads = queries.shape[2] // HD
    group = QHEADS // KVH
    kv_needed = max(local_heads // group, 1)
    per_kv = local_heads // kv_needed
    first_head = lax.axis_index("pp") * local_heads // group
    args = (queries, resp_kv, prompt_kv, lengths, group_of, first_head)
    if lax.axis_size("seq") == 4 and kv_needed == 2 and prompt_kv.shape[0] == 1:
        return relayed(*args, per_kv)
    return gathered(*args, kv_needed, per_kv)


def solution(mesh):
    placed = (
        P(("rep", "seq"), None, ("tp", "pp")),
        P(("rep", "seq"), None, "tp", None),
        P(("rep", "seq"), None, "tp", None),
        P(("rep", "seq")),
        P(("rep", "seq")),
    )
    return jax.shard_map(
        shards,
        mesh=mesh,
        in_specs=placed,
        out_specs=P(("rep", "seq"), None, ("tp", "pp")),
        check_vma=False,
    )
```

```python
import functools
import math

import jax
import jax.numpy as jnp
from jax import lax
from jax.experimental import pallas as pl
from jax.experimental.pallas import tpu as pltpu
from jax.sharding import PartitionSpec as P

QHEADS = 64
KVH = 8
HD = 128
LOG2E = math.log2(math.e)
VMEM_BYTES = 12 * 1024 * 1024
SLOTS = 8
HBM = pl.BlockSpec(memory_space=pl.ANY)
SMEM = pl.BlockSpec(memory_space=pltpu.SMEM)
VMEM = pl.BlockSpec(memory_space=pltpu.VMEM)


TN = (((0,), (0,)), ((), ()))
BLOCK = 512
SCORE_BLOCK = 1024
CHUNK = 32
GROUPS = 12


def stacked_heads(q_tile, per_kv):
    return jnp.concatenate([q_tile[:, g * HD:(g + 1) * HD] for g in range(per_kv)], axis=0)


def own_scores(own_tile, q_cols, rlen):
    own = jnp.dot(own_tile[:, :HD], q_cols, preferred_element_type=jnp.float32)
    own_at = lax.broadcasted_iota(jnp.int32, own.shape, 0)
    token_at = lax.broadcasted_iota(jnp.int32, own.shape, 1) % rlen
    return jnp.where(own_at <= token_at, own, -1e30)


def folded(values, op):
    return op(values.reshape(values.shape[0] // 8, 8, values.shape[1]), axis=0)


def turn(q_tile, per_kv, out_ref):
    out_ref[...] = stacked_heads(q_tile, per_kv).T


def finish(acc_ref, total_ref, length, per_kv, out_ref):
    out = (acc_ref[...] * (1.0 / total_ref[0:1, :])).T
    rlen = out_ref.shape[0]
    alive = lax.broadcasted_iota(jnp.int32, (rlen, HD), 0) < length
    for g in range(per_kv):
        part = jnp.where(alive, out[g * rlen:(g + 1) * rlen, :], 0.0)
        out_ref[:, g * HD:(g + 1) * HD] = part.astype(out_ref.dtype)


def scores_and_mix(q_cols, after_own, after_keys, after_s, after_u, after_peak, now):
    plen = after_keys.shape[0]
    scale = HD ** -0.5 * LOG2E
    own = own_scores(after_own, q_cols, after_own.shape[0])
    after_u[...] = own
    after_top = folded(own, jnp.max)
    if now is not None:
        s_ref, u_ref, peak_ref, own_tile, vt_ref, p_ref, acc_ref, total_ref = now
        peak = peak_ref[...]
        part = jnp.exp2((u_ref[...] - peak[0:1, :]) * scale)
        total = folded(part, jnp.sum)
        acc = lax.dot_general(own_tile[:, HD:], part.astype(jnp.bfloat16), TN, preferred_element_type=jnp.float32)
        spread = jnp.concatenate([peak] * (CHUNK // 8), axis=0)
    for at in range(0, plen, BLOCK):
        rows = pl.ds(at, BLOCK)
        if at % SCORE_BLOCK == 0:
            score_rows = pl.ds(at, SCORE_BLOCK)
            fresh = jnp.dot(after_keys[score_rows, :], q_cols, preferred_element_type=jnp.float32)
            after_s[score_rows, :] = fresh
            after_top = jnp.maximum(after_top, folded(fresh, jnp.max))
        if now is not None:
            for chunk in range(at, at + BLOCK, CHUNK):
                part = jnp.exp2((s_ref[chunk:chunk + CHUNK, :] - spread) * scale)
                total = total + folded(part, jnp.sum)
                p_ref[chunk:chunk + CHUNK, :] = part.astype(jnp.bfloat16)
            acc = acc + jnp.dot(vt_ref[:, rows], p_ref[rows, :], preferred_element_type=jnp.float32)
    after_peak[...] = jnp.broadcast_to(jnp.max(after_top, axis=0, keepdims=True), after_peak.shape)
    if now is not None:
        acc_ref[...] = acc
        total_ref[...] = jnp.broadcast_to(jnp.sum(total, axis=0, keepdims=True), total_ref.shape)


def listed(items, cap, count, facts, local, target, source, head):
    def look(at, n):
        hit = facts[GROUPS + at] == target

        @pl.when(hit)
        def _():
            items[n] = at
            items[cap + n] = source
            items[2 * cap + n] = facts[GROUPS + local + at]
            items[3 * cap + n] = head

        return n + hit.astype(jnp.int32)

    return lax.fori_loop(0, local, look, count)


def attend_kernel(passes, n_cand, per_kv, whole_head, two, fresh, waits, *refs):
    refs = list(refs)
    facts, refs = refs[0], refs[1:]
    if two:
        x_ref, refs = refs[0], refs[1:]
    q_ref, own_ref = refs[:2]
    cands, refs = refs[2:2 + n_cand], refs[2 + n_cand + waits:]
    n_out = 2 if two else 1
    if not fresh:
        refs = refs[1:]
    outs, token, refs = refs[:n_out], refs[n_out], refs[n_out + 1:]
    items, at_slot, q_buf, own_buf, key_buf, value_buf, vt_buf, s0, s1, u0, u1, peak0, peak1, turned0, turned1, acc0, acc1, total0, total1, p_buf, o0, o1, info, q_sem, own_sem, kv_sem, o_sem = refs
    s_buf, u_buf, peak_buf, o_buf = (s0, s1), (u0, u1), (peak0, peak1), (o0, o1)
    turned, acc_buf, total_buf = (turned0, turned1), (acc0, acc1), (total0, total1)
    local = (facts.shape[0] - GROUPS) // 2
    cap = items.shape[0] // 4
    width = per_kv * HD
    stacked = passes is None

    count = jnp.int32(0)
    if stacked:
        def one_prompt(prompt, n):
            return listed(items, cap, n, facts, local, prompt, prompt, whole_head)

        count = lax.fori_loop(0, cands[0].shape[0], one_prompt, count)
    else:
        for far, target, source, head in passes:
            if not far:
                count = listed(items, cap, count, facts, local, facts[target], facts[source], head)
                continue
            notes = pltpu.make_async_copy(x_ref.at[0, :, pl.ds(2 * (width + 2 * HD), HD)], info, kv_sem)
            notes.start()
            notes.wait()
            far_head = head
            handed = jnp.max(info[0:16, :].astype(jnp.float32)).astype(jnp.int32)
            handed = jnp.where(facts[target] >= 0, jnp.minimum(handed, SLOTS), 0)

            def take(slot, n):
                items[n] = local + slot
                items[cap + n] = facts[source]
                items[2 * cap + n] = q_buf.shape[1]
                items[3 * cap + n] = far_head
                return n + 1

            count = lax.fori_loop(0, handed, take, count)

    token[0] = count

    def each_array(i, act_local, act_far):
        at = items[i]
        if not two:
            act_local(at)
            return

        @pl.when(at < local)
        def _():
            act_local(at)

        @pl.when(at >= local)
        def _():
            act_far(at - local)

    first = pl.ds(0, width)

    def lanes(i, step, skip, size):
        return pl.ds(pl.multiple_of(items[3 * cap + i] * step + skip, HD), size)

    def mine(i):
        return lanes(i, width, 0, width)

    def fetch(i):
        slot, fourth = lax.rem(i, 2), lax.rem(i, 4)

        def here(at):
            pltpu.make_async_copy(q_ref.at[at, :, mine(i)], q_buf.at[slot], q_sem.at[slot]).start()
            pltpu.make_async_copy(own_ref.at[items[3 * cap + i], at], own_buf.at[fourth], own_sem.at[fourth]).start()

        def far(at):
            pltpu.make_async_copy(x_ref.at[at, :, lanes(i, width + 2 * HD, 0, width)], q_buf.at[slot], q_sem.at[slot]).start()
            pltpu.make_async_copy(x_ref.at[at, :, lanes(i, width + 2 * HD, width, 2 * HD)], own_buf.at[fourth], own_sem.at[fourth]).start()

        each_array(i, here, far)

    def fetched(i):
        slot, fourth = lax.rem(i, 2), lax.rem(i, 4)
        pltpu.make_async_copy(q_ref.at[0, :, first], q_buf.at[slot], q_sem.at[slot]).wait()
        pltpu.make_async_copy(own_ref.at[0, 0], own_buf.at[fourth], own_sem.at[fourth]).wait()

    def store(i, slot):
        def here(at):
            pltpu.make_async_copy(o_buf[slot], outs[0].at[at, :, mine(i)], o_sem.at[slot]).start()

        def far(at):
            pltpu.make_async_copy(o_buf[slot], outs[1].at[at], o_sem.at[slot]).start()

        each_array(i, here, far)

    def stored(slot):
        pltpu.make_async_copy(o_buf[slot], outs[0].at[0, :, first], o_sem.at[slot]).wait()

    keys, values = pl.ds(0, HD), pl.ds(HD, HD)

    def ask(i, into):
        source = items[cap + i]

        def bring(pairs):
            pltpu.make_async_copy(pairs.at[:, keys], key_buf.at[into], kv_sem).start()
            pltpu.make_async_copy(pairs.at[:, values], value_buf, kv_sem).start()

        if stacked:
            bring(cands[0].at[source])
        else:
            for which in range(n_cand):
                @pl.when(source == which)
                def _():
                    bring(cands[which].at[items[3 * cap + i]] if len(cands[which].shape) == 3 else cands[which])

    def receive(into):
        for _ in range(2):
            pltpu.make_async_copy(value_buf, value_buf, kv_sem).wait()
        vt_buf[into] = value_buf[...].T

    @pl.when(count > 0)
    def _():
        ask(0, 0)
        fetch(jnp.int32(0))

        @pl.when(count > 1)
        def _():
            fetch(jnp.int32(1))

        at_slot[0] = 0
        fetched(jnp.int32(0))
        turn(q_buf[0], per_kv, turned[0])

        @pl.when(count > 2)
        def _():
            fetch(jnp.int32(2))

        @pl.when(count > 1)
        def _():
            fetched(jnp.int32(1))

        turn(q_buf[1], per_kv, turned[1])
        receive(0)
        scores_and_mix(turned[0][...], own_buf[0], key_buf.at[0], s_buf[0], u_buf[0], peak_buf[0], None)

        def one(i, slot):
            other = 1 - slot
            held = at_slot[0]
            more = i + 1 < count
            after_i = jnp.minimum(i + 1, count - 1)
            moved = more & ((items[cap + after_i] != items[cap + i]) | (items[3 * cap + after_i] != items[3 * cap + i]))
            holds = jnp.where(moved, 1 - held, held)
            at_slot[0] = holds

            @pl.when(i + 2 < count)
            def _():
                fetched(i + 2)

            @pl.when(i + 3 < count)
            def _():
                fetch(i + 3)

            @pl.when(moved)
            def _():
                ask(i + 1, holds)
                receive(holds)

            @pl.when(i >= 3)
            def _():
                stored(other)

            now = (
                s_buf[slot], u_buf[slot], peak_buf[slot], own_buf[lax.rem(i, 4)], vt_buf.at[held], p_buf,
                acc_buf[slot], total_buf[slot])
            scores_and_mix(
                turned[other][...], own_buf[lax.rem(i + 1, 4)], key_buf.at[holds],
                s_buf[other], u_buf[other], peak_buf[other], now)
            turn(q_buf[slot], per_kv, turned[slot])
            finish(acc_buf[other], total_buf[other], items[2 * cap + jnp.maximum(i - 1, 0)], per_kv, o_buf[other])

            @pl.when(i >= 1)
            def _():
                store(i - 1, other)

        def pair(j, _):
            one(2 * j, 0)

            @pl.when(2 * j + 1 < count)
            def _():
                one(2 * j + 1, 1)

            return 0

        lax.fori_loop(0, lax.div(count + 1, 2), pair, 0)
        final = count - 1
        for slot in range(2):
            @pl.when(lax.rem(final, 2) == slot)
            def _():
                @pl.when(final >= 2)
                def _():
                    stored(slot)

                finish(acc_buf[slot], total_buf[slot], items[2 * cap + final], per_kv, o_buf[slot])
                store(final, slot)

        stored(0)

        @pl.when(count > 1)
        def _():
            stored(1)


def attend(facts, queries, own, cands, outs, head, per_kv, passes, items, far=None, fresh=False, wait_for=None):
    rlen = queries.shape[1]
    plen = cands[0].shape[-2]
    width = per_kv * HD
    small = [facts]
    large = ([far] if far is not None else []) + [queries, own] + cands
    operands = small + large + ([] if wait_for is None else [wait_for])
    aliases = {}
    if not fresh:
        aliases = {len(operands): 0}
        operands = operands + [outs[0]]
    cap = 2 * queries.shape[0] + (SLOTS if far is not None else 0)
    return pl.pallas_call(
        functools.partial(attend_kernel, passes, len(cands), per_kv, head, far is not None, fresh, wait_for is not None),
        out_shape=[jax.ShapeDtypeStruct(o.shape, o.dtype) for o in outs] + [jax.ShapeDtypeStruct((1,), jnp.int32)],
        in_specs=[SMEM] * len(small) + [HBM] * (len(operands) - len(small)),
        out_specs=[HBM] * len(outs) + [SMEM],
        input_output_aliases=aliases,
        scratch_shapes=[
            pltpu.SMEM((4 * cap,), jnp.int32),
            pltpu.SMEM((1,), jnp.int32),
            pltpu.VMEM((2, rlen, width), jnp.bfloat16),
            pltpu.VMEM((4, rlen, 2 * HD), jnp.bfloat16),
            pltpu.VMEM((2, plen, HD), jnp.bfloat16),
            pltpu.VMEM((plen, HD), jnp.bfloat16),
            pltpu.VMEM((2, HD, plen), jnp.bfloat16),
            pltpu.VMEM((plen, per_kv * rlen), jnp.float32),
            pltpu.VMEM((plen, per_kv * rlen), jnp.float32),
            pltpu.VMEM((rlen, per_kv * rlen), jnp.float32),
            pltpu.VMEM((rlen, per_kv * rlen), jnp.float32),
            pltpu.VMEM((8, per_kv * rlen), jnp.float32),
            pltpu.VMEM((8, per_kv * rlen), jnp.float32),
            pltpu.VMEM((HD, per_kv * rlen), jnp.bfloat16),
            pltpu.VMEM((HD, per_kv * rlen), jnp.bfloat16),
            pltpu.VMEM((HD, per_kv * rlen), jnp.float32),
            pltpu.VMEM((HD, per_kv * rlen), jnp.float32),
            pltpu.VMEM((8, per_kv * rlen), jnp.float32),
            pltpu.VMEM((8, per_kv * rlen), jnp.float32),
            pltpu.VMEM((plen, per_kv * rlen), jnp.bfloat16),
            pltpu.VMEM((rlen, width), jnp.bfloat16),
            pltpu.VMEM((rlen, width), jnp.bfloat16),
            pltpu.VMEM((rlen, HD), jnp.bfloat16),
            pltpu.SemaphoreType.DMA((2,)),
            pltpu.SemaphoreType.DMA((4,)),
            pltpu.SemaphoreType.DMA,
            pltpu.SemaphoreType.DMA((2,)),
        ],
        compiler_params=pltpu.CompilerParams(vmem_limit_bytes=VMEM_BYTES),
        cost_estimate=pl.CostEstimate(flops=items << 20, bytes_accessed=1 << 16, transcendentals=0),
    )(*operands)


def pack_kernel(target, width, facts, q_ref, own_ref, out, sem):
    step = width + 2 * HD
    local = q_ref.shape[0]

    def each(act):
        def look(at, slot):
            hit = facts[GROUPS + at] == facts[target]

            @pl.when(hit)
            def _():
                for head in range(2):
                    part = pl.ds(head * width, width)
                    act(pltpu.make_async_copy(q_ref.at[at, :, part], out.at[slot, :, pl.ds(head * step, width)], sem))
                    act(pltpu.make_async_copy(
                        own_ref.at[head, at], out.at[slot, :, pl.ds(head * step + width, 2 * HD)], sem))

            return slot + hit.astype(jnp.int32)

        return lax.fori_loop(0, local, look, jnp.int32(0))

    count = each(lambda copy: copy.start())
    out[0, :, 2 * step:] = jnp.full((out.shape[1], HD), count, jnp.int32).astype(jnp.float32).astype(out.dtype)
    each(lambda copy: copy.wait())


def pack(facts, target, queries, own, width):
    return pl.pallas_call(
        functools.partial(pack_kernel, target, width),
        out_shape=jax.ShapeDtypeStruct((SLOTS, queries.shape[1], 2 * width + 5 * HD), queries.dtype),
        in_specs=[SMEM, HBM, HBM],
        out_specs=VMEM,
        scratch_shapes=[pltpu.SemaphoreType.DMA],
        compiler_params=pltpu.CompilerParams(vmem_limit_bytes=1 << 23),
    )(facts, queries, own)


def gate_kernel(*refs):
    pass


def gate(value, *others):
    return pl.pallas_call(
        gate_kernel,
        out_shape=jax.ShapeDtypeStruct(value.shape, value.dtype),
        in_specs=[HBM] + [SMEM if other.ndim == 1 else HBM for other in others],
        out_specs=HBM,
        input_output_aliases={0: 0},
    )(value, *others)


def cut_kernel(pair, out0, out1, sem):
    copies = [pltpu.make_async_copy(pair.at[head], out, sem.at[head]) for head, out in enumerate((out0, out1))]
    for copy in copies:
        copy.start()
    for copy in copies:
        copy.wait()


def cut(pair):
    shape = jax.ShapeDtypeStruct(pair.shape[1:], pair.dtype)
    return pl.pallas_call(
        cut_kernel,
        out_shape=[shape, shape],
        in_specs=[HBM],
        out_specs=[VMEM, VMEM],
        scratch_shapes=[pltpu.SemaphoreType.DMA((2,))],
        compiler_params=pltpu.CompilerParams(vmem_limit_bytes=1 << 23),
    )(pair)


def merge_kernel(target, head, facts, groups, lengths, got, old, out, ready, sem):
    rlen, width = got.shape[1:]
    token_at = lax.broadcasted_iota(jnp.int32, (rlen, HD), 0)

    def each(act, fill):
        def look(at, slot):
            hit = groups[at] == facts[target]

            @pl.when(hit)
            def _():
                if fill:
                    alive = token_at < lengths[at]
                    for lane in range(0, width, HD):
                        part = got[slot, :, lane:lane + HD]
                        ready[slot, :, lane:lane + HD] = jnp.where(alive, part, jnp.zeros_like(part))
                act(pltpu.make_async_copy(ready.at[slot], out.at[at, :, pl.ds(head * width, width)], sem))

            return slot + hit.astype(jnp.int32)

        lax.fori_loop(0, groups.shape[0], look, jnp.int32(0))

    each(lambda copy: copy.start(), True)
    each(lambda copy: copy.wait(), False)


def merge(facts, target, groups, lengths, got, out, head):
    return pl.pallas_call(
        functools.partial(merge_kernel, target, head),
        out_shape=jax.ShapeDtypeStruct(out.shape, out.dtype),
        in_specs=[SMEM, SMEM, SMEM, VMEM, HBM],
        out_specs=HBM,
        input_output_aliases={4: 0},
        scratch_shapes=[pltpu.VMEM(got.shape, got.dtype), pltpu.SemaphoreType.DMA],
        compiler_params=pltpu.CompilerParams(vmem_limit_bytes=1 << 23),
    )(facts, groups, lengths, got, out)


def after(value, *others):
    return lax.optimization_barrier((value,) + others)[0]


def gathered(queries, resp_kv, prompt_kv, lengths, group_of, first_head, kv_needed, per_kv):
    out = jax.ShapeDtypeStruct(queries.shape, jnp.bfloat16)
    facts = jnp.concatenate([jnp.zeros((GROUPS,), jnp.int32), group_of, lengths])
    for head in range(kv_needed):
        mine = lax.dynamic_index_in_dim(prompt_kv, first_head + head, 2, keepdims=False)
        own = lax.dynamic_index_in_dim(resp_kv, first_head + head, 2, keepdims=False)[None]
        whole = lax.all_gather(mine, "seq", axis=0, tiled=True)
        out, _ = attend(facts, queries, own, [whole], [out], head, per_kv, None, 16, fresh=head == 0)
    return out


def relayed(queries, resp_kv, prompt_kv, lengths, group_of, first_head, per_kv):
    me = lax.axis_index("seq")
    width = per_kv * HD
    middle, inward, outward = [(1, 2), (2, 1)], [(0, 1), (3, 2)], [(1, 0), (2, 3)]

    def send(pairs, value):
        return lax.ppermute(value, "seq", pairs)

    def two_heads(start):
        return lambda pairs: jnp.transpose(pairs[:, start:start + 2], (1, 0, 2))

    def two_own(start):
        return lambda pairs: jnp.transpose(pairs[:, :, start:start + 2], (2, 0, 1, 3))

    splits = prompt_kv.shape[2] // 2
    mine = lax.switch(first_head // 2, [two_heads(2 * at) for at in range(splits)], prompt_kv[0])
    inner_prompt = send(outward, mine)
    parts = cut(mine)
    across, near = [], []
    for part in parts:
        across.append(send(middle, part))
        near.append(send(inward, part))

    low = me < 2
    is_inner = (me == 1) | (me == 2)
    outer, inner = jnp.where(low, 0, 3), jnp.where(low, 1, 2)
    far_inner, far_outer = jnp.where(low, 2, 1), jnp.where(low, 3, 0)
    facts = jnp.stack([
        me,
        jnp.zeros_like(me),
        jnp.where(is_inner, -1, inner),
        jnp.full_like(me, 3),
        jnp.where(is_inner, far_inner, -1),
        jnp.ones_like(me),
        jnp.where(is_inner, far_outer, -1),
        jnp.where(is_inner, far_outer, far_inner),
        jnp.where(is_inner, 0, 1),
        jnp.where(is_inner, -1, far_outer),
        jnp.where(is_inner, outer, -1),
        jnp.full_like(me, 2),
    ]).astype(jnp.int32)
    facts = jnp.concatenate([facts, group_of, lengths])

    own = lax.switch(first_head // 2, [two_own(2 * at) for at in range(splits)], resp_kv)
    packed = pack(facts, 9, queries, own, width)
    out = jax.ShapeDtypeStruct(queries.shape, jnp.bfloat16)
    back_shape = jax.ShapeDtypeStruct((SLOTS, queries.shape[1], width), jnp.bfloat16)

    def run(cands, outs, passes, items, far=None, fresh=False, wait_for=None):
        return attend(facts, queries, own, cands, outs, 0, per_kv, passes, items, far, fresh, wait_for)

    out, token = run([mine], [out], [(False, 0, 1, 0), (False, 0, 1, 1)], 8, fresh=True, wait_for=packed)
    near[0] = gate(near[0], token)
    last = [send(middle, near[0])]
    handed = send(inward, gate(packed, near[0]))
    across[0] = gate(across[0], token, inner_prompt)
    far_inner_prompt = [send(outward, across[0])]
    out, token = run([near[0]], [out], [(False, 10, 1, 0)], 4)
    near[1] = gate(near[1], token)
    last.append(send(middle, near[1]))
    across[1] = gate(across[1], token)
    far_inner_prompt.append(send(outward, across[1]))
    out, _ = run(
        [near[1], across[0], across[1], inner_prompt], [out],
        [(False, 2, 3, 0), (False, 2, 3, 1), (False, 10, 1, 1), (False, 4, 5, 0), (False, 4, 11, 1)], 16, wait_for=near[1])
    back = [None, None]
    out, back[0], _ = run(
        [last[0], far_inner_prompt[0]], [out, back_shape], [(True, 6, 1, 0), (False, 7, 8, 0)], 8, handed)
    back[0] = send(outward, back[0])
    out, back[1], _ = run([last[1]], [out, back_shape], [(True, 6, 1, 1)], 4, handed)
    back[1] = send(outward, back[1])
    out, _ = run([last[1], far_inner_prompt[1]], [out], [(False, 7, 8, 1)], 4)
    for head in range(2):
        out = merge(facts, 9, group_of, lengths, back[head], out, head)
    return out


def shards(queries, resp_kv, prompt_kv, lengths, group_of):
    local_heads = queries.shape[2] // HD
    group = QHEADS // KVH
    kv_needed = max(local_heads // group, 1)
    per_kv = local_heads // kv_needed
    first_head = lax.axis_index("pp") * local_heads // group
    args = (queries, resp_kv, prompt_kv, lengths, group_of, first_head)
    if lax.axis_size("seq") == 4 and kv_needed == 2 and prompt_kv.shape[0] == 1:
        return relayed(*args, per_kv)
    return gathered(*args, kv_needed, per_kv)


def solution(mesh):
    placed = (
        P(("rep", "seq"), None, ("tp", "pp")),
        P(("rep", "seq"), None, "tp", None),
        P(("rep", "seq"), None, "tp", None),
        P(("rep", "seq")),
        P(("rep", "seq")),
    )
    return jax.shard_map(
        shards,
        mesh=mesh,
        in_specs=placed,
        out_specs=P(("rep", "seq"), None, ("tp", "pp")),
        check_vma=False,
    )
```

```python
import functools
import math

import jax
import jax.numpy as jnp
from jax import lax
from jax.experimental import pallas as pl
from jax.experimental.pallas import tpu as pltpu
from jax.sharding import PartitionSpec as P

QHEADS = 64
KVH = 8
HD = 128
LOG2E = math.log2(math.e)
VMEM_BYTES = 12 * 1024 * 1024
SLOTS = 8
HBM = pl.BlockSpec(memory_space=pl.ANY)
SMEM = pl.BlockSpec(memory_space=pltpu.SMEM)
VMEM = pl.BlockSpec(memory_space=pltpu.VMEM)


TN = (((0,), (0,)), ((), ()))
BLOCK = 512
SCORE_BLOCK = 1024
CHUNK = 32
GROUPS = 12


def stacked_heads(q_tile, per_kv):
    return jnp.concatenate([q_tile[:, g * HD:(g + 1) * HD] for g in range(per_kv)], axis=0)


def own_scores(own_tile, q_cols, rlen):
    own = jnp.dot(own_tile[:, :HD], q_cols, preferred_element_type=jnp.float32)
    own_at = lax.broadcasted_iota(jnp.int32, own.shape, 0)
    token_at = lax.broadcasted_iota(jnp.int32, own.shape, 1) % rlen
    return jnp.where(own_at <= token_at, own, -1e30)


def folded(values, op):
    return op(values.reshape(values.shape[0] // 8, 8, values.shape[1]), axis=0)


def turn(q_tile, per_kv, out_ref):
    out_ref[...] = stacked_heads(q_tile, per_kv).T


def finish(acc_ref, total_ref, length, per_kv, out_ref):
    out = (acc_ref[...] * (1.0 / total_ref[0:1, :])).T
    rlen = out_ref.shape[0]
    alive = lax.broadcasted_iota(jnp.int32, (rlen, HD), 0) < length
    for g in range(per_kv):
        part = jnp.where(alive, out[g * rlen:(g + 1) * rlen, :], 0.0)
        out_ref[:, g * HD:(g + 1) * HD] = part.astype(out_ref.dtype)


def scores_and_mix(q_cols, after_own, after_keys, after_s, after_u, after_peak, now):
    plen = after_keys.shape[0]
    scale = HD ** -0.5 * LOG2E
    own = own_scores(after_own, q_cols, after_own.shape[0])
    after_u[...] = own
    after_top = folded(own, jnp.max)
    if now is not None:
        s_ref, u_ref, peak_ref, own_tile, vt_ref, p_ref, acc_ref, total_ref = now
        peak = peak_ref[...]
        part = jnp.exp2((u_ref[...] - peak[0:1, :]) * scale)
        total = folded(part, jnp.sum)
        acc = lax.dot_general(own_tile[:, HD:], part.astype(jnp.bfloat16), TN, preferred_element_type=jnp.float32)
        spread = jnp.concatenate([peak] * (CHUNK // 8), axis=0)
    for at in range(0, plen, BLOCK):
        rows = pl.ds(at, BLOCK)
        if at % SCORE_BLOCK == 0:
            score_rows = pl.ds(at, SCORE_BLOCK)
            fresh = jnp.dot(after_keys[score_rows, :], q_cols, preferred_element_type=jnp.float32)
            after_s[score_rows, :] = fresh
            after_top = jnp.maximum(after_top, folded(fresh, jnp.max))
        if now is not None:
            for chunk in range(at, at + BLOCK, CHUNK):
                part = jnp.exp2((s_ref[chunk:chunk + CHUNK, :] - spread) * scale)
                total = total + folded(part, jnp.sum)
                p_ref[chunk:chunk + CHUNK, :] = part.astype(jnp.bfloat16)
            acc = acc + jnp.dot(vt_ref[:, rows], p_ref[rows, :], preferred_element_type=jnp.float32)
    after_peak[...] = jnp.broadcast_to(jnp.max(after_top, axis=0, keepdims=True), after_peak.shape)
    if now is not None:
        acc_ref[...] = acc
        total_ref[...] = jnp.broadcast_to(jnp.sum(total, axis=0, keepdims=True), total_ref.shape)


def listed(items, cap, count, facts, local, target, source, head):
    def look(at, n):
        hit = facts[GROUPS + at] == target

        @pl.when(hit)
        def _():
            items[n] = at
            items[cap + n] = source
            items[2 * cap + n] = facts[GROUPS + local + at]
            items[3 * cap + n] = head

        return n + hit.astype(jnp.int32)

    return lax.fori_loop(0, local, look, count)


def attend_kernel(passes, n_cand, per_kv, whole_head, two, fresh, waits, *refs):
    refs = list(refs)
    facts, refs = refs[0], refs[1:]
    if two:
        x_ref, refs = refs[0], refs[1:]
    q_ref, own_ref = refs[:2]
    cands, refs = refs[2:2 + n_cand], refs[2 + n_cand + waits:]
    n_out = 2 if two else 1
    if not fresh:
        refs = refs[1:]
    outs, token, refs = refs[:n_out], refs[n_out], refs[n_out + 1:]
    items, at_slot, q_buf, own_buf, key_buf, value_buf, vt_buf, s0, s1, u0, u1, peak0, peak1, turned0, turned1, acc0, acc1, total0, total1, p_buf, o0, o1, info, q_sem, own_sem, kv_sem, o_sem = refs
    s_buf, u_buf, peak_buf, o_buf = (s0, s1), (u0, u1), (peak0, peak1), (o0, o1)
    turned, acc_buf, total_buf = (turned0, turned1), (acc0, acc1), (total0, total1)
    local = (facts.shape[0] - GROUPS) // 2
    cap = items.shape[0] // 4
    width = per_kv * HD
    stacked = passes is None

    count = jnp.int32(0)
    if stacked:
        def one_prompt(prompt, n):
            return listed(items, cap, n, facts, local, prompt, prompt, whole_head)

        count = lax.fori_loop(0, cands[0].shape[0], one_prompt, count)
    else:
        for far, target, source, head in passes:
            if not far:
                count = listed(items, cap, count, facts, local, facts[target], facts[source], head)
                continue
            notes = pltpu.make_async_copy(x_ref.at[0, :, pl.ds(2 * (width + 2 * HD), HD)], info, kv_sem)
            notes.start()
            notes.wait()
            far_head = head
            handed = jnp.max(info[0:16, :].astype(jnp.float32)).astype(jnp.int32)
            handed = jnp.where(facts[target] >= 0, jnp.minimum(handed, SLOTS), 0)

            def take(slot, n):
                items[n] = local + slot
                items[cap + n] = facts[source]
                items[2 * cap + n] = q_buf.shape[1]
                items[3 * cap + n] = far_head
                return n + 1

            count = lax.fori_loop(0, handed, take, count)

    token[0] = count

    def each_array(i, act_local, act_far):
        at = items[i]
        if not two:
            act_local(at)
            return

        @pl.when(at < local)
        def _():
            act_local(at)

        @pl.when(at >= local)
        def _():
            act_far(at - local)

    first = pl.ds(0, width)

    def lanes(i, step, skip, size):
        return pl.ds(pl.multiple_of(items[3 * cap + i] * step + skip, HD), size)

    def mine(i):
        return lanes(i, width, 0, width)

    def fetch(i):
        slot, fourth = lax.rem(i, 2), lax.rem(i, 4)

        def here(at):
            pltpu.make_async_copy(q_ref.at[at, :, mine(i)], q_buf.at[slot], q_sem.at[slot]).start()
            pltpu.make_async_copy(own_ref.at[items[3 * cap + i], at], own_buf.at[fourth], own_sem.at[fourth]).start()

        def far(at):
            pltpu.make_async_copy(x_ref.at[at, :, lanes(i, width + 2 * HD, 0, width)], q_buf.at[slot], q_sem.at[slot]).start()
            pltpu.make_async_copy(x_ref.at[at, :, lanes(i, width + 2 * HD, width, 2 * HD)], own_buf.at[fourth], own_sem.at[fourth]).start()

        each_array(i, here, far)

    def fetched(i):
        slot, fourth = lax.rem(i, 2), lax.rem(i, 4)
        pltpu.make_async_copy(q_ref.at[0, :, first], q_buf.at[slot], q_sem.at[slot]).wait()
        pltpu.make_async_copy(own_ref.at[0, 0], own_buf.at[fourth], own_sem.at[fourth]).wait()

    def store(i, slot):
        def here(at):
            pltpu.make_async_copy(o_buf[slot], outs[0].at[at, :, mine(i)], o_sem.at[slot]).start()

        def far(at):
            pltpu.make_async_copy(o_buf[slot], outs[1].at[at], o_sem.at[slot]).start()

        each_array(i, here, far)

    def stored(slot):
        pltpu.make_async_copy(o_buf[slot], outs[0].at[0, :, first], o_sem.at[slot]).wait()

    keys, values = pl.ds(0, HD), pl.ds(HD, HD)

    def ask(i, into):
        source = items[cap + i]

        def bring(pairs):
            pltpu.make_async_copy(pairs.at[:, keys], key_buf.at[into], kv_sem).start()
            pltpu.make_async_copy(pairs.at[:, values], value_buf, kv_sem).start()

        if stacked:
            bring(cands[0].at[source])
        else:
            for which in range(n_cand):
                @pl.when(source == which)
                def _():
                    bring(cands[which].at[items[3 * cap + i]] if len(cands[which].shape) == 3 else cands[which])

    def receive(into):
        for _ in range(2):
            pltpu.make_async_copy(value_buf, value_buf, kv_sem).wait()
        vt_buf[into] = value_buf[...].T

    @pl.when(count > 0)
    def _():
        ask(0, 0)
        fetch(jnp.int32(0))

        @pl.when(count > 1)
        def _():
            fetch(jnp.int32(1))

        at_slot[0] = 0
        fetched(jnp.int32(0))
        turn(q_buf[0], per_kv, turned[0])

        @pl.when(count > 2)
        def _():
            fetch(jnp.int32(2))

        @pl.when(count > 1)
        def _():
            fetched(jnp.int32(1))

        turn(q_buf[1], per_kv, turned[1])
        receive(0)
        scores_and_mix(turned[0][...], own_buf[0], key_buf.at[0], s_buf[0], u_buf[0], peak_buf[0], None)

        def one(i, slot):
            other = 1 - slot
            held = at_slot[0]
            more = i + 1 < count
            after_i = jnp.minimum(i + 1, count - 1)
            moved = more & ((items[cap + after_i] != items[cap + i]) | (items[3 * cap + after_i] != items[3 * cap + i]))
            holds = jnp.where(moved, 1 - held, held)
            at_slot[0] = holds

            @pl.when(i + 2 < count)
            def _():
                fetched(i + 2)

            @pl.when(i + 3 < count)
            def _():
                fetch(i + 3)

            @pl.when(moved)
            def _():
                ask(i + 1, holds)
                receive(holds)

            @pl.when(i >= 3)
            def _():
                stored(other)

            now = (
                s_buf[slot], u_buf[slot], peak_buf[slot], own_buf[lax.rem(i, 4)], vt_buf.at[held], p_buf,
                acc_buf[slot], total_buf[slot])
            scores_and_mix(
                turned[other][...], own_buf[lax.rem(i + 1, 4)], key_buf.at[holds],
                s_buf[other], u_buf[other], peak_buf[other], now)
            turn(q_buf[slot], per_kv, turned[slot])
            finish(acc_buf[other], total_buf[other], items[2 * cap + jnp.maximum(i - 1, 0)], per_kv, o_buf[other])

            @pl.when(i >= 1)
            def _():
                store(i - 1, other)

        def pair(j, _):
            one(2 * j, 0)

            @pl.when(2 * j + 1 < count)
            def _():
                one(2 * j + 1, 1)

            return 0

        lax.fori_loop(0, lax.div(count + 1, 2), pair, 0)
        final = count - 1
        for slot in range(2):
            @pl.when(lax.rem(final, 2) == slot)
            def _():
                @pl.when(final >= 2)
                def _():
                    stored(slot)

                finish(acc_buf[slot], total_buf[slot], items[2 * cap + final], per_kv, o_buf[slot])
                store(final, slot)

        stored(0)

        @pl.when(count > 1)
        def _():
            stored(1)


def attend(facts, queries, own, cands, outs, head, per_kv, passes, items, far=None, fresh=False, wait_for=None):
    rlen = queries.shape[1]
    plen = cands[0].shape[-2]
    width = per_kv * HD
    small = [facts]
    large = ([far] if far is not None else []) + [queries, own] + cands
    operands = small + large + ([] if wait_for is None else [wait_for])
    aliases = {}
    if not fresh:
        aliases = {len(operands): 0}
        operands = operands + [outs[0]]
    cap = 2 * queries.shape[0] + (SLOTS if far is not None else 0)
    return pl.pallas_call(
        functools.partial(attend_kernel, passes, len(cands), per_kv, head, far is not None, fresh, wait_for is not None),
        out_shape=[jax.ShapeDtypeStruct(o.shape, o.dtype) for o in outs] + [jax.ShapeDtypeStruct((1,), jnp.int32)],
        in_specs=[SMEM] * len(small) + [HBM] * (len(operands) - len(small)),
        out_specs=[HBM] * len(outs) + [SMEM],
        input_output_aliases=aliases,
        scratch_shapes=[
            pltpu.SMEM((4 * cap,), jnp.int32),
            pltpu.SMEM((1,), jnp.int32),
            pltpu.VMEM((2, rlen, width), jnp.bfloat16),
            pltpu.VMEM((4, rlen, 2 * HD), jnp.bfloat16),
            pltpu.VMEM((2, plen, HD), jnp.bfloat16),
            pltpu.VMEM((plen, HD), jnp.bfloat16),
            pltpu.VMEM((2, HD, plen), jnp.bfloat16),
            pltpu.VMEM((plen, per_kv * rlen), jnp.float32),
            pltpu.VMEM((plen, per_kv * rlen), jnp.float32),
            pltpu.VMEM((rlen, per_kv * rlen), jnp.float32),
            pltpu.VMEM((rlen, per_kv * rlen), jnp.float32),
            pltpu.VMEM((8, per_kv * rlen), jnp.float32),
            pltpu.VMEM((8, per_kv * rlen), jnp.float32),
            pltpu.VMEM((HD, per_kv * rlen), jnp.bfloat16),
            pltpu.VMEM((HD, per_kv * rlen), jnp.bfloat16),
            pltpu.VMEM((HD, per_kv * rlen), jnp.float32),
            pltpu.VMEM((HD, per_kv * rlen), jnp.float32),
            pltpu.VMEM((8, per_kv * rlen), jnp.float32),
            pltpu.VMEM((8, per_kv * rlen), jnp.float32),
            pltpu.VMEM((plen, per_kv * rlen), jnp.bfloat16),
            pltpu.VMEM((rlen, width), jnp.bfloat16),
            pltpu.VMEM((rlen, width), jnp.bfloat16),
            pltpu.VMEM((rlen, HD), jnp.bfloat16),
            pltpu.SemaphoreType.DMA((2,)),
            pltpu.SemaphoreType.DMA((4,)),
            pltpu.SemaphoreType.DMA,
            pltpu.SemaphoreType.DMA((2,)),
        ],
        compiler_params=pltpu.CompilerParams(vmem_limit_bytes=VMEM_BYTES),
        cost_estimate=pl.CostEstimate(flops=items << 20, bytes_accessed=1 << 16, transcendentals=0),
    )(*operands)


def pack_kernel(target, width, facts, q_ref, own_ref, out, sem):
    step = width + 2 * HD
    local = q_ref.shape[0]

    def each(act):
        def look(at, slot):
            hit = facts[GROUPS + at] == facts[target]

            @pl.when(hit)
            def _():
                for head in range(2):
                    part = pl.ds(head * width, width)
                    act(pltpu.make_async_copy(q_ref.at[at, :, part], out.at[slot, :, pl.ds(head * step, width)], sem))
                    act(pltpu.make_async_copy(
                        own_ref.at[head, at], out.at[slot, :, pl.ds(head * step + width, 2 * HD)], sem))

            return slot + hit.astype(jnp.int32)

        return lax.fori_loop(0, local, look, jnp.int32(0))

    count = each(lambda copy: copy.start())
    out[0, :, 2 * step:] = jnp.full((out.shape[1], HD), count, jnp.int32).astype(jnp.float32).astype(out.dtype)
    each(lambda copy: copy.wait())


def pack(facts, target, queries, own, width):
    return pl.pallas_call(
        functools.partial(pack_kernel, target, width),
        out_shape=jax.ShapeDtypeStruct((SLOTS, queries.shape[1], 2 * width + 5 * HD), queries.dtype),
        in_specs=[SMEM, HBM, HBM],
        out_specs=VMEM,
        scratch_shapes=[pltpu.SemaphoreType.DMA],
        compiler_params=pltpu.CompilerParams(vmem_limit_bytes=1 << 23),
    )(facts, queries, own)


def gate_kernel(*refs):
    pass


def gate(value, *others):
    return pl.pallas_call(
        gate_kernel,
        out_shape=jax.ShapeDtypeStruct(value.shape, value.dtype),
        in_specs=[HBM] + [SMEM if other.ndim == 1 else HBM for other in others],
        out_specs=HBM,
        input_output_aliases={0: 0},
    )(value, *others)


def cut_kernel(pair, out0, out1, sem):
    copies = [pltpu.make_async_copy(pair.at[head], out, sem.at[head]) for head, out in enumerate((out0, out1))]
    for copy in copies:
        copy.start()
    for copy in copies:
        copy.wait()


def cut(pair):
    shape = jax.ShapeDtypeStruct(pair.shape[1:], pair.dtype)
    return pl.pallas_call(
        cut_kernel,
        out_shape=[shape, shape],
        in_specs=[HBM],
        out_specs=[VMEM, VMEM],
        scratch_shapes=[pltpu.SemaphoreType.DMA((2,))],
        compiler_params=pltpu.CompilerParams(vmem_limit_bytes=1 << 23),
    )(pair)


def merge_kernel(target, head, facts, groups, lengths, got, old, out, ready, sem):
    rlen, width = got.shape[1:]
    token_at = lax.broadcasted_iota(jnp.int32, (rlen, HD), 0)

    def each(act, fill):
        def look(at, slot):
            hit = groups[at] == facts[target]

            @pl.when(hit)
            def _():
                if fill:
                    alive = token_at < lengths[at]
                    for lane in range(0, width, HD):
                        part = got[slot, :, lane:lane + HD]
                        ready[slot, :, lane:lane + HD] = jnp.where(alive, part, jnp.zeros_like(part))
                act(pltpu.make_async_copy(ready.at[slot], out.at[at, :, pl.ds(head * width, width)], sem))

            return slot + hit.astype(jnp.int32)

        lax.fori_loop(0, groups.shape[0], look, jnp.int32(0))

    each(lambda copy: copy.start(), True)
    each(lambda copy: copy.wait(), False)


def merge(facts, target, groups, lengths, got, out, head):
    return pl.pallas_call(
        functools.partial(merge_kernel, target, head),
        out_shape=jax.ShapeDtypeStruct(out.shape, out.dtype),
        in_specs=[SMEM, SMEM, SMEM, VMEM, HBM],
        out_specs=HBM,
        input_output_aliases={4: 0},
        scratch_shapes=[pltpu.VMEM(got.shape, got.dtype), pltpu.SemaphoreType.DMA],
        compiler_params=pltpu.CompilerParams(vmem_limit_bytes=1 << 23),
    )(facts, groups, lengths, got, out)


def after(value, *others):
    return lax.optimization_barrier((value,) + others)[0]


def gathered(queries, resp_kv, prompt_kv, lengths, group_of, first_head, kv_needed, per_kv):
    out = jax.ShapeDtypeStruct(queries.shape, jnp.bfloat16)
    facts = jnp.concatenate([jnp.zeros((GROUPS,), jnp.int32), group_of, lengths])
    for head in range(kv_needed):
        mine = lax.dynamic_index_in_dim(prompt_kv, first_head + head, 2, keepdims=False)
        own = lax.dynamic_index_in_dim(resp_kv, first_head + head, 2, keepdims=False)[None]
        whole = lax.all_gather(mine, "seq", axis=0, tiled=True)
        out, _ = attend(facts, queries, own, [whole], [out], head, per_kv, None, 16, fresh=head == 0)
    return out


def relayed(queries, resp_kv, prompt_kv, lengths, group_of, first_head, per_kv):
    me = lax.axis_index("seq")
    width = per_kv * HD
    middle, inward, outward = [(1, 2), (2, 1)], [(0, 1), (3, 2)], [(1, 0), (2, 3)]

    def send(pairs, value):
        return lax.ppermute(value, "seq", pairs)

    def two_heads(start):
        return lambda pairs: jnp.transpose(pairs[:, start:start + 2], (1, 0, 2))

    def two_own(start):
        return lambda pairs: jnp.transpose(pairs[:, :, start:start + 2], (2, 0, 1, 3))

    splits = prompt_kv.shape[2] // 2
    mine = lax.switch(first_head // 2, [two_heads(2 * at) for at in range(splits)], prompt_kv[0])
    inner_prompt = send(outward, mine)
    parts = cut(mine)
    across, near = [], []
    for part in parts:
        across.append(send(middle, part))
        near.append(send(inward, part))

    low = me < 2
    is_inner = (me == 1) | (me == 2)
    outer, inner = jnp.where(low, 0, 3), jnp.where(low, 1, 2)
    far_inner, far_outer = jnp.where(low, 2, 1), jnp.where(low, 3, 0)
    facts = jnp.stack([
        me,
        jnp.zeros_like(me),
        jnp.where(is_inner, -1, inner),
        jnp.full_like(me, 3),
        jnp.where(is_inner, far_inner, -1),
        jnp.ones_like(me),
        jnp.where(is_inner, far_outer, -1),
        jnp.where(is_inner, far_outer, far_inner),
        jnp.where(is_inner, 0, 1),
        jnp.where(is_inner, -1, far_outer),
        jnp.where(is_inner, outer, -1),
        jnp.full_like(me, 2),
    ]).astype(jnp.int32)
    facts = jnp.concatenate([facts, group_of, lengths])

    own = lax.switch(first_head // 2, [two_own(2 * at) for at in range(splits)], resp_kv)
    packed = pack(facts, 9, queries, own, width)
    out = jax.ShapeDtypeStruct(queries.shape, jnp.bfloat16)
    back_shape = jax.ShapeDtypeStruct((SLOTS, queries.shape[1], width), jnp.bfloat16)

    def run(cands, outs, passes, items, far=None, fresh=False, wait_for=None):
        return attend(facts, queries, own, cands, outs, 0, per_kv, passes, items, far, fresh, wait_for)

    out, token = run([mine], [out], [(False, 0, 1, 0), (False, 0, 1, 1)], 8, fresh=True, wait_for=packed)
    near[0] = gate(near[0], token)
    last = [send(middle, near[0])]
    handed = send(inward, gate(packed, near[0]))
    out, token = run([near[0]], [out], [(False, 10, 1, 0)], 4)
    across[0] = gate(across[0], token, inner_prompt)
    far_inner_prompt = [send(outward, across[0])]
    near[1] = gate(near[1], token)
    last.append(send(middle, near[1]))
    across[1] = gate(across[1], token)
    far_inner_prompt.append(send(outward, across[1]))
    out, _ = run(
        [near[1], across[0], across[1], inner_prompt], [out],
        [(False, 2, 3, 0), (False, 2, 3, 1), (False, 10, 1, 1), (False, 4, 5, 0), (False, 4, 11, 1)], 16, wait_for=near[1])
    back = [None, None]
    out, back[0], _ = run(
        [last[0], far_inner_prompt[0]], [out, back_shape], [(True, 6, 1, 0), (False, 7, 8, 0)], 8, handed)
    back[0] = send(outward, back[0])
    out, back[1], _ = run([last[1]], [out, back_shape], [(True, 6, 1, 1)], 4, handed)
    back[1] = send(outward, back[1])
    out, _ = run([last[1], far_inner_prompt[1]], [out], [(False, 7, 8, 1)], 4)
    for head in range(2):
        out = merge(facts, 9, group_of, lengths, back[head], out, head)
    return out


def shards(queries, resp_kv, prompt_kv, lengths, group_of):
    local_heads = queries.shape[2] // HD
    group = QHEADS // KVH
    kv_needed = max(local_heads // group, 1)
    per_kv = local_heads // kv_needed
    first_head = lax.axis_index("pp") * local_heads // group
    args = (queries, resp_kv, prompt_kv, lengths, group_of, first_head)
    if lax.axis_size("seq") == 4 and kv_needed == 2 and prompt_kv.shape[0] == 1:
        return relayed(*args, per_kv)
    return gathered(*args, kv_needed, per_kv)


def solution(mesh):
    placed = (
        P(("rep", "seq"), None, ("tp", "pp")),
        P(("rep", "seq"), None, "tp", None),
        P(("rep", "seq"), None, "tp", None),
        P(("rep", "seq")),
        P(("rep", "seq")),
    )
    return jax.shard_map(
        shards,
        mesh=mesh,
        in_specs=placed,
        out_specs=P(("rep", "seq"), None, ("tp", "pp")),
        check_vma=False,
    )
```

```python
import functools
import math

import jax
import jax.numpy as jnp
from jax import lax
from jax.experimental import pallas as pl
from jax.experimental.pallas import tpu as pltpu
from jax.sharding import PartitionSpec as P

QHEADS = 64
KVH = 8
HD = 128
LOG2E = math.log2(math.e)
VMEM_BYTES = 12 * 1024 * 1024
SLOTS = 8
HBM = pl.BlockSpec(memory_space=pl.ANY)
SMEM = pl.BlockSpec(memory_space=pltpu.SMEM)
VMEM = pl.BlockSpec(memory_space=pltpu.VMEM)


TN = (((0,), (0,)), ((), ()))
BLOCK = 512
SCORE_BLOCK = 2048
CHUNK = 32
GROUPS = 12


def stacked_heads(q_tile, per_kv):
    return jnp.concatenate([q_tile[:, g * HD:(g + 1) * HD] for g in range(per_kv)], axis=0)


def own_scores(own_tile, q_cols, rlen):
    own = jnp.dot(own_tile[:, :HD], q_cols, preferred_element_type=jnp.float32)
    own_at = lax.broadcasted_iota(jnp.int32, own.shape, 0)
    token_at = lax.broadcasted_iota(jnp.int32, own.shape, 1) % rlen
    return jnp.where(own_at <= token_at, own, -1e30)


def folded(values, op):
    return op(values.reshape(values.shape[0] // 8, 8, values.shape[1]), axis=0)


def turn(q_tile, per_kv, out_ref):
    out_ref[...] = stacked_heads(q_tile, per_kv).T


def finish(acc_ref, total_ref, length, per_kv, out_ref):
    out = (acc_ref[...] * (1.0 / total_ref[0:1, :])).T
    rlen = out_ref.shape[0]
    alive = lax.broadcasted_iota(jnp.int32, (rlen, HD), 0) < length
    for g in range(per_kv):
        part = jnp.where(alive, out[g * rlen:(g + 1) * rlen, :], 0.0)
        out_ref[:, g * HD:(g + 1) * HD] = part.astype(out_ref.dtype)


def scores_and_mix(q_cols, after_own, after_keys, after_s, after_u, after_peak, now):
    plen = after_keys.shape[0]
    scale = HD ** -0.5 * LOG2E
    own = own_scores(after_own, q_cols, after_own.shape[0])
    after_u[...] = own
    after_top = folded(own, jnp.max)
    if now is not None:
        s_ref, u_ref, peak_ref, own_tile, vt_ref, p_ref, acc_ref, total_ref = now
        peak = peak_ref[...]
        part = jnp.exp2((u_ref[...] - peak[0:1, :]) * scale)
        total = folded(part, jnp.sum)
        acc = lax.dot_general(own_tile[:, HD:], part.astype(jnp.bfloat16), TN, preferred_element_type=jnp.float32)
        spread = jnp.concatenate([peak] * (CHUNK // 8), axis=0)
    for at in range(0, plen, BLOCK):
        rows = pl.ds(at, BLOCK)
        if at % SCORE_BLOCK == 0:
            score_rows = pl.ds(at, SCORE_BLOCK)
            fresh = jnp.dot(after_keys[score_rows, :], q_cols, preferred_element_type=jnp.float32)
            after_s[score_rows, :] = fresh
            after_top = jnp.maximum(after_top, folded(fresh, jnp.max))
        if now is not None:
            for chunk in range(at, at + BLOCK, CHUNK):
                part = jnp.exp2((s_ref[chunk:chunk + CHUNK, :] - spread) * scale)
                total = total + folded(part, jnp.sum)
                p_ref[chunk:chunk + CHUNK, :] = part.astype(jnp.bfloat16)
            acc = acc + jnp.dot(vt_ref[:, rows], p_ref[rows, :], preferred_element_type=jnp.float32)
    after_peak[...] = jnp.broadcast_to(jnp.max(after_top, axis=0, keepdims=True), after_peak.shape)
    if now is not None:
        acc_ref[...] = acc
        total_ref[...] = jnp.broadcast_to(jnp.sum(total, axis=0, keepdims=True), total_ref.shape)


def listed(items, cap, count, facts, local, target, source, head):
    def look(at, n):
        hit = facts[GROUPS + at] == target

        @pl.when(hit)
        def _():
            items[n] = at
            items[cap + n] = source
            items[2 * cap + n] = facts[GROUPS + local + at]
            items[3 * cap + n] = head

        return n + hit.astype(jnp.int32)

    return lax.fori_loop(0, local, look, count)


def attend_kernel(passes, n_cand, per_kv, whole_head, two, fresh, waits, *refs):
    refs = list(refs)
    facts, refs = refs[0], refs[1:]
    if two:
        x_ref, refs = refs[0], refs[1:]
    q_ref, own_ref = refs[:2]
    cands, refs = refs[2:2 + n_cand], refs[2 + n_cand + waits:]
    n_out = 2 if two else 1
    if not fresh:
        refs = refs[1:]
    outs, token, refs = refs[:n_out], refs[n_out], refs[n_out + 1:]
    items, at_slot, q_buf, own_buf, key_buf, value_buf, vt_buf, s0, s1, u0, u1, peak0, peak1, turned0, turned1, acc0, acc1, total0, total1, p_buf, o0, o1, info, q_sem, own_sem, kv_sem, o_sem = refs
    s_buf, u_buf, peak_buf, o_buf = (s0, s1), (u0, u1), (peak0, peak1), (o0, o1)
    turned, acc_buf, total_buf = (turned0, turned1), (acc0, acc1), (total0, total1)
    local = (facts.shape[0] - GROUPS) // 2
    cap = items.shape[0] // 4
    width = per_kv * HD
    stacked = passes is None

    count = jnp.int32(0)
    if stacked:
        def one_prompt(prompt, n):
            return listed(items, cap, n, facts, local, prompt, prompt, whole_head)

        count = lax.fori_loop(0, cands[0].shape[0], one_prompt, count)
    else:
        for far, target, source, head in passes:
            if not far:
                count = listed(items, cap, count, facts, local, facts[target], facts[source], head)
                continue
            notes = pltpu.make_async_copy(x_ref.at[0, :, pl.ds(2 * (width + 2 * HD), HD)], info, kv_sem)
            notes.start()
            notes.wait()
            far_head = head
            handed = jnp.max(info[0:16, :].astype(jnp.float32)).astype(jnp.int32)
            handed = jnp.where(facts[target] >= 0, jnp.minimum(handed, SLOTS), 0)

            def take(slot, n):
                items[n] = local + slot
                items[cap + n] = facts[source]
                items[2 * cap + n] = q_buf.shape[1]
                items[3 * cap + n] = far_head
                return n + 1

            count = lax.fori_loop(0, handed, take, count)

    token[0] = count

    def each_array(i, act_local, act_far):
        at = items[i]
        if not two:
            act_local(at)
            return

        @pl.when(at < local)
        def _():
            act_local(at)

        @pl.when(at >= local)
        def _():
            act_far(at - local)

    first = pl.ds(0, width)

    def lanes(i, step, skip, size):
        return pl.ds(pl.multiple_of(items[3 * cap + i] * step + skip, HD), size)

    def mine(i):
        return lanes(i, width, 0, width)

    def fetch(i):
        slot, fourth = lax.rem(i, 2), lax.rem(i, 4)

        def here(at):
            pltpu.make_async_copy(q_ref.at[at, :, mine(i)], q_buf.at[slot], q_sem.at[slot]).start()
            pltpu.make_async_copy(own_ref.at[items[3 * cap + i], at], own_buf.at[fourth], own_sem.at[fourth]).start()

        def far(at):
            pltpu.make_async_copy(x_ref.at[at, :, lanes(i, width + 2 * HD, 0, width)], q_buf.at[slot], q_sem.at[slot]).start()
            pltpu.make_async_copy(x_ref.at[at, :, lanes(i, width + 2 * HD, width, 2 * HD)], own_buf.at[fourth], own_sem.at[fourth]).start()

        each_array(i, here, far)

    def fetched(i):
        slot, fourth = lax.rem(i, 2), lax.rem(i, 4)
        pltpu.make_async_copy(q_ref.at[0, :, first], q_buf.at[slot], q_sem.at[slot]).wait()
        pltpu.make_async_copy(own_ref.at[0, 0], own_buf.at[fourth], own_sem.at[fourth]).wait()

    def store(i, slot):
        def here(at):
            pltpu.make_async_copy(o_buf[slot], outs[0].at[at, :, mine(i)], o_sem.at[slot]).start()

        def far(at):
            pltpu.make_async_copy(o_buf[slot], outs[1].at[at], o_sem.at[slot]).start()

        each_array(i, here, far)

    def stored(slot):
        pltpu.make_async_copy(o_buf[slot], outs[0].at[0, :, first], o_sem.at[slot]).wait()

    keys, values = pl.ds(0, HD), pl.ds(HD, HD)

    def ask(i, into):
        source = items[cap + i]

        def bring(pairs):
            pltpu.make_async_copy(pairs.at[:, keys], key_buf.at[into], kv_sem).start()
            pltpu.make_async_copy(pairs.at[:, values], value_buf, kv_sem).start()

        if stacked:
            bring(cands[0].at[source])
        else:
            for which in range(n_cand):
                @pl.when(source == which)
                def _():
                    bring(cands[which].at[items[3 * cap + i]] if len(cands[which].shape) == 3 else cands[which])

    def receive(into):
        for _ in range(2):
            pltpu.make_async_copy(value_buf, value_buf, kv_sem).wait()
        vt_buf[into] = value_buf[...].T

    @pl.when(count > 0)
    def _():
        ask(0, 0)
        fetch(jnp.int32(0))

        @pl.when(count > 1)
        def _():
            fetch(jnp.int32(1))

        at_slot[0] = 0
        fetched(jnp.int32(0))
        turn(q_buf[0], per_kv, turned[0])

        @pl.when(count > 2)
        def _():
            fetch(jnp.int32(2))

        @pl.when(count > 1)
        def _():
            fetched(jnp.int32(1))

        turn(q_buf[1], per_kv, turned[1])
        receive(0)
        scores_and_mix(turned[0][...], own_buf[0], key_buf.at[0], s_buf[0], u_buf[0], peak_buf[0], None)

        def one(i, slot):
            other = 1 - slot
            held = at_slot[0]
            more = i + 1 < count
            after_i = jnp.minimum(i + 1, count - 1)
            moved = more & ((items[cap + after_i] != items[cap + i]) | (items[3 * cap + after_i] != items[3 * cap + i]))
            holds = jnp.where(moved, 1 - held, held)
            at_slot[0] = holds

            @pl.when(i + 2 < count)
            def _():
                fetched(i + 2)

            @pl.when(i + 3 < count)
            def _():
                fetch(i + 3)

            @pl.when(moved)
            def _():
                ask(i + 1, holds)
                receive(holds)

            @pl.when(i >= 3)
            def _():
                stored(other)

            now = (
                s_buf[slot], u_buf[slot], peak_buf[slot], own_buf[lax.rem(i, 4)], vt_buf.at[held], p_buf,
                acc_buf[slot], total_buf[slot])
            scores_and_mix(
                turned[other][...], own_buf[lax.rem(i + 1, 4)], key_buf.at[holds],
                s_buf[other], u_buf[other], peak_buf[other], now)
            turn(q_buf[slot], per_kv, turned[slot])
            finish(acc_buf[other], total_buf[other], items[2 * cap + jnp.maximum(i - 1, 0)], per_kv, o_buf[other])

            @pl.when(i >= 1)
            def _():
                store(i - 1, other)

        def pair(j, _):
            one(2 * j, 0)

            @pl.when(2 * j + 1 < count)
            def _():
                one(2 * j + 1, 1)

            return 0

        lax.fori_loop(0, lax.div(count + 1, 2), pair, 0)
        final = count - 1
        for slot in range(2):
            @pl.when(lax.rem(final, 2) == slot)
            def _():
                @pl.when(final >= 2)
                def _():
                    stored(slot)

                finish(acc_buf[slot], total_buf[slot], items[2 * cap + final], per_kv, o_buf[slot])
                store(final, slot)

        stored(0)

        @pl.when(count > 1)
        def _():
            stored(1)


def attend(facts, queries, own, cands, outs, head, per_kv, passes, items, far=None, fresh=False, wait_for=None):
    rlen = queries.shape[1]
    plen = cands[0].shape[-2]
    width = per_kv * HD
    small = [facts]
    large = ([far] if far is not None else []) + [queries, own] + cands
    operands = small + large + ([] if wait_for is None else [wait_for])
    aliases = {}
    if not fresh:
        aliases = {len(operands): 0}
        operands = operands + [outs[0]]
    cap = 2 * queries.shape[0] + (SLOTS if far is not None else 0)
    return pl.pallas_call(
        functools.partial(attend_kernel, passes, len(cands), per_kv, head, far is not None, fresh, wait_for is not None),
        out_shape=[jax.ShapeDtypeStruct(o.shape, o.dtype) for o in outs] + [jax.ShapeDtypeStruct((1,), jnp.int32)],
        in_specs=[SMEM] * len(small) + [HBM] * (len(operands) - len(small)),
        out_specs=[HBM] * len(outs) + [SMEM],
        input_output_aliases=aliases,
        scratch_shapes=[
            pltpu.SMEM((4 * cap,), jnp.int32),
            pltpu.SMEM((1,), jnp.int32),
            pltpu.VMEM((2, rlen, width), jnp.bfloat16),
            pltpu.VMEM((4, rlen, 2 * HD), jnp.bfloat16),
            pltpu.VMEM((2, plen, HD), jnp.bfloat16),
            pltpu.VMEM((plen, HD), jnp.bfloat16),
            pltpu.VMEM((2, HD, plen), jnp.bfloat16),
            pltpu.VMEM((plen, per_kv * rlen), jnp.float32),
            pltpu.VMEM((plen, per_kv * rlen), jnp.float32),
            pltpu.VMEM((rlen, per_kv * rlen), jnp.float32),
            pltpu.VMEM((rlen, per_kv * rlen), jnp.float32),
            pltpu.VMEM((8, per_kv * rlen), jnp.float32),
            pltpu.VMEM((8, per_kv * rlen), jnp.float32),
            pltpu.VMEM((HD, per_kv * rlen), jnp.bfloat16),
            pltpu.VMEM((HD, per_kv * rlen), jnp.bfloat16),
            pltpu.VMEM((HD, per_kv * rlen), jnp.float32),
            pltpu.VMEM((HD, per_kv * rlen), jnp.float32),
            pltpu.VMEM((8, per_kv * rlen), jnp.float32),
            pltpu.VMEM((8, per_kv * rlen), jnp.float32),
            pltpu.VMEM((plen, per_kv * rlen), jnp.bfloat16),
            pltpu.VMEM((rlen, width), jnp.bfloat16),
            pltpu.VMEM((rlen, width), jnp.bfloat16),
            pltpu.VMEM((rlen, HD), jnp.bfloat16),
            pltpu.SemaphoreType.DMA((2,)),
            pltpu.SemaphoreType.DMA((4,)),
            pltpu.SemaphoreType.DMA,
            pltpu.SemaphoreType.DMA((2,)),
        ],
        compiler_params=pltpu.CompilerParams(vmem_limit_bytes=VMEM_BYTES),
        cost_estimate=pl.CostEstimate(flops=items << 20, bytes_accessed=1 << 16, transcendentals=0),
    )(*operands)


def pack_kernel(target, width, facts, q_ref, own_ref, out, sem):
    step = width + 2 * HD
    local = q_ref.shape[0]

    def each(act):
        def look(at, slot):
            hit = facts[GROUPS + at] == facts[target]

            @pl.when(hit)
            def _():
                for head in range(2):
                    part = pl.ds(head * width, width)
                    act(pltpu.make_async_copy(q_ref.at[at, :, part], out.at[slot, :, pl.ds(head * step, width)], sem))
                    act(pltpu.make_async_copy(
                        own_ref.at[head, at], out.at[slot, :, pl.ds(head * step + width, 2 * HD)], sem))

            return slot + hit.astype(jnp.int32)

        return lax.fori_loop(0, local, look, jnp.int32(0))

    count = each(lambda copy: copy.start())
    out[0, :, 2 * step:] = jnp.full((out.shape[1], HD), count, jnp.int32).astype(jnp.float32).astype(out.dtype)
    each(lambda copy: copy.wait())


def pack(facts, target, queries, own, width):
    return pl.pallas_call(
        functools.partial(pack_kernel, target, width),
        out_shape=jax.ShapeDtypeStruct((SLOTS, queries.shape[1], 2 * width + 5 * HD), queries.dtype),
        in_specs=[SMEM, HBM, HBM],
        out_specs=VMEM,
        scratch_shapes=[pltpu.SemaphoreType.DMA],
        compiler_params=pltpu.CompilerParams(vmem_limit_bytes=1 << 23),
    )(facts, queries, own)


def gate_kernel(*refs):
    pass


def gate(value, *others):
    return pl.pallas_call(
        gate_kernel,
        out_shape=jax.ShapeDtypeStruct(value.shape, value.dtype),
        in_specs=[HBM] + [SMEM if other.ndim == 1 else HBM for other in others],
        out_specs=HBM,
        input_output_aliases={0: 0},
    )(value, *others)


def cut_kernel(pair, out0, out1, sem):
    copies = [pltpu.make_async_copy(pair.at[head], out, sem.at[head]) for head, out in enumerate((out0, out1))]
    for copy in copies:
        copy.start()
    for copy in copies:
        copy.wait()


def cut(pair):
    shape = jax.ShapeDtypeStruct(pair.shape[1:], pair.dtype)
    return pl.pallas_call(
        cut_kernel,
        out_shape=[shape, shape],
        in_specs=[HBM],
        out_specs=[VMEM, VMEM],
        scratch_shapes=[pltpu.SemaphoreType.DMA((2,))],
        compiler_params=pltpu.CompilerParams(vmem_limit_bytes=1 << 23),
    )(pair)


def merge_kernel(target, head, facts, groups, lengths, got, old, out, ready, sem):
    rlen, width = got.shape[1:]
    token_at = lax.broadcasted_iota(jnp.int32, (rlen, HD), 0)

    def each(act, fill):
        def look(at, slot):
            hit = groups[at] == facts[target]

            @pl.when(hit)
            def _():
                if fill:
                    alive = token_at < lengths[at]
                    for lane in range(0, width, HD):
                        part = got[slot, :, lane:lane + HD]
                        ready[slot, :, lane:lane + HD] = jnp.where(alive, part, jnp.zeros_like(part))
                act(pltpu.make_async_copy(ready.at[slot], out.at[at, :, pl.ds(head * width, width)], sem))

            return slot + hit.astype(jnp.int32)

        lax.fori_loop(0, groups.shape[0], look, jnp.int32(0))

    each(lambda copy: copy.start(), True)
    each(lambda copy: copy.wait(), False)


def merge(facts, target, groups, lengths, got, out, head):
    return pl.pallas_call(
        functools.partial(merge_kernel, target, head),
        out_shape=jax.ShapeDtypeStruct(out.shape, out.dtype),
        in_specs=[SMEM, SMEM, SMEM, VMEM, HBM],
        out_specs=HBM,
        input_output_aliases={4: 0},
        scratch_shapes=[pltpu.VMEM(got.shape, got.dtype), pltpu.SemaphoreType.DMA],
        compiler_params=pltpu.CompilerParams(vmem_limit_bytes=1 << 23),
    )(facts, groups, lengths, got, out)


def after(value, *others):
    return lax.optimization_barrier((value,) + others)[0]


def gathered(queries, resp_kv, prompt_kv, lengths, group_of, first_head, kv_needed, per_kv):
    out = jax.ShapeDtypeStruct(queries.shape, jnp.bfloat16)
    facts = jnp.concatenate([jnp.zeros((GROUPS,), jnp.int32), group_of, lengths])
    for head in range(kv_needed):
        mine = lax.dynamic_index_in_dim(prompt_kv, first_head + head, 2, keepdims=False)
        own = lax.dynamic_index_in_dim(resp_kv, first_head + head, 2, keepdims=False)[None]
        whole = lax.all_gather(mine, "seq", axis=0, tiled=True)
        out, _ = attend(facts, queries, own, [whole], [out], head, per_kv, None, 16, fresh=head == 0)
    return out


def relayed(queries, resp_kv, prompt_kv, lengths, group_of, first_head, per_kv):
    me = lax.axis_index("seq")
    width = per_kv * HD
    middle, inward, outward = [(1, 2), (2, 1)], [(0, 1), (3, 2)], [(1, 0), (2, 3)]

    def send(pairs, value):
        return lax.ppermute(value, "seq", pairs)

    def two_heads(start):
        return lambda pairs: jnp.transpose(pairs[:, start:start + 2], (1, 0, 2))

    def two_own(start):
        return lambda pairs: jnp.transpose(pairs[:, :, start:start + 2], (2, 0, 1, 3))

    splits = prompt_kv.shape[2] // 2
    mine = lax.switch(first_head // 2, [two_heads(2 * at) for at in range(splits)], prompt_kv[0])
    inner_prompt = send(outward, mine)
    parts = cut(mine)
    across, near = [], []
    for part in parts:
        across.append(send(middle, part))
        near.append(send(inward, part))

    low = me < 2
    is_inner = (me == 1) | (me == 2)
    outer, inner = jnp.where(low, 0, 3), jnp.where(low, 1, 2)
    far_inner, far_outer = jnp.where(low, 2, 1), jnp.where(low, 3, 0)
    facts = jnp.stack([
        me,
        jnp.zeros_like(me),
        jnp.where(is_inner, -1, inner),
        jnp.full_like(me, 3),
        jnp.where(is_inner, far_inner, -1),
        jnp.ones_like(me),
        jnp.where(is_inner, far_outer, -1),
        jnp.where(is_inner, far_outer, far_inner),
        jnp.where(is_inner, 0, 1),
        jnp.where(is_inner, -1, far_outer),
        jnp.where(is_inner, outer, -1),
        jnp.full_like(me, 2),
    ]).astype(jnp.int32)
    facts = jnp.concatenate([facts, group_of, lengths])

    own = lax.switch(first_head // 2, [two_own(2 * at) for at in range(splits)], resp_kv)
    packed = pack(facts, 9, queries, own, width)
    out = jax.ShapeDtypeStruct(queries.shape, jnp.bfloat16)
    back_shape = jax.ShapeDtypeStruct((SLOTS, queries.shape[1], width), jnp.bfloat16)

    def run(cands, outs, passes, items, far=None, fresh=False, wait_for=None):
        return attend(facts, queries, own, cands, outs, 0, per_kv, passes, items, far, fresh, wait_for)

    out, token = run([mine], [out], [(False, 0, 1, 0), (False, 0, 1, 1)], 8, fresh=True, wait_for=packed)
    near[0] = gate(near[0], token)
    last = [send(middle, near[0])]
    handed = send(inward, gate(packed, near[0]))
    out, token = run([near[0]], [out], [(False, 10, 1, 0)], 4)
    across[0] = gate(across[0], token, inner_prompt)
    far_inner_prompt = [send(outward, across[0])]
    near[1] = gate(near[1], token)
    last.append(send(middle, near[1]))
    across[1] = gate(across[1], token)
    far_inner_prompt.append(send(outward, across[1]))
    out, _ = run(
        [near[1], across[0], across[1], inner_prompt], [out],
        [(False, 2, 3, 0), (False, 2, 3, 1), (False, 10, 1, 1), (False, 4, 5, 0), (False, 4, 11, 1)], 16, wait_for=near[1])
    back = [None, None]
    out, back[0], _ = run(
        [last[0], far_inner_prompt[0]], [out, back_shape], [(True, 6, 1, 0), (False, 7, 8, 0)], 8, handed)
    back[0] = send(outward, back[0])
    out, back[1], _ = run([last[1]], [out, back_shape], [(True, 6, 1, 1)], 4, handed)
    back[1] = send(outward, back[1])
    out, _ = run([last[1], far_inner_prompt[1]], [out], [(False, 7, 8, 1)], 4)
    for head in range(2):
        out = merge(facts, 9, group_of, lengths, back[head], out, head)
    return out


def shards(queries, resp_kv, prompt_kv, lengths, group_of):
    local_heads = queries.shape[2] // HD
    group = QHEADS // KVH
    kv_needed = max(local_heads // group, 1)
    per_kv = local_heads // kv_needed
    first_head = lax.axis_index("pp") * local_heads // group
    args = (queries, resp_kv, prompt_kv, lengths, group_of, first_head)
    if lax.axis_size("seq") == 4 and kv_needed == 2 and prompt_kv.shape[0] == 1:
        return relayed(*args, per_kv)
    return gathered(*args, kv_needed, per_kv)


def solution(mesh):
    placed = (
        P(("rep", "seq"), None, ("tp", "pp")),
        P(("rep", "seq"), None, "tp", None),
        P(("rep", "seq"), None, "tp", None),
        P(("rep", "seq")),
        P(("rep", "seq")),
    )
    return jax.shard_map(
        shards,
        mesh=mesh,
        in_specs=placed,
        out_specs=P(("rep", "seq"), None, ("tp", "pp")),
        check_vma=False,
    )
```

```python
import functools
import math

import jax
import jax.numpy as jnp
from jax import lax
from jax.experimental import pallas as pl
from jax.experimental.pallas import tpu as pltpu
from jax.sharding import PartitionSpec as P

QHEADS = 64
KVH = 8
HD = 128
LOG2E = math.log2(math.e)
VMEM_BYTES = 12 * 1024 * 1024
SLOTS = 8
HBM = pl.BlockSpec(memory_space=pl.ANY)
SMEM = pl.BlockSpec(memory_space=pltpu.SMEM)
VMEM = pl.BlockSpec(memory_space=pltpu.VMEM)


TN = (((0,), (0,)), ((), ()))
BLOCK = 512
SCORE_BLOCK = 1024
CHUNK = 32
GROUPS = 12


def stacked_heads(q_tile, per_kv):
    return jnp.concatenate([q_tile[:, g * HD:(g + 1) * HD] for g in range(per_kv)], axis=0)


def own_scores(own_tile, q_cols, rlen):
    own = jnp.dot(own_tile[:, :HD], q_cols, preferred_element_type=jnp.float32)
    own_at = lax.broadcasted_iota(jnp.int32, own.shape, 0)
    token_at = lax.broadcasted_iota(jnp.int32, own.shape, 1) % rlen
    return jnp.where(own_at <= token_at, own, -1e30)


def folded(values, op):
    return op(values.reshape(values.shape[0] // 8, 8, values.shape[1]), axis=0)


def turn(q_tile, per_kv, out_ref):
    out_ref[...] = stacked_heads(q_tile, per_kv).T


def finish(acc_ref, total_ref, length, per_kv, out_ref):
    out = (acc_ref[...] * (1.0 / total_ref[0:1, :])).T
    rlen = out_ref.shape[0]
    alive = lax.broadcasted_iota(jnp.int32, (rlen, HD), 0) < length
    for g in range(per_kv):
        part = jnp.where(alive, out[g * rlen:(g + 1) * rlen, :], 0.0)
        out_ref[:, g * HD:(g + 1) * HD] = part.astype(out_ref.dtype)


def scores_and_mix(q_cols, after_own, after_keys, after_s, after_u, after_peak, now):
    plen = after_keys.shape[0]
    scale = HD ** -0.5 * LOG2E
    own = own_scores(after_own, q_cols, after_own.shape[0])
    after_u[...] = own
    after_top = folded(own, jnp.max)
    if now is not None:
        s_ref, u_ref, peak_ref, own_tile, vt_ref, p_ref, acc_ref, total_ref = now
        peak = peak_ref[...]
        part = jnp.exp2((u_ref[...] - peak[0:1, :]) * scale)
        total = folded(part, jnp.sum)
        acc = lax.dot_general(own_tile[:, HD:], part.astype(jnp.bfloat16), TN, preferred_element_type=jnp.float32)
        spread = jnp.concatenate([peak] * (CHUNK // 8), axis=0)
    for at in range(0, plen, BLOCK):
        rows = pl.ds(at, BLOCK)
        if at % SCORE_BLOCK == 0:
            score_rows = pl.ds(at, SCORE_BLOCK)
            fresh = jnp.dot(after_keys[score_rows, :], q_cols, preferred_element_type=jnp.float32)
            after_s[score_rows, :] = fresh
            after_top = jnp.maximum(after_top, folded(fresh, jnp.max))
        if now is not None:
            for chunk in range(at, at + BLOCK, CHUNK):
                part = jnp.exp2((s_ref[chunk:chunk + CHUNK, :] - spread) * scale)
                total = total + folded(part, jnp.sum)
                p_ref[chunk:chunk + CHUNK, :] = part.astype(jnp.bfloat16)
            acc = acc + jnp.dot(vt_ref[:, rows], p_ref[rows, :], preferred_element_type=jnp.float32)
    after_peak[...] = jnp.broadcast_to(jnp.max(after_top, axis=0, keepdims=True), after_peak.shape)
    if now is not None:
        acc_ref[...] = acc
        total_ref[...] = jnp.broadcast_to(jnp.sum(total, axis=0, keepdims=True), total_ref.shape)


def listed(items, cap, count, facts, local, target, source, head):
    def look(at, n):
        hit = facts[GROUPS + at] == target

        @pl.when(hit)
        def _():
            items[n] = at
            items[cap + n] = source
            items[2 * cap + n] = facts[GROUPS + local + at]
            items[3 * cap + n] = head

        return n + hit.astype(jnp.int32)

    return lax.fori_loop(0, local, look, count)


def attend_kernel(passes, n_cand, per_kv, whole_head, two, fresh, waits, *refs):
    refs = list(refs)
    facts, refs = refs[0], refs[1:]
    if two:
        x_ref, refs = refs[0], refs[1:]
    q_ref, own_ref = refs[:2]
    cands, refs = refs[2:2 + n_cand], refs[2 + n_cand + waits:]
    n_out = 2 if two else 1
    if not fresh:
        refs = refs[1:]
    outs, token, refs = refs[:n_out], refs[n_out], refs[n_out + 1:]
    items, at_slot, q_buf, own_buf, key_buf, value_buf, vt_buf, s0, s1, u0, u1, peak0, peak1, turned0, turned1, acc0, acc1, total0, total1, p_buf, o0, o1, info, q_sem, own_sem, kv_sem, o_sem = refs
    s_buf, u_buf, peak_buf, o_buf = (s0, s1), (u0, u1), (peak0, peak1), (o0, o1)
    turned, acc_buf, total_buf = (turned0, turned1), (acc0, acc1), (total0, total1)
    local = (facts.shape[0] - GROUPS) // 2
    cap = items.shape[0] // 4
    width = per_kv * HD
    stacked = passes is None

    count = jnp.int32(0)
    if stacked:
        def one_prompt(prompt, n):
            return listed(items, cap, n, facts, local, prompt, prompt, whole_head)

        count = lax.fori_loop(0, cands[0].shape[0], one_prompt, count)
    else:
        for far, target, source, head in passes:
            if not far:
                count = listed(items, cap, count, facts, local, facts[target], facts[source], head)
                continue
            notes = pltpu.make_async_copy(x_ref.at[0, :, pl.ds(2 * (width + 2 * HD), HD)], info, kv_sem)
            notes.start()
            notes.wait()
            far_head = head
            handed = jnp.max(info[0:16, :].astype(jnp.float32)).astype(jnp.int32)
            handed = jnp.where(facts[target] >= 0, jnp.minimum(handed, SLOTS), 0)

            def take(slot, n):
                items[n] = local + slot
                items[cap + n] = facts[source]
                items[2 * cap + n] = q_buf.shape[1]
                items[3 * cap + n] = far_head
                return n + 1

            count = lax.fori_loop(0, handed, take, count)

    token[0] = count

    def each_array(i, act_local, act_far):
        at = items[i]
        if not two:
            act_local(at)
            return

        @pl.when(at < local)
        def _():
            act_local(at)

        @pl.when(at >= local)
        def _():
            act_far(at - local)

    first = pl.ds(0, width)

    def lanes(i, step, skip, size):
        return pl.ds(pl.multiple_of(items[3 * cap + i] * step + skip, HD), size)

    def mine(i):
        return lanes(i, width, 0, width)

    def fetch(i):
        slot, fourth = lax.rem(i, 2), lax.rem(i, 4)

        def here(at):
            pltpu.make_async_copy(q_ref.at[at, :, mine(i)], q_buf.at[slot], q_sem.at[slot]).start()
            pltpu.make_async_copy(own_ref.at[items[3 * cap + i], at], own_buf.at[fourth], own_sem.at[fourth]).start()

        def far(at):
            pltpu.make_async_copy(x_ref.at[at, :, lanes(i, width + 2 * HD, 0, width)], q_buf.at[slot], q_sem.at[slot]).start()
            pltpu.make_async_copy(x_ref.at[at, :, lanes(i, width + 2 * HD, width, 2 * HD)], own_buf.at[fourth], own_sem.at[fourth]).start()

        each_array(i, here, far)

    def fetched(i):
        slot, fourth = lax.rem(i, 2), lax.rem(i, 4)
        pltpu.make_async_copy(q_ref.at[0, :, first], q_buf.at[slot], q_sem.at[slot]).wait()
        pltpu.make_async_copy(own_ref.at[0, 0], own_buf.at[fourth], own_sem.at[fourth]).wait()

    def store(i, slot):
        def here(at):
            pltpu.make_async_copy(o_buf[slot], outs[0].at[at, :, mine(i)], o_sem.at[slot]).start()

        def far(at):
            pltpu.make_async_copy(o_buf[slot], outs[1].at[at], o_sem.at[slot]).start()

        each_array(i, here, far)

    def stored(slot):
        pltpu.make_async_copy(o_buf[slot], outs[0].at[0, :, first], o_sem.at[slot]).wait()

    keys, values = pl.ds(0, HD), pl.ds(HD, HD)

    def ask(i, into):
        source = items[cap + i]

        def bring(pairs):
            pltpu.make_async_copy(pairs.at[:, keys], key_buf.at[into], kv_sem).start()
            pltpu.make_async_copy(pairs.at[:, values], value_buf, kv_sem).start()

        if stacked:
            bring(cands[0].at[source])
        else:
            for which in range(n_cand):
                @pl.when(source == which)
                def _():
                    bring(cands[which].at[items[3 * cap + i]] if len(cands[which].shape) == 3 else cands[which])

    def receive(into):
        for _ in range(2):
            pltpu.make_async_copy(value_buf, value_buf, kv_sem).wait()
        vt_buf[into] = value_buf[...].T

    @pl.when(count > 0)
    def _():
        ask(0, 0)
        fetch(jnp.int32(0))

        @pl.when(count > 1)
        def _():
            fetch(jnp.int32(1))

        at_slot[0] = 0
        fetched(jnp.int32(0))
        turn(q_buf[0], per_kv, turned[0])

        @pl.when(count > 2)
        def _():
            fetch(jnp.int32(2))

        @pl.when(count > 1)
        def _():
            fetched(jnp.int32(1))

        turn(q_buf[1], per_kv, turned[1])
        receive(0)
        scores_and_mix(turned[0][...], own_buf[0], key_buf.at[0], s_buf[0], u_buf[0], peak_buf[0], None)

        def one(i, slot):
            other = 1 - slot
            held = at_slot[0]
            more = i + 1 < count
            after_i = jnp.minimum(i + 1, count - 1)
            moved = more & ((items[cap + after_i] != items[cap + i]) | (items[3 * cap + after_i] != items[3 * cap + i]))
            holds = jnp.where(moved, 1 - held, held)
            at_slot[0] = holds

            @pl.when(i + 2 < count)
            def _():
                fetched(i + 2)

            @pl.when(i + 3 < count)
            def _():
                fetch(i + 3)

            @pl.when(moved)
            def _():
                ask(i + 1, holds)
                receive(holds)

            @pl.when(i >= 3)
            def _():
                stored(other)

            now = (
                s_buf[slot], u_buf[slot], peak_buf[slot], own_buf[lax.rem(i, 4)], vt_buf.at[held], p_buf,
                acc_buf[slot], total_buf[slot])
            scores_and_mix(
                turned[other][...], own_buf[lax.rem(i + 1, 4)], key_buf.at[holds],
                s_buf[other], u_buf[other], peak_buf[other], now)
            turn(q_buf[slot], per_kv, turned[slot])
            finish(acc_buf[other], total_buf[other], items[2 * cap + jnp.maximum(i - 1, 0)], per_kv, o_buf[other])

            @pl.when(i >= 1)
            def _():
                store(i - 1, other)

        def pair(j, _):
            one(2 * j, 0)

            @pl.when(2 * j + 1 < count)
            def _():
                one(2 * j + 1, 1)

            return 0

        lax.fori_loop(0, lax.div(count + 1, 2), pair, 0)
        final = count - 1
        for slot in range(2):
            @pl.when(lax.rem(final, 2) == slot)
            def _():
                @pl.when(final >= 2)
                def _():
                    stored(slot)

                finish(acc_buf[slot], total_buf[slot], items[2 * cap + final], per_kv, o_buf[slot])
                store(final, slot)

        stored(0)

        @pl.when(count > 1)
        def _():
            stored(1)


def attend(facts, queries, own, cands, outs, head, per_kv, passes, items, far=None, fresh=False, wait_for=None):
    rlen = queries.shape[1]
    plen = cands[0].shape[-2]
    width = per_kv * HD
    small = [facts]
    large = ([far] if far is not None else []) + [queries, own] + cands
    operands = small + large + ([] if wait_for is None else [wait_for])
    aliases = {}
    if not fresh:
        aliases = {len(operands): 0}
        operands = operands + [outs[0]]
    cap = 2 * queries.shape[0] + (SLOTS if far is not None else 0)
    return pl.pallas_call(
        functools.partial(attend_kernel, passes, len(cands), per_kv, head, far is not None, fresh, wait_for is not None),
        out_shape=[jax.ShapeDtypeStruct(o.shape, o.dtype) for o in outs] + [jax.ShapeDtypeStruct((1,), jnp.int32)],
        in_specs=[SMEM] * len(small) + [HBM] * (len(operands) - len(small)),
        out_specs=[HBM] * len(outs) + [SMEM],
        input_output_aliases=aliases,
        scratch_shapes=[
            pltpu.SMEM((4 * cap,), jnp.int32),
            pltpu.SMEM((1,), jnp.int32),
            pltpu.VMEM((2, rlen, width), jnp.bfloat16),
            pltpu.VMEM((4, rlen, 2 * HD), jnp.bfloat16),
            pltpu.VMEM((2, plen, HD), jnp.bfloat16),
            pltpu.VMEM((plen, HD), jnp.bfloat16),
            pltpu.VMEM((2, HD, plen), jnp.bfloat16),
            pltpu.VMEM((plen, per_kv * rlen), jnp.float32),
            pltpu.VMEM((plen, per_kv * rlen), jnp.float32),
            pltpu.VMEM((rlen, per_kv * rlen), jnp.float32),
            pltpu.VMEM((rlen, per_kv * rlen), jnp.float32),
            pltpu.VMEM((8, per_kv * rlen), jnp.float32),
            pltpu.VMEM((8, per_kv * rlen), jnp.float32),
            pltpu.VMEM((HD, per_kv * rlen), jnp.bfloat16),
            pltpu.VMEM((HD, per_kv * rlen), jnp.bfloat16),
            pltpu.VMEM((HD, per_kv * rlen), jnp.float32),
            pltpu.VMEM((HD, per_kv * rlen), jnp.float32),
            pltpu.VMEM((8, per_kv * rlen), jnp.float32),
            pltpu.VMEM((8, per_kv * rlen), jnp.float32),
            pltpu.VMEM((plen, per_kv * rlen), jnp.bfloat16),
            pltpu.VMEM((rlen, width), jnp.bfloat16),
            pltpu.VMEM((rlen, width), jnp.bfloat16),
            pltpu.VMEM((rlen, HD), jnp.bfloat16),
            pltpu.SemaphoreType.DMA((2,)),
            pltpu.SemaphoreType.DMA((4,)),
            pltpu.SemaphoreType.DMA,
            pltpu.SemaphoreType.DMA((2,)),
        ],
        compiler_params=pltpu.CompilerParams(vmem_limit_bytes=VMEM_BYTES),
        cost_estimate=pl.CostEstimate(flops=items << 20, bytes_accessed=1 << 16, transcendentals=0),
    )(*operands)


def pack_kernel(target, width, facts, q_ref, own_ref, out, sem):
    step = width + 2 * HD
    local = q_ref.shape[0]

    def each(act):
        def look(at, slot):
            hit = facts[GROUPS + at] == facts[target]

            @pl.when(hit)
            def _():
                for head in range(2):
                    part = pl.ds(head * width, width)
                    act(pltpu.make_async_copy(q_ref.at[at, :, part], out.at[slot, :, pl.ds(head * step, width)], sem))
                    act(pltpu.make_async_copy(
                        own_ref.at[head, at], out.at[slot, :, pl.ds(head * step + width, 2 * HD)], sem))

            return slot + hit.astype(jnp.int32)

        return lax.fori_loop(0, local, look, jnp.int32(0))

    count = each(lambda copy: copy.start())
    out[0, :, 2 * step:] = jnp.full((out.shape[1], HD), count, jnp.int32).astype(jnp.float32).astype(out.dtype)
    each(lambda copy: copy.wait())


def pack(facts, target, queries, own, width):
    return pl.pallas_call(
        functools.partial(pack_kernel, target, width),
        out_shape=jax.ShapeDtypeStruct((SLOTS, queries.shape[1], 2 * width + 5 * HD), queries.dtype),
        in_specs=[SMEM, HBM, HBM],
        out_specs=VMEM,
        scratch_shapes=[pltpu.SemaphoreType.DMA],
        compiler_params=pltpu.CompilerParams(vmem_limit_bytes=1 << 23),
    )(facts, queries, own)


def gate_kernel(*refs):
    pass


def gate(value, *others):
    return pl.pallas_call(
        gate_kernel,
        out_shape=jax.ShapeDtypeStruct(value.shape, value.dtype),
        in_specs=[HBM] + [SMEM if other.ndim == 1 else HBM for other in others],
        out_specs=HBM,
        input_output_aliases={0: 0},
    )(value, *others)


def cut_kernel(pair, out0, out1, sem):
    copies = [pltpu.make_async_copy(pair.at[head], out, sem.at[head]) for head, out in enumerate((out0, out1))]
    for copy in copies:
        copy.start()
    for copy in copies:
        copy.wait()


def cut(pair):
    shape = jax.ShapeDtypeStruct(pair.shape[1:], pair.dtype)
    return pl.pallas_call(
        cut_kernel,
        out_shape=[shape, shape],
        in_specs=[HBM],
        out_specs=[VMEM, VMEM],
        scratch_shapes=[pltpu.SemaphoreType.DMA((2,))],
        compiler_params=pltpu.CompilerParams(vmem_limit_bytes=1 << 23),
    )(pair)


def merge_kernel(target, head, facts, groups, lengths, got, old, out, ready, sem):
    rlen, width = got.shape[1:]
    token_at = lax.broadcasted_iota(jnp.int32, (rlen, HD), 0)

    def each(act, fill):
        def look(at, slot):
            hit = groups[at] == facts[target]

            @pl.when(hit)
            def _():
                if fill:
                    alive = token_at < lengths[at]
                    for lane in range(0, width, HD):
                        part = got[slot, :, lane:lane + HD]
                        ready[slot, :, lane:lane + HD] = jnp.where(alive, part, jnp.zeros_like(part))
                act(pltpu.make_async_copy(ready.at[slot], out.at[at, :, pl.ds(head * width, width)], sem))

            return slot + hit.astype(jnp.int32)

        lax.fori_loop(0, groups.shape[0], look, jnp.int32(0))

    each(lambda copy: copy.start(), True)
    each(lambda copy: copy.wait(), False)


def merge(facts, target, groups, lengths, got, out, head):
    return pl.pallas_call(
        functools.partial(merge_kernel, target, head),
        out_shape=jax.ShapeDtypeStruct(out.shape, out.dtype),
        in_specs=[SMEM, SMEM, SMEM, VMEM, HBM],
        out_specs=HBM,
        input_output_aliases={4: 0},
        scratch_shapes=[pltpu.VMEM(got.shape, got.dtype), pltpu.SemaphoreType.DMA],
        compiler_params=pltpu.CompilerParams(vmem_limit_bytes=1 << 23),
    )(facts, groups, lengths, got, out)


def after(value, *others):
    return lax.optimization_barrier((value,) + others)[0]


def gathered(queries, resp_kv, prompt_kv, lengths, group_of, first_head, kv_needed, per_kv):
    out = jax.ShapeDtypeStruct(queries.shape, jnp.bfloat16)
    facts = jnp.concatenate([jnp.zeros((GROUPS,), jnp.int32), group_of, lengths])
    for head in range(kv_needed):
        mine = lax.dynamic_index_in_dim(prompt_kv, first_head + head, 2, keepdims=False)
        own = lax.dynamic_index_in_dim(resp_kv, first_head + head, 2, keepdims=False)[None]
        whole = lax.all_gather(mine, "seq", axis=0, tiled=True)
        out, _ = attend(facts, queries, own, [whole], [out], head, per_kv, None, 16, fresh=head == 0)
    return out


def relayed(queries, resp_kv, prompt_kv, lengths, group_of, first_head, per_kv):
    me = lax.axis_index("seq")
    width = per_kv * HD
    middle, inward, outward = [(1, 2), (2, 1)], [(0, 1), (3, 2)], [(1, 0), (2, 3)]

    def send(pairs, value):
        return lax.ppermute(value, "seq", pairs)

    def two_heads(start):
        return lambda pairs: jnp.transpose(pairs[:, start:start + 2], (1, 0, 2))

    def two_own(start):
        return lambda pairs: jnp.transpose(pairs[:, :, start:start + 2], (2, 0, 1, 3))

    splits = prompt_kv.shape[2] // 2
    mine = lax.switch(first_head // 2, [two_heads(2 * at) for at in range(splits)], prompt_kv[0])
    inner_prompt = send(outward, mine)
    parts = cut(mine)
    across, near = [], []
    for part in parts:
        across.append(send(middle, part))
        near.append(send(inward, part))

    low = me < 2
    is_inner = (me == 1) | (me == 2)
    outer, inner = jnp.where(low, 0, 3), jnp.where(low, 1, 2)
    far_inner, far_outer = jnp.where(low, 2, 1), jnp.where(low, 3, 0)
    facts = jnp.stack([
        me,
        jnp.zeros_like(me),
        jnp.where(is_inner, -1, inner),
        jnp.full_like(me, 3),
        jnp.where(is_inner, far_inner, -1),
        jnp.ones_like(me),
        jnp.where(is_inner, far_outer, -1),
        jnp.where(is_inner, far_outer, far_inner),
        jnp.where(is_inner, 0, 1),
        jnp.where(is_inner, -1, far_outer),
        jnp.where(is_inner, outer, -1),
        jnp.full_like(me, 2),
    ]).astype(jnp.int32)
    facts = jnp.concatenate([facts, group_of, lengths])

    own = lax.switch(first_head // 2, [two_own(2 * at) for at in range(splits)], resp_kv)
    packed = pack(facts, 9, queries, own, width)
    out = jax.ShapeDtypeStruct(queries.shape, jnp.bfloat16)
    back_shape = jax.ShapeDtypeStruct((SLOTS, queries.shape[1], width), jnp.bfloat16)

    def run(cands, outs, passes, items, far=None, fresh=False, wait_for=None):
        return attend(facts, queries, own, cands, outs, 0, per_kv, passes, items, far, fresh, wait_for)

    out, token = run([mine], [out], [(False, 0, 1, 0), (False, 0, 1, 1)], 8, fresh=True, wait_for=packed)
    near[0] = gate(near[0], token)
    last = [send(middle, near[0])]
    handed = send(inward, gate(packed, near[0]))
    out, token = run([near[0]], [out], [(False, 10, 1, 0)], 4)
    across[0] = gate(across[0], token)
    far_inner_prompt = [send(outward, across[0])]
    near[1] = gate(near[1], token)
    last.append(send(middle, near[1]))
    across[1] = gate(across[1], token)
    far_inner_prompt.append(send(outward, across[1]))
    out, _ = run(
        [near[1], across[0], across[1], inner_prompt], [out],
        [(False, 2, 3, 0), (False, 2, 3, 1), (False, 10, 1, 1), (False, 4, 5, 0), (False, 4, 11, 1)], 16, wait_for=near[1])
    back = [None, None]
    out, back[0], _ = run(
        [last[0], far_inner_prompt[0]], [out, back_shape], [(True, 6, 1, 0), (False, 7, 8, 0)], 8, handed)
    back[0] = send(outward, back[0])
    out, back[1], _ = run([last[1]], [out, back_shape], [(True, 6, 1, 1)], 4, handed)
    back[1] = send(outward, back[1])
    out, _ = run([last[1], far_inner_prompt[1]], [out], [(False, 7, 8, 1)], 4)
    for head in range(2):
        out = merge(facts, 9, group_of, lengths, back[head], out, head)
    return out


def shards(queries, resp_kv, prompt_kv, lengths, group_of):
    local_heads = queries.shape[2] // HD
    group = QHEADS // KVH
    kv_needed = max(local_heads // group, 1)
    per_kv = local_heads // kv_needed
    first_head = lax.axis_index("pp") * local_heads // group
    args = (queries, resp_kv, prompt_kv, lengths, group_of, first_head)
    if lax.axis_size("seq") == 4 and kv_needed == 2 and prompt_kv.shape[0] == 1:
        return relayed(*args, per_kv)
    return gathered(*args, kv_needed, per_kv)


def solution(mesh):
    placed = (
        P(("rep", "seq"), None, ("tp", "pp")),
        P(("rep", "seq"), None, "tp", None),
        P(("rep", "seq"), None, "tp", None),
        P(("rep", "seq")),
        P(("rep", "seq")),
    )
    return jax.shard_map(
        shards,
        mesh=mesh,
        in_specs=placed,
        out_specs=P(("rep", "seq"), None, ("tp", "pp")),
        check_vma=False,
    )
```

```python
import functools
import math

import jax
import jax.numpy as jnp
from jax import lax
from jax.experimental import pallas as pl
from jax.experimental.pallas import tpu as pltpu
from jax.sharding import PartitionSpec as P

QHEADS = 64
KVH = 8
HD = 128
LOG2E = math.log2(math.e)
VMEM_BYTES = 12 * 1024 * 1024
SLOTS = 8
HBM = pl.BlockSpec(memory_space=pl.ANY)
SMEM = pl.BlockSpec(memory_space=pltpu.SMEM)
VMEM = pl.BlockSpec(memory_space=pltpu.VMEM)


TN = (((0,), (0,)), ((), ()))
BLOCK = 512
SCORE_BLOCK = 1024
CHUNK = 64
GROUPS = 12


def stacked_heads(q_tile, per_kv):
    return jnp.concatenate([q_tile[:, g * HD:(g + 1) * HD] for g in range(per_kv)], axis=0)


def own_scores(own_tile, q_cols, rlen):
    own = jnp.dot(own_tile[:, :HD], q_cols, preferred_element_type=jnp.float32)
    own_at = lax.broadcasted_iota(jnp.int32, own.shape, 0)
    token_at = lax.broadcasted_iota(jnp.int32, own.shape, 1) % rlen
    return jnp.where(own_at <= token_at, own, -1e30)


def folded(values, op):
    return op(values.reshape(values.shape[0] // 8, 8, values.shape[1]), axis=0)


def turn(q_tile, per_kv, out_ref):
    out_ref[...] = stacked_heads(q_tile, per_kv).T


def finish(acc_ref, total_ref, length, per_kv, out_ref):
    out = (acc_ref[...] * (1.0 / total_ref[0:1, :])).T
    rlen = out_ref.shape[0]
    alive = lax.broadcasted_iota(jnp.int32, (rlen, HD), 0) < length
    for g in range(per_kv):
        part = jnp.where(alive, out[g * rlen:(g + 1) * rlen, :], 0.0)
        out_ref[:, g * HD:(g + 1) * HD] = part.astype(out_ref.dtype)


def scores_and_mix(q_cols, after_own, after_keys, after_s, after_u, after_peak, now):
    plen = after_keys.shape[0]
    scale = HD ** -0.5 * LOG2E
    own = own_scores(after_own, q_cols, after_own.shape[0])
    after_u[...] = own
    after_top = folded(own, jnp.max)
    if now is not None:
        s_ref, u_ref, peak_ref, own_tile, vt_ref, p_ref, acc_ref, total_ref = now
        peak = peak_ref[...]
        part = jnp.exp2((u_ref[...] - peak[0:1, :]) * scale)
        total = folded(part, jnp.sum)
        acc = lax.dot_general(own_tile[:, HD:], part.astype(jnp.bfloat16), TN, preferred_element_type=jnp.float32)
        spread = jnp.concatenate([peak] * (CHUNK // 8), axis=0)
    for at in range(0, plen, BLOCK):
        rows = pl.ds(at, BLOCK)
        if at % SCORE_BLOCK == 0:
            score_rows = pl.ds(at, SCORE_BLOCK)
            fresh = jnp.dot(after_keys[score_rows, :], q_cols, preferred_element_type=jnp.float32)
            after_s[score_rows, :] = fresh
            after_top = jnp.maximum(after_top, folded(fresh, jnp.max))
        if now is not None:
            for chunk in range(at, at + BLOCK, CHUNK):
                part = jnp.exp2((s_ref[chunk:chunk + CHUNK, :] - spread) * scale)
                total = total + folded(part, jnp.sum)
                p_ref[chunk:chunk + CHUNK, :] = part.astype(jnp.bfloat16)
            acc = acc + jnp.dot(vt_ref[:, rows], p_ref[rows, :], preferred_element_type=jnp.float32)
    after_peak[...] = jnp.broadcast_to(jnp.max(after_top, axis=0, keepdims=True), after_peak.shape)
    if now is not None:
        acc_ref[...] = acc
        total_ref[...] = jnp.broadcast_to(jnp.sum(total, axis=0, keepdims=True), total_ref.shape)


def listed(items, cap, count, facts, local, target, source, head):
    def look(at, n):
        hit = facts[GROUPS + at] == target

        @pl.when(hit)
        def _():
            items[n] = at
            items[cap + n] = source
            items[2 * cap + n] = facts[GROUPS + local + at]
            items[3 * cap + n] = head

        return n + hit.astype(jnp.int32)

    return lax.fori_loop(0, local, look, count)


def attend_kernel(passes, n_cand, per_kv, whole_head, two, fresh, waits, *refs):
    refs = list(refs)
    facts, refs = refs[0], refs[1:]
    if two:
        x_ref, refs = refs[0], refs[1:]
    q_ref, own_ref = refs[:2]
    cands, refs = refs[2:2 + n_cand], refs[2 + n_cand + waits:]
    n_out = 2 if two else 1
    if not fresh:
        refs = refs[1:]
    outs, token, refs = refs[:n_out], refs[n_out], refs[n_out + 1:]
    items, at_slot, q_buf, own_buf, key_buf, value_buf, vt_buf, s0, s1, u0, u1, peak0, peak1, turned0, turned1, acc0, acc1, total0, total1, p_buf, o0, o1, info, q_sem, own_sem, kv_sem, o_sem = refs
    s_buf, u_buf, peak_buf, o_buf = (s0, s1), (u0, u1), (peak0, peak1), (o0, o1)
    turned, acc_buf, total_buf = (turned0, turned1), (acc0, acc1), (total0, total1)
    local = (facts.shape[0] - GROUPS) // 2
    cap = items.shape[0] // 4
    width = per_kv * HD
    stacked = passes is None

    count = jnp.int32(0)
    if stacked:
        def one_prompt(prompt, n):
            return listed(items, cap, n, facts, local, prompt, prompt, whole_head)

        count = lax.fori_loop(0, cands[0].shape[0], one_prompt, count)
    else:
        for far, target, source, head in passes:
            if not far:
                count = listed(items, cap, count, facts, local, facts[target], facts[source], head)
                continue
            notes = pltpu.make_async_copy(x_ref.at[0, :, pl.ds(2 * (width + 2 * HD), HD)], info, kv_sem)
            notes.start()
            notes.wait()
            far_head = head
            handed = jnp.max(info[0:16, :].astype(jnp.float32)).astype(jnp.int32)
            handed = jnp.where(facts[target] >= 0, jnp.minimum(handed, SLOTS), 0)

            def take(slot, n):
                items[n] = local + slot
                items[cap + n] = facts[source]
                items[2 * cap + n] = q_buf.shape[1]
                items[3 * cap + n] = far_head
                return n + 1

            count = lax.fori_loop(0, handed, take, count)

    token[0] = count

    def each_array(i, act_local, act_far):
        at = items[i]
        if not two:
            act_local(at)
            return

        @pl.when(at < local)
        def _():
            act_local(at)

        @pl.when(at >= local)
        def _():
            act_far(at - local)

    first = pl.ds(0, width)

    def lanes(i, step, skip, size):
        return pl.ds(pl.multiple_of(items[3 * cap + i] * step + skip, HD), size)

    def mine(i):
        return lanes(i, width, 0, width)

    def fetch(i):
        slot, fourth = lax.rem(i, 2), lax.rem(i, 4)

        def here(at):
            pltpu.make_async_copy(q_ref.at[at, :, mine(i)], q_buf.at[slot], q_sem.at[slot]).start()
            pltpu.make_async_copy(own_ref.at[items[3 * cap + i], at], own_buf.at[fourth], own_sem.at[fourth]).start()

        def far(at):
            pltpu.make_async_copy(x_ref.at[at, :, lanes(i, width + 2 * HD, 0, width)], q_buf.at[slot], q_sem.at[slot]).start()
            pltpu.make_async_copy(x_ref.at[at, :, lanes(i, width + 2 * HD, width, 2 * HD)], own_buf.at[fourth], own_sem.at[fourth]).start()

        each_array(i, here, far)

    def fetched(i):
        slot, fourth = lax.rem(i, 2), lax.rem(i, 4)
        pltpu.make_async_copy(q_ref.at[0, :, first], q_buf.at[slot], q_sem.at[slot]).wait()
        pltpu.make_async_copy(own_ref.at[0, 0], own_buf.at[fourth], own_sem.at[fourth]).wait()

    def store(i, slot):
        def here(at):
            pltpu.make_async_copy(o_buf[slot], outs[0].at[at, :, mine(i)], o_sem.at[slot]).start()

        def far(at):
            pltpu.make_async_copy(o_buf[slot], outs[1].at[at], o_sem.at[slot]).start()

        each_array(i, here, far)

    def stored(slot):
        pltpu.make_async_copy(o_buf[slot], outs[0].at[0, :, first], o_sem.at[slot]).wait()

    keys, values = pl.ds(0, HD), pl.ds(HD, HD)

    def ask(i, into):
        source = items[cap + i]

        def bring(pairs):
            pltpu.make_async_copy(pairs.at[:, keys], key_buf.at[into], kv_sem).start()
            pltpu.make_async_copy(pairs.at[:, values], value_buf, kv_sem).start()

        if stacked:
            bring(cands[0].at[source])
        else:
            for which in range(n_cand):
                @pl.when(source == which)
                def _():
                    bring(cands[which].at[items[3 * cap + i]] if len(cands[which].shape) == 3 else cands[which])

    def receive(into):
        for _ in range(2):
            pltpu.make_async_copy(value_buf, value_buf, kv_sem).wait()
        vt_buf[into] = value_buf[...].T

    @pl.when(count > 0)
    def _():
        ask(0, 0)
        fetch(jnp.int32(0))

        @pl.when(count > 1)
        def _():
            fetch(jnp.int32(1))

        at_slot[0] = 0
        fetched(jnp.int32(0))
        turn(q_buf[0], per_kv, turned[0])

        @pl.when(count > 2)
        def _():
            fetch(jnp.int32(2))

        @pl.when(count > 1)
        def _():
            fetched(jnp.int32(1))

        turn(q_buf[1], per_kv, turned[1])
        receive(0)
        scores_and_mix(turned[0][...], own_buf[0], key_buf.at[0], s_buf[0], u_buf[0], peak_buf[0], None)

        def one(i, slot):
            other = 1 - slot
            held = at_slot[0]
            more = i + 1 < count
            after_i = jnp.minimum(i + 1, count - 1)
            moved = more & ((items[cap + after_i] != items[cap + i]) | (items[3 * cap + after_i] != items[3 * cap + i]))
            holds = jnp.where(moved, 1 - held, held)
            at_slot[0] = holds

            @pl.when(i + 2 < count)
            def _():
                fetched(i + 2)

            @pl.when(i + 3 < count)
            def _():
                fetch(i + 3)

            @pl.when(moved)
            def _():
                ask(i + 1, holds)
                receive(holds)

            @pl.when(i >= 3)
            def _():
                stored(other)

            now = (
                s_buf[slot], u_buf[slot], peak_buf[slot], own_buf[lax.rem(i, 4)], vt_buf.at[held], p_buf,
                acc_buf[slot], total_buf[slot])
            scores_and_mix(
                turned[other][...], own_buf[lax.rem(i + 1, 4)], key_buf.at[holds],
                s_buf[other], u_buf[other], peak_buf[other], now)
            turn(q_buf[slot], per_kv, turned[slot])
            finish(acc_buf[other], total_buf[other], items[2 * cap + jnp.maximum(i - 1, 0)], per_kv, o_buf[other])

            @pl.when(i >= 1)
            def _():
                store(i - 1, other)

        def pair(j, _):
            one(2 * j, 0)

            @pl.when(2 * j + 1 < count)
            def _():
                one(2 * j + 1, 1)

            return 0

        lax.fori_loop(0, lax.div(count + 1, 2), pair, 0)
        final = count - 1
        for slot in range(2):
            @pl.when(lax.rem(final, 2) == slot)
            def _():
                @pl.when(final >= 2)
                def _():
                    stored(slot)

                finish(acc_buf[slot], total_buf[slot], items[2 * cap + final], per_kv, o_buf[slot])
                store(final, slot)

        stored(0)

        @pl.when(count > 1)
        def _():
            stored(1)


def attend(facts, queries, own, cands, outs, head, per_kv, passes, items, far=None, fresh=False, wait_for=None):
    rlen = queries.shape[1]
    plen = cands[0].shape[-2]
    width = per_kv * HD
    small = [facts]
    large = ([far] if far is not None else []) + [queries, own] + cands
    operands = small + large + ([] if wait_for is None else [wait_for])
    aliases = {}
    if not fresh:
        aliases = {len(operands): 0}
        operands = operands + [outs[0]]
    cap = 2 * queries.shape[0] + (SLOTS if far is not None else 0)
    return pl.pallas_call(
        functools.partial(attend_kernel, passes, len(cands), per_kv, head, far is not None, fresh, wait_for is not None),
        out_shape=[jax.ShapeDtypeStruct(o.shape, o.dtype) for o in outs] + [jax.ShapeDtypeStruct((1,), jnp.int32)],
        in_specs=[SMEM] * len(small) + [HBM] * (len(operands) - len(small)),
        out_specs=[HBM] * len(outs) + [SMEM],
        input_output_aliases=aliases,
        scratch_shapes=[
            pltpu.SMEM((4 * cap,), jnp.int32),
            pltpu.SMEM((1,), jnp.int32),
            pltpu.VMEM((2, rlen, width), jnp.bfloat16),
            pltpu.VMEM((4, rlen, 2 * HD), jnp.bfloat16),
            pltpu.VMEM((2, plen, HD), jnp.bfloat16),
            pltpu.VMEM((plen, HD), jnp.bfloat16),
            pltpu.VMEM((2, HD, plen), jnp.bfloat16),
            pltpu.VMEM((plen, per_kv * rlen), jnp.float32),
            pltpu.VMEM((plen, per_kv * rlen), jnp.float32),
            pltpu.VMEM((rlen, per_kv * rlen), jnp.float32),
            pltpu.VMEM((rlen, per_kv * rlen), jnp.float32),
            pltpu.VMEM((8, per_kv * rlen), jnp.float32),
            pltpu.VMEM((8, per_kv * rlen), jnp.float32),
            pltpu.VMEM((HD, per_kv * rlen), jnp.bfloat16),
            pltpu.VMEM((HD, per_kv * rlen), jnp.bfloat16),
            pltpu.VMEM((HD, per_kv * rlen), jnp.float32),
            pltpu.VMEM((HD, per_kv * rlen), jnp.float32),
            pltpu.VMEM((8, per_kv * rlen), jnp.float32),
            pltpu.VMEM((8, per_kv * rlen), jnp.float32),
            pltpu.VMEM((plen, per_kv * rlen), jnp.bfloat16),
            pltpu.VMEM((rlen, width), jnp.bfloat16),
            pltpu.VMEM((rlen, width), jnp.bfloat16),
            pltpu.VMEM((rlen, HD), jnp.bfloat16),
            pltpu.SemaphoreType.DMA((2,)),
            pltpu.SemaphoreType.DMA((4,)),
            pltpu.SemaphoreType.DMA,
            pltpu.SemaphoreType.DMA((2,)),
        ],
        compiler_params=pltpu.CompilerParams(vmem_limit_bytes=VMEM_BYTES),
        cost_estimate=pl.CostEstimate(flops=items << 20, bytes_accessed=1 << 16, transcendentals=0),
    )(*operands)


def pack_kernel(target, width, facts, q_ref, own_ref, out, sem):
    step = width + 2 * HD
    local = q_ref.shape[0]

    def each(act):
        def look(at, slot):
            hit = facts[GROUPS + at] == facts[target]

            @pl.when(hit)
            def _():
                for head in range(2):
                    part = pl.ds(head * width, width)
                    act(pltpu.make_async_copy(q_ref.at[at, :, part], out.at[slot, :, pl.ds(head * step, width)], sem))
                    act(pltpu.make_async_copy(
                        own_ref.at[head, at], out.at[slot, :, pl.ds(head * step + width, 2 * HD)], sem))

            return slot + hit.astype(jnp.int32)

        return lax.fori_loop(0, local, look, jnp.int32(0))

    count = each(lambda copy: copy.start())
    out[0, :, 2 * step:] = jnp.full((out.shape[1], HD), count, jnp.int32).astype(jnp.float32).astype(out.dtype)
    each(lambda copy: copy.wait())


def pack(facts, target, queries, own, width):
    return pl.pallas_call(
        functools.partial(pack_kernel, target, width),
        out_shape=jax.ShapeDtypeStruct((SLOTS, queries.shape[1], 2 * width + 5 * HD), queries.dtype),
        in_specs=[SMEM, HBM, HBM],
        out_specs=VMEM,
        scratch_shapes=[pltpu.SemaphoreType.DMA],
        compiler_params=pltpu.CompilerParams(vmem_limit_bytes=1 << 23),
    )(facts, queries, own)


def gate_kernel(*refs):
    pass


def gate(value, *others):
    return pl.pallas_call(
        gate_kernel,
        out_shape=jax.ShapeDtypeStruct(value.shape, value.dtype),
        in_specs=[HBM] + [SMEM if other.ndim == 1 else HBM for other in others],
        out_specs=HBM,
        input_output_aliases={0: 0},
    )(value, *others)


def cut_kernel(pair, out0, out1, sem):
    copies = [pltpu.make_async_copy(pair.at[head], out, sem.at[head]) for head, out in enumerate((out0, out1))]
    for copy in copies:
        copy.start()
    for copy in copies:
        copy.wait()


def cut(pair):
    shape = jax.ShapeDtypeStruct(pair.shape[1:], pair.dtype)
    return pl.pallas_call(
        cut_kernel,
        out_shape=[shape, shape],
        in_specs=[HBM],
        out_specs=[VMEM, VMEM],
        scratch_shapes=[pltpu.SemaphoreType.DMA((2,))],
        compiler_params=pltpu.CompilerParams(vmem_limit_bytes=1 << 23),
    )(pair)


def merge_kernel(target, head, facts, groups, lengths, got, old, out, ready, sem):
    rlen, width = got.shape[1:]
    token_at = lax.broadcasted_iota(jnp.int32, (rlen, HD), 0)

    def each(act, fill):
        def look(at, slot):
            hit = groups[at] == facts[target]

            @pl.when(hit)
            def _():
                if fill:
                    alive = token_at < lengths[at]
                    for lane in range(0, width, HD):
                        part = got[slot, :, lane:lane + HD]
                        ready[slot, :, lane:lane + HD] = jnp.where(alive, part, jnp.zeros_like(part))
                act(pltpu.make_async_copy(ready.at[slot], out.at[at, :, pl.ds(head * width, width)], sem))

            return slot + hit.astype(jnp.int32)

        lax.fori_loop(0, groups.shape[0], look, jnp.int32(0))

    each(lambda copy: copy.start(), True)
    each(lambda copy: copy.wait(), False)


def merge(facts, target, groups, lengths, got, out, head):
    return pl.pallas_call(
        functools.partial(merge_kernel, target, head),
        out_shape=jax.ShapeDtypeStruct(out.shape, out.dtype),
        in_specs=[SMEM, SMEM, SMEM, VMEM, HBM],
        out_specs=HBM,
        input_output_aliases={4: 0},
        scratch_shapes=[pltpu.VMEM(got.shape, got.dtype), pltpu.SemaphoreType.DMA],
        compiler_params=pltpu.CompilerParams(vmem_limit_bytes=1 << 23),
    )(facts, groups, lengths, got, out)


def after(value, *others):
    return lax.optimization_barrier((value,) + others)[0]


def gathered(queries, resp_kv, prompt_kv, lengths, group_of, first_head, kv_needed, per_kv):
    out = jax.ShapeDtypeStruct(queries.shape, jnp.bfloat16)
    facts = jnp.concatenate([jnp.zeros((GROUPS,), jnp.int32), group_of, lengths])
    for head in range(kv_needed):
        mine = lax.dynamic_index_in_dim(prompt_kv, first_head + head, 2, keepdims=False)
        own = lax.dynamic_index_in_dim(resp_kv, first_head + head, 2, keepdims=False)[None]
        whole = lax.all_gather(mine, "seq", axis=0, tiled=True)
        out, _ = attend(facts, queries, own, [whole], [out], head, per_kv, None, 16, fresh=head == 0)
    return out


def relayed(queries, resp_kv, prompt_kv, lengths, group_of, first_head, per_kv):
    me = lax.axis_index("seq")
    width = per_kv * HD
    middle, inward, outward = [(1, 2), (2, 1)], [(0, 1), (3, 2)], [(1, 0), (2, 3)]

    def send(pairs, value):
        return lax.ppermute(value, "seq", pairs)

    def two_heads(start):
        return lambda pairs: jnp.transpose(pairs[:, start:start + 2], (1, 0, 2))

    def two_own(start):
        return lambda pairs: jnp.transpose(pairs[:, :, start:start + 2], (2, 0, 1, 3))

    splits = prompt_kv.shape[2] // 2
    mine = lax.switch(first_head // 2, [two_heads(2 * at) for at in range(splits)], prompt_kv[0])
    inner_prompt = send(outward, mine)
    parts = cut(mine)
    across, near = [], []
    for part in parts:
        across.append(send(middle, part))
        near.append(send(inward, part))

    low = me < 2
    is_inner = (me == 1) | (me == 2)
    outer, inner = jnp.where(low, 0, 3), jnp.where(low, 1, 2)
    far_inner, far_outer = jnp.where(low, 2, 1), jnp.where(low, 3, 0)
    facts = jnp.stack([
        me,
        jnp.zeros_like(me),
        jnp.where(is_inner, -1, inner),
        jnp.full_like(me, 3),
        jnp.where(is_inner, far_inner, -1),
        jnp.ones_like(me),
        jnp.where(is_inner, far_outer, -1),
        jnp.where(is_inner, far_outer, far_inner),
        jnp.where(is_inner, 0, 1),
        jnp.where(is_inner, -1, far_outer),
        jnp.where(is_inner, outer, -1),
        jnp.full_like(me, 2),
    ]).astype(jnp.int32)
    facts = jnp.concatenate([facts, group_of, lengths])

    own = lax.switch(first_head // 2, [two_own(2 * at) for at in range(splits)], resp_kv)
    packed = pack(facts, 9, queries, own, width)
    out = jax.ShapeDtypeStruct(queries.shape, jnp.bfloat16)
    back_shape = jax.ShapeDtypeStruct((SLOTS, queries.shape[1], width), jnp.bfloat16)

    def run(cands, outs, passes, items, far=None, fresh=False, wait_for=None):
        return attend(facts, queries, own, cands, outs, 0, per_kv, passes, items, far, fresh, wait_for)

    out, token = run([mine], [out], [(False, 0, 1, 0), (False, 0, 1, 1)], 8, fresh=True, wait_for=packed)
    near[0] = gate(near[0], token)
    last = [send(middle, near[0])]
    handed = send(inward, gate(packed, near[0]))
    out, token = run([near[0]], [out], [(False, 10, 1, 0)], 4)
    across[0] = gate(across[0], token, inner_prompt)
    far_inner_prompt = [send(outward, across[0])]
    near[1] = gate(near[1], token)
    last.append(send(middle, near[1]))
    across[1] = gate(across[1], token)
    far_inner_prompt.append(send(outward, across[1]))
    out, _ = run(
        [near[1], across[0], across[1], inner_prompt], [out],
        [(False, 2, 3, 0), (False, 2, 3, 1), (False, 10, 1, 1), (False, 4, 5, 0), (False, 4, 11, 1)], 16, wait_for=near[1])
    back = [None, None]
    out, back[0], _ = run(
        [last[0], far_inner_prompt[0]], [out, back_shape], [(True, 6, 1, 0), (False, 7, 8, 0)], 8, handed)
    back[0] = send(outward, back[0])
    out, back[1], _ = run([last[1]], [out, back_shape], [(True, 6, 1, 1)], 4, handed)
    back[1] = send(outward, back[1])
    out, _ = run([last[1], far_inner_prompt[1]], [out], [(False, 7, 8, 1)], 4)
    for head in range(2):
        out = merge(facts, 9, group_of, lengths, back[head], out, head)
    return out


def shards(queries, resp_kv, prompt_kv, lengths, group_of):
    local_heads = queries.shape[2] // HD
    group = QHEADS // KVH
    kv_needed = max(local_heads // group, 1)
    per_kv = local_heads // kv_needed
    first_head = lax.axis_index("pp") * local_heads // group
    args = (queries, resp_kv, prompt_kv, lengths, group_of, first_head)
    if lax.axis_size("seq") == 4 and kv_needed == 2 and prompt_kv.shape[0] == 1:
        return relayed(*args, per_kv)
    return gathered(*args, kv_needed, per_kv)


def solution(mesh):
    placed = (
        P(("rep", "seq"), None, ("tp", "pp")),
        P(("rep", "seq"), None, "tp", None),
        P(("rep", "seq"), None, "tp", None),
        P(("rep", "seq")),
        P(("rep", "seq")),
    )
    return jax.shard_map(
        shards,
        mesh=mesh,
        in_specs=placed,
        out_specs=P(("rep", "seq"), None, ("tp", "pp")),
        check_vma=False,
    )
```
